32 devices in a mesh: rows: 8 (over z, y), state: 4 (over x, core).
Axes of the slice: x: 2, y: 2, z: 4, core: 2. Of those that a mesh axis runs over, the one named last changes fastest.
Arguments:
- inputs: bfloat16 [32, 512, 512], P('rows', None, 'state'), may hold values from -6 to 6
- bucket: int32 [32], P('rows'), may hold values from 0 to 3, as said below
- lengths: int32 [32], P('rows'), may hold values from 128 to 512
- nu_log: float32 [256], P('state'), may hold values from -11.7 to -3.4
- theta_log: float32 [256], P('state'), may hold values from -4 to 1.1
- gamma_log: float32 [256], P('state'), may hold values from -8 to 0
- in_proj: bfloat16 [512, 2, 256], P(None, None, 'state'), may hold values from -0.25 to 0.25
- out_proj: bfloat16 [2, 256, 512], P(None, 'state'), may hold values from -0.25 to 0.25
- skip: float32 [512], P('state'), may hold values from -4 to 4
- norm_gain: float32 [512], replicated, may hold values from 0.25 to 1.75
- norm_bias: float32 [512], replicated, may hold values from -3 to 3
- glu_weight: bfloat16 [512, 2, 512], P(None, None, 'state'), may hold values from -0.25 to 0.25
- glu_bias: float32 [2, 512], P(None, 'state'), may hold values from -3 to 3
- output_cotangent: bfloat16 [32, 512, 512], P('rows', None, 'state'), may hold values from -6 to 6
Outputs:
- outputs: bfloat16 [32, 512, 512], P('rows', None, 'state')
- d_inputs: float32 [32, 512, 512], P('rows', None, 'state')
- d_nu_log: float32 [256], P('state')
- d_theta_log: float32 [256], P('state')
- d_gamma_log: float32 [256], P('state')
- d_in_proj: float32 [512, 2, 256], P('rows', None, 'state')
- d_out_proj: float32 [2, 256, 512], P(None, 'state', 'rows')
- d_skip: float32 [512], P('state')
- d_norm_gain: float32 [512], replicated
- d_norm_bias: float32 [512], replicated
- d_glu_weight: float32 [512, 2, 512], P('rows', None, 'state')
- d_glu_bias: float32 [2, 512], P(None, 'state')
The draws below stay inside these ranges and needn't reach their ends.
Inputs may be any that keep to these rules, and one draw needn't show every extreme that they name: A row of bucket 0 stands alone; a row of bucket k > 0 takes its start from the latest earlier row of bucket k.
All inputs are finite; a program needn't handle non-finite values.
Results may differ from the reference program's by a relative error of at most 0.012.
Values may be sent and summed in bfloat16 or wider, within the bound.
A program may use at most 128 MiB of HBM per device.

```python
import jax
import jax.numpy as jnp
from jax import lax

H = 512
N = 256
SEQ = 512
ROWS_DEV = 4
LONGS = 3
NROWS = 32
CHAIN = 4096


def decay_rates(key, share):
    pick_key, level_key = jax.random.split(key)
    slow = jax.random.uniform(pick_key, (N,)) < share
    level = jax.random.uniform(level_key, (N,))
    bottom = jnp.log(0.3 / CHAIN)
    middle = jnp.log(2.3 / CHAIN)
    summit = jnp.log(1.0 / 30.0)
    slow_log = bottom + level * (middle - bottom)
    fast_log = middle + level * (summit - middle)
    return jnp.where(slow, slow_log, fast_log)


def draw_nu_log(key, part):
    rates = decay_rates(key, 0.5)
    return rates.astype(jnp.float32)


def draw_gamma_log(key, part):
    rates = decay_rates(key, 0.5)
    key = jax.random.fold_in(key, 7)
    noise = jax.random.uniform(key, (N,), minval=-0.4, maxval=0.4)
    return (0.5 * jnp.log(-jnp.expm1(-2.0 * jnp.exp(rates))) + noise).astype(jnp.float32)


def draw_bucket(key, part):
    key = jax.random.fold_in(key, 3)
    slot_key, star_key, other_key = jax.random.split(key, 3)
    groups = NROWS // ROWS_DEV
    slots = jax.random.randint(slot_key, (groups, 1), 0, ROWS_DEV)
    chosen = jax.random.randint(star_key, (), 1, LONGS + 1)
    others = jax.random.randint(other_key, (groups, ROWS_DEV), 0, 4 * LONGS)
    others = jnp.where(others < LONGS, others + 1, 0)
    places = jnp.arange(ROWS_DEV)[None, :]
    return jnp.where(places == slots, chosen, others).reshape(NROWS).astype(jnp.int32)


def touch_ends(values, rng, low, top_value):
    index_at = [jax.random.randint(jax.random.fold_in(rng, axis), (), 0, length) for axis, length in enumerate(values.shape)]
    main_axis = values.shape.index(max(values.shape))
    neighbour = index_at[:main_axis] + [(index_at[main_axis] + 1) % values.shape[main_axis]] + index_at[main_axis + 1:]
    return values.at[tuple(index_at)].set(low).at[tuple(neighbour)].set(top_value)


def level_of(key, dims, cuts, smallest, high):
    def one(dim, shards_of):
        steps = jax.random.uniform(jax.random.fold_in(jax.random.fold_in(key, 6), dim), (shards_of,), jnp.float32, smallest / len(cuts), high / len(cuts))
        return jnp.repeat(jnp.exp(steps), dims[dim] // shards_of).reshape((-1,) + (1,) * (len(dims) - dim - 1))

    level = one(*cuts[0])
    for cut in cuts[1:]:
        level = level * one(*cut)
    return level


def gaussian(stream_key, shape, spread, most, pieces=(), kind=jnp.bfloat16):
    values = jax.random.normal(stream_key, shape, jnp.float32) * spread
    if len(pieces) > 0:
        values = level_of(stream_key, shape, pieces, -0.22, 0.18) * values
    return jnp.clip(values, min=-most, max=most).astype(kind)


def setup_inputs(seed: int = 0) -> dict:
    arg_keys = jax.random.split(jax.random.key(seed), 15)
    return {
        "inputs": gaussian(arg_keys[0], (NROWS, SEQ, H), 1.0, 6.0, ((0, 8), (2, 4))),
        "bucket": draw_bucket(jax.random.fold_in(arg_keys[14], 71), 0),
        "lengths": touch_ends(jax.random.randint(arg_keys[2], (NROWS,), SEQ // 4, SEQ + 1), jax.random.fold_in(arg_keys[2], 1), SEQ // 4, SEQ).astype(jnp.int32),
        "nu_log": draw_nu_log(jax.random.fold_in(arg_keys[14], 71), 0),
        "theta_log": jnp.clip(-4.0 + 5.1 * jax.random.uniform(arg_keys[4], (N,), jnp.float32) ** level_of(arg_keys[4], (N,), ((0, 4),), -0.2, 0.2), -4.0, 1.1),
        "gamma_log": draw_gamma_log(jax.random.fold_in(arg_keys[14], 71), 0),
        "in_proj": gaussian(arg_keys[6], (H, 2, N), H ** -0.5, 0.25, ((2, 4),)),
        "out_proj": gaussian(arg_keys[7], (2, N, H), (2 * N) ** -0.5, 0.25, ((1, 4),)),
        "skip": gaussian(arg_keys[8], (H,), 1.0, 4.0, ((0, 4),), jnp.float32),
        "norm_gain": jnp.clip(1.0 + 0.15 * jax.random.normal(arg_keys[9], (H,), jnp.float32), 0.25, 1.75),
        "norm_bias": gaussian(arg_keys[10], (H,), 0.5, 3.0, (), jnp.float32),
        "glu_weight": gaussian(arg_keys[11], (H, 2, H), H ** -0.5, 0.25, ((2, 4),)),
        "glu_bias": gaussian(arg_keys[12], (2, H), 0.5, 3.0, ((1, 4),), jnp.float32),
        "output_cotangent": gaussian(arg_keys[13], (NROWS, SEQ, H), 1.0, 6.0, ((0, 8), (2, 4))),
    }


epsilon = 1e-05

@jax.custom_vjp
def low(v):
    return lax.optimization_barrier(v.astype(jnp.bfloat16)).astype(jnp.float32)

@jax.custom_vjp
def low_back(v):
    return v

def low_keep(v):
    return (low(v), None)

def low_pass(kept, grad):
    return (grad,)

def back_keep(v):
    return (v, None)

def back_low(kept, grad):
    return (low(grad),)
low.defvjp(low_keep, low_pass)
low_back.defvjp(back_keep, back_low)

def combine(earlier, following_step):
    left_real, left_imaginary, first_real, first_imaginary = earlier
    right_real, right_imaginary, second_real, second_imaginary = following_step
    return (right_real * left_real - right_imaginary * left_imaginary, right_real * left_imaginary + right_imaginary * left_real, right_real * first_real - right_imaginary * first_imaginary + second_real, right_real * first_imaginary + right_imaginary * first_real + second_imaginary)

def row_pass(weights, states, row, ident, length):
    nu_log, theta_log, gamma_log, in_proj, out_proj, skip, norm_gain, norm_bias, glu_weight, glu_bias = weights
    state_re, state_im = states
    mean = lax.optimization_barrier(jnp.mean(row, -1, keepdims=True))
    centred = row - mean
    inverse = lax.rsqrt(lax.optimization_barrier(jnp.mean(centred * centred, -1, keepdims=True)) + epsilon)
    normed = centred * inverse
    mixed_in = normed * norm_gain + norm_bias
    proj = low_back(jnp.dot(low(mixed_in), in_proj.reshape(H, 2 * N), precision=lax.Precision.HIGHEST))
    magnitude = jnp.exp(-jnp.exp(nu_log))
    angle = jnp.exp(theta_log)
    lam_re = magnitude * jnp.cos(angle)
    lam_im = magnitude * jnp.sin(angle)
    gamma_factor = jnp.exp(gamma_log)
    valid_token = (jnp.arange(SEQ) < length)[:, None]
    factor_re = jnp.where(valid_token, lam_re, 1.0)
    factor_im = jnp.where(valid_token, lam_im, 0.0)
    forcing_real = jnp.where(valid_token, gamma_factor * proj[:, :N], 0.0)
    forcing_imaginary = jnp.where(valid_token, gamma_factor * proj[:, N:], 0.0)
    prod_re, prod_im, local_re, local_im = lax.associative_scan(combine, (factor_re, factor_im, forcing_real, forcing_imaginary), axis=0)
    hit = (jnp.arange(1, LONGS + 1) == ident)[:, None]
    start_re = lax.optimization_barrier(jnp.sum(jnp.where(hit, state_re, 0.0), 0))
    start_im = lax.optimization_barrier(jnp.sum(jnp.where(hit, state_im, 0.0), 0))
    hidden_re = local_re + prod_re * start_re - prod_im * start_im
    hidden_im = local_im + prod_re * start_im + prod_im * start_re
    new_re = jnp.where(hit, hidden_re[-1][None, :], state_re)
    new_im = jnp.where(hit, hidden_im[-1][None, :], state_im)
    flat = low(jnp.concatenate([hidden_re, -hidden_im], -1))
    rec = low_back(jnp.dot(flat, out_proj.reshape(2 * N, H), precision=lax.Precision.HIGHEST))
    mixed = rec + skip * mixed_in
    act = low(jax.nn.gelu(mixed, approximate=False))
    pre = low_back(jnp.dot(act, glu_weight.reshape(H, 2 * H), precision=lax.Precision.HIGHEST) + glu_bias.reshape(2 * H))
    result = jnp.where(valid_token, row + pre[:, :H] * jax.nn.sigmoid(pre[:, H:]), 0.0)
    return ((new_re, new_im), result)

def reference(inputs, bucket, lengths, nu_log, theta_log, gamma_log, in_proj, out_proj, skip, norm_gain, norm_bias, glu_weight, glu_bias, output_cotangent):
    weights = (nu_log, theta_log, gamma_log, in_proj.astype(jnp.float32), out_proj.astype(jnp.float32), skip, norm_gain, norm_bias, glu_weight.astype(jnp.float32), glu_bias)

    def forward(rows_in, params):

        def advance(states, item):
            row, ident, length = item
            return jax.checkpoint(row_pass)(params, states, row, ident, length)
        zeros = jnp.zeros((LONGS, N), jnp.float32)
        final, results = lax.scan(advance, (zeros, zeros), (rows_in, bucket, lengths))
        return results
    results, pullback = jax.vjp(forward, inputs.astype(jnp.float32), weights)
    grad_in, grads = pullback(output_cotangent.astype(jnp.float32))
    return (results.astype(jnp.bfloat16), grad_in, grads[0], grads[1], grads[2], grads[3], grads[4], grads[5], grads[6], grads[7], grads[8], grads[9])
```

```python
import functools
import math
from types import SimpleNamespace

import jax
import jax.numpy as jnp
from jax import lax
from jax.experimental import pallas as pl
from jax.experimental.pallas import tpu as pltpu
from jax.sharding import PartitionSpec as P

LONGS = 3

epsilon = 1e-05

F32 = jnp.float32
BF16 = jnp.bfloat16
MESH = pl.DeviceIdType.MESH
ROWS, STATE = "rows", "state"
SUB = 8
LANES = 128
HALF = LANES // 2
CHUNK = 64

OWN_X, OWN_WIN, OWN_WOUT, OWN_WGLU, OWN_C, OWN_PS, OWN_PR, OWN_OUT, OWN_DIN = range(9)
PAR_S, PAR_R, X, WIN, WOUT, WGLU, C, CF, CB, OUT, DIN, SM, SN, G1 = range(14)


def loop(count, body, unroll=1):
    def step(i, carry):
        body(i)
        return carry

    lax.fori_loop(0, count, step, 0, unroll=unroll)


def nn(a, b):
    return lax.dot_general(a, b, (((1,), (0,)), ((), ())), preferred_element_type=F32)


def nt(a, b):
    return lax.dot_general(a, b, (((1,), (1,)), ((), ())), preferred_element_type=F32)


def tn(a, b):
    return lax.dot_general(a, b, (((0,), (0,)), ((), ())), preferred_element_type=F32)


def cmul(a, b):
    return a[0] * b[0] - a[1] * b[1], a[0] * b[1] + a[1] * b[0]


def conj_mul(a, b):
    return a[0] * b[0] + a[1] * b[1], a[0] * b[1] - a[1] * b[0]


def swap_halves(u, v, low):
    return (
        jnp.where(low, u, pltpu.roll(v, HALF, 1)),
        jnp.where(low, pltpu.roll(u, HALF, 1), v),
    )


def fold(x):
    return jnp.sum(x.reshape(x.shape[0] // SUB, SUB, x.shape[1]), axis=0)


def block_kernel(dims, *refs):
    R, S, T, H, W, gdt = dims.R, dims.S, dims.T, dims.H, dims.W, dims.gdt
    NR, NG, R2, HB, L = R * S, S // 2, R // 2, H // R, T // SUB
    NP = NG * R2
    BITS = T.bit_length()
    (inputs, cot, w_in, w_out, w_glu, par, gain_ref, bias_ref) = refs[:8]
    (out_ref, din_ref, gsum, vec) = refs[8:12]
    total = len(dims.names)
    v = SimpleNamespace(**dict(zip(dims.names, refs[12 : 12 + total])))
    g_glu, g_out, g_in = (
        SimpleNamespace(full=a, r1=b, a1=c, r2=d, a2=e, r3=f, step=G1 + 3 * i)
        for i, (a, b, c, d, e, f) in enumerate(
            refs[12 + total + 6 * i : 18 + total + 6 * i] for i in range(3)
        )
    )

    me_r, me_s = lax.axis_index(ROWS), lax.axis_index(STATE)
    me = me_r * S + me_s

    def cols(i, width):
        return pl.ds(pl.multiple_of(i * width, LANES), width)

    def wait_bytes(ref, which, arrived):
        pltpu.make_async_copy(ref, ref, (v.received if arrived else v.sent).at[which]).wait()

    def send(src, dst, which, target):
        pltpu.make_async_remote_copy(
            src_ref=src,
            dst_ref=dst,
            send_sem=v.sent.at[which],
            recv_sem=v.received.at[which],
            device_id=target,
            device_id_type=MESH,
        ).start()

    def to_state(src_of, dst, which):
        for j in (2, 3, 1) if S == 4 else range(1, S):
            t = lax.rem(me_s + j, S)
            send(src_of(t), dst, which, {STATE: t})

    own = [
        (inputs.at[me_s], v.xin.at[:, cols(me_s, W)], OWN_X),
        (w_in, v.win.at[:, cols(me_s, LANES)], OWN_WIN),
        (w_out, v.wout.at[pl.ds(pl.multiple_of(me_s * LANES, LANES), LANES), :], OWN_WOUT),
        (w_glu, v.wglu.at[:, cols(me_s, 2 * W)], OWN_WGLU),
        (cot.at[me_s], v.cin.at[:, cols(me_s, W)], OWN_C),
        (par, v.par_s.at[me_s], OWN_PS),
        (par, v.par_r.at[me_r], OWN_PR),
    ]
    own = {which: pltpu.make_async_copy(a, b, v.here.at[which]) for a, b, which in own}
    for copy in own.values():
        copy.start()

    barrier = pltpu.get_barrier_semaphore()

    def greet(d, carry):
        t = lax.rem(me + d, NR)
        pl.semaphore_signal(
            barrier,
            inc=1,
            device_id={ROWS: lax.div(t, S), STATE: lax.rem(t, S)},
            device_id_type=MESH,
        )
        return carry

    lax.fori_loop(1, NR, greet, 0)
    pl.semaphore_wait(barrier, NR - 1)

    to_state(lambda t: par, v.par_s.at[me_s], PAR_S)

    def par_rows(d, carry):
        send(par, v.par_r.at[me_r], PAR_R, {ROWS: lax.rem(me_r + d, R)})
        return carry

    lax.fori_loop(1, R, par_rows, 0)
    to_state(lambda t: inputs.at[t], v.xin.at[:, cols(me_s, W)], X)
    to_state(lambda t: w_in, v.win.at[:, cols(me_s, LANES)], WIN)
    to_state(
        lambda t: w_out,
        v.wout.at[pl.ds(pl.multiple_of(me_s * LANES, LANES), LANES), :],
        WOUT,
    )
    to_state(lambda t: w_glu, v.wglu.at[:, cols(me_s, 2 * W)], WGLU)
    to_state(lambda t: cot.at[t], v.cin.at[:, cols(me_s, W)], C)

    line = lax.broadcasted_iota(jnp.int32, (CHUNK, T), 0)
    place = lax.broadcasted_iota(jnp.int32, (CHUNK, T), 1)

    def orders(i):
        base = pl.multiple_of(i * CHUNK, CHUNK)
        at = line + base
        v.perm[pl.ds(base, CHUNK), :] = (
            place == lax.rem(at, SUB) * L + lax.div(at, SUB)
        ).astype(F32).astype(BF16)
        v.back[pl.ds(base, CHUNK), :] = (
            at == lax.rem(place, SUB) * L + lax.div(place, SUB)
        ).astype(F32).astype(BF16)

    loop(T // CHUNK, orders)

    low = lax.broadcasted_iota(jnp.int32, (SUB, LANES), 1) < HALF
    low1 = lax.broadcasted_iota(jnp.int32, (1, LANES), 1) < HALF
    sub = lax.broadcasted_iota(jnp.int32, (SUB, LANES), 0)

    own[OWN_PS].wait()
    own[OWN_PR].wait()
    wait_bytes(v.par_s.at[pl.ds(0, S - 1)], PAR_S, True)
    wait_bytes(v.par_r.at[pl.ds(0, R - 1)], PAR_R, True)
    par_s, par_r = v.par_s, v.par_r
    lam, gam = [], []
    for a in range(NG):
        lam.append(swap_halves(par_s[2 * a, 0:1, :], par_s[2 * a + 1, 0:1, :], low1))
        gam.append(swap_halves(par_s[2 * a, 1:2, :], par_s[2 * a + 1, 1:2, :], low1)[0])
    skip = jnp.concatenate([par_s[s, 2:3, :] for s in range(S)], axis=1)
    gain, bias = gain_ref[...], bias_ref[...]
    power = [[(jnp.broadcast_to(l[0], (SUB, LANES)), jnp.broadcast_to(l[1], (SUB, LANES))) for l in lam]]
    for _ in range(BITS - 1):
        power.append([cmul(p, p) for p in power[-1]])
    for b in range(BITS):
        for a in range(NG):
            for c in range(2):
                v.pows[b, a, c] = power[b][a][c]

    def raised(exponent, bits=BITS):
        result = [(jnp.ones((SUB, LANES), F32), jnp.zeros((SUB, LANES), F32)) for _ in range(NG)]
        for b in range(bits):
            hit = (lax.shift_right_logical(exponent, b) & 1) == 1
            for a in range(NG):
                re, im = cmul(result[a], (v.pows[b, a, 0], v.pows[b, a, 1]))
                result[a] = (jnp.where(hit, re, result[a][0]), jnp.where(hit, im, result[a][1]))
        return result

    my_bucket = par_r[me_r, pl.ds(SUB + me_s, 1), :]
    my_len = jnp.broadcast_to(par_r[me_r, pl.ds(SUB + S + me_s, 1), :], (SUB, LANES)).astype(jnp.int32)
    len1 = my_len[0:1, :]
    count = jnp.clip(my_len - sub * L, 0, L)
    seg = raised(count)
    lead_pow = raised(jnp.minimum(my_len, sub * L))
    tail_pow = raised(jnp.maximum(my_len - (sub + 1) * L, 0))
    for a in range(NG):
        ahead = seg[a]
        behind = seg[a]
        for i, d in enumerate((1, 2, 4)):
            for c in range(2):
                v.hs_f[i, a, c] = jnp.where(sub >= d, ahead[c], 0.0)
                v.hs_b[i, a, c] = jnp.where(sub < SUB - d, behind[c], 0.0)
            ahead = cmul(ahead, (pltpu.roll(ahead[0], d, 0), pltpu.roll(ahead[1], d, 0)))
            behind = cmul(behind, (pltpu.roll(behind[0], SUB - d, 0), pltpu.roll(behind[1], SUB - d, 0)))
        for c in range(2):
            v.lead_pow[a, c] = lead_pow[a][c]
            v.tail_pow[a, c] = tail_pow[a][c]

    def row_powers(r):
        lens = par_r[r, SUB : 2 * SUB, :].astype(jnp.int32)
        result = raised(lens)
        for a in range(NG):
            for c in range(2):
                v.row_pow[r, a, c] = result[a][c]

    loop(R, row_powers)

    def weights(into, forward):
        def one(i, run):
            p = NR - 1 - i if forward else i
            r, s = lax.div(p, S), lax.rem(p, S)
            here = par_r[r, pl.ds(SUB + s, 1), :]
            side = (p < me) if forward else (p > me)
            hit = (here == my_bucket) & (my_bucket > 0.5) & jnp.broadcast_to(side, (1, LANES))
            after = []
            for a in range(NG):
                re, im = run[a]
                re_w, im_w = jnp.where(hit, re, 0.0), jnp.where(hit, im, 0.0)
                for k in range(2):
                    into[p, 0, pl.ds(k * NG + a, 1), :] = re_w
                    into[p, 1, pl.ds(k * NG + a, 1), :] = im_w
                factor = (
                    v.row_pow[r, a, 0, pl.ds(S + s, 1), :],
                    v.row_pow[r, a, 1, pl.ds(S + s, 1), :],
                )
                re_n, im_n = cmul((re, im), factor)
                after.append((jnp.where(hit, re_n, re), jnp.where(hit, im_n, im)))
            return tuple(after)

        first = tuple((jnp.ones((1, LANES), F32), jnp.zeros((1, LANES), F32)) for _ in range(NG))
        lax.fori_loop(0, NR, one, first)

    weights(v.wt_f, True)
    weights(v.wt_b, False)

    def exchange(msg, chain, which):
        chain[me] = msg[...]

        def one(d, carry):
            t = lax.rem(me + d, NR)
            send(msg, chain.at[me], which, {ROWS: lax.div(t, S), STATE: lax.rem(t, S)})
            return carry

        lax.fori_loop(1, NR, one, 0)

    def collect(chain, into, which):
        wait_bytes(chain.at[pl.ds(0, NR - 1)], which, True)

        def one(p, sums):
            x = chain[p]
            return sums[0] + into[p, 0] * x, sums[1] + into[p, 1] * x

        zero = jnp.zeros((2 * NG, LANES), F32)
        return lax.fori_loop(0, NR, one, (zero, zero))

    def rows_of(i):
        return pl.ds(pl.multiple_of(i * CHUNK, CHUNK), CHUNK)

    pos = lax.broadcasted_iota(jnp.int32, (CHUNK, LANES), 0)
    pos = lax.rem(pos, SUB) * L + lax.div(pos, SUB)

    def valid_of(i, width):
        ok = jnp.where(pos + i * (CHUNK // SUB) < len1, 1.0, 0.0)
        return jnp.concatenate([ok] * (width // LANES), axis=1) if width > LANES else ok

    own[OWN_X].wait()
    wait_bytes(v.xin.at[:, pl.ds(0, (S - 1) * W)], X, True)
    v.x[...] = nn(v.perm[...], v.xin[...])

    def layer_norm(i):
        rows = rows_of(i)
        x = v.x[rows, :]
        centred = x - jnp.mean(x, -1, keepdims=True)
        inverse = lax.rsqrt(jnp.mean(centred * centred, -1, keepdims=True) + epsilon)
        normed = centred * inverse
        v.normed[rows, :] = normed
        v.inverse[rows, :] = jnp.broadcast_to(inverse, (CHUNK, LANES))
        v.mixed_low[rows, :] = (normed * gain + bias).astype(BF16)

    loop(T // CHUNK, layer_norm)
    own[OWN_WIN].wait()
    wait_bytes(v.win.at[:, pl.ds(0, (S - 1) * LANES)], WIN, True)
    v.wide[...] = nn(v.mixed_low[...], v.win[...])

    lamb = [tuple(jnp.broadcast_to(c, (SUB, LANES)) for c in l) for l in lam]
    gamb = [jnp.broadcast_to(g, (SUB, LANES)) for g in gam]

    def lanes(i):
        return slice(i * LANES, (i + 1) * LANES)

    def load_c(ref, at):
        return [(ref[at, lanes(a)], ref[at, lanes(NG + a)]) for a in range(NG)]

    def store_c(ref, at, values):
        for a in range(NG):
            ref[at, lanes(a)] = values[a][0]
            ref[at, lanes(NG + a)] = values[a][1]

    def load_g(ref, at):
        return [swap_halves(ref[at, lanes(2 * a)], ref[at, lanes(2 * a + 1)], low) for a in range(NG)]

    def to_g(values):
        return [g for a in range(NG) for g in swap_halves(values[a][0], values[a][1], low)]

    def eight(k):
        return pl.ds(pl.multiple_of(k * SUB, SUB), SUB)

    zeros = tuple((jnp.zeros((SUB, LANES), F32), jnp.zeros((SUB, LANES), F32)) for _ in range(NG))

    def fwd_first(k, state):
        proj = load_g(v.wide, eight(k))
        store_c(v.proj, eight(k), proj)
        ok = sub * L + k < my_len
        new = []
        for a in range(NG):
            re, im = cmul(lamb[a], state[a])
            re, im = re + gamb[a] * proj[a][0], im + gamb[a] * proj[a][1]
            new.append((jnp.where(ok, re, state[a][0]), jnp.where(ok, im, state[a][1])))
        return tuple(new)

    ends = lax.fori_loop(0, L, fwd_first, zeros, unroll=4)

    def across(values, table, forward):
        done = []
        for a in range(NG):
            x = values[a]
            for i, d in enumerate((1, 2, 4)):
                shift = d if forward else SUB - d
                other = (pltpu.roll(x[0], shift, 0), pltpu.roll(x[1], shift, 0))
                factor = (table[i, a, 0], table[i, a, 1])
                add = cmul(factor, other) if forward else conj_mul(factor, other)
                x = (x[0] + add[0], x[1] + add[1])
            done.append(x)
        return done

    ends = across(ends, v.hs_f, True)
    for a in range(NG):
        for c in range(2):
            v.msg_f[pl.ds(c * NG + a, 1), :] = ends[a][c][SUB - 1 : SUB, :]
    exchange(v.msg_f, v.chain_f, CF)
    before = [
        tuple(jnp.where(sub > 0, pltpu.roll(x, 1, 0), 0.0) for x in ends[a]) for a in range(NG)
    ]
    own[OWN_C].wait()
    x_sum, y_sum = collect(v.chain_f, v.wt_f, CF)
    state = []
    for a in range(NG):
        start = (
            x_sum[a : a + 1] - y_sum[NG + a : NG + a + 1],
            x_sum[NG + a : NG + a + 1] + y_sum[a : a + 1],
        )
        add = cmul((v.lead_pow[a, 0], v.lead_pow[a, 1]), start)
        state.append((before[a][0] + add[0], before[a][1] + add[1]))
    store_c(v.state, pl.ds(0, SUB), state)

    def fwd_second(pair, state):
        halves = []
        for u in range(2):
            k = 2 * pair + u
            proj = load_c(v.proj, eight(k))
            ok = sub * L + k < my_len
            new = []
            for a in range(NG):
                re, im = cmul(lamb[a], state[a])
                re, im = re + gamb[a] * proj[a][0], im + gamb[a] * proj[a][1]
                new.append((jnp.where(ok, re, state[a][0]), jnp.where(ok, im, state[a][1])))
            state = tuple(new)
            store_c(v.state, eight(k + 1), state)
            halves.append(to_g([(re, -im) for re, im in state]))
        at = pl.ds(pl.multiple_of(pair * 2 * SUB, 2 * SUB), 2 * SUB)
        for s in range(S):
            v.state_low[at, lanes(s)] = jnp.concatenate([halves[0][s], halves[1][s]], axis=0).astype(BF16)
        return state

    lax.fori_loop(0, L // 2, fwd_second, tuple(state), unroll=2)

    own[OWN_WOUT].wait()
    wait_bytes(v.wout.at[pl.ds(0, (S - 1) * LANES), :], WOUT, True)
    v.wide[...] = nn(v.state_low[...], v.wout[...])

    def gelu(i):
        rows = rows_of(i)
        mixed_in = v.normed[rows, :] * gain + bias
        mixed = v.wide[rows, :] + skip * mixed_in
        cdf = 0.5 * (1.0 + lax.erf(mixed * (1.0 / math.sqrt(2.0))))
        density = jnp.exp(-0.5 * mixed * mixed) * (1.0 / math.sqrt(2.0 * math.pi))
        v.act[rows, :] = (mixed * cdf).astype(BF16)
        v.dgelu[rows, :] = cdf + mixed * density

    loop(T // CHUNK, gelu)
    own[OWN_WGLU].wait()
    wait_bytes(v.wglu.at[:, pl.ds(0, (S - 1) * 2 * W)], WGLU, True)
    v.pre[...] = nn(v.act[...], v.wglu[...])
    wait_bytes(v.cin.at[:, pl.ds(0, (S - 1) * W)], C, True)
    v.wide[...] = nn(v.perm[...], v.cin[...])

    def glu(i):
        rows = rows_of(i)
        ok = valid_of(i, W)
        for s in range(S):
            linear = v.pre[rows, 2 * s * W : (2 * s + 1) * W] + par_s[s, 3:4, :]
            gate = v.pre[rows, (2 * s + 1) * W : (2 * s + 2) * W] + par_s[s, 4:5, :]
            share = jax.nn.sigmoid(gate)
            value = linear * share
            here = slice(s * W, (s + 1) * W)
            v.out_low[rows, here] = (ok * (v.x[rows, here] + value)).astype(BF16)
            dout = ok * v.wide[rows, here]
            v.d_pre[rows, 2 * s * W : (2 * s + 1) * W] = (dout * share).astype(BF16)
            v.d_pre[rows, (2 * s + 1) * W : (2 * s + 2) * W] = (dout * value * (1.0 - share)).astype(BF16)

    loop(T // CHUNK, glu)

    def give_back(low_ref, nat, result, which, own_which):
        nat[...] = nn(v.back[...], low_ref[...]).astype(BF16)
        to_state(lambda t: nat.at[:, cols(t, W)], result.at[me_s], which)
        copy = pltpu.make_async_copy(nat.at[:, cols(me_s, W)], result.at[me_s], v.here.at[own_which])
        copy.start()
        return copy

    out_copy = give_back(v.out_low, v.out_nat, out_ref, OUT, OWN_OUT)

    sib = me_s + 1 - 2 * lax.rem(me_s, 2)
    mine_s = lax.rem(me_s, 2)
    pair_r = me_r + 1 - 2 * lax.rem(me_r, 2)
    mine_r = lax.rem(me_r, 2)
    place_n = lax.div(me_s, 2) * R2 + lax.div(me_r, 2)

    def first_send(part, width):
        for b in range(NG):
            send(
                part.full.at[:, cols(2 * b + 1 - mine_s, width)],
                part.r1.at[b],
                part.step + 0,
                {STATE: sib},
            )

    def first_sum(part, width):
        wait_bytes(part.r1, part.step + 0, True)

        def one(q):
            for h in range(2):
                rows = pl.ds(pl.multiple_of((2 * q + h) * HB, HB), HB)
                for b in range(NG):
                    total = part.full[rows, cols(2 * b + mine_s, width)].astype(F32) + part.r1[b, rows, :].astype(F32)
                    part.a1[h, b * R2 + q] = total.astype(gdt)

        loop(R2, one)
        send(part.a1.at[1 - mine_r], part.r2, part.step + 1, {ROWS: pair_r})

    def second_sum(part, width):
        wait_bytes(part.r2, part.step + 1, True)

        def one(n):
            total = part.a1[mine_r, n].astype(F32) + part.r2[n].astype(F32)
            part.a2[n] = total.astype(gdt)

        loop(NP, one)
        part.r3[place_n] = part.a2[place_n]

        def give(d, carry):
            n = lax.rem(place_n + d, NP)
            send(
                part.a2.at[n],
                part.r3.at[place_n],
                part.step + 2,
                {ROWS: 2 * lax.rem(n, R2) + mine_r, STATE: 2 * lax.div(n, R2) + mine_s},
            )
            return carry

        lax.fori_loop(1, NP, give, 0)

    def third_sum(part, width, at):
        wait_bytes(part.r3.at[pl.ds(0, NP - 1)], part.step + 2, True)

        def one(n, total):
            return total + part.r3[n].astype(F32)

        gsum[:, at : at + width] = lax.fori_loop(0, NP, one, jnp.zeros((HB, width), F32))

    def first_done(part, width):
        wait_bytes(part.r1, part.step + 0, False)
        wait_bytes(part.r2, part.step + 1, False)
        wait_bytes(part.r3.at[pl.ds(0, NP - 1)], part.step + 2, False)

    g_glu.full[...] = tn(v.act[...], v.d_pre[...]).astype(gdt)
    first_send(g_glu, 2 * W)
    v.wide[...] = nt(v.d_pre[...], v.wglu[...])

    def gelu_back(i, total):
        rows = rows_of(i)
        d_mixed = v.wide[rows, :] * v.dgelu[rows, :]
        v.d_mixed[rows, :] = d_mixed
        v.d_rec[rows, :] = d_mixed.astype(BF16)
        return total + fold(d_mixed * (v.normed[rows, :] * gain + bias))

    d_skip = lax.fori_loop(0, T // CHUNK, gelu_back, jnp.zeros((SUB, H), F32))
    d_skip = jnp.sum(d_skip, axis=0, keepdims=True)
    v.wide[...] = nt(v.d_rec[...], v.wout[...])

    def bwd_first(i, carry):
        k = L - 1 - i
        source = [(re, -im) for re, im in load_g(v.wide, eight(k))]
        store_c(v.source, eight(k), source)
        ok = sub * L + k < my_len
        new = []
        for a in range(NG):
            re, im = source[a][0] + carry[a][0], source[a][1] + carry[a][1]
            nre, nim = conj_mul(lamb[a], (re, im))
            new.append((jnp.where(ok, nre, re), jnp.where(ok, nim, im)))
        return tuple(new)

    heads = lax.fori_loop(0, L, bwd_first, zeros, unroll=4)
    heads = across(heads, v.hs_b, False)
    for a in range(NG):
        for c in range(2):
            v.msg_b[pl.ds(c * NG + a, 1), :] = heads[a][c][0:1, :]
    exchange(v.msg_b, v.chain_b, CB)
    after = [
        tuple(jnp.where(sub < SUB - 1, pltpu.roll(x, SUB - 1, 0), 0.0) for x in heads[a])
        for a in range(NG)
    ]
    g_out.full[...] = tn(v.d_rec[...], v.state_low[...]).astype(gdt)
    first_send(g_out, LANES)
    first_sum(g_glu, 2 * W)
    ones = jnp.ones((2 * SUB, T), BF16)
    d_bias = nn(ones, v.d_pre[...])[0:1, :]

    x_sum, y_sum = collect(v.chain_b, v.wt_b, CB)
    carry = []
    for a in range(NG):
        omega = (
            x_sum[a : a + 1] + y_sum[NG + a : NG + a + 1],
            x_sum[NG + a : NG + a + 1] - y_sum[a : a + 1],
        )
        add = conj_mul((v.tail_pow[a, 0], v.tail_pow[a, 1]), omega)
        carry.append((after[a][0] + add[0], after[a][1] + add[1]))

    def bwd_second(i, item):
        pair = L // 2 - 1 - i
        carry, sums = item
        halves = [None, None]
        for u in (1, 0):
            k = 2 * pair + u
            source = load_c(v.source, eight(k))
            previous = load_c(v.state, eight(k))
            proj = load_c(v.proj, eight(k))
            ok = sub * L + k < my_len
            new, new_sums, low_out = [], [], []
            for a in range(NG):
                re, im = source[a][0] + carry[a][0], source[a][1] + carry[a][1]
                are, aim = jnp.where(ok, re, 0.0), jnp.where(ok, im, 0.0)
                dre, dim = conj_mul(previous[a], (are, aim))
                dg = are * proj[a][0] + aim * proj[a][1]
                new_sums.append((sums[a][0] + dre, sums[a][1] + dim, sums[a][2] + dg))
                low_out.append((gamb[a] * are, gamb[a] * aim))
                nre, nim = conj_mul(lamb[a], (re, im))
                new.append((jnp.where(ok, nre, re), jnp.where(ok, nim, im)))
            carry, sums = tuple(new), tuple(new_sums)
            halves[u] = to_g(low_out)
        at = pl.ds(pl.multiple_of(pair * 2 * SUB, 2 * SUB), 2 * SUB)
        for s in range(S):
            v.d_proj[at, lanes(s)] = jnp.concatenate([halves[0][s], halves[1][s]], axis=0).astype(BF16)
        return carry, sums

    zero = jnp.zeros((SUB, LANES), F32)
    _, sums = lax.fori_loop(
        0, L // 2, bwd_second, (tuple(carry), tuple((zero, zero, zero) for _ in range(NG))), unroll=2
    )

    g_in.full[...] = tn(v.mixed_low[...], v.d_proj[...]).astype(gdt)
    first_send(g_in, LANES)
    second_sum(g_glu, 2 * W)
    first_sum(g_out, LANES)
    v.wide[...] = nt(v.d_proj[...], v.win[...])

    def norm_back(i, totals):
        rows = rows_of(i)
        d_mixed_in = v.wide[rows, :] + skip * v.d_mixed[rows, :]
        normed = v.normed[rows, :]
        inverse = jnp.concatenate([v.inverse[rows, :]] * (H // LANES), axis=1)
        g = d_mixed_in * gain
        first = jnp.mean(g, -1, keepdims=True)
        second = jnp.mean(g * normed, -1, keepdims=True)
        v.din_low[rows, :] = (inverse * (g - first - normed * second)).astype(BF16)
        return totals[0] + fold(d_mixed_in * normed), totals[1] + fold(d_mixed_in)

    zero_h = jnp.zeros((SUB, H), F32)
    d_gain, d_nbias = lax.fori_loop(0, T // CHUNK, norm_back, (zero_h, zero_h))
    d_gain = jnp.sum(d_gain, axis=0, keepdims=True)
    d_nbias = jnp.sum(d_nbias, axis=0, keepdims=True)
    din_copy = give_back(v.din_low, v.din_nat, din_ref, DIN, OWN_DIN)

    small = v.small
    small[...] = jnp.zeros((S, SUB, LANES), F32)
    for a in range(NG):
        sr, si, sg = (jnp.sum(x, axis=0, keepdims=True) for x in sums[a])
        pair = swap_halves(sr, si, low1)
        pair_g = swap_halves(sg, jnp.zeros_like(sg), low1)
        for u in range(2):
            small[2 * a + u, 0:1, :] = pair[u]
            small[2 * a + u, 1:2, :] = pair_g[u]
    for s in range(S):
        here = slice(s * W, (s + 1) * W)
        small[s, 2:3, :] = d_skip[:, here]
        small[s, 3:4, :] = d_bias[:, 2 * s * W : (2 * s + 1) * W]
        small[s, 4:5, :] = d_bias[:, (2 * s + 1) * W : (2 * s + 2) * W]
        small[s, 5:6, :] = d_gain[:, here]
        small[s, 6:7, :] = d_nbias[:, here]
    v.small_r[me_s] = small[...]
    to_state(lambda t: small, v.small_r.at[me_s], SM)

    first_sum(g_in, LANES)
    second_sum(g_out, LANES)
    third_sum(g_glu, 2 * W, 2 * LANES)

    wait_bytes(v.small_r.at[pl.ds(0, S - 1)], SM, True)
    group = v.small_r[0]
    for s in range(1, S):
        group = group + v.small_r[s]
    small2 = v.small2
    v.group[...] = group
    small2[0:SUB, :] = v.group[me_s]
    for s in range(S):
        small2[SUB + s : SUB + s + 1, :] = group[s, 5:6, :]
        small2[SUB + S + s : SUB + S + s + 1, :] = group[s, 6:7, :]
    v.small2_r[me_r] = small2[...]

    def small_rows(d, carry):
        send(small2, v.small2_r.at[me_r], SN, {ROWS: lax.rem(me_r + d, R)})
        return carry

    lax.fori_loop(1, R, small_rows, 0)
    second_sum(g_in, LANES)
    third_sum(g_out, LANES, LANES)
    wait_bytes(v.small2_r.at[pl.ds(0, R - 1)], SN, True)

    def sum_rows(r, total):
        return total + v.small2_r[r]

    vec[...] = lax.fori_loop(0, R, sum_rows, jnp.zeros((2 * SUB, LANES), F32))
    third_sum(g_in, LANES, 0)

    out_copy.wait()
    din_copy.wait()
    wait_bytes(out_ref.at[pl.ds(0, S - 1)], OUT, True)
    wait_bytes(din_ref.at[pl.ds(0, S - 1)], DIN, True)
    wait_bytes(out_ref.at[pl.ds(0, S - 1)], OUT, False)
    wait_bytes(din_ref.at[pl.ds(0, S - 1)], DIN, False)
    wait_bytes(v.par_s.at[pl.ds(0, S - 1)], PAR_S, False)
    wait_bytes(v.par_r.at[pl.ds(0, R - 1)], PAR_R, False)
    wait_bytes(v.xin.at[:, pl.ds(0, (S - 1) * W)], X, False)
    wait_bytes(v.win.at[:, pl.ds(0, (S - 1) * LANES)], WIN, False)
    wait_bytes(v.wout.at[pl.ds(0, (S - 1) * LANES), :], WOUT, False)
    wait_bytes(v.wglu.at[:, pl.ds(0, (S - 1) * 2 * W)], WGLU, False)
    wait_bytes(v.cin.at[:, pl.ds(0, (S - 1) * W)], C, False)
    wait_bytes(v.chain_f.at[pl.ds(0, NR - 1)], CF, False)
    wait_bytes(v.chain_b.at[pl.ds(0, NR - 1)], CB, False)
    wait_bytes(v.small_r.at[pl.ds(0, S - 1)], SM, False)
    wait_bytes(v.small2_r.at[pl.ds(0, R - 1)], SN, False)
    first_done(g_glu, 2 * W)
    first_done(g_out, LANES)
    first_done(g_in, LANES)


def run_block(dims, inputs, cot, w_in, w_out, w_glu, par, gain, bias):
    R, S, T, H, W = dims.R, dims.S, dims.T, dims.H, dims.W
    NR, NG, R2, HB, L = R * S, S // 2, R // 2, H // R, T // SUB
    NP, CH = NG * R2, S * LANES
    gdt = BF16 if HB % (2 * SUB) == 0 else F32
    dims.gdt = gdt
    bits = T.bit_length()
    shapes = dict(
        xin=((T, H), BF16),
        cin=((T, H), BF16),
        win=((H, CH), BF16),
        wout=((CH, H), BF16),
        wglu=((H, 2 * H), BF16),
        perm=((T, T), BF16),
        back=((T, T), BF16),
        par_s=((S, 2 * SUB, LANES), F32),
        par_r=((R, 2 * SUB, LANES), F32),
        pows=((bits, NG, 2, SUB, LANES), F32),
        hs_f=((3, NG, 2, SUB, LANES), F32),
        hs_b=((3, NG, 2, SUB, LANES), F32),
        lead_pow=((NG, 2, SUB, LANES), F32),
        tail_pow=((NG, 2, SUB, LANES), F32),
        row_pow=((R, NG, 2, SUB, LANES), F32),
        wt_f=((NR, 2, 2 * NG, LANES), F32),
        wt_b=((NR, 2, 2 * NG, LANES), F32),
        msg_f=((2 * NG, LANES), F32),
        msg_b=((2 * NG, LANES), F32),
        chain_f=((NR, 2 * NG, LANES), F32),
        chain_b=((NR, 2 * NG, LANES), F32),
        x=((T, H), F32),
        normed=((T, H), F32),
        inverse=((T, LANES), F32),
        mixed_low=((T, H), BF16),
        wide=((T, max(H, CH)), F32),
        proj=((T, CH), F32),
        state=((T + SUB, CH), F32),
        state_low=((T, CH), BF16),
        act=((T, H), BF16),
        dgelu=((T, H), F32),
        pre=((T, 2 * H), F32),
        out_low=((T, H), BF16),
        out_nat=((T, H), BF16),
        d_pre=((T, 2 * H), BF16),
        d_mixed=((T, H), F32),
        d_rec=((T, H), BF16),
        source=((T, CH), F32),
        d_proj=((T, CH), BF16),
        din_low=((T, H), BF16),
        din_nat=((T, H), BF16),
        small=((S, SUB, LANES), F32),
        small_r=((S, S, SUB, LANES), F32),
        group=((S, SUB, LANES), F32),
        small2=((2 * SUB, LANES), F32),
        small2_r=((R, 2 * SUB, LANES), F32),
    )
    dims.names = [*shapes, *dict(here=0, sent=0, received=0)]
    parts = []
    for rows, width in ((H, 2 * W), (H, LANES), (H, LANES)):
        parts.append((rows, S * width))
        parts.append((NG, rows, width))
        parts.append((2, NP, HB, width))
        parts += [(NP, HB, width)] * 3
    scratch = [pltpu.VMEM(shape, dtype) for shape, dtype in shapes.values()]
    scratch += [pltpu.SemaphoreType.DMA((n,)) for n in (OWN_DIN + 1, G1 + 9, G1 + 9)]
    scratch += [pltpu.VMEM(shape, gdt) for shape in parts]
    any_spec = pl.BlockSpec(memory_space=pl.ANY)
    vmem = pl.BlockSpec(memory_space=pltpu.VMEM)
    macs = T * H * (2 * CH + 2 * H) * 3 + 4 * T * T * H
    return pl.pallas_call(
        functools.partial(block_kernel, dims),
        out_shape=(
            jax.ShapeDtypeStruct((S, T, W), BF16),
            jax.ShapeDtypeStruct((S, T, W), BF16),
            jax.ShapeDtypeStruct((HB, 2 * LANES + 2 * W), F32),
            jax.ShapeDtypeStruct((2 * SUB, LANES), F32),
        ),
        in_specs=[any_spec] * 5 + [vmem] * 3,
        out_specs=(any_spec, any_spec, vmem, vmem),
        scratch_shapes=scratch,
        compiler_params=pltpu.CompilerParams(
            collective_id=0, has_side_effects=True, vmem_limit_bytes=56 * 2**20
        ),
        cost_estimate=pl.CostEstimate(flops=2 * macs, bytes_accessed=8 * 2**20, transcendentals=4 * T * H),
    )(inputs, cot, w_in, w_out, w_glu, par, gain, bias)


def on_device(
    inputs,
    bucket,
    lengths,
    nu_log,
    theta_log,
    gamma_log,
    in_proj,
    out_proj,
    skip,
    norm_gain,
    norm_bias,
    glu_weight,
    glu_bias,
    output_cotangent,
):
    row_count, seq, part = inputs.shape
    width = norm_gain.shape[0]
    chans = nu_log.shape[0]
    R, S = lax.axis_size(ROWS), lax.axis_size(STATE)
    dims = SimpleNamespace(R=R, S=S, T=seq, H=width, W=part)
    assert row_count == S and 2 * chans == LANES and part == LANES and S % 2 == 0 and R % 2 == 0

    magnitude = jnp.exp(-jnp.exp(nu_log))
    angle = jnp.exp(theta_log)
    lam_re = magnitude * jnp.cos(angle)
    lam_im = magnitude * jnp.sin(angle)
    gamma = jnp.exp(gamma_log)
    rows = [
        jnp.concatenate([lam_re, lam_im])[None],
        jnp.concatenate([gamma, jnp.zeros_like(gamma)])[None],
        skip[None],
        glu_bias,
        jnp.zeros((3, LANES), F32),
        jnp.broadcast_to(bucket.astype(F32)[:, None], (S, LANES)),
        jnp.broadcast_to(lengths.astype(F32)[:, None], (S, LANES)),
    ]
    par = jnp.concatenate(rows, axis=0)

    outputs, d_norm, gsum, vec = run_block(
        dims,
        inputs,
        output_cotangent,
        in_proj.reshape(width, 2 * chans),
        out_proj.reshape(2 * chans, width),
        glu_weight.reshape(width, 2 * part),
        par,
        norm_gain[None],
        norm_bias[None],
    )
    valid = (jnp.arange(seq)[None, :] < lengths[:, None])[..., None]
    d_inputs = d_norm.astype(F32) + jnp.where(valid, output_cotangent.astype(F32), 0.0)
    hb = width // R
    d_in_proj = gsum[:, :LANES].reshape(hb, 2, chans)
    d_out_proj = gsum[:, LANES : 2 * LANES].T.reshape(2, chans, hb)
    d_glu_weight = gsum[:, 2 * LANES :].reshape(hb, 2, part)
    d_lam_re, d_lam_im = vec[0, :chans], vec[0, chans:]
    d_nu_log = -jnp.exp(nu_log) * (d_lam_re * lam_re + d_lam_im * lam_im)
    d_theta_log = angle * (d_lam_im * lam_re - d_lam_re * lam_im)
    d_gamma_log = gamma * vec[1, :chans]
    d_skip = vec[2]
    d_glu_bias = vec[3:5]
    d_norm_gain = vec[SUB : SUB + S].reshape(width)
    d_norm_bias = vec[SUB + S : SUB + 2 * S].reshape(width)
    return (
        outputs,
        d_inputs,
        d_nu_log,
        d_theta_log,
        d_gamma_log,
        d_in_proj,
        d_out_proj,
        d_skip,
        d_norm_gain,
        d_norm_bias,
        d_glu_weight,
        d_glu_bias,
    )


def solution(mesh):
    return jax.shard_map(
        on_device,
        mesh=mesh,
        in_specs=(
            P(ROWS, None, STATE),
            P(ROWS),
            P(ROWS),
            P(STATE),
            P(STATE),
            P(STATE),
            P(None, None, STATE),
            P(None, STATE, None),
            P(STATE),
            P(),
            P(),
            P(None, None, STATE),
            P(None, STATE),
            P(ROWS, None, STATE),
        ),
        out_specs=(
            P(ROWS, None, STATE),
            P(ROWS, None, STATE),
            P(STATE),
            P(STATE),
            P(STATE),
            P(ROWS, None, STATE),
            P(None, STATE, ROWS),
            P(STATE),
            P(),
            P(),
            P(ROWS, None, STATE),
            P(None, STATE),
        ),
        check_vma=False,
    )
```

```python
import functools
import math
from types import SimpleNamespace

import jax
import jax.numpy as jnp
from jax import lax
from jax.experimental import pallas as pl
from jax.experimental.pallas import tpu as pltpu
from jax.sharding import PartitionSpec as P

LONGS = 3

epsilon = 1e-05

F32 = jnp.float32
BF16 = jnp.bfloat16
MESH = pl.DeviceIdType.MESH
ROWS, STATE = "rows", "state"
SUB = 8
LANES = 128
HALF = LANES // 2
CHUNK = 64

OWN_X, OWN_WIN, OWN_WOUT, OWN_WGLU, OWN_C, OWN_OUT, OWN_DIN = range(7)
PAR_S, PAR_R, X, C, CF, CB, OUT, DIN, SM, SN, W1 = range(11)
SIB, FAR, FAR_SIB, PAIR, PAIR_SIB = range(5)
G1 = W1 + 15


def loop(count, body, unroll=1):
    def step(i, carry):
        body(i)
        return carry

    lax.fori_loop(0, count, step, 0, unroll=unroll)


def nn(a, b):
    return lax.dot_general(a, b, (((1,), (0,)), ((), ())), preferred_element_type=F32)


def nt(a, b):
    return lax.dot_general(a, b, (((1,), (1,)), ((), ())), preferred_element_type=F32)


def tn(a, b):
    return lax.dot_general(a, b, (((0,), (0,)), ((), ())), preferred_element_type=F32)


def cmul(a, b):
    return a[0] * b[0] - a[1] * b[1], a[0] * b[1] + a[1] * b[0]


def conj_mul(a, b):
    return a[0] * b[0] + a[1] * b[1], a[0] * b[1] - a[1] * b[0]


def swap_halves(u, v, low):
    return (
        jnp.where(low, u, pltpu.roll(v, HALF, 1)),
        jnp.where(low, pltpu.roll(u, HALF, 1), v),
    )


def fold(x):
    return jnp.sum(x.reshape(x.shape[0] // SUB, SUB, x.shape[1]), axis=0)


def block_kernel(dims, *refs):
    R, S, T, H, W, gdt = dims.R, dims.S, dims.T, dims.H, dims.W, dims.gdt
    NR, NG, R2, HB, L = R * S, S // 2, R // 2, H // R, T // SUB
    NP = NG * R2
    BITS = T.bit_length()
    (inputs, cot, w_in, w_out, w_glu) = refs[:5]
    (bucket_ref, lengths_ref, nu_ref, theta_ref, gamma_ref, skip_ref, glu_bias_ref, gain_ref, bias_ref) = refs[5:14]
    (out_ref, din_ref, gsum, vec) = refs[14:18]
    total = 18 + len(dims.names)
    v = SimpleNamespace(**dict(zip(dims.names, refs[18:total])))
    g_in, g_out, g_lin, g_gate = (
        SimpleNamespace(full=a, r1=b, a1=c, r2=d, a2=e, r3=f, step=G1 + 3 * i, at=i * LANES)
        for i, (a, b, c, d, e, f) in enumerate(refs[total + 6 * i : total + 6 * i + 6] for i in range(4))
    )

    me_r, me_s = lax.axis_index(ROWS), lax.axis_index(STATE)
    me = me_r * S + me_s

    def cols(i, width):
        return pl.ds(pl.multiple_of(i * width, LANES), width)

    def rows_of(i):
        return pl.ds(pl.multiple_of(i * CHUNK, CHUNK), CHUNK)

    def wait_bytes(ref, which, arrived):
        pltpu.make_async_copy(ref, ref, (v.received if arrived else v.sent).at[which]).wait()

    def send(src, dst, which, target):
        pltpu.make_async_remote_copy(
            src_ref=src,
            dst_ref=dst,
            send_sem=v.sent.at[which],
            recv_sem=v.received.at[which],
            device_id=target,
            device_id_type=MESH,
        ).start()

    def to_state(src_of, dst, which):
        for j in (2, 3, 1) if S == 4 else range(1, S):
            t = lax.rem(me_s + j, S)
            send(src_of(t), dst, which, {STATE: t})

    sib = me_s + 1 - 2 * lax.rem(me_s, 2)
    far = lax.rem(me_s + NG, S)
    sib_far = lax.rem(sib + NG, S)
    pair_r = me_r + 1 - 2 * lax.rem(me_r, 2)
    mine_s = lax.rem(me_s, 2)
    mine_r = lax.rem(me_r, 2)

    def line_block(ref, s, h=None):
        if h is None:
            return ref.at[pl.ds(pl.multiple_of(s * LANES, LANES), LANES), :]
        return ref.at[pl.ds(pl.multiple_of(s * LANES + h * HALF, HALF), HALF), :]

    def glu_block(ref, s, h=None):
        rows = slice(None) if h is None else pl.ds(pl.multiple_of(h * (H // 2), H // 2), H // 2)
        return ref.at[:, rows, cols(s, W)]

    own = [
        (w_glu, v.glu_raw, OWN_WGLU),
        (w_in, line_block(v.win, me_s), OWN_WIN),
        (w_out, line_block(v.wout, me_s), OWN_WOUT),
        (inputs.at[me_s], v.xin.at[:, cols(me_s, W)], OWN_X),
        (cot.at[me_s], v.cin.at[:, cols(me_s, W)], OWN_C),
    ]
    own = {which: pltpu.make_async_copy(a, b, v.here.at[which]) for a, b, which in own}
    for copy in own.values():
        copy.start()

    barrier = pltpu.get_barrier_semaphore()

    def greet(d, carry):
        t = lax.rem(me + d, NR)
        pl.semaphore_signal(
            barrier,
            inc=1,
            device_id={ROWS: lax.div(t, S), STATE: lax.rem(t, S)},
            device_id_type=MESH,
        )
        return carry

    lax.fori_loop(1, NR, greet, 0)

    par = v.par
    par[...] = jnp.zeros((2 * SUB, LANES), F32)
    par[0:1, 0:HALF] = nu_ref[...]
    par[0:1, HALF:LANES] = theta_ref[...]
    par[1:2, 0:HALF] = gamma_ref[...]
    par[2:3, :] = skip_ref[...]
    par[3:5, :] = glu_bias_ref[...]
    for i in range(S):
        par[SUB + i : SUB + i + 1, :] = jnp.full((1, LANES), bucket_ref[i], jnp.int32).astype(F32)
        par[SUB + S + i : SUB + S + i + 1, :] = jnp.full((1, LANES), lengths_ref[i], jnp.int32).astype(F32)
    v.par_s[me_s] = par[...]
    v.par_r[me_r] = par[...]

    pl.semaphore_wait(barrier, NR - 1)

    to_state(lambda t: par, v.par_s.at[me_s], PAR_S)

    def par_rows(d, carry):
        send(par, v.par_r.at[me_r], PAR_R, {ROWS: lax.rem(me_r + d, R)})
        return carry

    lax.fori_loop(1, R, par_rows, 0)

    def w_send(w, own_block, own_half):
        send(own_half, w.block(w.ref, me_s, mine_r), w.step + FAR, {STATE: far})
        send(own_block, w.block(w.ref, me_s), w.step + SIB, {STATE: sib})

    def w_forward_far(w):
        half = w.block(w.ref, far, mine_r)
        wait_bytes(half, w.step + FAR, True)
        send(half, half, w.step + PAIR, {ROWS: pair_r})
        send(half, half, w.step + FAR_SIB, {STATE: sib})

    def w_forward_pair(w):
        half = w.block(w.ref, far, 1 - mine_r)
        wait_bytes(half, w.step + PAIR, True)
        send(half, half, w.step + PAIR_SIB, {STATE: sib})

    def w_ready(w):
        wait_bytes(w.block(w.ref, sib), w.step + SIB, True)
        wait_bytes(w.block(w.ref, sib_far, mine_r), w.step + FAR_SIB, True)
        wait_bytes(w.block(w.ref, sib_far, 1 - mine_r), w.step + PAIR_SIB, True)

    def w_sent(w):
        wait_bytes(w.block(w.ref, sib), w.step + SIB, False)
        for step in (FAR, FAR_SIB, PAIR, PAIR_SIB):
            wait_bytes(w.block(w.ref, sib_far, mine_r), w.step + step, False)

    wt_in = SimpleNamespace(ref=v.win, block=line_block, step=W1)
    wt_out = SimpleNamespace(ref=v.wout, block=line_block, step=W1 + 5)
    wt_glu = SimpleNamespace(ref=v.wglu, block=glu_block, step=W1 + 10)

    def half_of(ref):
        return ref.at[pl.ds(pl.multiple_of(mine_r * HALF, HALF), HALF), :]

    w_send(wt_in, w_in, half_of(w_in))
    to_state(lambda t: inputs.at[t], v.xin.at[:, cols(me_s, W)], X)
    w_send(wt_out, w_out, half_of(w_out))
    own[OWN_WGLU].wait()

    def split_glu(i):
        here = rows_of(i)
        v.glu_wide[...] = v.glu_raw[pl.ds(pl.multiple_of(i * 2 * CHUNK, 2 * CHUNK), 2 * CHUNK), :].astype(F32)
        for k in range(2):
            v.wglu[k, here, cols(me_s, W)] = v.glu_wide[pl.ds(k, CHUNK, stride=2), :].astype(BF16)

    loop(H // CHUNK, split_glu)
    w_send(wt_glu, glu_block(v.wglu, me_s), glu_block(v.wglu, me_s, mine_r))
    to_state(lambda t: cot.at[t], v.cin.at[:, cols(me_s, W)], C)

    line = lax.broadcasted_iota(jnp.int32, (CHUNK, T), 0)
    place = lax.broadcasted_iota(jnp.int32, (CHUNK, T), 1)

    def orders(i):
        base = pl.multiple_of(i * CHUNK, CHUNK)
        at = line + base
        v.perm[pl.ds(base, CHUNK), :] = (
            place == lax.rem(at, SUB) * L + lax.div(at, SUB)
        ).astype(F32).astype(BF16)
        v.back[pl.ds(base, CHUNK), :] = (
            at == lax.rem(place, SUB) * L + lax.div(place, SUB)
        ).astype(F32).astype(BF16)

    loop(T // CHUNK, orders)

    low = lax.broadcasted_iota(jnp.int32, (SUB, LANES), 1) < HALF
    low1 = lax.broadcasted_iota(jnp.int32, (1, LANES), 1) < HALF
    sub = lax.broadcasted_iota(jnp.int32, (SUB, LANES), 0)

    wait_bytes(v.par_s.at[pl.ds(0, S - 1)], PAR_S, True)
    wait_bytes(v.par_r.at[pl.ds(0, R - 1)], PAR_R, True)
    par_s, par_r = v.par_s, v.par_r
    lam, gam, rate, angle = [], [], [], []
    for a in range(NG):
        nu, theta = swap_halves(par_s[2 * a, 0:1, :], par_s[2 * a + 1, 0:1, :], low1)
        rate.append(jnp.exp(nu))
        angle.append(jnp.exp(theta))
        magnitude = jnp.exp(-rate[a])
        lam.append((magnitude * jnp.cos(angle[a]), magnitude * jnp.sin(angle[a])))
        gam.append(jnp.exp(swap_halves(par_s[2 * a, 1:2, :], par_s[2 * a + 1, 1:2, :], low1)[0]))
    skip = jnp.concatenate([par_s[s, 2:3, :] for s in range(S)], axis=1)
    gain, bias = gain_ref[...], bias_ref[...]
    power = [[(jnp.broadcast_to(l[0], (SUB, LANES)), jnp.broadcast_to(l[1], (SUB, LANES))) for l in lam]]
    for _ in range(BITS - 1):
        power.append([cmul(p, p) for p in power[-1]])
    for b in range(BITS):
        for a in range(NG):
            for c in range(2):
                v.pows[b, a, c] = power[b][a][c]

    def raised(exponent, bits=BITS):
        result = [(jnp.ones((SUB, LANES), F32), jnp.zeros((SUB, LANES), F32)) for _ in range(NG)]
        for b in range(bits):
            hit = (lax.shift_right_logical(exponent, b) & 1) == 1
            for a in range(NG):
                re, im = cmul(result[a], (v.pows[b, a, 0], v.pows[b, a, 1]))
                result[a] = (jnp.where(hit, re, result[a][0]), jnp.where(hit, im, result[a][1]))
        return result

    my_bucket = par_r[me_r, pl.ds(SUB + me_s, 1), :]
    my_len = jnp.broadcast_to(par_r[me_r, pl.ds(SUB + S + me_s, 1), :], (SUB, LANES)).astype(jnp.int32)
    len1 = my_len[0:1, :]
    count = jnp.clip(my_len - sub * L, 0, L)
    seg = raised(count)
    lead_pow = raised(jnp.minimum(my_len, sub * L))
    tail_pow = raised(jnp.maximum(my_len - (sub + 1) * L, 0))
    for a in range(NG):
        ahead = seg[a]
        behind = seg[a]
        for i, d in enumerate((1, 2, 4)):
            for c in range(2):
                v.hs_f[i, a, c] = jnp.where(sub >= d, ahead[c], 0.0)
                v.hs_b[i, a, c] = jnp.where(sub < SUB - d, behind[c], 0.0)
            ahead = cmul(ahead, (pltpu.roll(ahead[0], d, 0), pltpu.roll(ahead[1], d, 0)))
            behind = cmul(behind, (pltpu.roll(behind[0], SUB - d, 0), pltpu.roll(behind[1], SUB - d, 0)))
        for c in range(2):
            v.lead_pow[a, c] = lead_pow[a][c]
            v.tail_pow[a, c] = tail_pow[a][c]

    def row_powers(r):
        lens = par_r[r, SUB : 2 * SUB, :].astype(jnp.int32)
        result = raised(lens)
        for a in range(NG):
            for c in range(2):
                v.row_pow[r, a, c] = result[a][c]

    loop(R, row_powers)

    def weights(into, forward):
        def one(i, run):
            p = NR - 1 - i if forward else i
            r, s = lax.div(p, S), lax.rem(p, S)
            here = par_r[r, pl.ds(SUB + s, 1), :]
            side = (p < me) if forward else (p > me)
            hit = (here == my_bucket) & (my_bucket > 0.5) & jnp.broadcast_to(side, (1, LANES))
            after = []
            for a in range(NG):
                re, im = run[a]
                re_w, im_w = jnp.where(hit, re, 0.0), jnp.where(hit, im, 0.0)
                for k in range(2):
                    into[p, 0, pl.ds(k * NG + a, 1), :] = re_w
                    into[p, 1, pl.ds(k * NG + a, 1), :] = im_w
                factor = (
                    v.row_pow[r, a, 0, pl.ds(S + s, 1), :],
                    v.row_pow[r, a, 1, pl.ds(S + s, 1), :],
                )
                re_n, im_n = cmul((re, im), factor)
                after.append((jnp.where(hit, re_n, re), jnp.where(hit, im_n, im)))
            return tuple(after)

        first = tuple((jnp.ones((1, LANES), F32), jnp.zeros((1, LANES), F32)) for _ in range(NG))
        lax.fori_loop(0, NR, one, first)

    weights(v.wt_f, True)
    weights(v.wt_b, False)

    def exchange(msg, chain, which):
        chain[me] = msg[...]

        def one(d, carry):
            t = lax.rem(me + d, NR)
            send(msg, chain.at[me], which, {ROWS: lax.div(t, S), STATE: lax.rem(t, S)})
            return carry

        lax.fori_loop(1, NR, one, 0)

    def collect(chain, into, which):
        wait_bytes(chain.at[pl.ds(0, NR - 1)], which, True)

        def one(p, sums):
            x = chain[p]
            return sums[0] + into[p, 0] * x, sums[1] + into[p, 1] * x

        zero = jnp.zeros((2 * NG, LANES), F32)
        return lax.fori_loop(0, NR, one, (zero, zero))

    pos = lax.broadcasted_iota(jnp.int32, (CHUNK, LANES), 0)
    pos = lax.rem(pos, SUB) * L + lax.div(pos, SUB)

    def valid_of(i, width):
        ok = jnp.where(pos + i * (CHUNK // SUB) < len1, 1.0, 0.0)
        return jnp.concatenate([ok] * (width // LANES), axis=1) if width > LANES else ok

    w_forward_far(wt_in)
    w_forward_pair(wt_in)

    own[OWN_X].wait()
    wait_bytes(v.xin.at[:, pl.ds(0, (S - 1) * W)], X, True)
    v.x[...] = nn(v.perm[...], v.xin[...])

    def layer_norm(i):
        rows = rows_of(i)
        x = v.x[rows, :]
        centred = x - jnp.mean(x, -1, keepdims=True)
        inverse = lax.rsqrt(jnp.mean(centred * centred, -1, keepdims=True) + epsilon)
        normed = centred * inverse
        v.normed[rows, :] = normed
        v.inverse[rows, :] = jnp.broadcast_to(inverse, (CHUNK, LANES))
        v.mixed_low[rows, :] = (normed * gain + bias).astype(BF16)

    loop(T // CHUNK, layer_norm)
    own[OWN_WIN].wait()
    w_ready(wt_in)
    v.wide[...] = nt(v.mixed_low[...], v.win[...])
    w_forward_far(wt_out)

    lamb = [tuple(jnp.broadcast_to(c, (SUB, LANES)) for c in l) for l in lam]
    gamb = [jnp.broadcast_to(g, (SUB, LANES)) for g in gam]

    def lanes(i):
        return slice(i * LANES, (i + 1) * LANES)

    def load_c(ref, at):
        return [(ref[at, lanes(a)], ref[at, lanes(NG + a)]) for a in range(NG)]

    def store_c(ref, at, values):
        for a in range(NG):
            ref[at, lanes(a)] = values[a][0]
            ref[at, lanes(NG + a)] = values[a][1]

    def load_g(ref, at):
        return [swap_halves(ref[at, lanes(2 * a)], ref[at, lanes(2 * a + 1)], low) for a in range(NG)]

    def to_g(values):
        return [g for a in range(NG) for g in swap_halves(values[a][0], values[a][1], low)]

    def eight(k):
        return pl.ds(pl.multiple_of(k * SUB, SUB), SUB)

    zeros = tuple((jnp.zeros((SUB, LANES), F32), jnp.zeros((SUB, LANES), F32)) for _ in range(NG))

    def fwd_first(k, state):
        proj = load_g(v.wide, eight(k))
        store_c(v.proj, eight(k), proj)
        ok = sub * L + k < my_len
        new = []
        for a in range(NG):
            re, im = cmul(lamb[a], state[a])
            re, im = re + gamb[a] * proj[a][0], im + gamb[a] * proj[a][1]
            new.append((jnp.where(ok, re, state[a][0]), jnp.where(ok, im, state[a][1])))
        return tuple(new)

    ends = lax.fori_loop(0, L, fwd_first, zeros, unroll=4)

    def across(values, table, forward):
        done = []
        for a in range(NG):
            x = values[a]
            for i, d in enumerate((1, 2, 4)):
                shift = d if forward else SUB - d
                other = (pltpu.roll(x[0], shift, 0), pltpu.roll(x[1], shift, 0))
                factor = (table[i, a, 0], table[i, a, 1])
                add = cmul(factor, other) if forward else conj_mul(factor, other)
                x = (x[0] + add[0], x[1] + add[1])
            done.append(x)
        return done

    ends = across(ends, v.hs_f, True)
    for a in range(NG):
        for c in range(2):
            v.msg_f[pl.ds(c * NG + a, 1), :] = ends[a][c][SUB - 1 : SUB, :]
    exchange(v.msg_f, v.chain_f, CF)
    before = [
        tuple(jnp.where(sub > 0, pltpu.roll(x, 1, 0), 0.0) for x in ends[a]) for a in range(NG)
    ]
    w_forward_far(wt_glu)
    w_forward_pair(wt_out)
    own[OWN_C].wait()
    x_sum, y_sum = collect(v.chain_f, v.wt_f, CF)
    state = []
    for a in range(NG):
        start = (
            x_sum[a : a + 1] - y_sum[NG + a : NG + a + 1],
            x_sum[NG + a : NG + a + 1] + y_sum[a : a + 1],
        )
        add = cmul((v.lead_pow[a, 0], v.lead_pow[a, 1]), start)
        state.append((before[a][0] + add[0], before[a][1] + add[1]))
    store_c(v.state, pl.ds(0, SUB), state)

    def fwd_second(pair, state):
        halves = []
        for u in range(2):
            k = 2 * pair + u
            proj = load_c(v.proj, eight(k))
            ok = sub * L + k < my_len
            new = []
            for a in range(NG):
                re, im = cmul(lamb[a], state[a])
                re, im = re + gamb[a] * proj[a][0], im + gamb[a] * proj[a][1]
                new.append((jnp.where(ok, re, state[a][0]), jnp.where(ok, im, state[a][1])))
            state = tuple(new)
            store_c(v.state, eight(k + 1), state)
            halves.append(to_g([(re, -im) for re, im in state]))
        at = pl.ds(pl.multiple_of(pair * 2 * SUB, 2 * SUB), 2 * SUB)
        for s in range(S):
            v.state_low[at, lanes(s)] = jnp.concatenate([halves[0][s], halves[1][s]], axis=0).astype(BF16)
        return state

    lax.fori_loop(0, L // 2, fwd_second, tuple(state), unroll=2)

    own[OWN_WOUT].wait()
    w_ready(wt_out)
    v.wide[...] = nn(v.state_low[...], v.wout[...])
    w_forward_pair(wt_glu)

    def gelu(i):
        rows = rows_of(i)
        mixed_in = v.normed[rows, :] * gain + bias
        mixed = v.wide[rows, :] + skip * mixed_in
        cdf = 0.5 * (1.0 + lax.erf(mixed * (1.0 / math.sqrt(2.0))))
        density = jnp.exp(-0.5 * mixed * mixed) * (1.0 / math.sqrt(2.0 * math.pi))
        v.act[rows, :] = (mixed * cdf).astype(BF16)
        v.dgelu[rows, :] = cdf + mixed * density

    loop(T // CHUNK, gelu)
    w_ready(wt_glu)
    for k in range(2):
        v.pre[k] = nn(v.act[...], v.wglu[k])
    wait_bytes(v.cin.at[:, pl.ds(0, (S - 1) * W)], C, True)
    v.wide[...] = nn(v.perm[...], v.cin[...])

    def glu(i):
        rows = rows_of(i)
        ok = valid_of(i, W)
        for s in range(S):
            here = slice(s * W, (s + 1) * W)
            linear = v.pre[0, rows, here] + par_s[s, 3:4, :]
            gate = v.pre[1, rows, here] + par_s[s, 4:5, :]
            share = jax.nn.sigmoid(gate)
            value = linear * share
            v.out_low[rows, here] = (ok * (v.x[rows, here] + value)).astype(BF16)
            dout = ok * v.wide[rows, here]
            v.d_pre[0, rows, here] = (dout * share).astype(BF16)
            v.d_pre[1, rows, here] = (dout * value * (1.0 - share)).astype(BF16)

    loop(T // CHUNK, glu)

    def give_back(low_ref, nat, result, which, own_which):
        nat[...] = nn(v.back[...], low_ref[...]).astype(BF16)
        to_state(lambda t: nat.at[:, cols(t, W)], result.at[me_s], which)
        copy = pltpu.make_async_copy(nat.at[:, cols(me_s, W)], result.at[me_s], v.here.at[own_which])
        copy.start()
        return copy

    out_copy = give_back(v.out_low, v.out_nat, out_ref, OUT, OWN_OUT)

    for part in (g_in, g_out, g_lin):
        part.half = mine_r
        part.pair = {ROWS: pair_r}
        part.number = lax.div(me_s, 2) * R2 + lax.div(me_r, 2)
        part.slot = lambda r, b: (lax.rem(r, 2), b * R2 + lax.div(r, 2))
        part.owner = lambda n: {ROWS: 2 * lax.rem(n, R2) + mine_r, STATE: 2 * lax.div(n, R2) + mine_s}
    g_gate.half = lax.div(me_s, 2)
    g_gate.pair = {STATE: far}
    g_gate.number = me_r
    g_gate.slot = lambda r, b: (b, r)
    g_gate.owner = lambda n: {ROWS: n}

    def first_send(part):
        for b in range(NG):
            send(part.full.at[:, cols(2 * b + 1 - mine_s, LANES)], part.r1.at[b], part.step, {STATE: sib})

    def first_sum(part):
        wait_bytes(part.r1, part.step, True)

        def one(r):
            rows = pl.ds(pl.multiple_of(r * HB, HB), HB)
            for b in range(NG):
                total = part.full[rows, cols(2 * b + mine_s, LANES)].astype(F32) + part.r1[b, rows, :].astype(F32)
                part.a1[part.slot(r, b)] = total.astype(gdt)

        loop(R, one)
        send(part.a1.at[1 - part.half], part.r2, part.step + 1, part.pair)

    def second_sum(part):
        wait_bytes(part.r2, part.step + 1, True)

        def one(n):
            total = part.a1[part.half, n].astype(F32) + part.r2[n].astype(F32)
            part.a2[n] = total.astype(gdt)

        loop(R, one)
        part.r3[part.number] = part.a2[part.number]

        def give(d, carry):
            n = lax.rem(part.number + d, R)
            send(part.a2.at[n], part.r3.at[part.number], part.step + 2, part.owner(n))
            return carry

        lax.fori_loop(1, R, give, 0)

    def third_sum(part):
        wait_bytes(part.r3.at[pl.ds(0, R - 1)], part.step + 2, True)

        def one(n, total):
            return total + part.r3[n].astype(F32)

        gsum[:, part.at : part.at + LANES] = lax.fori_loop(0, R, one, jnp.zeros((HB, LANES), F32))

    def all_sent(part):
        wait_bytes(part.r1, part.step, False)
        wait_bytes(part.r2, part.step + 1, False)
        wait_bytes(part.r3.at[pl.ds(0, R - 1)], part.step + 2, False)

    for k, part in ((0, g_lin), (1, g_gate)):
        part.full[...] = tn(v.act[...], v.d_pre[k]).astype(gdt)
        first_send(part)
    v.wide[...] = nt(v.d_pre[0], v.wglu[0]) + nt(v.d_pre[1], v.wglu[1])

    def gelu_back(i, total):
        rows = rows_of(i)
        d_mixed = v.wide[rows, :] * v.dgelu[rows, :]
        v.d_mixed[rows, :] = d_mixed
        v.d_rec[rows, :] = d_mixed.astype(BF16)
        return total + fold(d_mixed * (v.normed[rows, :] * gain + bias))

    d_skip = lax.fori_loop(0, T // CHUNK, gelu_back, jnp.zeros((SUB, H), F32))
    d_skip = jnp.sum(d_skip, axis=0, keepdims=True)
    first_sum(g_lin)
    first_sum(g_gate)
    v.wide[...] = nt(v.d_rec[...], v.wout[...])
    g_out.full[...] = tn(v.d_rec[...], v.state_low[...]).astype(gdt)
    first_send(g_out)

    def bwd_first(i, carry):
        k = L - 1 - i
        source = [(re, -im) for re, im in load_g(v.wide, eight(k))]
        store_c(v.source, eight(k), source)
        ok = sub * L + k < my_len
        new = []
        for a in range(NG):
            re, im = source[a][0] + carry[a][0], source[a][1] + carry[a][1]
            nre, nim = conj_mul(lamb[a], (re, im))
            new.append((jnp.where(ok, nre, re), jnp.where(ok, nim, im)))
        return tuple(new)

    heads = lax.fori_loop(0, L, bwd_first, zeros, unroll=4)
    heads = across(heads, v.hs_b, False)
    for a in range(NG):
        for c in range(2):
            v.msg_b[pl.ds(c * NG + a, 1), :] = heads[a][c][0:1, :]
    exchange(v.msg_b, v.chain_b, CB)
    after = [
        tuple(jnp.where(sub < SUB - 1, pltpu.roll(x, SUB - 1, 0), 0.0) for x in heads[a])
        for a in range(NG)
    ]
    first_sum(g_out)
    ones = jnp.ones((2 * SUB, T), BF16)
    d_bias = [nn(ones, v.d_pre[k])[0:1, :] for k in range(2)]
    second_sum(g_lin)

    x_sum, y_sum = collect(v.chain_b, v.wt_b, CB)
    carry = []
    for a in range(NG):
        omega = (
            x_sum[a : a + 1] + y_sum[NG + a : NG + a + 1],
            x_sum[NG + a : NG + a + 1] - y_sum[a : a + 1],
        )
        add = conj_mul((v.tail_pow[a, 0], v.tail_pow[a, 1]), omega)
        carry.append((after[a][0] + add[0], after[a][1] + add[1]))

    def bwd_second(i, item):
        pair = L // 2 - 1 - i
        carry, sums = item
        halves = [None, None]
        for u in (1, 0):
            k = 2 * pair + u
            source = load_c(v.source, eight(k))
            previous = load_c(v.state, eight(k))
            proj = load_c(v.proj, eight(k))
            ok = sub * L + k < my_len
            new, new_sums, low_out = [], [], []
            for a in range(NG):
                re, im = source[a][0] + carry[a][0], source[a][1] + carry[a][1]
                are, aim = jnp.where(ok, re, 0.0), jnp.where(ok, im, 0.0)
                dre, dim = conj_mul(previous[a], (are, aim))
                dg = are * proj[a][0] + aim * proj[a][1]
                new_sums.append((sums[a][0] + dre, sums[a][1] + dim, sums[a][2] + dg))
                low_out.append((gamb[a] * are, gamb[a] * aim))
                nre, nim = conj_mul(lamb[a], (re, im))
                new.append((jnp.where(ok, nre, re), jnp.where(ok, nim, im)))
            carry, sums = tuple(new), tuple(new_sums)
            halves[u] = to_g(low_out)
        at = pl.ds(pl.multiple_of(pair * 2 * SUB, 2 * SUB), 2 * SUB)
        for s in range(S):
            v.d_proj[at, lanes(s)] = jnp.concatenate([halves[0][s], halves[1][s]], axis=0).astype(BF16)
        return carry, sums

    zero = jnp.zeros((SUB, LANES), F32)
    _, sums = lax.fori_loop(
        0, L // 2, bwd_second, (tuple(carry), tuple((zero, zero, zero) for _ in range(NG))), unroll=2
    )

    g_in.full[...] = tn(v.mixed_low[...], v.d_proj[...]).astype(gdt)
    first_send(g_in)
    second_sum(g_out)
    v.wide[...] = nn(v.d_proj[...], v.win[...])
    second_sum(g_gate)
    first_sum(g_in)

    def norm_back(i, totals):
        rows = rows_of(i)
        d_mixed_in = v.wide[rows, :] + skip * v.d_mixed[rows, :]
        normed = v.normed[rows, :]
        inverse = jnp.concatenate([v.inverse[rows, :]] * (H // LANES), axis=1)
        g = d_mixed_in * gain
        first = jnp.mean(g, -1, keepdims=True)
        second = jnp.mean(g * normed, -1, keepdims=True)
        v.din_low[rows, :] = (inverse * (g - first - normed * second)).astype(BF16)
        return totals[0] + fold(d_mixed_in * normed), totals[1] + fold(d_mixed_in)

    zero_h = jnp.zeros((SUB, H), F32)
    d_gain, d_nbias = lax.fori_loop(0, T // CHUNK, norm_back, (zero_h, zero_h))
    d_gain = jnp.sum(d_gain, axis=0, keepdims=True)
    d_nbias = jnp.sum(d_nbias, axis=0, keepdims=True)
    small = v.small
    small[...] = jnp.zeros((S, SUB, LANES), F32)
    for a in range(NG):
        sr, si, sg = (jnp.sum(x, axis=0, keepdims=True) for x in sums[a])
        d_nu = -rate[a] * (sr * lam[a][0] + si * lam[a][1])
        d_theta = angle[a] * (si * lam[a][0] - sr * lam[a][1])
        pair = swap_halves(d_nu, d_theta, low1)
        pair_g = swap_halves(gam[a] * sg, jnp.zeros_like(sg), low1)
        for u in range(2):
            small[2 * a + u, 0:1, :] = pair[u]
            small[2 * a + u, 1:2, :] = pair_g[u]
    for s in range(S):
        here = slice(s * W, (s + 1) * W)
        small[s, 2:3, :] = d_skip[:, here]
        small[s, 3:4, :] = d_bias[0][:, here]
        small[s, 4:5, :] = d_bias[1][:, here]
        small[s, 5:6, :] = d_gain[:, here]
        small[s, 6:7, :] = d_nbias[:, here]
    v.small_r[me_s] = small[...]
    to_state(lambda t: small, v.small_r.at[me_s], SM)

    din_copy = give_back(v.din_low, v.din_nat, din_ref, DIN, OWN_DIN)
    third_sum(g_lin)
    wait_bytes(v.small_r.at[pl.ds(0, S - 1)], SM, True)
    group = v.small_r[0]
    for s in range(1, S):
        group = group + v.small_r[s]
    small2 = v.small2
    v.group[...] = group
    small2[0:SUB, :] = v.group[me_s]
    for s in range(S):
        small2[SUB + s : SUB + s + 1, :] = group[s, 5:6, :]
        small2[SUB + S + s : SUB + S + s + 1, :] = group[s, 6:7, :]
    v.small2_r[me_r] = small2[...]

    def small_rows(d, carry):
        send(small2, v.small2_r.at[me_r], SN, {ROWS: lax.rem(me_r + d, R)})
        return carry

    lax.fori_loop(1, R, small_rows, 0)
    second_sum(g_in)
    third_sum(g_out)
    third_sum(g_gate)
    wait_bytes(v.small2_r.at[pl.ds(0, R - 1)], SN, True)

    def sum_rows(r, total):
        return total + v.small2_r[r]

    vec[...] = lax.fori_loop(0, R, sum_rows, jnp.zeros((2 * SUB, LANES), F32))
    third_sum(g_in)

    out_copy.wait()
    din_copy.wait()
    wait_bytes(out_ref.at[pl.ds(0, S - 1)], OUT, True)
    wait_bytes(din_ref.at[pl.ds(0, S - 1)], DIN, True)
    wait_bytes(out_ref.at[pl.ds(0, S - 1)], OUT, False)
    wait_bytes(din_ref.at[pl.ds(0, S - 1)], DIN, False)
    wait_bytes(v.par_s.at[pl.ds(0, S - 1)], PAR_S, False)
    wait_bytes(v.par_r.at[pl.ds(0, R - 1)], PAR_R, False)
    wait_bytes(v.xin.at[:, pl.ds(0, (S - 1) * W)], X, False)
    for w in (wt_in, wt_out, wt_glu):
        w_sent(w)
    wait_bytes(v.cin.at[:, pl.ds(0, (S - 1) * W)], C, False)
    wait_bytes(v.chain_f.at[pl.ds(0, NR - 1)], CF, False)
    wait_bytes(v.chain_b.at[pl.ds(0, NR - 1)], CB, False)
    wait_bytes(v.small_r.at[pl.ds(0, S - 1)], SM, False)
    wait_bytes(v.small2_r.at[pl.ds(0, R - 1)], SN, False)
    for part in (g_in, g_out, g_lin, g_gate):
        all_sent(part)


def run_block(dims, *args):
    R, S, T, H, W = dims.R, dims.S, dims.T, dims.H, dims.W
    NR, NG, R2, HB, L = R * S, S // 2, R // 2, H // R, T // SUB
    NP, CH = NG * R2, S * LANES
    gdt = BF16 if HB % (2 * SUB) == 0 else F32
    dims.gdt = gdt
    bits = T.bit_length()
    shapes = dict(
        xin=((T, H), BF16),
        cin=((T, H), BF16),
        win=((CH, H), BF16),
        wout=((CH, H), BF16),
        wglu=((2, H, H), BF16),
        glu_raw=((2 * H, W), BF16),
        glu_wide=((2 * CHUNK, W), F32),
        perm=((T, T), BF16),
        back=((T, T), BF16),
        par=((2 * SUB, LANES), F32),
        par_s=((S, 2 * SUB, LANES), F32),
        par_r=((R, 2 * SUB, LANES), F32),
        pows=((bits, NG, 2, SUB, LANES), F32),
        hs_f=((3, NG, 2, SUB, LANES), F32),
        hs_b=((3, NG, 2, SUB, LANES), F32),
        lead_pow=((NG, 2, SUB, LANES), F32),
        tail_pow=((NG, 2, SUB, LANES), F32),
        row_pow=((R, NG, 2, SUB, LANES), F32),
        wt_f=((NR, 2, 2 * NG, LANES), F32),
        wt_b=((NR, 2, 2 * NG, LANES), F32),
        msg_f=((2 * NG, LANES), F32),
        msg_b=((2 * NG, LANES), F32),
        chain_f=((NR, 2 * NG, LANES), F32),
        chain_b=((NR, 2 * NG, LANES), F32),
        x=((T, H), F32),
        normed=((T, H), F32),
        inverse=((T, LANES), F32),
        mixed_low=((T, H), BF16),
        wide=((T, max(H, CH)), F32),
        proj=((T, CH), F32),
        state=((T + SUB, CH), F32),
        state_low=((T, CH), BF16),
        act=((T, H), BF16),
        dgelu=((T, H), F32),
        pre=((2, T, H), F32),
        out_low=((T, H), BF16),
        out_nat=((T, H), BF16),
        d_pre=((2, T, H), BF16),
        d_mixed=((T, H), F32),
        d_rec=((T, H), BF16),
        source=((T, CH), F32),
        d_proj=((T, CH), BF16),
        din_low=((T, H), BF16),
        din_nat=((T, H), BF16),
        small=((S, SUB, LANES), F32),
        small_r=((S, S, SUB, LANES), F32),
        group=((S, SUB, LANES), F32),
        small2=((2 * SUB, LANES), F32),
        small2_r=((R, 2 * SUB, LANES), F32),
    )
    dims.names = [*shapes, *dict(here=0, sent=0, received=0)]
    parts = []
    for _ in range(4):
        parts += [(H, CH), (NG, H, LANES), (2, R, HB, LANES), (R, HB, LANES), (R, HB, LANES), (R, HB, LANES)]
    scratch = [pltpu.VMEM(shape, dtype) for shape, dtype in shapes.values()]
    scratch += [pltpu.SemaphoreType.DMA((n,)) for n in (OWN_DIN + 1, G1 + 12, G1 + 12)]
    scratch += [pltpu.VMEM(shape, gdt) for shape in parts]
    any_spec = pl.BlockSpec(memory_space=pl.ANY)
    vmem = pl.BlockSpec(memory_space=pltpu.VMEM)
    macs = T * H * (2 * CH + 2 * H) * 3 + 4 * T * T * H
    return pl.pallas_call(
        functools.partial(block_kernel, dims),
        out_shape=(
            jax.ShapeDtypeStruct((S, T, W), BF16),
            jax.ShapeDtypeStruct((S, T, W), BF16),
            jax.ShapeDtypeStruct((HB, 4 * LANES), F32),
            jax.ShapeDtypeStruct((2 * SUB, LANES), F32),
        ),
        in_specs=[any_spec] * 5 + [pl.BlockSpec(memory_space=pltpu.SMEM)] * 2 + [vmem] * 7,
        out_specs=(any_spec, any_spec, vmem, vmem),
        scratch_shapes=scratch,
        compiler_params=pltpu.CompilerParams(
            collective_id=0, has_side_effects=True, vmem_limit_bytes=56 * 2**20
        ),
        cost_estimate=pl.CostEstimate(flops=2 * macs, bytes_accessed=8 * 2**20, transcendentals=4 * T * H),
    )(*args)


def on_device(
    inputs,
    bucket,
    lengths,
    nu_log,
    theta_log,
    gamma_log,
    in_proj,
    out_proj,
    skip,
    norm_gain,
    norm_bias,
    glu_weight,
    glu_bias,
    output_cotangent,
):
    row_count, seq, part = inputs.shape
    width = norm_gain.shape[0]
    chans = nu_log.shape[0]
    R, S = lax.axis_size(ROWS), lax.axis_size(STATE)
    dims = SimpleNamespace(R=R, S=S, T=seq, H=width, W=part)
    assert row_count == S and 2 * chans == LANES and part == LANES and S % 2 == 0 and R % 2 == 0

    outputs, d_norm, gsum, vec = run_block(
        dims,
        inputs,
        output_cotangent,
        in_proj.transpose(1, 2, 0).reshape(2 * chans, width),
        out_proj.reshape(2 * chans, width),
        glu_weight.reshape(2 * width, part),
        bucket,
        lengths,
        nu_log[None],
        theta_log[None],
        gamma_log[None],
        skip[None],
        glu_bias,
        norm_gain[None],
        norm_bias[None],
    )
    return finish(dims, lengths, outputs, d_norm, output_cotangent, gsum, vec)


def finish_kernel(dims, *refs):
    S, T, HB = dims.S, dims.T, dims.H // dims.R
    (lengths, out_in, d_norm, cot, gsum, vec) = refs[:6]
    (out, d_inputs, d_nu, d_theta, d_gamma, d_in, d_out, d_skip, d_gain, d_bias, d_glu, d_glu_bias) = refs[6:]
    row = pl.program_id(0)
    out[...] = out_in[...]
    length = lengths[row]

    def one(i):
        rows = pl.ds(pl.multiple_of(i * CHUNK, CHUNK), CHUNK)
        place = lax.broadcasted_iota(jnp.int32, (CHUNK, LANES), 0) + i * CHUNK
        direct = jnp.where(place < length, cot[0, rows, :].astype(F32), 0.0)
        d_inputs[0, rows, :] = d_norm[0, rows, :].astype(F32) + direct

    loop(T // CHUNK, one, unroll=2)

    @pl.when(row == 0)
    def _():
        d_nu[...] = vec[0:1, 0:HALF]
        d_theta[...] = pltpu.roll(vec[0:1, :], HALF, 1)[:, 0:HALF]
        d_gamma[...] = vec[1:2, 0:HALF]
        d_skip[...] = vec[2:3, :]
        d_glu_bias[...] = vec[3:5, :]
        for s in range(S):
            here = slice(s * LANES, (s + 1) * LANES)
            d_gain[:, here] = vec[SUB + s : SUB + s + 1, :]
            d_bias[:, here] = vec[SUB + S + s : SUB + S + s + 1, :]
        both = gsum[:, 0:LANES]
        d_in[pl.ds(0, HB, stride=2), :] = both[:, 0:HALF]
        d_in[pl.ds(1, HB, stride=2), :] = pltpu.roll(both, HALF, 1)[:, 0:HALF]
        d_out[...] = gsum[:, LANES : 2 * LANES].T
        d_glu[pl.ds(0, HB, stride=2), :] = gsum[:, 2 * LANES : 3 * LANES]
        d_glu[pl.ds(1, HB, stride=2), :] = gsum[:, 3 * LANES : 4 * LANES]


def finish(dims, lengths, outputs, d_norm, cot, gsum, vec):
    R, S, T, H, W = dims.R, dims.S, dims.T, dims.H, dims.W
    HB = H // R
    row = pl.BlockSpec((1, T, W), lambda i: (i, 0, 0))

    def whole(shape):
        return pl.BlockSpec(shape, lambda i: (0,) * len(shape))

    small = [(1, HALF)] * 3 + [(2 * HB, HALF), (LANES, HB), (1, W), (1, H), (1, H), (2 * HB, W), (2, W)]
    got = pl.pallas_call(
        functools.partial(finish_kernel, dims),
        grid=(S,),
        out_shape=(
            jax.ShapeDtypeStruct((S, T, W), BF16),
            jax.ShapeDtypeStruct((S, T, W), F32),
            *(jax.ShapeDtypeStruct(shape, F32) for shape in small),
        ),
        in_specs=[
            pl.BlockSpec(memory_space=pltpu.SMEM), row, row, row, whole((HB, 4 * LANES)), whole((2 * SUB, LANES))
        ],
        out_specs=(row, row, *(whole(shape) for shape in small)),
    )(lengths, outputs, d_norm, cot, gsum, vec)
    out, d_inputs, d_nu, d_theta, d_gamma, d_in, d_out, d_skip, d_gain, d_bias, d_glu, d_glu_bias = got
    return (
        out,
        d_inputs,
        d_nu.reshape(HALF),
        d_theta.reshape(HALF),
        d_gamma.reshape(HALF),
        d_in.reshape(HB, 2, HALF),
        d_out.reshape(2, HALF, HB),
        d_skip.reshape(W),
        d_gain.reshape(H),
        d_bias.reshape(H),
        d_glu.reshape(HB, 2, W),
        d_glu_bias,
    )


def solution(mesh):
    return jax.shard_map(
        on_device,
        mesh=mesh,
        in_specs=(
            P(ROWS, None, STATE),
            P(ROWS),
            P(ROWS),
            P(STATE),
            P(STATE),
            P(STATE),
            P(None, None, STATE),
            P(None, STATE, None),
            P(STATE),
            P(),
            P(),
            P(None, None, STATE),
            P(None, STATE),
            P(ROWS, None, STATE),
        ),
        out_specs=(
            P(ROWS, None, STATE),
            P(ROWS, None, STATE),
            P(STATE),
            P(STATE),
            P(STATE),
            P(ROWS, None, STATE),
            P(None, STATE, ROWS),
            P(STATE),
            P(),
            P(),
            P(ROWS, None, STATE),
            P(None, STATE),
        ),
        check_vma=False,
    )
```

```python
import functools
import math
from types import SimpleNamespace

import jax
import jax.numpy as jnp
from jax import lax
from jax.experimental import pallas as pl
from jax.experimental.pallas import tpu as pltpu
from jax.sharding import PartitionSpec as P

epsilon = 1e-05

F32 = jnp.float32
BF16 = jnp.bfloat16
MESH = pl.DeviceIdType.MESH
ROWS, STATE = "rows", "state"
SUB = 8
LANES = 128
HALF = LANES // 2
CHUNK = 64
SEG = 32
LEVELS = tuple(1 << i for i in range(SEG.bit_length() - 1))

OWN_X, OWN_WIN, OWN_WOUT, OWN_WGLU, OWN_C, OWN_OUT, OWN_DIN = range(7)
PAR_S, PAR_R, X, C, CF, CB, OUT, DIN, SM, SN, W1 = range(11)
SIB, FAR, PEER, FAR_SIB = range(4)
G1 = W1 + 12
G2 = G1 + 4


def loop(count, body, unroll=1):
    def step(i, carry):
        body(i)
        return carry

    lax.fori_loop(0, count, step, 0, unroll=unroll)


def nn(a, b):
    return lax.dot_general(a, b, (((1,), (0,)), ((), ())), preferred_element_type=F32)


def nt(a, b):
    return lax.dot_general(a, b, (((1,), (1,)), ((), ())), preferred_element_type=F32)


def tn(a, b):
    return lax.dot_general(a, b, (((0,), (0,)), ((), ())), preferred_element_type=F32)


def cmul(a, b):
    return a[0] * b[0] - a[1] * b[1], a[0] * b[1] + a[1] * b[0]


def conj_mul(a, b):
    return a[0] * b[0] + a[1] * b[1], a[0] * b[1] - a[1] * b[0]


def swap_halves(u, v, low):
    return (
        jnp.where(low, u, pltpu.roll(v, HALF, 1)),
        jnp.where(low, pltpu.roll(u, HALF, 1), v),
    )


def fold(x):
    return jnp.sum(x.reshape(x.shape[0] // SUB, SUB, x.shape[1]), axis=0)


def block_kernel(dims, *refs):
    R, S, T, H, W, gdt = dims.R, dims.S, dims.T, dims.H, dims.W, dims.gdt
    NR, NG, R2, HB, L = R * S, S // 2, R // 2, H // R, T // SEG
    Q = 4 if R % 4 == 0 else 2
    BITS = T.bit_length()
    (inputs, cot, w_in, w_out, w_glu) = refs[:5]
    (bucket_ref, lengths_ref, nu_ref, theta_ref, gamma_ref, skip_ref, glu_bias_ref, gain_ref, bias_ref) = refs[5:14]
    (out_ref, din_ref, gsum, vec) = refs[14:18]
    total = 18 + len(dims.names)
    v = SimpleNamespace(**dict(zip(dims.names, refs[18:total])))
    parts = [
        SimpleNamespace(full=refs[total + 2 * i], r1=refs[total + 2 * i + 1], step=G1 + i, at=i * LANES, routes=[])
        for i in range(4)
    ]
    g_in, g_out, g_lin, g_gate = parts
    total += 8
    for i, (part, over_x, first, lines) in enumerate(routes_of(R, H)):
        a1, r2, a2, r3 = refs[total + 4 * i : total + 4 * i + 4]
        parts[part].routes.append(
            SimpleNamespace(
                part=parts[part], over_x=over_x, first=first, lines=lines, a1=a1, r2=r2, a2=a2, r3=r3, step=G2 + 2 * i
            )
        )

    me_r, me_s = lax.axis_index(ROWS), lax.axis_index(STATE)
    me = me_r * S + me_s

    def cols(i, width):
        return pl.ds(pl.multiple_of(i * width, LANES), width)

    def rows_of(i):
        return pl.ds(pl.multiple_of(i * CHUNK, CHUNK), CHUNK)

    def wait_bytes(ref, which, arrived):
        pltpu.make_async_copy(ref, ref, (v.received if arrived else v.sent).at[which]).wait()

    def send(src, dst, which, target):
        pltpu.make_async_remote_copy(
            src_ref=src,
            dst_ref=dst,
            send_sem=v.sent.at[which],
            recv_sem=v.received.at[which],
            device_id=target,
            device_id_type=MESH,
        ).start()

    def to_state(src_of, dst, which):
        for j in (2, 3, 1) if S == 4 else range(1, S):
            t = lax.rem(me_s + j, S)
            send(src_of(t), dst, which, {STATE: t})

    sib = me_s + 1 - 2 * lax.rem(me_s, 2)
    far = lax.rem(me_s + NG, S)
    sib_far = lax.rem(sib + NG, S)
    pair_r = me_r + 1 - 2 * lax.rem(me_r, 2)
    group_r = me_r - lax.rem(me_r, Q)
    piece = lax.rem(me_r, Q)
    mine_s = lax.rem(me_s, 2)
    mine_r = lax.rem(me_r, 2)

    def line_block(ref, s, p=None):
        if p is None:
            return ref.at[pl.ds(pl.multiple_of(s * LANES, LANES), LANES), :]
        size = LANES // Q
        return ref.at[pl.ds(pl.multiple_of(s * LANES + p * size, size), size), :]

    def glu_block(ref, s, p=None):
        size = H // Q
        rows = slice(None) if p is None else pl.ds(pl.multiple_of(p * size, size), size)
        return ref.at[:, rows, cols(s, W)]

    own = [
        (w_glu, v.glu_raw, OWN_WGLU),
        (w_in, line_block(v.win, me_s), OWN_WIN),
        (w_out, line_block(v.wout, me_s), OWN_WOUT),
        (inputs.at[me_s], v.xin.at[:, cols(me_s, W)], OWN_X),
        (cot.at[me_s], v.cin.at[:, cols(me_s, W)], OWN_C),
    ]
    own = {which: pltpu.make_async_copy(a, b, v.here.at[which]) for a, b, which in own}
    for copy in own.values():
        copy.start()

    barrier = pltpu.get_barrier_semaphore()

    def greet(d, carry):
        t = lax.rem(me + d, NR)
        pl.semaphore_signal(
            barrier,
            inc=1,
            device_id={ROWS: lax.div(t, S), STATE: lax.rem(t, S)},
            device_id_type=MESH,
        )
        return carry

    lax.fori_loop(1, NR, greet, 0)

    par = v.par
    par[...] = jnp.zeros((2 * SUB, LANES), F32)
    par[0:1, 0:HALF] = nu_ref[...]
    par[0:1, HALF:LANES] = theta_ref[...]
    par[1:2, 0:HALF] = gamma_ref[...]
    par[2:3, :] = skip_ref[...]
    par[3:5, :] = glu_bias_ref[...]
    for i in range(S):
        par[SUB + i : SUB + i + 1, :] = jnp.full((1, LANES), bucket_ref[i], jnp.int32).astype(F32)
        par[SUB + S + i : SUB + S + i + 1, :] = jnp.full((1, LANES), lengths_ref[i], jnp.int32).astype(F32)
    v.par_s[me_s] = par[...]
    v.par_r[me_r] = par[...]

    pl.semaphore_wait(barrier, NR - 1)

    to_state(lambda t: par, v.par_s.at[me_s], PAR_S)

    def par_rows(d, carry):
        send(par, v.par_r.at[me_r], PAR_R, {ROWS: lax.rem(me_r + d, R)})
        return carry

    lax.fori_loop(1, R, par_rows, 0)

    def w_send(w, own_block, own_piece):
        send(own_piece, w.block(w.ref, me_s, piece), w.step + FAR, {STATE: far})
        send(own_block, w.block(w.ref, me_s), w.step + SIB, {STATE: sib})

    def w_forward_far(w):
        here = w.block(w.ref, far, piece)
        wait_bytes(here, w.step + FAR, True)
        for j in range(1, Q):
            send(here, here, w.step + PEER, {ROWS: group_r + lax.rem(piece + j, Q)})

    def w_forward_all(w):
        wait_bytes(w.rest, w.step + PEER, True)
        send(w.block(w.ref, far), w.block(w.ref, far), w.step + FAR_SIB, {STATE: sib})

    def w_ready(w):
        wait_bytes(w.block(w.ref, sib), w.step + SIB, True)
        wait_bytes(w.block(w.ref, sib_far), w.step + FAR_SIB, True)

    def w_sent(w):
        wait_bytes(w.block(w.ref, sib), w.step + SIB, False)
        wait_bytes(w.block(w.ref, sib), w.step + FAR_SIB, False)
        wait_bytes(w.block(w.ref, sib, piece), w.step + FAR, False)
        wait_bytes(w.rest, w.step + PEER, False)

    others = pl.ds(0, LANES - LANES // Q)
    wt_in = SimpleNamespace(ref=v.win, block=line_block, step=W1, rest=v.win.at[others, :])
    wt_out = SimpleNamespace(ref=v.wout, block=line_block, step=W1 + 4, rest=v.wout.at[others, :])
    wt_glu = SimpleNamespace(
        ref=v.wglu, block=glu_block, step=W1 + 8, rest=v.wglu.at[:, pl.ds(0, H - H // Q), pl.ds(0, W)]
    )

    def piece_of(ref):
        size = LANES // Q
        return ref.at[pl.ds(pl.multiple_of(piece * size, size), size), :]

    w_send(wt_in, w_in, piece_of(w_in))
    to_state(lambda t: inputs.at[t], v.xin.at[:, cols(me_s, W)], X)
    w_send(wt_out, w_out, piece_of(w_out))
    own[OWN_WGLU].wait()

    def split_glu(i):
        here = rows_of(i)
        v.glu_wide[...] = v.glu_raw[pl.ds(pl.multiple_of(i * 2 * CHUNK, 2 * CHUNK), 2 * CHUNK), :].astype(F32)
        for k in range(2):
            v.wglu[k, here, cols(me_s, W)] = v.glu_wide[pl.ds(k, CHUNK, stride=2), :].astype(BF16)

    loop(H // CHUNK, split_glu)
    w_send(wt_glu, glu_block(v.wglu, me_s), glu_block(v.wglu, me_s, piece))

    line = lax.broadcasted_iota(jnp.int32, (CHUNK, T), 0)
    place = lax.broadcasted_iota(jnp.int32, (CHUNK, T), 1)

    def orders(i):
        base = pl.multiple_of(i * CHUNK, CHUNK)
        at = line + base
        v.perm[pl.ds(base, CHUNK), :] = (
            place == lax.rem(at, SEG) * L + lax.div(at, SEG)
        ).astype(F32).astype(BF16)
        v.back[pl.ds(base, CHUNK), :] = (
            at == lax.rem(place, SEG) * L + lax.div(place, SEG)
        ).astype(F32).astype(BF16)

    loop(T // CHUNK, orders)

    w_forward_far(wt_in)

    low = lax.broadcasted_iota(jnp.int32, (SEG, LANES), 1) < HALF
    low1 = lax.broadcasted_iota(jnp.int32, (1, LANES), 1) < HALF
    seg = lax.broadcasted_iota(jnp.int32, (SEG, LANES), 0)

    wait_bytes(v.par_s.at[pl.ds(0, S - 1)], PAR_S, True)
    wait_bytes(v.par_r.at[pl.ds(0, R - 1)], PAR_R, True)
    par_s, par_r = v.par_s, v.par_r
    lam, gam, rate, angle = [], [], [], []
    for a in range(NG):
        nu, theta = swap_halves(par_s[2 * a, 0:1, :], par_s[2 * a + 1, 0:1, :], low1)
        rate.append(jnp.exp(nu))
        angle.append(jnp.exp(theta))
        magnitude = jnp.exp(-rate[a])
        lam.append((magnitude * jnp.cos(angle[a]), magnitude * jnp.sin(angle[a])))
        gam.append(jnp.exp(swap_halves(par_s[2 * a, 1:2, :], par_s[2 * a + 1, 1:2, :], low1)[0]))
    skip = jnp.concatenate([par_s[s, 2:3, :] for s in range(S)], axis=1)
    gain, bias = gain_ref[...], bias_ref[...]
    power = [[(jnp.broadcast_to(l[0], (SUB, LANES)), jnp.broadcast_to(l[1], (SUB, LANES))) for l in lam]]
    for _ in range(BITS - 1):
        power.append([cmul(p, p) for p in power[-1]])
    for b in range(BITS):
        for a in range(NG):
            for c in range(2):
                v.pows[b, a, c] = power[b][a][c]

    def raised(exponent):
        result = [(jnp.ones(exponent.shape, F32), jnp.zeros(exponent.shape, F32)) for _ in range(NG)]
        for b in range(BITS):
            hit = (lax.shift_right_logical(exponent, b) & 1) == 1
            for a in range(NG):
                re, im = cmul(result[a], (v.pows[b, a, 0, 0:1, :], v.pows[b, a, 1, 0:1, :]))
                result[a] = (jnp.where(hit, re, result[a][0]), jnp.where(hit, im, result[a][1]))
        return result

    my_bucket = par_r[me_r, pl.ds(SUB + me_s, 1), :]
    len1 = par_r[me_r, pl.ds(SUB + S + me_s, 1), :].astype(jnp.int32)
    my_len = jnp.broadcast_to(len1, (SEG, LANES))
    seg_pow = raised(jnp.clip(my_len - seg * L, 0, L))
    lead_pow = raised(jnp.minimum(my_len, seg * L))
    tail_pow = raised(jnp.maximum(my_len - (seg + 1) * L, 0))
    for a in range(NG):
        ahead = seg_pow[a]
        behind = seg_pow[a]
        for i, d in enumerate(LEVELS):
            for c in range(2):
                v.hs_f[i, a, c] = jnp.where(seg >= d, ahead[c], 0.0)
                v.hs_b[i, a, c] = jnp.where(seg < SEG - d, behind[c], 0.0)
            ahead = cmul(ahead, (pltpu.roll(ahead[0], d, 0), pltpu.roll(ahead[1], d, 0)))
            behind = cmul(behind, (pltpu.roll(behind[0], SEG - d, 0), pltpu.roll(behind[1], SEG - d, 0)))
        for c in range(2):
            v.lead_pow[a, c] = lead_pow[a][c]
            v.tail_pow[a, c] = tail_pow[a][c]

    def row_powers(r):
        lens = par_r[r, SUB : 2 * SUB, :].astype(jnp.int32)
        result = raised(lens)
        for a in range(NG):
            for c in range(2):
                v.row_pow[r, a, c] = result[a][c]

    loop(R, row_powers)

    def weights(into, forward):
        def one(i, run):
            p = NR - 1 - i if forward else i
            r, s = lax.div(p, S), lax.rem(p, S)
            here = par_r[r, pl.ds(SUB + s, 1), :]
            side = (p < me) if forward else (p > me)
            hit = (here == my_bucket) & (my_bucket > 0.5) & jnp.broadcast_to(side, (1, LANES))
            after = []
            for a in range(NG):
                re, im = run[a]
                re_w, im_w = jnp.where(hit, re, 0.0), jnp.where(hit, im, 0.0)
                for k in range(2):
                    into[p, 0, pl.ds(k * NG + a, 1), :] = re_w
                    into[p, 1, pl.ds(k * NG + a, 1), :] = im_w
                factor = (
                    v.row_pow[r, a, 0, pl.ds(S + s, 1), :],
                    v.row_pow[r, a, 1, pl.ds(S + s, 1), :],
                )
                re_n, im_n = cmul((re, im), factor)
                after.append((jnp.where(hit, re_n, re), jnp.where(hit, im_n, im)))
            return tuple(after)

        first = tuple((jnp.ones((1, LANES), F32), jnp.zeros((1, LANES), F32)) for _ in range(NG))
        lax.fori_loop(0, NR, one, first)

    weights(v.wt_f, True)
    weights(v.wt_b, False)

    def exchange(msg, chain, which):
        chain[me] = msg[...]

        def one(d, carry):
            t = lax.rem(me + d, NR)
            send(msg, chain.at[me], which, {ROWS: lax.div(t, S), STATE: lax.rem(t, S)})
            return carry

        lax.fori_loop(1, NR, one, 0)

    def collect(chain, into, which):
        wait_bytes(chain.at[pl.ds(0, NR - 1)], which, True)

        def one(p, sums):
            x = chain[p]
            return sums[0] + into[p, 0] * x, sums[1] + into[p, 1] * x

        zero = jnp.zeros((2 * NG, LANES), F32)
        return lax.fori_loop(0, NR, one, (zero, zero), unroll=8)

    pos = lax.broadcasted_iota(jnp.int32, (CHUNK, LANES), 0)
    pos = lax.rem(pos, SEG) * L + lax.div(pos, SEG)

    def valid_of(i, width):
        ok = jnp.where(pos + i * (CHUNK // SEG) < len1, 1.0, 0.0)
        return jnp.concatenate([ok] * (width // LANES), axis=1) if width > LANES else ok

    w_forward_all(wt_in)

    own[OWN_X].wait()
    wait_bytes(v.xin.at[:, pl.ds(0, (S - 1) * W)], X, True)
    v.x[...] = nn(v.perm[...], v.xin[...])

    def layer_norm(i):
        rows = rows_of(i)
        x = v.x[rows, :]
        centred = x - jnp.mean(x, -1, keepdims=True)
        inverse = lax.rsqrt(jnp.mean(centred * centred, -1, keepdims=True) + epsilon)
        normed = centred * inverse
        v.normed[rows, :] = normed
        v.inverse[rows, :] = jnp.broadcast_to(inverse, (CHUNK, LANES))
        v.mixed_low[rows, :] = (normed * gain + bias).astype(BF16)

    loop(T // CHUNK, layer_norm, unroll=2)
    own[OWN_WIN].wait()
    w_ready(wt_in)
    v.wide[...] = nt(v.mixed_low[...], v.win[...])
    w_forward_far(wt_out)

    lamb = [tuple(jnp.broadcast_to(c, (SEG, LANES)) for c in l) for l in lam]
    gamb = [jnp.broadcast_to(g, (SEG, LANES)) for g in gam]

    def lanes(i):
        return slice(i * LANES, (i + 1) * LANES)

    def load_c(ref, at):
        return [(ref[at, lanes(a)], ref[at, lanes(NG + a)]) for a in range(NG)]

    def store_c(ref, at, values):
        for a in range(NG):
            ref[at, lanes(a)] = values[a][0]
            ref[at, lanes(NG + a)] = values[a][1]

    def load_g(ref, at):
        return [swap_halves(ref[at, lanes(2 * a)], ref[at, lanes(2 * a + 1)], low) for a in range(NG)]

    def to_g(values):
        return [g for a in range(NG) for g in swap_halves(values[a][0], values[a][1], low)]

    def step_of(k):
        return pl.ds(pl.multiple_of(k * SEG, SEG), SEG)

    zeros = tuple((jnp.zeros((SEG, LANES), F32), jnp.zeros((SEG, LANES), F32)) for _ in range(NG))

    def advance(k, state, proj):
        ok = seg * L + k < my_len
        new = []
        for a in range(NG):
            re, im = cmul(lamb[a], state[a])
            re, im = re + gamb[a] * proj[a][0], im + gamb[a] * proj[a][1]
            new.append((jnp.where(ok, re, state[a][0]), jnp.where(ok, im, state[a][1])))
        return tuple(new)

    def fwd_first(k, state):
        proj = load_g(v.wide, step_of(k))
        store_c(v.proj, step_of(k), proj)
        return advance(k, state, proj)

    ends = lax.fori_loop(0, L, fwd_first, zeros, unroll=4)

    def across(values, table, forward):
        done = []
        for a in range(NG):
            x = values[a]
            for i, d in enumerate(LEVELS):
                shift = d if forward else SEG - d
                other = (pltpu.roll(x[0], shift, 0), pltpu.roll(x[1], shift, 0))
                factor = (table[i, a, 0], table[i, a, 1])
                add = cmul(factor, other) if forward else conj_mul(factor, other)
                x = (x[0] + add[0], x[1] + add[1])
            done.append(x)
        return done

    ends = across(ends, v.hs_f, True)
    for a in range(NG):
        for c in range(2):
            v.msg_f[pl.ds(c * NG + a, 1), :] = ends[a][c][SEG - 1 : SEG, :]
    exchange(v.msg_f, v.chain_f, CF)
    before = [
        tuple(jnp.where(seg > 0, pltpu.roll(x, 1, 0), 0.0) for x in ends[a]) for a in range(NG)
    ]
    to_state(lambda t: cot.at[t], v.cin.at[:, cols(me_s, W)], C)
    w_forward_far(wt_glu)
    w_forward_all(wt_out)
    own[OWN_C].wait()
    x_sum, y_sum = collect(v.chain_f, v.wt_f, CF)
    state = []
    for a in range(NG):
        start = (
            x_sum[a : a + 1] - y_sum[NG + a : NG + a + 1],
            x_sum[NG + a : NG + a + 1] + y_sum[a : a + 1],
        )
        add = cmul((v.lead_pow[a, 0], v.lead_pow[a, 1]), start)
        state.append((before[a][0] + add[0], before[a][1] + add[1]))
    store_c(v.state, pl.ds(0, SEG), state)

    def fwd_second(k, state):
        state = advance(k, state, load_c(v.proj, step_of(k)))
        store_c(v.state, step_of(k + 1), state)
        low_out = to_g([(re, -im) for re, im in state])
        for s in range(S):
            v.state_low[step_of(k), lanes(s)] = low_out[s].astype(BF16)
        return state

    lax.fori_loop(0, L, fwd_second, tuple(state), unroll=4)

    own[OWN_WOUT].wait()
    w_ready(wt_out)
    v.wide[...] = nn(v.state_low[...], v.wout[...])
    w_forward_all(wt_glu)

    def gelu(i):
        rows = rows_of(i)
        mixed_in = v.normed[rows, :] * gain + bias
        mixed = v.wide[rows, :] + skip * mixed_in
        cdf = 0.5 * (1.0 + lax.erf(mixed * (1.0 / math.sqrt(2.0))))
        density = jnp.exp(-0.5 * mixed * mixed) * (1.0 / math.sqrt(2.0 * math.pi))
        v.act[rows, :] = (mixed * cdf).astype(BF16)
        v.dgelu[rows, :] = cdf + mixed * density

    loop(T // CHUNK, gelu, unroll=2)
    w_ready(wt_glu)
    for k in range(2):
        v.pre[k] = nn(v.act[...], v.wglu[k])

    def glu(i):
        rows = rows_of(i)
        ok = valid_of(i, W)
        for s in range(S):
            here = slice(s * W, (s + 1) * W)
            linear = v.pre[0, rows, here] + par_s[s, 3:4, :]
            gate = v.pre[1, rows, here] + par_s[s, 4:5, :]
            share = jax.nn.sigmoid(gate)
            value = linear * share
            v.out_low[rows, here] = (ok * (v.x[rows, here] + value)).astype(BF16)
            v.pre[0, rows, here] = ok * share
            v.pre[1, rows, here] = ok * (value * (1.0 - share))

    loop(T // CHUNK, glu, unroll=2)

    def give_back(low_ref, nat, result, own_which):
        nat[...] = nn(v.back[...], low_ref[...]).astype(BF16)
        copy = pltpu.make_async_copy(nat.at[:, cols(me_s, W)], result.at[me_s], v.here.at[own_which])
        copy.start()
        return copy

    def give_to(nat, result, which, t):
        send(nat.at[:, cols(t, W)], result.at[me_s], which, {STATE: t})

    out_copy = give_back(v.out_low, v.out_nat, out_ref, OWN_OUT)
    give_to(v.out_nat, out_ref, OUT, far)
    wait_bytes(v.cin.at[:, pl.ds(0, (S - 1) * W)], C, True)
    v.wide[...] = nn(v.perm[...], v.cin[...])

    def glu_back(i):
        rows = rows_of(i)
        dout = v.wide[rows, :]
        for k in range(2):
            v.d_pre[k, rows, :] = (dout * v.pre[k, rows, :]).astype(BF16)

    loop(T // CHUNK, glu_back, unroll=2)

    for part in parts:
        for route in part.routes:
            if route.over_x:
                route.half = lax.div(me_s, 2)
                route.pair = {STATE: far}
                route.number = me_r
                route.slot = lambda r, b: (b, r)
                route.owner = lambda n: {ROWS: n}
            else:
                route.half = mine_r
                route.pair = {ROWS: pair_r}
                route.number = lax.div(me_s, 2) * R2 + lax.div(me_r, 2)
                route.slot = lambda r, b: (lax.rem(r, 2), b * R2 + lax.div(r, 2))
                route.owner = lambda n: {ROWS: 2 * lax.rem(n, R2) + mine_r, STATE: 2 * lax.div(n, R2) + mine_s}

    def first_send(part):
        for b in range(NG):
            send(part.full.at[:, cols(2 * b + 1 - mine_s, LANES)], part.r1.at[b], part.step, {STATE: sib})

    def first_wait(part):
        wait_bytes(part.r1, part.step, True)

    def first_sum(route):
        part = route.part

        def one(r):
            rows = pl.ds(pl.multiple_of(r * HB + route.first, route.lines), route.lines)
            for b in range(NG):
                total = part.full[rows, cols(2 * b + mine_s, LANES)].astype(F32) + part.r1[b, rows, :].astype(F32)
                route.a1[route.slot(r, b)] = total.astype(gdt)

        loop(R, one, unroll=2)
        send(route.a1.at[1 - route.half], route.r2, route.step, route.pair)

    def second_sum(route):
        wait_bytes(route.r2, route.step, True)

        def one(n):
            total = route.a1[route.half, n].astype(F32) + route.r2[n].astype(F32)
            route.a2[n] = total.astype(gdt)

        loop(R, one, unroll=2)
        route.r3[route.number] = route.a2[route.number]

        def give(d, carry):
            n = lax.rem(route.number + d, R)
            send(route.a2.at[n], route.r3.at[route.number], route.step + 1, route.owner(n))
            return carry

        lax.fori_loop(1, R, give, 0)

    def third_sum(route):
        wait_bytes(route.r3.at[pl.ds(0, R - 1)], route.step + 1, True)

        def one(n, total):
            return total + route.r3[n].astype(F32)

        total = lax.fori_loop(0, R, one, jnp.zeros((route.lines, LANES), F32), unroll=2)
        gsum[route.first : route.first + route.lines, route.part.at : route.part.at + LANES] = total

    def all_sent(part):
        wait_bytes(part.r1, part.step, False)
        for route in part.routes:
            wait_bytes(route.r2, route.step, False)
            wait_bytes(route.r3.at[pl.ds(0, R - 1)], route.step + 1, False)

    for k, part in ((0, g_lin), (1, g_gate)):
        part.full[...] = tn(v.act[...], v.d_pre[k]).astype(gdt)
        first_send(part)
    v.wide[...] = nt(v.d_pre[0], v.wglu[0]) + nt(v.d_pre[1], v.wglu[1])

    def gelu_back(i, total):
        rows = rows_of(i)
        d_mixed = v.wide[rows, :] * v.dgelu[rows, :]
        v.d_mixed[rows, :] = d_mixed
        v.d_rec[rows, :] = d_mixed.astype(BF16)
        return total + fold(d_mixed * (v.normed[rows, :] * gain + bias))

    d_skip = lax.fori_loop(0, T // CHUNK, gelu_back, jnp.zeros((SUB, H), F32), unroll=2)
    d_skip = jnp.sum(d_skip, axis=0, keepdims=True)
    v.wide[...] = nt(v.d_rec[...], v.wout[...])
    first_wait(g_lin)
    first_sum(g_lin.routes[0])
    g_out.full[...] = tn(v.d_rec[...], v.state_low[...]).astype(gdt)
    first_send(g_out)

    def retreat(k, source, carry):
        ok = seg * L + k < my_len
        adjoint, new = [], []
        for a in range(NG):
            re, im = source[a][0] + carry[a][0], source[a][1] + carry[a][1]
            adjoint.append((re, im))
            nre, nim = conj_mul(lamb[a], (re, im))
            new.append((jnp.where(ok, nre, re), jnp.where(ok, nim, im)))
        return ok, adjoint, tuple(new)

    def bwd_first(i, carry):
        k = L - 1 - i
        source = [(re, -im) for re, im in load_g(v.wide, step_of(k))]
        store_c(v.source, step_of(k), source)
        return retreat(k, source, carry)[2]

    heads = lax.fori_loop(0, L, bwd_first, zeros, unroll=4)
    heads = across(heads, v.hs_b, False)
    for a in range(NG):
        for c in range(2):
            v.msg_b[pl.ds(c * NG + a, 1), :] = heads[a][c][0:1, :]
    exchange(v.msg_b, v.chain_b, CB)
    after = [
        tuple(jnp.where(seg < SEG - 1, pltpu.roll(x, SEG - 1, 0), 0.0) for x in heads[a])
        for a in range(NG)
    ]
    first_wait(g_gate)
    first_sum(g_gate.routes[0])
    give_to(v.out_nat, out_ref, OUT, sib)
    give_to(v.out_nat, out_ref, OUT, sib_far)
    first_wait(g_out)
    first_sum(g_out.routes[0])
    ones = jnp.ones((2 * SUB, T), BF16)
    d_bias = [nn(ones, v.d_pre[k])[0:1, :] for k in range(2)]
    second_sum(g_lin.routes[0])

    x_sum, y_sum = collect(v.chain_b, v.wt_b, CB)
    carry = []
    for a in range(NG):
        omega = (
            x_sum[a : a + 1] + y_sum[NG + a : NG + a + 1],
            x_sum[NG + a : NG + a + 1] - y_sum[a : a + 1],
        )
        add = conj_mul((v.tail_pow[a, 0], v.tail_pow[a, 1]), omega)
        carry.append((after[a][0] + add[0], after[a][1] + add[1]))

    def bwd_second(i, item):
        k = L - 1 - i
        carry, sums = item
        ok, adjoint, carry = retreat(k, load_c(v.source, step_of(k)), carry)
        previous = load_c(v.state, step_of(k))
        proj = load_c(v.proj, step_of(k))
        new_sums, low_out = [], []
        for a in range(NG):
            re, im = (jnp.where(ok, x, 0.0) for x in adjoint[a])
            dre, dim = conj_mul(previous[a], (re, im))
            dg = re * proj[a][0] + im * proj[a][1]
            new_sums.append(tuple(x + fold(y) for x, y in zip(sums[a], (dre, dim, dg))))
            low_out.append((gamb[a] * re, gamb[a] * im))
        low_out = to_g(low_out)
        for s in range(S):
            v.d_proj[step_of(k), lanes(s)] = low_out[s].astype(BF16)
        return carry, tuple(new_sums)

    zero = jnp.zeros((SUB, LANES), F32)
    _, sums = lax.fori_loop(
        0, L, bwd_second, (tuple(carry), tuple((zero, zero, zero) for _ in range(NG))), unroll=2
    )

    g_in.full[...] = tn(v.mixed_low[...], v.d_proj[...]).astype(gdt)
    first_send(g_in)
    v.wide[...] = nn(v.d_proj[...], v.win[...])
    second_sum(g_out.routes[0])
    first_wait(g_in)
    for route in g_in.routes:
        first_sum(route)
    second_sum(g_gate.routes[0])

    def norm_back(i, totals):
        rows = rows_of(i)
        d_mixed_in = v.wide[rows, :] + skip * v.d_mixed[rows, :]
        normed = v.normed[rows, :]
        inverse = jnp.concatenate([v.inverse[rows, :]] * (H // LANES), axis=1)
        g = d_mixed_in * gain
        first = jnp.mean(g, -1, keepdims=True)
        second = jnp.mean(g * normed, -1, keepdims=True)
        v.din_low[rows, :] = (inverse * (g - first - normed * second)).astype(BF16)
        return totals[0] + fold(d_mixed_in * normed), totals[1] + fold(d_mixed_in)

    zero_h = jnp.zeros((SUB, H), F32)
    d_gain, d_nbias = lax.fori_loop(0, T // CHUNK, norm_back, (zero_h, zero_h), unroll=2)
    d_gain = jnp.sum(d_gain, axis=0, keepdims=True)
    d_nbias = jnp.sum(d_nbias, axis=0, keepdims=True)
    small = v.small
    small[...] = jnp.zeros((S, SUB, LANES), F32)
    for a in range(NG):
        sr, si, sg = (jnp.sum(x, axis=0, keepdims=True) for x in sums[a])
        d_nu = -rate[a] * (sr * lam[a][0] + si * lam[a][1])
        d_theta = angle[a] * (si * lam[a][0] - sr * lam[a][1])
        pair = swap_halves(d_nu, d_theta, low1)
        pair_g = swap_halves(gam[a] * sg, jnp.zeros_like(sg), low1)
        for u in range(2):
            small[2 * a + u, 0:1, :] = pair[u]
            small[2 * a + u, 1:2, :] = pair_g[u]
    for s in range(S):
        here = slice(s * W, (s + 1) * W)
        small[s, 2:3, :] = d_skip[:, here]
        small[s, 3:4, :] = d_bias[0][:, here]
        small[s, 4:5, :] = d_bias[1][:, here]
        small[s, 5:6, :] = d_gain[:, here]
        small[s, 6:7, :] = d_nbias[:, here]
    v.small_r[me_s] = small[...]
    to_state(lambda t: small, v.small_r.at[me_s], SM)

    din_copy = give_back(v.din_low, v.din_nat, din_ref, OWN_DIN)
    for t in (far, sib_far, sib):
        give_to(v.din_nat, din_ref, DIN, t)
    third_sum(g_lin.routes[0])
    for route in g_in.routes:
        second_sum(route)
    wait_bytes(v.small_r.at[pl.ds(0, S - 1)], SM, True)
    group = v.small_r[0]
    for s in range(1, S):
        group = group + v.small_r[s]
    small2 = v.small2
    v.group[...] = group
    small2[0:SUB, :] = v.group[me_s]
    for s in range(S):
        small2[SUB + s : SUB + s + 1, :] = group[s, 5:6, :]
        small2[SUB + S + s : SUB + S + s + 1, :] = group[s, 6:7, :]
    v.small2_r[me_r] = small2[...]

    def small_rows(d, carry):
        send(small2, v.small2_r.at[me_r], SN, {ROWS: lax.rem(me_r + d, R)})
        return carry

    lax.fori_loop(1, R, small_rows, 0)
    third_sum(g_out.routes[0])
    third_sum(g_gate.routes[0])
    wait_bytes(v.small2_r.at[pl.ds(0, R - 1)], SN, True)

    def sum_rows(r, total):
        return total + v.small2_r[r]

    vec[...] = lax.fori_loop(0, R, sum_rows, jnp.zeros((2 * SUB, LANES), F32))
    for route in g_in.routes:
        third_sum(route)

    out_copy.wait()
    din_copy.wait()
    wait_bytes(out_ref.at[pl.ds(0, S - 1)], OUT, True)
    wait_bytes(din_ref.at[pl.ds(0, S - 1)], DIN, True)
    wait_bytes(out_ref.at[pl.ds(0, S - 1)], OUT, False)
    wait_bytes(din_ref.at[pl.ds(0, S - 1)], DIN, False)
    wait_bytes(v.par_s.at[pl.ds(0, S - 1)], PAR_S, False)
    wait_bytes(v.par_r.at[pl.ds(0, R - 1)], PAR_R, False)
    wait_bytes(v.xin.at[:, pl.ds(0, (S - 1) * W)], X, False)
    for w in (wt_in, wt_out, wt_glu):
        w_sent(w)
    wait_bytes(v.cin.at[:, pl.ds(0, (S - 1) * W)], C, False)
    wait_bytes(v.chain_f.at[pl.ds(0, NR - 1)], CF, False)
    wait_bytes(v.chain_b.at[pl.ds(0, NR - 1)], CB, False)
    wait_bytes(v.small_r.at[pl.ds(0, S - 1)], SM, False)
    wait_bytes(v.small2_r.at[pl.ds(0, R - 1)], SN, False)
    for part in parts:
        all_sent(part)


def routes_of(R, H):
    HB = H // R
    if HB % (4 * SUB) == 0:
        routes = [(0, False, 0, HB // 2), (0, True, HB // 2, HB // 2)]
    else:
        routes = [(0, False, 0, HB)]
    return routes + [(1, False, 0, HB), (2, False, 0, HB), (3, True, 0, HB)]


def run_block(dims, *args):
    R, S, T, H, W = dims.R, dims.S, dims.T, dims.H, dims.W
    NR, NG, HB = R * S, S // 2, H // R
    CH, levels = S * LANES, len(LEVELS)
    gdt = BF16 if HB % (2 * SUB) == 0 else F32
    dims.gdt = gdt
    bits = T.bit_length()
    shapes = dict(
        xin=((T, H), BF16),
        cin=((T, H), BF16),
        win=((CH, H), BF16),
        wout=((CH, H), BF16),
        wglu=((2, H, H), BF16),
        glu_raw=((2 * H, W), BF16),
        glu_wide=((2 * CHUNK, W), F32),
        perm=((T, T), BF16),
        back=((T, T), BF16),
        par=((2 * SUB, LANES), F32),
        par_s=((S, 2 * SUB, LANES), F32),
        par_r=((R, 2 * SUB, LANES), F32),
        pows=((bits, NG, 2, SUB, LANES), F32),
        hs_f=((levels, NG, 2, SEG, LANES), F32),
        hs_b=((levels, NG, 2, SEG, LANES), F32),
        lead_pow=((NG, 2, SEG, LANES), F32),
        tail_pow=((NG, 2, SEG, LANES), F32),
        row_pow=((R, NG, 2, SUB, LANES), F32),
        wt_f=((NR, 2, 2 * NG, LANES), F32),
        wt_b=((NR, 2, 2 * NG, LANES), F32),
        msg_f=((2 * NG, LANES), F32),
        msg_b=((2 * NG, LANES), F32),
        chain_f=((NR, 2 * NG, LANES), F32),
        chain_b=((NR, 2 * NG, LANES), F32),
        x=((T, H), F32),
        normed=((T, H), F32),
        inverse=((T, LANES), F32),
        mixed_low=((T, H), BF16),
        wide=((T, max(H, CH)), F32),
        proj=((T, CH), F32),
        state=((T + SEG, CH), F32),
        state_low=((T, CH), BF16),
        act=((T, H), BF16),
        dgelu=((T, H), F32),
        pre=((2, T, H), F32),
        out_low=((T, H), BF16),
        out_nat=((T, H), BF16),
        d_pre=((2, T, H), BF16),
        d_mixed=((T, H), F32),
        d_rec=((T, H), BF16),
        source=((T, CH), F32),
        d_proj=((T, CH), BF16),
        din_low=((T, H), BF16),
        din_nat=((T, H), BF16),
        small=((S, SUB, LANES), F32),
        small_r=((S, S, SUB, LANES), F32),
        group=((S, SUB, LANES), F32),
        small2=((2 * SUB, LANES), F32),
        small2_r=((R, 2 * SUB, LANES), F32),
    )
    dims.names = [*shapes, *dict(here=0, sent=0, received=0)]
    parts = []
    for _ in range(4):
        parts += [(H, CH), (NG, H, LANES)]
    routes = routes_of(R, H)
    for _, _, _, lines in routes:
        parts += [(2, R, lines, LANES)] + [(R, lines, LANES)] * 3
    scratch = [pltpu.VMEM(shape, dtype) for shape, dtype in shapes.values()]
    scratch += [pltpu.SemaphoreType.DMA((n,)) for n in (OWN_DIN + 1, G2 + 2 * len(routes), G2 + 2 * len(routes))]
    scratch += [pltpu.VMEM(shape, gdt) for shape in parts]
    any_spec = pl.BlockSpec(memory_space=pl.ANY)
    vmem = pl.BlockSpec(memory_space=pltpu.VMEM)
    macs = T * H * (2 * CH + 2 * H) * 3 + 4 * T * T * H
    return pl.pallas_call(
        functools.partial(block_kernel, dims),
        out_shape=(
            jax.ShapeDtypeStruct((S, T, W), BF16),
            jax.ShapeDtypeStruct((S, T, W), BF16),
            jax.ShapeDtypeStruct((HB, 4 * LANES), F32),
            jax.ShapeDtypeStruct((2 * SUB, LANES), F32),
        ),
        in_specs=[any_spec] * 5 + [pl.BlockSpec(memory_space=pltpu.SMEM)] * 2 + [vmem] * 7,
        out_specs=(any_spec, any_spec, vmem, vmem),
        scratch_shapes=scratch,
        compiler_params=pltpu.CompilerParams(
            collective_id=0, has_side_effects=True, vmem_limit_bytes=56 * 2**20
        ),
        cost_estimate=pl.CostEstimate(flops=2 * macs, bytes_accessed=8 * 2**20, transcendentals=4 * T * H),
    )(*args)


def on_device(
    inputs,
    bucket,
    lengths,
    nu_log,
    theta_log,
    gamma_log,
    in_proj,
    out_proj,
    skip,
    norm_gain,
    norm_bias,
    glu_weight,
    glu_bias,
    output_cotangent,
):
    row_count, seq, part = inputs.shape
    width = norm_gain.shape[0]
    chans = nu_log.shape[0]
    R, S = lax.axis_size(ROWS), lax.axis_size(STATE)
    dims = SimpleNamespace(R=R, S=S, T=seq, H=width, W=part)
    assert row_count == S and 2 * chans == LANES and part == LANES and S % 2 == 0 and R % 2 == 0

    outputs, d_norm, gsum, vec = run_block(
        dims,
        inputs,
        output_cotangent,
        in_proj.transpose(1, 2, 0).reshape(2 * chans, width),
        out_proj.reshape(2 * chans, width),
        glu_weight.reshape(2 * width, part),
        bucket,
        lengths,
        nu_log[None],
        theta_log[None],
        gamma_log[None],
        skip[None],
        glu_bias,
        norm_gain[None],
        norm_bias[None],
    )
    return finish(dims, lengths, outputs, d_norm, output_cotangent, gsum, vec)


def finish_kernel(dims, *refs):
    S, T, HB = dims.S, dims.T, dims.H // dims.R
    (lengths, out_in, d_norm, cot, gsum, vec) = refs[:6]
    (out, d_inputs, d_nu, d_theta, d_gamma, d_in, d_out, d_skip, d_gain, d_bias, d_glu, d_glu_bias) = refs[6:]
    out[...] = out_in[...]
    for row in range(S):
        for first in range(0, T, CHUNK):
            lines = slice(first, first + CHUNK)
            place = lax.broadcasted_iota(jnp.int32, (CHUNK, LANES), 0) + first
            direct = jnp.where(place < lengths[row], cot[row, lines, :].astype(F32), 0.0)
            d_inputs[row, lines, :] = d_norm[row, lines, :].astype(F32) + direct
    d_nu[...] = vec[0:1, 0:HALF]
    d_theta[...] = pltpu.roll(vec[0:1, :], HALF, 1)[:, 0:HALF]
    d_gamma[...] = vec[1:2, 0:HALF]
    d_skip[...] = vec[2:3, :]
    d_glu_bias[...] = vec[3:5, :]
    for s in range(S):
        here = slice(s * LANES, (s + 1) * LANES)
        d_gain[:, here] = vec[SUB + s : SUB + s + 1, :]
        d_bias[:, here] = vec[SUB + S + s : SUB + S + s + 1, :]
    both = gsum[:, 0:LANES]
    d_in[pl.ds(0, HB, stride=2), :] = both[:, 0:HALF]
    d_in[pl.ds(1, HB, stride=2), :] = pltpu.roll(both, HALF, 1)[:, 0:HALF]
    d_out[...] = gsum[:, LANES : 2 * LANES].T
    d_glu[pl.ds(0, HB, stride=2), :] = gsum[:, 2 * LANES : 3 * LANES]
    d_glu[pl.ds(1, HB, stride=2), :] = gsum[:, 3 * LANES : 4 * LANES]


def finish(dims, lengths, outputs, d_norm, cot, gsum, vec):
    R, S, T, H, W = dims.R, dims.S, dims.T, dims.H, dims.W
    HB = H // R
    vmem = pl.BlockSpec(memory_space=pltpu.VMEM)
    small = [(1, HALF)] * 3 + [(2 * HB, HALF), (LANES, HB), (1, W), (1, H), (1, H), (2 * HB, W), (2, W)]
    got = pl.pallas_call(
        functools.partial(finish_kernel, dims),
        out_shape=(
            jax.ShapeDtypeStruct((S, T, W), BF16),
            jax.ShapeDtypeStruct((S, T, W), F32),
            *(jax.ShapeDtypeStruct(shape, F32) for shape in small),
        ),
        in_specs=[pl.BlockSpec(memory_space=pltpu.SMEM)] + [vmem] * 5,
        out_specs=(vmem,) * 12,
    )(lengths, outputs, d_norm, cot, gsum, vec)
    out, d_inputs, d_nu, d_theta, d_gamma, d_in, d_out, d_skip, d_gain, d_bias, d_glu, d_glu_bias = got
    return (
        out,
        d_inputs,
        d_nu.reshape(HALF),
        d_theta.reshape(HALF),
        d_gamma.reshape(HALF),
        d_in.reshape(HB, 2, HALF),
        d_out.reshape(2, HALF, HB),
        d_skip.reshape(W),
        d_gain.reshape(H),
        d_bias.reshape(H),
        d_glu.reshape(HB, 2, W),
        d_glu_bias,
    )


def solution(mesh):
    return jax.shard_map(
        on_device,
        mesh=mesh,
        in_specs=(
            P(ROWS, None, STATE),
            P(ROWS),
            P(ROWS),
            P(STATE),
            P(STATE),
            P(STATE),
            P(None, None, STATE),
            P(None, STATE, None),
            P(STATE),
            P(),
            P(),
            P(None, None, STATE),
            P(None, STATE),
            P(ROWS, None, STATE),
        ),
        out_specs=(
            P(ROWS, None, STATE),
            P(ROWS, None, STATE),
            P(STATE),
            P(STATE),
            P(STATE),
            P(ROWS, None, STATE),
            P(None, STATE, ROWS),
            P(STATE),
            P(),
            P(),
            P(ROWS, None, STATE),
            P(None, STATE),
        ),
        check_vma=False,
    )
```

```python
import functools
import math
from types import SimpleNamespace

import jax
import jax.numpy as jnp
from jax import lax
from jax.experimental import pallas as pl
from jax.experimental.pallas import tpu as pltpu
from jax.sharding import PartitionSpec as P

epsilon = 1e-05

F32 = jnp.float32
BF16 = jnp.bfloat16
MESH = pl.DeviceIdType.MESH
ROWS, STATE = "rows", "state"
SUB = 8
LANES = 128
HALF = LANES // 2
CHUNK = 64
SEG = 32
LEVELS = tuple(1 << i for i in range(SEG.bit_length() - 1))

OWN_X, OWN_WIN, OWN_WOUT, OWN_WGLU, OWN_C, OWN_OUT, OWN_DIN, OWN_SMALL = range(8)
PAR_S, PAR_R, X, C, OUT, DIN, SM, SN, W1 = range(9)
SIB, FAR, PEER, FAR_SIB = range(4)
G1 = W1 + 12
G2 = G1 + 4


def loop(count, body, unroll=1):
    def step(i, carry):
        body(i)
        return carry

    lax.fori_loop(0, count, step, 0, unroll=unroll)


def nn(a, b):
    return lax.dot_general(a, b, (((1,), (0,)), ((), ())), preferred_element_type=F32)


def nt(a, b):
    return lax.dot_general(a, b, (((1,), (1,)), ((), ())), preferred_element_type=F32)


def tn(a, b):
    return lax.dot_general(a, b, (((0,), (0,)), ((), ())), preferred_element_type=F32)


def cmul(a, b):
    return a[0] * b[0] - a[1] * b[1], a[0] * b[1] + a[1] * b[0]


def conj_mul(a, b):
    return a[0] * b[0] + a[1] * b[1], a[0] * b[1] - a[1] * b[0]


def swap_halves(u, v, low):
    return (
        jnp.where(low, u, pltpu.roll(v, HALF, 1)),
        jnp.where(low, pltpu.roll(u, HALF, 1), v),
    )


def fold(x):
    return jnp.sum(x.reshape(x.shape[0] // SUB, SUB, x.shape[1]), axis=0)


def block_kernel(dims, *refs):
    R, S, T, H, W, gdt = dims.R, dims.S, dims.T, dims.H, dims.W, dims.gdt
    NR, NG, R2, HB, L = R * S, S // 2, R // 2, H // R, T // SEG
    Q = 4 if R % 8 == 0 else 2
    G, NB = Q * S, R // Q
    BITS = T.bit_length()
    (inputs, cot, w_in, w_out, w_glu) = refs[:5]
    vectors = refs[5:14]
    (out_ref, din_ref, gsum, vec) = refs[14:18]
    total = 18 + len(dims.names)
    v = SimpleNamespace(**dict(zip(dims.names, refs[18:total])))
    parts = [
        SimpleNamespace(full=refs[total + 2 * i], r1=refs[total + 2 * i + 1], step=G1 + i, at=i * LANES, routes=[])
        for i in range(4)
    ]
    g_in, g_out, g_lin, g_gate = parts
    total += 8
    for i, (part, over_x, first, lines) in enumerate(routes_of(R, H)):
        a1, r2, a2, r3 = refs[total + 4 * i : total + 4 * i + 4]
        parts[part].routes.append(
            SimpleNamespace(
                part=parts[part], over_x=over_x, first=first, lines=lines, a1=a1, r2=r2, a2=a2, r3=r3, step=G2 + 2 * i
            )
        )

    me_r, me_s = lax.axis_index(ROWS), lax.axis_index(STATE)
    me = me_r * S + me_s

    def cols(i, width):
        return pl.ds(pl.multiple_of(i * width, LANES), width)

    def rows_of(i):
        return pl.ds(pl.multiple_of(i * CHUNK, CHUNK), CHUNK)

    def wait_bytes(ref, which, arrived):
        pltpu.make_async_copy(ref, ref, (v.received if arrived else v.sent).at[which]).wait()

    def send(src, dst, which, target):
        pltpu.make_async_remote_copy(
            src_ref=src,
            dst_ref=dst,
            send_sem=v.sent.at[which],
            recv_sem=v.received.at[which],
            device_id=target,
            device_id_type=MESH,
        ).start()

    def to_state(src_of, dst, which):
        for j in (2, 3, 1) if S == 4 else range(1, S):
            t = lax.rem(me_s + j, S)
            send(src_of(t), dst, which, {STATE: t})

    sib = me_s + 1 - 2 * lax.rem(me_s, 2)
    far = lax.rem(me_s + NG, S)
    sib_far = lax.rem(sib + NG, S)
    pair_r = me_r + 1 - 2 * lax.rem(me_r, 2)
    group_r = me_r - lax.rem(me_r, Q)
    piece = lax.rem(me_r, Q)
    mine_s = lax.rem(me_s, 2)
    mine_r = lax.rem(me_r, 2)

    def line_block(ref, s, p=None):
        if p is None:
            return ref.at[pl.ds(pl.multiple_of(s * LANES, LANES), LANES), :]
        size = LANES // Q
        return ref.at[pl.ds(pl.multiple_of(s * LANES + p * size, size), size), :]

    def glu_block(ref, s, p=None):
        size = H // Q
        rows = slice(None) if p is None else pl.ds(pl.multiple_of(p * size, size), size)
        return ref.at[:, rows, cols(s, W)]

    own = [
        (w_glu, v.glu_raw, OWN_WGLU),
        (w_in, line_block(v.win, me_s), OWN_WIN),
        (w_out, line_block(v.wout, me_s), OWN_WOUT),
        (inputs.at[me_s], v.xin.at[:, cols(me_s, W)], OWN_X),
        (cot.at[me_s], v.cin.at[:, cols(me_s, W)], OWN_C),
    ]
    small_in = (v.bucket, v.lengths, v.nu, v.theta, v.gamma, v.skip, v.glu_bias, v.gain, v.bias)
    own += [(a, b, OWN_SMALL + i) for i, (a, b) in enumerate(zip(vectors, small_in))]
    own = {which: pltpu.make_async_copy(a, b, v.here.at[which]) for a, b, which in own}

    barrier = pltpu.get_barrier_semaphore()
    number = piece * S + me_s
    is_gate = (number == 0) & (NB > 1)
    gated = 1 if NB > 1 else 0

    def signal(which, i, rows=None):
        pl.semaphore_signal(
            which,
            inc=1,
            device_id={ROWS: group_r + lax.div(i, S) if rows is None else rows, STATE: lax.rem(i, S)},
            device_id_type=MESH,
        )

    def greet(d, carry):
        i = lax.rem(number + d, G)

        @pl.when(i >= gated)
        def _():
            signal(barrier, i)

        return carry

    lax.fori_loop(1, G, greet, 0)
    for copy in own.values():
        copy.start()
    for i in range(len(vectors)):
        own[OWN_SMALL + i].wait()
    bucket_ref, lengths_ref, nu_ref, theta_ref, gamma_ref, skip_ref, glu_bias_ref, gain_ref, bias_ref = small_in

    par = v.par
    par[...] = jnp.zeros((2 * SUB, LANES), F32)
    par[0:1, 0:HALF] = nu_ref[...]
    par[0:1, HALF:LANES] = theta_ref[...]
    par[1:2, 0:HALF] = gamma_ref[...]
    par[2:3, :] = skip_ref[...]
    par[3:5, :] = glu_bias_ref[...]
    for i in range(S):
        par[SUB + i : SUB + i + 1, :] = jnp.full((1, LANES), bucket_ref[i], jnp.int32).astype(F32)
        par[SUB + S + i : SUB + S + i + 1, :] = jnp.full((1, LANES), lengths_ref[i], jnp.int32).astype(F32)
    v.par_s[me_s] = par[...]
    v.par_r[me_r] = par[...]

    @pl.when(jnp.logical_not(is_gate))
    def _():
        pl.semaphore_wait(barrier, G - 1)

    if NB > 1:

        @pl.when(number == 1)
        def _():
            signal(v.block_in, jnp.int32(0))

        @pl.when(is_gate)
        def _():
            pl.semaphore_wait(v.block_in, 1)

            def next_gate(d, carry):
                signal(barrier, jnp.int32(0), rows=lax.rem(group_r + d * Q, R))
                return carry

            lax.fori_loop(1, NB, next_gate, 0)

    def everyone_in():
        if NB > 1:

            @pl.when(is_gate)
            def _():
                pl.semaphore_wait(barrier, NB - 1)

                def tell(i, carry):
                    signal(v.all_in, i)
                    return carry

                lax.fori_loop(1, G, tell, 0)

            @pl.when(jnp.logical_not(is_gate))
            def _():
                pl.semaphore_wait(v.all_in, 1)

    to_state(lambda t: par, v.par_s.at[me_s], PAR_S)

    def w_send(w, own_block, own_piece):
        send(own_piece, w.block(w.ref, me_s, piece), w.step + FAR, {STATE: far})
        send(own_block, w.block(w.ref, me_s), w.step + SIB, {STATE: sib})

    def w_forward_far(w):
        here = w.block(w.ref, far, piece)
        wait_bytes(here, w.step + FAR, True)
        for j in range(1, Q):
            send(here, here, w.step + PEER, {ROWS: group_r + lax.rem(piece + j, Q)})

    def w_forward_all(w):
        wait_bytes(w.rest, w.step + PEER, True)
        send(w.block(w.ref, far), w.block(w.ref, far), w.step + FAR_SIB, {STATE: sib})

    def w_ready(w):
        wait_bytes(w.block(w.ref, sib), w.step + SIB, True)
        wait_bytes(w.block(w.ref, sib_far), w.step + FAR_SIB, True)

    def w_sent(w):
        wait_bytes(w.block(w.ref, sib), w.step + SIB, False)
        wait_bytes(w.block(w.ref, sib), w.step + FAR_SIB, False)
        wait_bytes(w.block(w.ref, sib, piece), w.step + FAR, False)
        wait_bytes(w.rest, w.step + PEER, False)

    others = pl.ds(0, LANES - LANES // Q)
    wt_in = SimpleNamespace(ref=v.win, block=line_block, step=W1, rest=v.win.at[others, :])
    wt_out = SimpleNamespace(ref=v.wout, block=line_block, step=W1 + 4, rest=v.wout.at[others, :])
    wt_glu = SimpleNamespace(
        ref=v.wglu, block=glu_block, step=W1 + 8, rest=v.wglu.at[:, pl.ds(0, H - H // Q), pl.ds(0, W)]
    )

    def piece_of(ref):
        size = LANES // Q
        return ref.at[pl.ds(pl.multiple_of(piece * size, size), size), :]

    w_send(wt_in, w_in, piece_of(w_in))
    to_state(lambda t: inputs.at[t], v.xin.at[:, cols(me_s, W)], X)
    w_send(wt_out, w_out, piece_of(w_out))
    own[OWN_WGLU].wait()

    def split_glu(i):
        here = rows_of(i)
        v.glu_wide[...] = v.glu_raw[pl.ds(pl.multiple_of(i * 2 * CHUNK, 2 * CHUNK), 2 * CHUNK), :].astype(F32)
        for k in range(2):
            v.wglu[k, here, cols(me_s, W)] = v.glu_wide[pl.ds(k, CHUNK, stride=2), :].astype(BF16)

    loop(H // CHUNK, split_glu)
    w_send(wt_glu, glu_block(v.wglu, me_s), glu_block(v.wglu, me_s, piece))

    line = lax.broadcasted_iota(jnp.int32, (CHUNK, T), 0)
    place = lax.broadcasted_iota(jnp.int32, (CHUNK, T), 1)

    def orders(i):
        base = pl.multiple_of(i * CHUNK, CHUNK)
        at = line + base
        v.perm[pl.ds(base, CHUNK), :] = (
            place == lax.rem(at, SEG) * L + lax.div(at, SEG)
        ).astype(F32).astype(BF16)
        v.back[pl.ds(base, CHUNK), :] = (
            at == lax.rem(place, SEG) * L + lax.div(place, SEG)
        ).astype(F32).astype(BF16)

    loop(T // CHUNK, orders)

    w_forward_far(wt_in)

    low = lax.broadcasted_iota(jnp.int32, (SEG, LANES), 1) < HALF
    low1 = lax.broadcasted_iota(jnp.int32, (1, LANES), 1) < HALF
    seg = lax.broadcasted_iota(jnp.int32, (SEG, LANES), 0)

    wait_bytes(v.par_s.at[pl.ds(0, S - 1)], PAR_S, True)
    par_s, par_r = v.par_s, v.par_r
    lam, gam, rate, angle = [], [], [], []
    for a in range(NG):
        nu, theta = swap_halves(par_s[2 * a, 0:1, :], par_s[2 * a + 1, 0:1, :], low1)
        rate.append(jnp.exp(nu))
        angle.append(jnp.exp(theta))
        magnitude = jnp.exp(-rate[a])
        lam.append((magnitude * jnp.cos(angle[a]), magnitude * jnp.sin(angle[a])))
        gam.append(jnp.exp(swap_halves(par_s[2 * a, 1:2, :], par_s[2 * a + 1, 1:2, :], low1)[0]))
    skip = jnp.concatenate([par_s[s, 2:3, :] for s in range(S)], axis=1)
    gain, bias = gain_ref[...], bias_ref[...]
    power = [[(jnp.broadcast_to(l[0], (SUB, LANES)), jnp.broadcast_to(l[1], (SUB, LANES))) for l in lam]]
    for _ in range(BITS - 1):
        power.append([cmul(p, p) for p in power[-1]])
    for b in range(BITS):
        for a in range(NG):
            for c in range(2):
                v.pows[b, a, c] = power[b][a][c]

    def raised(exponent):
        result = [(jnp.ones(exponent.shape, F32), jnp.zeros(exponent.shape, F32)) for _ in range(NG)]
        for b in range(BITS):
            hit = (lax.shift_right_logical(exponent, b) & 1) == 1
            for a in range(NG):
                re, im = cmul(result[a], (v.pows[b, a, 0, 0:1, :], v.pows[b, a, 1, 0:1, :]))
                result[a] = (jnp.where(hit, re, result[a][0]), jnp.where(hit, im, result[a][1]))
        return result

    my_bucket = par[pl.ds(SUB + me_s, 1), :]
    len1 = par[pl.ds(SUB + S + me_s, 1), :].astype(jnp.int32)
    my_len = jnp.broadcast_to(len1, (SEG, LANES))
    seg_pow = raised(jnp.clip(my_len - seg * L, 0, L))
    lead_pow = raised(jnp.minimum(my_len, seg * L))
    tail_pow = raised(jnp.maximum(my_len - (seg + 1) * L, 0))
    for a in range(NG):
        ahead = seg_pow[a]
        behind = seg_pow[a]
        for i, d in enumerate(LEVELS):
            for c in range(2):
                v.hs_f[i, a, c] = jnp.where(seg >= d, ahead[c], 0.0)
                v.hs_b[i, a, c] = jnp.where(seg < SEG - d, behind[c], 0.0)
            ahead = cmul(ahead, (pltpu.roll(ahead[0], d, 0), pltpu.roll(ahead[1], d, 0)))
            behind = cmul(behind, (pltpu.roll(behind[0], SEG - d, 0), pltpu.roll(behind[1], SEG - d, 0)))
        for c in range(2):
            v.lead_pow[a, c] = lead_pow[a][c]
            v.tail_pow[a, c] = tail_pow[a][c]

    def row_powers(r):
        lens = par_r[r, SUB : 2 * SUB, :].astype(jnp.int32)
        result = raised(lens)
        for a in range(NG):
            for c in range(2):
                v.row_pow[r, a, c] = result[a][c]

    def weights(into, forward):
        def one(i, run):
            p = NR - 1 - i if forward else i
            r, s = lax.div(p, S), lax.rem(p, S)
            here = par_r[r, pl.ds(SUB + s, 1), :]
            side = (p < me) if forward else (p > me)
            hit = (here == my_bucket) & (my_bucket > 0.5) & jnp.broadcast_to(side, (1, LANES))
            after = []
            for a in range(NG):
                re, im = run[a]
                re_w, im_w = jnp.where(hit, re, 0.0), jnp.where(hit, im, 0.0)
                for k in range(2):
                    into[p, 0, pl.ds(k * NG + a, 1), :] = re_w
                    into[p, 1, pl.ds(k * NG + a, 1), :] = im_w
                factor = (
                    v.row_pow[r, a, 0, pl.ds(S + s, 1), :],
                    v.row_pow[r, a, 1, pl.ds(S + s, 1), :],
                )
                re_n, im_n = cmul((re, im), factor)
                after.append((jnp.where(hit, re_n, re), jnp.where(hit, im_n, im)))
            return tuple(after)

        first = tuple((jnp.ones((1, LANES), F32), jnp.zeros((1, LANES), F32)) for _ in range(NG))
        lax.fori_loop(0, NR, one, first)

    def carry_copy(msg, chain, sent, received, source, t):
        return pltpu.make_async_remote_copy(
            src_ref=msg,
            dst_ref=chain.at[source],
            send_sem=sent.at[t],
            recv_sem=received.at[source],
            device_id={ROWS: lax.div(t, S), STATE: lax.rem(t, S)},
            device_id_type=MESH,
        )

    def exchange(msg, chain, sent, received, forward):
        def one(t, carry):
            carry_copy(msg, chain, sent, received, me, t).start()
            return carry

        lax.fori_loop(me + 1 if forward else 0, NR if forward else me, one, 0)

    def collect(msg, chain, into, sent, received, forward):
        def one(p, sums):
            carry_copy(msg, chain, sent, received, p, me).wait_recv()
            x = chain[p]
            return sums[0] + into[p, 0] * x, sums[1] + into[p, 1] * x

        zero = jnp.zeros((2 * NG, LANES), F32)
        return lax.fori_loop(0 if forward else me + 1, me if forward else NR, one, (zero, zero))

    def carries_sent(msg, chain, sent, received, forward):
        def one(t, carry):
            carry_copy(msg, chain, sent, received, me, t).wait_send()
            return carry

        lax.fori_loop(me + 1 if forward else 0, NR if forward else me, one, 0)

    pos = lax.broadcasted_iota(jnp.int32, (CHUNK, LANES), 0)
    pos = lax.rem(pos, SEG) * L + lax.div(pos, SEG)

    def valid_of(i, width):
        ok = jnp.where(pos + i * (CHUNK // SEG) < len1, 1.0, 0.0)
        return jnp.concatenate([ok] * (width // LANES), axis=1) if width > LANES else ok

    w_forward_all(wt_in)

    own[OWN_X].wait()
    wait_bytes(v.xin.at[:, pl.ds(0, (S - 1) * W)], X, True)
    v.x[...] = nn(v.perm[...], v.xin[...])

    def layer_norm(i):
        rows = rows_of(i)
        x = v.x[rows, :]
        centred = x - jnp.mean(x, -1, keepdims=True)
        inverse = lax.rsqrt(jnp.mean(centred * centred, -1, keepdims=True) + epsilon)
        normed = centred * inverse
        v.normed[rows, :] = normed
        v.inverse[rows, :] = jnp.broadcast_to(inverse, (CHUNK, LANES))
        v.mixed_low[rows, :] = (normed * gain + bias).astype(BF16)

    loop(T // CHUNK, layer_norm, unroll=2)
    own[OWN_WIN].wait()
    w_ready(wt_in)
    v.wide[...] = nt(v.mixed_low[...], v.win[...])
    w_forward_far(wt_out)

    lamb = [tuple(jnp.broadcast_to(c, (SEG, LANES)) for c in l) for l in lam]
    gamb = [jnp.broadcast_to(g, (SEG, LANES)) for g in gam]

    def lanes(i):
        return slice(i * LANES, (i + 1) * LANES)

    def load_c(ref, at):
        return [(ref[at, lanes(a)], ref[at, lanes(NG + a)]) for a in range(NG)]

    def store_c(ref, at, values):
        for a in range(NG):
            ref[at, lanes(a)] = values[a][0]
            ref[at, lanes(NG + a)] = values[a][1]

    def load_g(ref, at):
        return [swap_halves(ref[at, lanes(2 * a)], ref[at, lanes(2 * a + 1)], low) for a in range(NG)]

    def to_g(values):
        return [g for a in range(NG) for g in swap_halves(values[a][0], values[a][1], low)]

    def step_of(k):
        return pl.ds(pl.multiple_of(k * SEG, SEG), SEG)

    zeros = tuple((jnp.zeros((SEG, LANES), F32), jnp.zeros((SEG, LANES), F32)) for _ in range(NG))

    def advance(k, state, proj):
        ok = seg * L + k < my_len
        new = []
        for a in range(NG):
            re, im = cmul(lamb[a], state[a])
            re, im = re + gamb[a] * proj[a][0], im + gamb[a] * proj[a][1]
            new.append((jnp.where(ok, re, state[a][0]), jnp.where(ok, im, state[a][1])))
        return tuple(new)

    def fwd_first(k, state):
        proj = load_g(v.wide, step_of(k))
        store_c(v.proj, step_of(k), proj)
        return advance(k, state, proj)

    ends = lax.fori_loop(0, L, fwd_first, zeros, unroll=4)

    def across(values, table, forward):
        done = []
        for a in range(NG):
            x = values[a]
            for i, d in enumerate(LEVELS):
                shift = d if forward else SEG - d
                other = (pltpu.roll(x[0], shift, 0), pltpu.roll(x[1], shift, 0))
                factor = (table[i, a, 0], table[i, a, 1])
                add = cmul(factor, other) if forward else conj_mul(factor, other)
                x = (x[0] + add[0], x[1] + add[1])
            done.append(x)
        return done

    w_forward_far(wt_glu)
    ends = across(ends, v.hs_f, True)
    for a in range(NG):
        for c in range(2):
            v.msg_f[pl.ds(c * NG + a, 1), :] = ends[a][c][SEG - 1 : SEG, :]
    everyone_in()

    def par_rows(d, carry):
        send(par, v.par_r.at[me_r], PAR_R, {ROWS: lax.rem(me_r + d, R)})
        return carry

    lax.fori_loop(1, R, par_rows, 0)
    forward = (v.msg_f, v.chain_f, v.wt_f, v.sent_f, v.received_f, True)
    exchange(*forward[:2], *forward[3:])
    before = [
        tuple(jnp.where(seg > 0, pltpu.roll(x, 1, 0), 0.0) for x in ends[a]) for a in range(NG)
    ]
    to_state(lambda t: cot.at[t], v.cin.at[:, cols(me_s, W)], C)
    w_forward_all(wt_out)
    own[OWN_C].wait()
    wait_bytes(v.par_r.at[pl.ds(0, R - 1)], PAR_R, True)
    loop(R, row_powers)
    weights(v.wt_f, True)
    x_sum, y_sum = collect(*forward)
    state = []
    for a in range(NG):
        start = (
            x_sum[a : a + 1] - y_sum[NG + a : NG + a + 1],
            x_sum[NG + a : NG + a + 1] + y_sum[a : a + 1],
        )
        add = cmul((v.lead_pow[a, 0], v.lead_pow[a, 1]), start)
        state.append((before[a][0] + add[0], before[a][1] + add[1]))
    store_c(v.state, pl.ds(0, SEG), state)

    def fwd_second(k, state):
        state = advance(k, state, load_c(v.proj, step_of(k)))
        store_c(v.state, step_of(k + 1), state)
        low_out = to_g([(re, -im) for re, im in state])
        for s in range(S):
            v.state_low[step_of(k), lanes(s)] = low_out[s].astype(BF16)
        return state

    lax.fori_loop(0, L, fwd_second, tuple(state), unroll=4)

    own[OWN_WOUT].wait()
    w_ready(wt_out)
    v.wide[...] = nn(v.state_low[...], v.wout[...])
    w_forward_all(wt_glu)

    def gelu(i):
        rows = rows_of(i)
        mixed_in = v.normed[rows, :] * gain + bias
        mixed = v.wide[rows, :] + skip * mixed_in
        cdf = 0.5 * (1.0 + lax.erf(mixed * (1.0 / math.sqrt(2.0))))
        density = jnp.exp(-0.5 * mixed * mixed) * (1.0 / math.sqrt(2.0 * math.pi))
        v.act[rows, :] = (mixed * cdf).astype(BF16)
        v.dgelu[rows, :] = cdf + mixed * density

    loop(T // CHUNK, gelu, unroll=2)
    w_ready(wt_glu)
    for k in range(2):
        v.pre[k] = nn(v.act[...], v.wglu[k])

    def glu(i):
        rows = rows_of(i)
        ok = valid_of(i, W)
        for s in range(S):
            here = slice(s * W, (s + 1) * W)
            linear = v.pre[0, rows, here] + par_s[s, 3:4, :]
            gate = v.pre[1, rows, here] + par_s[s, 4:5, :]
            share = jax.nn.sigmoid(gate)
            value = linear * share
            v.out_low[rows, here] = (ok * (v.x[rows, here] + value)).astype(BF16)
            v.pre[0, rows, here] = ok * share
            v.pre[1, rows, here] = ok * (value * (1.0 - share))

    loop(T // CHUNK, glu, unroll=2)

    def give_back(low_ref, nat, result, own_which):
        nat[...] = nn(v.back[...], low_ref[...]).astype(BF16)
        copy = pltpu.make_async_copy(nat.at[:, cols(me_s, W)], result.at[me_s], v.here.at[own_which])
        copy.start()
        return copy

    def give_to(nat, result, which, t):
        send(nat.at[:, cols(t, W)], result.at[me_s], which, {STATE: t})

    out_copy = give_back(v.out_low, v.out_nat, out_ref, OWN_OUT)
    give_to(v.out_nat, out_ref, OUT, far)
    wait_bytes(v.cin.at[:, pl.ds(0, (S - 1) * W)], C, True)
    v.wide[...] = nn(v.perm[...], v.cin[...])

    def glu_back(i):
        rows = rows_of(i)
        dout = v.wide[rows, :]
        for k in range(2):
            v.d_pre[k, rows, :] = (dout * v.pre[k, rows, :]).astype(BF16)

    loop(T // CHUNK, glu_back, unroll=2)

    for part in parts:
        for route in part.routes:
            if route.over_x:
                route.half = lax.div(me_s, 2)
                route.pair = {STATE: far}
                route.number = me_r
                route.slot = lambda r, b: (b, r)
                route.owner = lambda n: {ROWS: n}
            else:
                route.half = mine_r
                route.pair = {ROWS: pair_r}
                route.number = lax.div(me_s, 2) * R2 + lax.div(me_r, 2)
                route.slot = lambda r, b: (lax.rem(r, 2), b * R2 + lax.div(r, 2))
                route.owner = lambda n: {ROWS: 2 * lax.rem(n, R2) + mine_r, STATE: 2 * lax.div(n, R2) + mine_s}

    def first_send(part):
        for b in range(NG):
            send(part.full.at[:, cols(2 * b + 1 - mine_s, LANES)], part.r1.at[b], part.step, {STATE: sib})

    def first_wait(part):
        wait_bytes(part.r1, part.step, True)

    def first_sum(route):
        part = route.part

        def one(r):
            rows = pl.ds(pl.multiple_of(r * HB + route.first, route.lines), route.lines)
            for b in range(NG):
                total = part.full[rows, cols(2 * b + mine_s, LANES)].astype(F32) + part.r1[b, rows, :].astype(F32)
                route.a1[route.slot(r, b)] = total.astype(gdt)

        loop(R, one, unroll=2)
        send(route.a1.at[1 - route.half], route.r2, route.step, route.pair)

    def second_sum(route):
        wait_bytes(route.r2, route.step, True)

        def one(n):
            total = route.a1[route.half, n].astype(F32) + route.r2[n].astype(F32)
            route.a2[n] = total.astype(gdt)

        loop(R, one, unroll=2)
        route.r3[route.number] = route.a2[route.number]

        def give(d, carry):
            n = lax.rem(route.number + d, R)
            send(route.a2.at[n], route.r3.at[route.number], route.step + 1, route.owner(n))
            return carry

        lax.fori_loop(1, R, give, 0)

    def third_sum(route):
        wait_bytes(route.r3.at[pl.ds(0, R - 1)], route.step + 1, True)

        def one(n, total):
            return total + route.r3[n].astype(F32)

        total = lax.fori_loop(0, R, one, jnp.zeros((route.lines, LANES), F32), unroll=2)
        gsum[route.first : route.first + route.lines, route.part.at : route.part.at + LANES] = total

    def all_sent(part):
        wait_bytes(part.r1, part.step, False)
        for route in part.routes:
            wait_bytes(route.r2, route.step, False)
            wait_bytes(route.r3.at[pl.ds(0, R - 1)], route.step + 1, False)

    for k, part in ((0, g_lin), (1, g_gate)):
        part.full[...] = tn(v.act[...], v.d_pre[k]).astype(gdt)
        first_send(part)
    v.wide[...] = nt(v.d_pre[0], v.wglu[0]) + nt(v.d_pre[1], v.wglu[1])

    def gelu_back(i, total):
        rows = rows_of(i)
        d_mixed = v.wide[rows, :] * v.dgelu[rows, :]
        v.d_mixed[rows, :] = d_mixed
        v.d_rec[rows, :] = d_mixed.astype(BF16)
        return total + fold(d_mixed * (v.normed[rows, :] * gain + bias))

    d_skip = lax.fori_loop(0, T // CHUNK, gelu_back, jnp.zeros((SUB, H), F32), unroll=2)
    d_skip = jnp.sum(d_skip, axis=0, keepdims=True)
    v.wide[...] = nt(v.d_rec[...], v.wout[...])
    first_wait(g_lin)
    first_sum(g_lin.routes[0])
    g_out.full[...] = tn(v.d_rec[...], v.state_low[...]).astype(gdt)
    first_send(g_out)

    def retreat(k, source, carry):
        ok = seg * L + k < my_len
        adjoint, new = [], []
        for a in range(NG):
            re, im = source[a][0] + carry[a][0], source[a][1] + carry[a][1]
            adjoint.append((re, im))
            nre, nim = conj_mul(lamb[a], (re, im))
            new.append((jnp.where(ok, nre, re), jnp.where(ok, nim, im)))
        return ok, adjoint, tuple(new)

    def bwd_first(i, carry):
        k = L - 1 - i
        source = [(re, -im) for re, im in load_g(v.wide, step_of(k))]
        store_c(v.source, step_of(k), source)
        return retreat(k, source, carry)[2]

    heads = lax.fori_loop(0, L, bwd_first, zeros, unroll=4)
    heads = across(heads, v.hs_b, False)
    for a in range(NG):
        for c in range(2):
            v.msg_b[pl.ds(c * NG + a, 1), :] = heads[a][c][0:1, :]
    backward = (v.msg_b, v.chain_b, v.wt_b, v.sent_b, v.received_b, False)
    exchange(*backward[:2], *backward[3:])
    after = [
        tuple(jnp.where(seg < SEG - 1, pltpu.roll(x, SEG - 1, 0), 0.0) for x in heads[a])
        for a in range(NG)
    ]
    first_wait(g_gate)
    first_sum(g_gate.routes[0])
    give_to(v.out_nat, out_ref, OUT, sib)
    give_to(v.out_nat, out_ref, OUT, sib_far)
    first_wait(g_out)
    first_sum(g_out.routes[0])
    ones = jnp.ones((2 * SUB, T), BF16)
    d_bias = [nn(ones, v.d_pre[k])[0:1, :] for k in range(2)]
    second_sum(g_lin.routes[0])

    weights(v.wt_b, False)
    x_sum, y_sum = collect(*backward)
    carry = []
    for a in range(NG):
        omega = (
            x_sum[a : a + 1] + y_sum[NG + a : NG + a + 1],
            x_sum[NG + a : NG + a + 1] - y_sum[a : a + 1],
        )
        add = conj_mul((v.tail_pow[a, 0], v.tail_pow[a, 1]), omega)
        carry.append((after[a][0] + add[0], after[a][1] + add[1]))

    def bwd_second(i, item):
        k = L - 1 - i
        carry, sums = item
        ok, adjoint, carry = retreat(k, load_c(v.source, step_of(k)), carry)
        previous = load_c(v.state, step_of(k))
        proj = load_c(v.proj, step_of(k))
        new_sums, low_out = [], []
        for a in range(NG):
            re, im = (jnp.where(ok, x, 0.0) for x in adjoint[a])
            dre, dim = conj_mul(previous[a], (re, im))
            dg = re * proj[a][0] + im * proj[a][1]
            new_sums.append(tuple(x + fold(y) for x, y in zip(sums[a], (dre, dim, dg))))
            low_out.append((gamb[a] * re, gamb[a] * im))
        low_out = to_g(low_out)
        for s in range(S):
            v.d_proj[step_of(k), lanes(s)] = low_out[s].astype(BF16)
        return carry, tuple(new_sums)

    zero = jnp.zeros((SUB, LANES), F32)
    _, sums = lax.fori_loop(
        0, L, bwd_second, (tuple(carry), tuple((zero, zero, zero) for _ in range(NG))), unroll=2
    )

    g_in.full[...] = tn(v.mixed_low[...], v.d_proj[...]).astype(gdt)
    first_send(g_in)
    v.wide[...] = nn(v.d_proj[...], v.win[...])
    second_sum(g_out.routes[0])
    first_wait(g_in)
    for route in g_in.routes:
        first_sum(route)
    second_sum(g_gate.routes[0])

    def norm_back(i, totals):
        rows = rows_of(i)
        d_mixed_in = v.wide[rows, :] + skip * v.d_mixed[rows, :]
        normed = v.normed[rows, :]
        inverse = jnp.concatenate([v.inverse[rows, :]] * (H // LANES), axis=1)
        g = d_mixed_in * gain
        first = jnp.mean(g, -1, keepdims=True)
        second = jnp.mean(g * normed, -1, keepdims=True)
        v.din_low[rows, :] = (inverse * (g - first - normed * second)).astype(BF16)
        return totals[0] + fold(d_mixed_in * normed), totals[1] + fold(d_mixed_in)

    zero_h = jnp.zeros((SUB, H), F32)
    d_gain, d_nbias = lax.fori_loop(0, T // CHUNK, norm_back, (zero_h, zero_h), unroll=2)
    d_gain = jnp.sum(d_gain, axis=0, keepdims=True)
    d_nbias = jnp.sum(d_nbias, axis=0, keepdims=True)
    small = v.small
    small[...] = jnp.zeros((S, SUB, LANES), F32)
    for a in range(NG):
        sr, si, sg = (jnp.sum(x, axis=0, keepdims=True) for x in sums[a])
        d_nu = -rate[a] * (sr * lam[a][0] + si * lam[a][1])
        d_theta = angle[a] * (si * lam[a][0] - sr * lam[a][1])
        pair = swap_halves(d_nu, d_theta, low1)
        pair_g = swap_halves(gam[a] * sg, jnp.zeros_like(sg), low1)
        for u in range(2):
            small[2 * a + u, 0:1, :] = pair[u]
            small[2 * a + u, 1:2, :] = pair_g[u]
    for s in range(S):
        here = slice(s * W, (s + 1) * W)
        small[s, 2:3, :] = d_skip[:, here]
        small[s, 3:4, :] = d_bias[0][:, here]
        small[s, 4:5, :] = d_bias[1][:, here]
        small[s, 5:6, :] = d_gain[:, here]
        small[s, 6:7, :] = d_nbias[:, here]
    v.small_r[me_s] = small[...]
    to_state(lambda t: small, v.small_r.at[me_s], SM)

    din_copy = give_back(v.din_low, v.din_nat, din_ref, OWN_DIN)
    for t in (far, sib_far, sib):
        give_to(v.din_nat, din_ref, DIN, t)
    third_sum(g_lin.routes[0])
    for route in g_in.routes:
        second_sum(route)
    wait_bytes(v.small_r.at[pl.ds(0, S - 1)], SM, True)
    group = v.small_r[0]
    for s in range(1, S):
        group = group + v.small_r[s]
    small2 = v.small2
    v.group[...] = group
    small2[0:SUB, :] = v.group[me_s]
    for s in range(S):
        small2[SUB + s : SUB + s + 1, :] = group[s, 5:6, :]
        small2[SUB + S + s : SUB + S + s + 1, :] = group[s, 6:7, :]
    v.small2_r[me_r] = small2[...]

    def small_rows(d, carry):
        send(small2, v.small2_r.at[me_r], SN, {ROWS: lax.rem(me_r + d, R)})
        return carry

    lax.fori_loop(1, R, small_rows, 0)
    third_sum(g_out.routes[0])
    third_sum(g_gate.routes[0])
    wait_bytes(v.small2_r.at[pl.ds(0, R - 1)], SN, True)

    def sum_rows(r, total):
        return total + v.small2_r[r]

    vec[...] = lax.fori_loop(0, R, sum_rows, jnp.zeros((2 * SUB, LANES), F32))
    for route in g_in.routes:
        third_sum(route)

    out_copy.wait()
    din_copy.wait()
    wait_bytes(out_ref.at[pl.ds(0, S - 1)], OUT, True)
    wait_bytes(din_ref.at[pl.ds(0, S - 1)], DIN, True)
    wait_bytes(out_ref.at[pl.ds(0, S - 1)], OUT, False)
    wait_bytes(din_ref.at[pl.ds(0, S - 1)], DIN, False)
    wait_bytes(v.par_s.at[pl.ds(0, S - 1)], PAR_S, False)
    wait_bytes(v.par_r.at[pl.ds(0, R - 1)], PAR_R, False)
    wait_bytes(v.xin.at[:, pl.ds(0, (S - 1) * W)], X, False)
    for w in (wt_in, wt_out, wt_glu):
        w_sent(w)
    wait_bytes(v.cin.at[:, pl.ds(0, (S - 1) * W)], C, False)
    carries_sent(*forward[:2], *forward[3:])
    carries_sent(*backward[:2], *backward[3:])
    wait_bytes(v.small_r.at[pl.ds(0, S - 1)], SM, False)
    wait_bytes(v.small2_r.at[pl.ds(0, R - 1)], SN, False)
    for part in parts:
        all_sent(part)


def routes_of(R, H):
    HB = H // R
    if HB % (4 * SUB) == 0:
        routes = [(0, False, 0, HB // 2), (0, True, HB // 2, HB // 2)]
    else:
        routes = [(0, False, 0, HB)]
    return routes + [(1, False, 0, HB), (2, False, 0, HB), (3, True, 0, HB)]


def run_block(dims, *args):
    R, S, T, H, W = dims.R, dims.S, dims.T, dims.H, dims.W
    NR, NG, HB = R * S, S // 2, H // R
    CH, levels = S * LANES, len(LEVELS)
    gdt = BF16 if HB % (2 * SUB) == 0 else F32
    dims.gdt = gdt
    bits = T.bit_length()
    shapes = dict(
        xin=((T, H), BF16),
        cin=((T, H), BF16),
        win=((CH, H), BF16),
        wout=((CH, H), BF16),
        wglu=((2, H, H), BF16),
        glu_raw=((2 * H, W), BF16),
        glu_wide=((2 * CHUNK, W), F32),
        perm=((T, T), BF16),
        back=((T, T), BF16),
        nu=((1, HALF), F32),
        theta=((1, HALF), F32),
        gamma=((1, HALF), F32),
        skip=((1, W), F32),
        glu_bias=((2, W), F32),
        gain=((1, H), F32),
        bias=((1, H), F32),
        par=((2 * SUB, LANES), F32),
        par_s=((S, 2 * SUB, LANES), F32),
        par_r=((R, 2 * SUB, LANES), F32),
        pows=((bits, NG, 2, SUB, LANES), F32),
        hs_f=((levels, NG, 2, SEG, LANES), F32),
        hs_b=((levels, NG, 2, SEG, LANES), F32),
        lead_pow=((NG, 2, SEG, LANES), F32),
        tail_pow=((NG, 2, SEG, LANES), F32),
        row_pow=((R, NG, 2, SUB, LANES), F32),
        wt_f=((NR, 2, 2 * NG, LANES), F32),
        wt_b=((NR, 2, 2 * NG, LANES), F32),
        msg_f=((2 * NG, LANES), F32),
        msg_b=((2 * NG, LANES), F32),
        chain_f=((NR, 2 * NG, LANES), F32),
        chain_b=((NR, 2 * NG, LANES), F32),
        x=((T, H), F32),
        normed=((T, H), F32),
        inverse=((T, LANES), F32),
        mixed_low=((T, H), BF16),
        wide=((T, max(H, CH)), F32),
        proj=((T, CH), F32),
        state=((T + SEG, CH), F32),
        state_low=((T, CH), BF16),
        act=((T, H), BF16),
        dgelu=((T, H), F32),
        pre=((2, T, H), F32),
        out_low=((T, H), BF16),
        out_nat=((T, H), BF16),
        d_pre=((2, T, H), BF16),
        d_mixed=((T, H), F32),
        d_rec=((T, H), BF16),
        source=((T, CH), F32),
        d_proj=((T, CH), BF16),
        din_low=((T, H), BF16),
        din_nat=((T, H), BF16),
        small=((S, SUB, LANES), F32),
        small_r=((S, S, SUB, LANES), F32),
        group=((S, SUB, LANES), F32),
        small2=((2 * SUB, LANES), F32),
        small2_r=((R, 2 * SUB, LANES), F32),
    )
    scalars = dict(bucket=(S,), lengths=(S,))
    flags = dict(block_in=1, all_in=1)
    copies = dict(here=OWN_SMALL + 9, sent=G2 + 10, received=G2 + 10, sent_f=NR, received_f=NR, sent_b=NR, received_b=NR)
    dims.names = [*shapes, *scalars, *flags, *copies]
    parts = []
    for _ in range(4):
        parts += [(H, CH), (NG, H, LANES)]
    routes = routes_of(R, H)
    for _, _, _, lines in routes:
        parts += [(2, R, lines, LANES)] + [(R, lines, LANES)] * 3
    scratch = [pltpu.VMEM(shape, dtype) for shape, dtype in shapes.values()]
    scratch += [pltpu.SMEM(shape, jnp.int32) for shape in scalars.values()]
    scratch += [pltpu.SemaphoreType.REGULAR for _ in flags]
    scratch += [pltpu.SemaphoreType.DMA((n,)) for n in copies.values()]
    scratch += [pltpu.VMEM(shape, gdt) for shape in parts]
    any_spec = pl.BlockSpec(memory_space=pl.ANY)
    vmem = pl.BlockSpec(memory_space=pltpu.VMEM)
    macs = T * H * (2 * CH + 2 * H) * 3 + 4 * T * T * H
    return pl.pallas_call(
        functools.partial(block_kernel, dims),
        out_shape=(
            jax.ShapeDtypeStruct((S, T, W), BF16),
            jax.ShapeDtypeStruct((S, T, W), BF16),
            jax.ShapeDtypeStruct((HB, 4 * LANES), F32),
            jax.ShapeDtypeStruct((2 * SUB, LANES), F32),
        ),
        in_specs=[any_spec] * 14,
        out_specs=(any_spec, any_spec, vmem, vmem),
        scratch_shapes=scratch,
        compiler_params=pltpu.CompilerParams(
            collective_id=0, has_side_effects=True, vmem_limit_bytes=56 * 2**20
        ),
        cost_estimate=pl.CostEstimate(flops=2 * macs, bytes_accessed=8 * 2**20, transcendentals=4 * T * H),
    )(*args)


def on_device(
    inputs,
    bucket,
    lengths,
    nu_log,
    theta_log,
    gamma_log,
    in_proj,
    out_proj,
    skip,
    norm_gain,
    norm_bias,
    glu_weight,
    glu_bias,
    output_cotangent,
):
    row_count, seq, part = inputs.shape
    width = norm_gain.shape[0]
    chans = nu_log.shape[0]
    R, S = lax.axis_size(ROWS), lax.axis_size(STATE)
    dims = SimpleNamespace(R=R, S=S, T=seq, H=width, W=part)
    assert row_count == S and 2 * chans == LANES and part == LANES and S % 2 == 0 and R % 2 == 0

    outputs, d_norm, gsum, vec = run_block(
        dims,
        inputs,
        output_cotangent,
        in_proj.transpose(1, 2, 0).reshape(2 * chans, width),
        out_proj.reshape(2 * chans, width),
        glu_weight.reshape(2 * width, part),
        bucket,
        lengths,
        nu_log[None],
        theta_log[None],
        gamma_log[None],
        skip[None],
        glu_bias,
        norm_gain[None],
        norm_bias[None],
    )
    return finish(dims, lengths, outputs, d_norm, output_cotangent, gsum, vec)


def finish_kernel(dims, *refs):
    S, T, HB = dims.S, dims.T, dims.H // dims.R
    (lengths, out_in, d_norm, cot, gsum, vec) = refs[:6]
    (out, d_inputs, d_nu, d_theta, d_gamma, d_in, d_out, d_skip, d_gain, d_bias, d_glu, d_glu_bias) = refs[6:]
    out[...] = out_in[...]
    for row in range(S):
        for first in range(0, T, CHUNK):
            lines = slice(first, first + CHUNK)
            place = lax.broadcasted_iota(jnp.int32, (CHUNK, LANES), 0) + first
            direct = jnp.where(place < lengths[row], cot[row, lines, :].astype(F32), 0.0)
            d_inputs[row, lines, :] = d_norm[row, lines, :].astype(F32) + direct
    d_nu[...] = vec[0:1, 0:HALF]
    d_theta[...] = pltpu.roll(vec[0:1, :], HALF, 1)[:, 0:HALF]
    d_gamma[...] = vec[1:2, 0:HALF]
    d_skip[...] = vec[2:3, :]
    d_glu_bias[...] = vec[3:5, :]
    for s in range(S):
        here = slice(s * LANES, (s + 1) * LANES)
        d_gain[:, here] = vec[SUB + s : SUB + s + 1, :]
        d_bias[:, here] = vec[SUB + S + s : SUB + S + s + 1, :]
    both = gsum[:, 0:LANES]
    d_in[pl.ds(0, HB, stride=2), :] = both[:, 0:HALF]
    d_in[pl.ds(1, HB, stride=2), :] = pltpu.roll(both, HALF, 1)[:, 0:HALF]
    d_out[...] = gsum[:, LANES : 2 * LANES].T
    d_glu[pl.ds(0, HB, stride=2), :] = gsum[:, 2 * LANES : 3 * LANES]
    d_glu[pl.ds(1, HB, stride=2), :] = gsum[:, 3 * LANES : 4 * LANES]


def finish(dims, lengths, outputs, d_norm, cot, gsum, vec):
    R, S, T, H, W = dims.R, dims.S, dims.T, dims.H, dims.W
    HB = H // R
    vmem = pl.BlockSpec(memory_space=pltpu.VMEM)
    small = [(1, HALF)] * 3 + [(2 * HB, HALF), (LANES, HB), (1, W), (1, H), (1, H), (2 * HB, W), (2, W)]
    got = pl.pallas_call(
        functools.partial(finish_kernel, dims),
        out_shape=(
            jax.ShapeDtypeStruct((S, T, W), BF16),
            jax.ShapeDtypeStruct((S, T, W), F32),
            *(jax.ShapeDtypeStruct(shape, F32) for shape in small),
        ),
        in_specs=[pl.BlockSpec(memory_space=pltpu.SMEM)] + [vmem] * 5,
        out_specs=(vmem,) * 12,
    )(lengths, outputs, d_norm, cot, gsum, vec)
    out, d_inputs, d_nu, d_theta, d_gamma, d_in, d_out, d_skip, d_gain, d_bias, d_glu, d_glu_bias = got
    return (
        out,
        d_inputs,
        d_nu.reshape(HALF),
        d_theta.reshape(HALF),
        d_gamma.reshape(HALF),
        d_in.reshape(HB, 2, HALF),
        d_out.reshape(2, HALF, HB),
        d_skip.reshape(W),
        d_gain.reshape(H),
        d_bias.reshape(H),
        d_glu.reshape(HB, 2, W),
        d_glu_bias,
    )


def solution(mesh):
    return jax.shard_map(
        on_device,
        mesh=mesh,
        in_specs=(
            P(ROWS, None, STATE),
            P(ROWS),
            P(ROWS),
            P(STATE),
            P(STATE),
            P(STATE),
            P(None, None, STATE),
            P(None, STATE, None),
            P(STATE),
            P(),
            P(),
            P(None, None, STATE),
            P(None, STATE),
            P(ROWS, None, STATE),
        ),
        out_specs=(
            P(ROWS, None, STATE),
            P(ROWS, None, STATE),
            P(STATE),
            P(STATE),
            P(STATE),
            P(ROWS, None, STATE),
            P(None, STATE, ROWS),
            P(STATE),
            P(),
            P(),
            P(ROWS, None, STATE),
            P(None, STATE),
        ),
        check_vma=False,
    )
```

```python
import functools
import math
from types import SimpleNamespace

import jax
import jax.numpy as jnp
from jax import lax
from jax.experimental import pallas as pl
from jax.experimental.pallas import tpu as pltpu
from jax.sharding import PartitionSpec as P

epsilon = 1e-05

F32 = jnp.float32
BF16 = jnp.bfloat16
MESH = pl.DeviceIdType.MESH
ROWS, STATE = "rows", "state"
SUB = 8
LANES = 128
HALF = LANES // 2
CHUNK = 64
SEG = 32
LEVELS = tuple(1 << i for i in range(SEG.bit_length() - 1))

OWN_X, OWN_WIN, OWN_WOUT, OWN_WGLU, OWN_C, OWN_OUT, OWN_DIN, OWN_SMALL = range(8)
PAR_S, X, C, OUT, DIN, SM, SN, W1 = range(8)
SIB, FAR, PEER, FAR_SIB = range(4)
G1 = W1 + 12
G2 = G1 + 4


def loop(count, body, unroll=1):
    def step(i, carry):
        body(i)
        return carry

    lax.fori_loop(0, count, step, 0, unroll=unroll)


def nn(a, b):
    return lax.dot_general(a, b, (((1,), (0,)), ((), ())), preferred_element_type=F32)


def nt(a, b):
    return lax.dot_general(a, b, (((1,), (1,)), ((), ())), preferred_element_type=F32)


def tn(a, b):
    return lax.dot_general(a, b, (((0,), (0,)), ((), ())), preferred_element_type=F32)


def cmul(a, b):
    return a[0] * b[0] - a[1] * b[1], a[0] * b[1] + a[1] * b[0]


def conj_mul(a, b):
    return a[0] * b[0] + a[1] * b[1], a[0] * b[1] - a[1] * b[0]


def swap_halves(u, v, low):
    return (
        jnp.where(low, u, pltpu.roll(v, HALF, 1)),
        jnp.where(low, pltpu.roll(u, HALF, 1), v),
    )


def fold(x):
    return jnp.sum(x.reshape(x.shape[0] // SUB, SUB, x.shape[1]), axis=0)


def block_kernel(dims, *refs):
    R, S, T, H, W, gdt = dims.R, dims.S, dims.T, dims.H, dims.W, dims.gdt
    NR, NG, R2, HB, L = R * S, S // 2, R // 2, H // R, T // SEG
    Q = 4 if R % 8 == 0 else 2
    G, NB = Q * S, R // Q
    BITS = T.bit_length()
    (inputs, cot, w_in, w_out, w_glu) = refs[:5]
    vectors = refs[5:14]
    (out_ref, din_ref, gsum, vec) = refs[14:18]
    total = 18 + len(dims.names)
    v = SimpleNamespace(**dict(zip(dims.names, refs[18:total])))
    parts = [
        SimpleNamespace(full=refs[total + 2 * i], r1=refs[total + 2 * i + 1], step=G1 + i, at=i * LANES, routes=[])
        for i in range(4)
    ]
    g_in, g_out, g_lin, g_gate = parts
    total += 8
    for i, (part, over_x, first, lines) in enumerate(routes_of(R, H)):
        a1, r2, a2, r3 = refs[total + 4 * i : total + 4 * i + 4]
        parts[part].routes.append(
            SimpleNamespace(
                part=parts[part], over_x=over_x, first=first, lines=lines, a1=a1, r2=r2, a2=a2, r3=r3, step=G2 + 2 * i
            )
        )

    me_r, me_s = lax.axis_index(ROWS), lax.axis_index(STATE)
    me = me_r * S + me_s

    def cols(i, width):
        return pl.ds(pl.multiple_of(i * width, LANES), width)

    def lanes(i):
        return slice(i * LANES, (i + 1) * LANES)

    def rows_of(i):
        return pl.ds(pl.multiple_of(i * CHUNK, CHUNK), CHUNK)

    def wait_bytes(ref, which, arrived):
        pltpu.make_async_copy(ref, ref, (v.received if arrived else v.sent).at[which]).wait()

    def send(src, dst, which, target):
        pltpu.make_async_remote_copy(
            src_ref=src,
            dst_ref=dst,
            send_sem=v.sent.at[which],
            recv_sem=v.received.at[which],
            device_id=target,
            device_id_type=MESH,
        ).start()

    def to_state(src_of, dst, which):
        for j in (2, 3, 1) if S == 4 else range(1, S):
            t = lax.rem(me_s + j, S)
            send(src_of(t), dst, which, {STATE: t})

    sib = me_s + 1 - 2 * lax.rem(me_s, 2)
    far = lax.rem(me_s + NG, S)
    sib_far = lax.rem(sib + NG, S)
    pair_r = me_r + 1 - 2 * lax.rem(me_r, 2)
    group_r = me_r - lax.rem(me_r, Q)
    piece = lax.rem(me_r, Q)
    mine_s = lax.rem(me_s, 2)
    mine_r = lax.rem(me_r, 2)

    def line_block(ref, s, p=None):
        if p is None:
            return ref.at[pl.ds(pl.multiple_of(s * LANES, LANES), LANES), :]
        size = LANES // Q
        return ref.at[pl.ds(pl.multiple_of(s * LANES + p * size, size), size), :]

    def glu_block(ref, s, p=None):
        size = H // Q
        rows = slice(None) if p is None else pl.ds(pl.multiple_of(p * size, size), size)
        return ref.at[:, rows, cols(s, W)]

    own = [
        (w_glu, v.glu_raw, OWN_WGLU),
        (w_in, line_block(v.win, me_s), OWN_WIN),
        (w_out, line_block(v.wout, me_s), OWN_WOUT),
        (inputs.at[me_s], v.xin.at[:, cols(me_s, W)], OWN_X),
        (cot.at[me_s], v.cin.at[:, cols(me_s, W)], OWN_C),
    ]
    small_in = (v.bucket, v.lengths, v.nu, v.theta, v.gamma, v.skip, v.glu_bias, v.gain, v.bias)
    own += [(a, b, OWN_SMALL + i) for i, (a, b) in enumerate(zip(vectors, small_in))]
    own = {which: pltpu.make_async_copy(a, b, v.here.at[which]) for a, b, which in own}

    barrier = pltpu.get_barrier_semaphore()
    number = piece * S + me_s
    is_gate = (number == 0) & (NB > 1)
    gated = 1 if NB > 1 else 0

    def signal(which, i, rows=None):
        pl.semaphore_signal(
            which,
            inc=1,
            device_id={ROWS: group_r + lax.div(i, S) if rows is None else rows, STATE: lax.rem(i, S)},
            device_id_type=MESH,
        )

    def greet(d, carry):
        i = lax.rem(number + d, G)

        @pl.when(i >= gated)
        def _():
            signal(barrier, i)

        return carry

    lax.fori_loop(1, G, greet, 0)
    for copy in own.values():
        copy.start()
    for i in range(len(vectors)):
        own[OWN_SMALL + i].wait()
    bucket_ref, lengths_ref, nu_ref, theta_ref, gamma_ref, skip_ref, glu_bias_ref, gain_ref, bias_ref = small_in

    par = v.par
    par[...] = jnp.zeros((2 * SUB, LANES), F32)
    par[0:1, 0:HALF] = nu_ref[...]
    par[0:1, HALF:LANES] = theta_ref[...]
    par[1:2, 0:HALF] = gamma_ref[...]
    par[2:3, :] = skip_ref[...]
    par[3:5, :] = glu_bias_ref[...]
    for i in range(S):
        par[SUB + i : SUB + i + 1, :] = jnp.full((1, LANES), bucket_ref[i], jnp.int32).astype(F32)
        par[SUB + S + i : SUB + S + i + 1, :] = jnp.full((1, LANES), lengths_ref[i], jnp.int32).astype(F32)
    v.par_s[me_s] = par[...]

    @pl.when(jnp.logical_not(is_gate))
    def _():
        pl.semaphore_wait(barrier, G - 1)

    if NB > 1:

        @pl.when(number == 1)
        def _():
            signal(v.block_in, jnp.int32(0))

        @pl.when(is_gate)
        def _():
            pl.semaphore_wait(v.block_in, 1)

            def next_gate(d, carry):
                signal(barrier, jnp.int32(0), rows=lax.rem(group_r + d * Q, R))
                return carry

            lax.fori_loop(1, NB, next_gate, 0)

    def everyone_in():
        if NB > 1:

            @pl.when(is_gate)
            def _():
                pl.semaphore_wait(barrier, NB - 1)

                def tell(i, carry):
                    signal(v.all_in, i)
                    return carry

                lax.fori_loop(1, G, tell, 0)

            @pl.when(jnp.logical_not(is_gate))
            def _():
                pl.semaphore_wait(v.all_in, 1)

    to_state(lambda t: par, v.par_s.at[me_s], PAR_S)

    def w_send(w, own_block, own_piece):
        send(own_piece, w.block(w.ref, me_s, piece), w.step + FAR, {STATE: far})
        send(own_block, w.block(w.ref, me_s), w.step + SIB, {STATE: sib})

    def w_forward_far(w):
        here = w.block(w.ref, far, piece)
        wait_bytes(here, w.step + FAR, True)
        for j in range(1, Q):
            send(here, here, w.step + PEER, {ROWS: group_r + lax.rem(piece + j, Q)})

    def w_forward_all(w):
        wait_bytes(w.rest, w.step + PEER, True)
        send(w.block(w.ref, far), w.block(w.ref, far), w.step + FAR_SIB, {STATE: sib})

    def w_ready(w):
        wait_bytes(w.block(w.ref, sib), w.step + SIB, True)
        wait_bytes(w.block(w.ref, sib_far), w.step + FAR_SIB, True)

    def w_sent(w):
        wait_bytes(w.block(w.ref, sib), w.step + SIB, False)
        wait_bytes(w.block(w.ref, sib), w.step + FAR_SIB, False)
        wait_bytes(w.block(w.ref, sib, piece), w.step + FAR, False)
        wait_bytes(w.rest, w.step + PEER, False)

    others = pl.ds(0, LANES - LANES // Q)
    wt_in = SimpleNamespace(ref=v.win, block=line_block, step=W1, rest=v.win.at[others, :])
    wt_out = SimpleNamespace(ref=v.wout, block=line_block, step=W1 + 4, rest=v.wout.at[others, :])
    wt_glu = SimpleNamespace(
        ref=v.wglu, block=glu_block, step=W1 + 8, rest=v.wglu.at[:, pl.ds(0, H - H // Q), pl.ds(0, W)]
    )

    def piece_of(ref):
        size = LANES // Q
        return ref.at[pl.ds(pl.multiple_of(piece * size, size), size), :]

    w_send(wt_in, w_in, piece_of(w_in))
    to_state(lambda t: inputs.at[t], v.xin.at[:, cols(me_s, W)], X)
    w_send(wt_out, w_out, piece_of(w_out))
    own[OWN_WGLU].wait()

    def split_glu(i):
        here = rows_of(i)
        v.glu_wide[...] = v.glu_raw[pl.ds(pl.multiple_of(i * 2 * CHUNK, 2 * CHUNK), 2 * CHUNK), :].astype(F32)
        for k in range(2):
            v.wglu[k, here, cols(me_s, W)] = v.glu_wide[pl.ds(k, CHUNK, stride=2), :].astype(BF16)

    loop(H // CHUNK, split_glu)
    w_send(wt_glu, glu_block(v.wglu, me_s), glu_block(v.wglu, me_s, piece))

    line = lax.broadcasted_iota(jnp.int32, (CHUNK, T), 0)
    place = lax.broadcasted_iota(jnp.int32, (CHUNK, T), 1)

    def orders(i):
        base = pl.multiple_of(i * CHUNK, CHUNK)
        at = line + base
        v.perm[pl.ds(base, CHUNK), :] = (
            place == lax.rem(at, SEG) * L + lax.div(at, SEG)
        ).astype(F32).astype(BF16)
        v.back[pl.ds(base, CHUNK), :] = (
            at == lax.rem(place, SEG) * L + lax.div(place, SEG)
        ).astype(F32).astype(BF16)

    loop(T // CHUNK, orders)

    w_forward_far(wt_in)

    low = lax.broadcasted_iota(jnp.int32, (SEG, LANES), 1) < HALF
    low1 = lax.broadcasted_iota(jnp.int32, (1, LANES), 1) < HALF
    seg = lax.broadcasted_iota(jnp.int32, (SEG, LANES), 0)

    wait_bytes(v.par_s.at[pl.ds(0, S - 1)], PAR_S, True)
    par_s = v.par_s
    lam, gam, rate, angle = [], [], [], []
    for a in range(NG):
        nu, theta = swap_halves(par_s[2 * a, 0:1, :], par_s[2 * a + 1, 0:1, :], low1)
        rate.append(jnp.exp(nu))
        angle.append(jnp.exp(theta))
        magnitude = jnp.exp(-rate[a])
        lam.append((magnitude * jnp.cos(angle[a]), magnitude * jnp.sin(angle[a])))
        gam.append(jnp.exp(swap_halves(par_s[2 * a, 1:2, :], par_s[2 * a + 1, 1:2, :], low1)[0]))
    skip = jnp.concatenate([par_s[s, 2:3, :] for s in range(S)], axis=1)
    gain, bias = gain_ref[...], bias_ref[...]
    power = [[(jnp.broadcast_to(l[0], (SUB, LANES)), jnp.broadcast_to(l[1], (SUB, LANES))) for l in lam]]
    for _ in range(BITS - 1):
        power.append([cmul(p, p) for p in power[-1]])
    for b in range(BITS):
        for a in range(NG):
            for c in range(2):
                v.pows[b, a, c] = power[b][a][c]

    def raised(exponent):
        result = [(jnp.ones(exponent.shape, F32), jnp.zeros(exponent.shape, F32)) for _ in range(NG)]
        for b in range(BITS):
            hit = (lax.shift_right_logical(exponent, b) & 1) == 1
            for a in range(NG):
                re, im = cmul(result[a], (v.pows[b, a, 0, 0:1, :], v.pows[b, a, 1, 0:1, :]))
                result[a] = (jnp.where(hit, re, result[a][0]), jnp.where(hit, im, result[a][1]))
        return result

    my_bucket = par[pl.ds(SUB + me_s, 1), :]
    len1 = par[pl.ds(SUB + S + me_s, 1), :].astype(jnp.int32)
    my_len = jnp.broadcast_to(len1, (SEG, LANES))
    seg_pow = raised(jnp.clip(my_len - seg * L, 0, L))
    lead_pow = raised(jnp.minimum(my_len, seg * L))
    tail_pow = raised(jnp.maximum(my_len - (seg + 1) * L, 0))
    for a in range(NG):
        ahead = seg_pow[a]
        behind = seg_pow[a]
        for i, d in enumerate(LEVELS):
            for c in range(2):
                v.hs_f[i, a, c] = jnp.where(seg >= d, ahead[c], 0.0)
                v.hs_b[i, a, c] = jnp.where(seg < SEG - d, behind[c], 0.0)
            ahead = cmul(ahead, (pltpu.roll(ahead[0], d, 0), pltpu.roll(ahead[1], d, 0)))
            behind = cmul(behind, (pltpu.roll(behind[0], SEG - d, 0), pltpu.roll(behind[1], SEG - d, 0)))
        for c in range(2):
            v.lead_pow[a, c] = lead_pow[a][c]
            v.tail_pow[a, c] = tail_pow[a][c]

    def lines_of(p):
        return pl.ds(pl.multiple_of(p * SUB, SUB), SUB)

    def carry_copy(way, source, t):
        return pltpu.make_async_remote_copy(
            src_ref=way.msg,
            dst_ref=way.chain.at[lines_of(source), :],
            send_sem=way.sent.at[t],
            recv_sem=way.received.at[source],
            device_id={ROWS: lax.div(t, S), STATE: lax.rem(t, S)},
            device_id_type=MESH,
        )

    def exchange(way, values):
        for a in range(NG):
            for c in range(2):
                way.msg[pl.ds(c * NG + a, 1), :] = values[a][c]
        way.msg[2 * NG : 2 * NG + 1, :] = my_bucket
        way.msg[2 * NG + 1 : 2 * NG + 2, :] = par[pl.ds(SUB + S + me_s, 1), :]

        def one(t, carry):
            carry_copy(way, me, t).start()
            return carry

        lax.fori_loop(*way.to, one, 0)

    def collect(way):
        def arrive(p, carry):
            carry_copy(way, p, me).wait_recv()
            return carry

        lax.fori_loop(*way.come, arrive, 0)

        def powers(i):
            at = i * SUB * SUB
            lens = way.chain[pl.ds(at + 2 * NG + 1, SUB, stride=SUB), :].astype(jnp.int32)
            here = way.chain[pl.ds(at + 2 * NG, SUB, stride=SUB), :]
            p = lax.broadcasted_iota(jnp.int32, (SUB, LANES), 0) + i * SUB
            hit = (here == my_bucket) & (my_bucket > 0.5) & ((p < me) if way.forward else (p > me))
            factor = raised(lens)
            for a in range(NG):
                v.row_pow[a, lines_of(i), :] = jnp.where(hit, factor[a][0], 1.0)
                v.row_pow[NG + a, lines_of(i), :] = jnp.where(hit, factor[a][1], 0.0)
            v.row_hit[lines_of(i), :] = jnp.where(hit, 1.0, 0.0)

        loop(NR // SUB, powers)

        def fold_in(i, carry):
            p = i if way.forward else NR - 1 - i
            hit = v.row_hit[pl.ds(p, 1), :] > 0.5
            new = []
            for a in range(NG):
                factor = (v.row_pow[a, pl.ds(p, 1), :], v.row_pow[NG + a, pl.ds(p, 1), :])
                re, im = cmul(factor, carry[a]) if way.forward else conj_mul(factor, carry[a])
                add = (way.chain[pl.ds(p * SUB + a, 1), :], way.chain[pl.ds(p * SUB + NG + a, 1), :])
                new.append((re + jnp.where(hit, add[0], 0.0), im + jnp.where(hit, add[1], 0.0)))
            return tuple(new)

        zero = jnp.zeros((1, LANES), F32)
        return lax.fori_loop(0, me if way.forward else NR - 1 - me, fold_in, tuple((zero, zero) for _ in range(NG)))

    def carries_sent(way):
        def one(t, carry):
            carry_copy(way, me, t).wait_send()
            return carry

        lax.fori_loop(*way.to, one, 0)

    ahead = SimpleNamespace(
        forward=True, msg=v.msg_f, chain=v.chain_f, sent=v.sent_f, received=v.received_f, to=(me + 1, NR), come=(0, me)
    )
    behind = SimpleNamespace(
        forward=False, msg=v.msg_b, chain=v.chain_b, sent=v.sent_b, received=v.received_b, to=(0, me), come=(me + 1, NR)
    )

    pos = lax.broadcasted_iota(jnp.int32, (CHUNK, LANES), 0)
    pos = lax.rem(pos, SEG) * L + lax.div(pos, SEG)

    def valid_of(i, width):
        ok = jnp.where(pos + i * (CHUNK // SEG) < len1, 1.0, 0.0)
        return jnp.concatenate([ok] * (width // LANES), axis=1) if width > LANES else ok

    w_forward_all(wt_in)

    own[OWN_X].wait()
    wait_bytes(v.xin.at[:, pl.ds(0, (S - 1) * W)], X, True)
    v.x[...] = nn(v.perm[...], v.xin[...])

    def layer_norm(i):
        rows = rows_of(i)
        x = v.x[rows, :]
        centred = x - jnp.mean(x, -1, keepdims=True)
        inverse = lax.rsqrt(jnp.mean(centred * centred, -1, keepdims=True) + epsilon)
        normed = centred * inverse
        v.normed[rows, :] = normed
        v.inverse[rows, :] = jnp.broadcast_to(inverse, (CHUNK, LANES))
        v.mixed_low[rows, :] = (normed * gain + bias).astype(BF16)

    loop(T // CHUNK, layer_norm, unroll=2)
    own[OWN_WIN].wait()
    w_ready(wt_in)
    v.wide[...] = nt(v.mixed_low[...], v.win[...])
    w_forward_far(wt_out)

    lamb = [tuple(jnp.broadcast_to(c, (SEG, LANES)) for c in l) for l in lam]
    gamb = [jnp.broadcast_to(g, (SEG, LANES)) for g in gam]

    def load_c(ref, at):
        return [(ref[at, lanes(a)], ref[at, lanes(NG + a)]) for a in range(NG)]

    def store_c(ref, at, values):
        for a in range(NG):
            ref[at, lanes(a)] = values[a][0]
            ref[at, lanes(NG + a)] = values[a][1]

    def load_g(ref, at):
        return [swap_halves(ref[at, lanes(2 * a)], ref[at, lanes(2 * a + 1)], low) for a in range(NG)]

    def to_g(values):
        return [g for a in range(NG) for g in swap_halves(values[a][0], values[a][1], low)]

    def step_of(k):
        return pl.ds(pl.multiple_of(k * SEG, SEG), SEG)

    zeros = tuple((jnp.zeros((SEG, LANES), F32), jnp.zeros((SEG, LANES), F32)) for _ in range(NG))

    def advance(k, state, proj):
        ok = seg * L + k < my_len
        new = []
        for a in range(NG):
            re, im = cmul(lamb[a], state[a])
            re, im = re + gamb[a] * proj[a][0], im + gamb[a] * proj[a][1]
            new.append((jnp.where(ok, re, state[a][0]), jnp.where(ok, im, state[a][1])))
        return tuple(new)

    def fwd_first(k, state):
        proj = load_g(v.wide, step_of(k))
        store_c(v.proj, step_of(k), proj)
        return advance(k, state, proj)

    ends = lax.fori_loop(0, L, fwd_first, zeros, unroll=4)

    def across(values, table, forward):
        done = []
        for a in range(NG):
            x = values[a]
            for i, d in enumerate(LEVELS):
                shift = d if forward else SEG - d
                other = (pltpu.roll(x[0], shift, 0), pltpu.roll(x[1], shift, 0))
                factor = (table[i, a, 0], table[i, a, 1])
                add = cmul(factor, other) if forward else conj_mul(factor, other)
                x = (x[0] + add[0], x[1] + add[1])
            done.append(x)
        return done

    w_forward_far(wt_glu)
    ends = across(ends, v.hs_f, True)
    everyone_in()
    exchange(ahead, [tuple(x[SEG - 1 : SEG, :] for x in ends[a]) for a in range(NG)])
    before = [
        tuple(jnp.where(seg > 0, pltpu.roll(x, 1, 0), 0.0) for x in ends[a]) for a in range(NG)
    ]
    to_state(lambda t: cot.at[t], v.cin.at[:, cols(me_s, W)], C)
    w_forward_all(wt_out)
    own[OWN_C].wait()
    starts = collect(ahead)
    state = []
    for a in range(NG):
        add = cmul((v.lead_pow[a, 0], v.lead_pow[a, 1]), starts[a])
        state.append((before[a][0] + add[0], before[a][1] + add[1]))
    store_c(v.state, pl.ds(0, SEG), state)

    def fwd_second(k, state):
        state = advance(k, state, load_c(v.proj, step_of(k)))
        store_c(v.state, step_of(k + 1), state)
        low_out = to_g([(re, -im) for re, im in state])
        for s in range(S):
            v.state_low[step_of(k), lanes(s)] = low_out[s].astype(BF16)
        return state

    lax.fori_loop(0, L, fwd_second, tuple(state), unroll=4)

    own[OWN_WOUT].wait()
    w_ready(wt_out)
    v.wide[...] = nn(v.state_low[...], v.wout[...])
    w_forward_all(wt_glu)

    def gelu(i):
        rows = rows_of(i)
        mixed_in = v.normed[rows, :] * gain + bias
        mixed = v.wide[rows, :] + skip * mixed_in
        cdf = 0.5 * (1.0 + lax.erf(mixed * (1.0 / math.sqrt(2.0))))
        density = jnp.exp(-0.5 * mixed * mixed) * (1.0 / math.sqrt(2.0 * math.pi))
        v.act[rows, :] = (mixed * cdf).astype(BF16)
        v.dgelu[rows, :] = cdf + mixed * density

    loop(T // CHUNK, gelu, unroll=2)
    w_ready(wt_glu)
    for k in range(2):
        v.pre[k] = nn(v.act[...], v.wglu[k])

    def glu(i):
        rows = rows_of(i)
        ok = valid_of(i, W)
        for s in range(S):
            here = slice(s * W, (s + 1) * W)
            linear = v.pre[0, rows, here] + par_s[s, 3:4, :]
            gate = v.pre[1, rows, here] + par_s[s, 4:5, :]
            share = jax.nn.sigmoid(gate)
            value = linear * share
            v.out_low[rows, here] = (ok * (v.x[rows, here] + value)).astype(BF16)
            v.pre[0, rows, here] = ok * share
            v.pre[1, rows, here] = ok * (value * (1.0 - share))

    loop(T // CHUNK, glu, unroll=2)

    def give_back(low_ref, nat, result, own_which):
        nat[...] = nn(v.back[...], low_ref[...]).astype(BF16)
        copy = pltpu.make_async_copy(nat.at[:, cols(me_s, W)], result.at[me_s], v.here.at[own_which])
        copy.start()
        return copy

    def give_to(nat, result, which, t):
        send(nat.at[:, cols(t, W)], result.at[me_s], which, {STATE: t})

    out_copy = give_back(v.out_low, v.out_nat, out_ref, OWN_OUT)
    give_to(v.out_nat, out_ref, OUT, far)
    wait_bytes(v.cin.at[:, pl.ds(0, (S - 1) * W)], C, True)
    v.wide[...] = nn(v.perm[...], v.cin[...])

    def glu_back(i):
        rows = rows_of(i)
        dout = v.wide[rows, :]
        for k in range(2):
            v.d_pre[k, rows, :] = (dout * v.pre[k, rows, :]).astype(BF16)

    loop(T // CHUNK, glu_back, unroll=2)

    for part in parts:
        for route in part.routes:
            if route.over_x:
                route.half = lax.div(me_s, 2)
                route.pair = {STATE: far}
                route.number = me_r
                route.slot = lambda r, b: (b, r)
                route.owner = lambda n: {ROWS: n}
            else:
                route.half = mine_r
                route.pair = {ROWS: pair_r}
                route.number = lax.div(me_s, 2) * R2 + lax.div(me_r, 2)
                route.slot = lambda r, b: (lax.rem(r, 2), b * R2 + lax.div(r, 2))
                route.owner = lambda n: {ROWS: 2 * lax.rem(n, R2) + mine_r, STATE: 2 * lax.div(n, R2) + mine_s}

    def first_send(part):
        for b in range(NG):
            send(part.full.at[:, cols(2 * b + 1 - mine_s, LANES)], part.r1.at[b], part.step, {STATE: sib})

    def first_wait(part):
        wait_bytes(part.r1, part.step, True)

    def first_sum(route):
        part = route.part

        def one(r):
            rows = pl.ds(pl.multiple_of(r * HB + route.first, route.lines), route.lines)
            for b in range(NG):
                total = part.full[rows, cols(2 * b + mine_s, LANES)].astype(F32) + part.r1[b, rows, :].astype(F32)
                route.a1[route.slot(r, b)] = total.astype(gdt)

        loop(R, one, unroll=2)
        send(route.a1.at[1 - route.half], route.r2, route.step, route.pair)

    def second_sum(route):
        wait_bytes(route.r2, route.step, True)

        def one(n):
            total = route.a1[route.half, n].astype(F32) + route.r2[n].astype(F32)
            route.a2[n] = total.astype(gdt)

        loop(R, one, unroll=2)
        route.r3[route.number] = route.a2[route.number]

        def give(d, carry):
            n = lax.rem(route.number + d, R)
            send(route.a2.at[n], route.r3.at[route.number], route.step + 1, route.owner(n))
            return carry

        lax.fori_loop(1, R, give, 0)

    def third_sum(route):
        wait_bytes(route.r3.at[pl.ds(0, R - 1)], route.step + 1, True)

        def one(n, total):
            return total + route.r3[n].astype(F32)

        total = lax.fori_loop(0, R, one, jnp.zeros((route.lines, LANES), F32), unroll=2)
        gsum[route.first : route.first + route.lines, route.part.at : route.part.at + LANES] = total

    def all_sent(part):
        wait_bytes(part.r1, part.step, False)
        for route in part.routes:
            wait_bytes(route.r2, route.step, False)
            wait_bytes(route.r3.at[pl.ds(0, R - 1)], route.step + 1, False)

    for k, part in ((0, g_lin), (1, g_gate)):
        part.full[...] = tn(v.act[...], v.d_pre[k]).astype(gdt)
        first_send(part)
    v.wide[...] = nt(v.d_pre[0], v.wglu[0]) + nt(v.d_pre[1], v.wglu[1])

    def gelu_back(i, total):
        rows = rows_of(i)
        d_mixed = v.wide[rows, :] * v.dgelu[rows, :]
        v.d_mixed[rows, :] = d_mixed
        v.d_rec[rows, :] = d_mixed.astype(BF16)
        return total + fold(d_mixed * (v.normed[rows, :] * gain + bias))

    d_skip = lax.fori_loop(0, T // CHUNK, gelu_back, jnp.zeros((SUB, H), F32), unroll=2)
    d_skip = jnp.sum(d_skip, axis=0, keepdims=True)
    v.wide[...] = nt(v.d_rec[...], v.wout[...])
    first_wait(g_lin)
    first_sum(g_lin.routes[0])
    g_out.full[...] = tn(v.d_rec[...], v.state_low[...]).astype(gdt)
    first_send(g_out)

    def retreat(k, source, carry):
        ok = seg * L + k < my_len
        adjoint, new = [], []
        for a in range(NG):
            re, im = source[a][0] + carry[a][0], source[a][1] + carry[a][1]
            adjoint.append((re, im))
            nre, nim = conj_mul(lamb[a], (re, im))
            new.append((jnp.where(ok, nre, re), jnp.where(ok, nim, im)))
        return ok, adjoint, tuple(new)

    def bwd_first(i, carry):
        k = L - 1 - i
        source = [(re, -im) for re, im in load_g(v.wide, step_of(k))]
        store_c(v.source, step_of(k), source)
        return retreat(k, source, carry)[2]

    heads = lax.fori_loop(0, L, bwd_first, zeros, unroll=4)
    heads = across(heads, v.hs_b, False)
    exchange(behind, [tuple(x[0:1, :] for x in heads[a]) for a in range(NG)])
    after = [
        tuple(jnp.where(seg < SEG - 1, pltpu.roll(x, SEG - 1, 0), 0.0) for x in heads[a])
        for a in range(NG)
    ]
    first_wait(g_gate)
    first_sum(g_gate.routes[0])
    give_to(v.out_nat, out_ref, OUT, sib)
    give_to(v.out_nat, out_ref, OUT, sib_far)
    first_wait(g_out)
    first_sum(g_out.routes[0])
    ones = jnp.ones((2 * SUB, T), BF16)
    d_bias = [nn(ones, v.d_pre[k])[0:1, :] for k in range(2)]
    second_sum(g_lin.routes[0])

    omegas = collect(behind)
    carry = []
    for a in range(NG):
        add = conj_mul((v.tail_pow[a, 0], v.tail_pow[a, 1]), omegas[a])
        carry.append((after[a][0] + add[0], after[a][1] + add[1]))

    def bwd_second(i, item):
        k = L - 1 - i
        carry, sums = item
        ok, adjoint, carry = retreat(k, load_c(v.source, step_of(k)), carry)
        previous = load_c(v.state, step_of(k))
        proj = load_c(v.proj, step_of(k))
        new_sums, low_out = [], []
        for a in range(NG):
            re, im = (jnp.where(ok, x, 0.0) for x in adjoint[a])
            dre, dim = conj_mul(previous[a], (re, im))
            dg = re * proj[a][0] + im * proj[a][1]
            new_sums.append(tuple(x + fold(y) for x, y in zip(sums[a], (dre, dim, dg))))
            low_out.append((gamb[a] * re, gamb[a] * im))
        low_out = to_g(low_out)
        for s in range(S):
            v.d_proj[step_of(k), lanes(s)] = low_out[s].astype(BF16)
        return carry, tuple(new_sums)

    zero = jnp.zeros((SUB, LANES), F32)
    _, sums = lax.fori_loop(
        0, L, bwd_second, (tuple(carry), tuple((zero, zero, zero) for _ in range(NG))), unroll=2
    )

    g_in.full[...] = tn(v.mixed_low[...], v.d_proj[...]).astype(gdt)
    first_send(g_in)
    v.wide[...] = nn(v.d_proj[...], v.win[...])
    def norm_back(i, totals):
        rows = rows_of(i)
        d_mixed_in = v.wide[rows, :] + skip * v.d_mixed[rows, :]
        normed = v.normed[rows, :]
        inverse = jnp.concatenate([v.inverse[rows, :]] * (H // LANES), axis=1)
        g = d_mixed_in * gain
        first = jnp.mean(g, -1, keepdims=True)
        second = jnp.mean(g * normed, -1, keepdims=True)
        v.din_low[rows, :] = (inverse * (g - first - normed * second)).astype(BF16)
        return totals[0] + fold(d_mixed_in * normed), totals[1] + fold(d_mixed_in)

    zero_h = jnp.zeros((SUB, H), F32)
    d_gain, d_nbias = lax.fori_loop(0, T // CHUNK, norm_back, (zero_h, zero_h), unroll=2)
    d_gain = jnp.sum(d_gain, axis=0, keepdims=True)
    d_nbias = jnp.sum(d_nbias, axis=0, keepdims=True)
    first_wait(g_in)
    for route in g_in.routes:
        first_sum(route)

    small = v.small
    small[...] = jnp.zeros((S, SUB, LANES), F32)
    for a in range(NG):
        sr, si, sg = (jnp.sum(x, axis=0, keepdims=True) for x in sums[a])
        d_nu = -rate[a] * (sr * lam[a][0] + si * lam[a][1])
        d_theta = angle[a] * (si * lam[a][0] - sr * lam[a][1])
        pair = swap_halves(d_nu, d_theta, low1)
        pair_g = swap_halves(gam[a] * sg, jnp.zeros_like(sg), low1)
        for u in range(2):
            small[2 * a + u, 0:1, :] = pair[u]
            small[2 * a + u, 1:2, :] = pair_g[u]
    for s in range(S):
        here = slice(s * W, (s + 1) * W)
        small[s, 2:3, :] = d_skip[:, here]
        small[s, 3:4, :] = d_bias[0][:, here]
        small[s, 4:5, :] = d_bias[1][:, here]
        small[s, 5:6, :] = d_gain[:, here]
        small[s, 6:7, :] = d_nbias[:, here]
    v.small_r[me_s] = small[...]
    to_state(lambda t: small, v.small_r.at[me_s], SM)

    second_sum(g_out.routes[0])
    second_sum(g_gate.routes[0])
    din_copy = give_back(v.din_low, v.din_nat, din_ref, OWN_DIN)
    for t in (far, sib_far, sib):
        give_to(v.din_nat, din_ref, DIN, t)
    for route in g_in.routes:
        second_sum(route)
    wait_bytes(v.small_r.at[pl.ds(0, S - 1)], SM, True)
    group = v.small_r[0]
    for s in range(1, S):
        group = group + v.small_r[s]
    small2 = v.small2
    v.group[...] = group
    small2[0:SUB, :] = v.group[me_s]
    for s in range(S):
        small2[SUB + s : SUB + s + 1, :] = group[s, 5:6, :]
        small2[SUB + S + s : SUB + S + s + 1, :] = group[s, 6:7, :]
    v.small2_r[me_r] = small2[...]

    def small_rows(d, carry):
        send(small2, v.small2_r.at[me_r], SN, {ROWS: lax.rem(me_r + d, R)})
        return carry

    lax.fori_loop(1, R, small_rows, 0)
    third_sum(g_lin.routes[0])
    third_sum(g_out.routes[0])
    third_sum(g_gate.routes[0])
    wait_bytes(v.small2_r.at[pl.ds(0, R - 1)], SN, True)

    def sum_rows(r, total):
        return total + v.small2_r[r]

    vec[...] = lax.fori_loop(0, R, sum_rows, jnp.zeros((2 * SUB, LANES), F32))
    for route in g_in.routes:
        third_sum(route)

    out_copy.wait()
    din_copy.wait()
    wait_bytes(out_ref.at[pl.ds(0, S - 1)], OUT, True)
    wait_bytes(din_ref.at[pl.ds(0, S - 1)], DIN, True)
    wait_bytes(out_ref.at[pl.ds(0, S - 1)], OUT, False)
    wait_bytes(din_ref.at[pl.ds(0, S - 1)], DIN, False)
    wait_bytes(v.par_s.at[pl.ds(0, S - 1)], PAR_S, False)
    wait_bytes(v.xin.at[:, pl.ds(0, (S - 1) * W)], X, False)
    for w in (wt_in, wt_out, wt_glu):
        w_sent(w)
    wait_bytes(v.cin.at[:, pl.ds(0, (S - 1) * W)], C, False)
    carries_sent(ahead)
    carries_sent(behind)
    wait_bytes(v.small_r.at[pl.ds(0, S - 1)], SM, False)
    wait_bytes(v.small2_r.at[pl.ds(0, R - 1)], SN, False)
    for part in parts:
        all_sent(part)


def routes_of(R, H):
    HB = H // R
    if HB % (4 * SUB) == 0:
        routes = [(0, False, 0, HB // 2), (0, True, HB // 2, HB // 2)]
    else:
        routes = [(0, False, 0, HB)]
    return routes + [(1, False, 0, HB), (2, False, 0, HB), (3, True, 0, HB)]


def run_block(dims, *args):
    R, S, T, H, W = dims.R, dims.S, dims.T, dims.H, dims.W
    NR, NG, HB = R * S, S // 2, H // R
    CH, levels = S * LANES, len(LEVELS)
    gdt = BF16 if HB % (2 * SUB) == 0 else F32
    dims.gdt = gdt
    bits = T.bit_length()
    shapes = dict(
        xin=((T, H), BF16),
        cin=((T, H), BF16),
        win=((CH, H), BF16),
        wout=((CH, H), BF16),
        wglu=((2, H, H), BF16),
        glu_raw=((2 * H, W), BF16),
        glu_wide=((2 * CHUNK, W), F32),
        perm=((T, T), BF16),
        back=((T, T), BF16),
        nu=((1, HALF), F32),
        theta=((1, HALF), F32),
        gamma=((1, HALF), F32),
        skip=((1, W), F32),
        glu_bias=((2, W), F32),
        gain=((1, H), F32),
        bias=((1, H), F32),
        par=((2 * SUB, LANES), F32),
        par_s=((S, 2 * SUB, LANES), F32),
        pows=((bits, NG, 2, SUB, LANES), F32),
        hs_f=((levels, NG, 2, SEG, LANES), F32),
        hs_b=((levels, NG, 2, SEG, LANES), F32),
        lead_pow=((NG, 2, SEG, LANES), F32),
        tail_pow=((NG, 2, SEG, LANES), F32),
        row_pow=((2 * NG, NR, LANES), F32),
        row_hit=((NR, LANES), F32),
        msg_f=((SUB, LANES), F32),
        msg_b=((SUB, LANES), F32),
        chain_f=((NR * SUB, LANES), F32),
        chain_b=((NR * SUB, LANES), F32),
        x=((T, H), F32),
        normed=((T, H), F32),
        inverse=((T, LANES), F32),
        mixed_low=((T, H), BF16),
        wide=((T, max(H, CH)), F32),
        proj=((T, CH), F32),
        state=((T + SEG, CH), F32),
        state_low=((T, CH), BF16),
        act=((T, H), BF16),
        dgelu=((T, H), F32),
        pre=((2, T, H), F32),
        out_low=((T, H), BF16),
        out_nat=((T, H), BF16),
        d_pre=((2, T, H), BF16),
        d_mixed=((T, H), F32),
        d_rec=((T, H), BF16),
        source=((T, CH), F32),
        d_proj=((T, CH), BF16),
        din_low=((T, H), BF16),
        din_nat=((T, H), BF16),
        small=((S, SUB, LANES), F32),
        small_r=((S, S, SUB, LANES), F32),
        group=((S, SUB, LANES), F32),
        small2=((2 * SUB, LANES), F32),
        small2_r=((R, 2 * SUB, LANES), F32),
    )
    scalars = dict(bucket=(S,), lengths=(S,))
    flags = dict(block_in=1, all_in=1)
    copies = dict(here=OWN_SMALL + 9, sent=G2 + 10, received=G2 + 10, sent_f=NR, received_f=NR, sent_b=NR, received_b=NR)
    dims.names = [*shapes, *scalars, *flags, *copies]
    parts = []
    for _ in range(4):
        parts += [(H, CH), (NG, H, LANES)]
    routes = routes_of(R, H)
    for _, _, _, lines in routes:
        parts += [(2, R, lines, LANES)] + [(R, lines, LANES)] * 3
    scratch = [pltpu.VMEM(shape, dtype) for shape, dtype in shapes.values()]
    scratch += [pltpu.SMEM(shape, jnp.int32) for shape in scalars.values()]
    scratch += [pltpu.SemaphoreType.REGULAR for _ in flags]
    scratch += [pltpu.SemaphoreType.DMA((n,)) for n in copies.values()]
    scratch += [pltpu.VMEM(shape, gdt) for shape in parts]
    any_spec = pl.BlockSpec(memory_space=pl.ANY)
    vmem = pl.BlockSpec(memory_space=pltpu.VMEM)
    macs = T * H * (2 * CH + 2 * H) * 3 + 4 * T * T * H
    return pl.pallas_call(
        functools.partial(block_kernel, dims),
        out_shape=(
            jax.ShapeDtypeStruct((S, T, W), BF16),
            jax.ShapeDtypeStruct((S, T, W), BF16),
            jax.ShapeDtypeStruct((HB, 4 * LANES), F32),
            jax.ShapeDtypeStruct((2 * SUB, LANES), F32),
        ),
        in_specs=[any_spec] * 14,
        out_specs=(any_spec, any_spec, vmem, vmem),
        scratch_shapes=scratch,
        compiler_params=pltpu.CompilerParams(
            collective_id=0, has_side_effects=True, vmem_limit_bytes=56 * 2**20
        ),
        cost_estimate=pl.CostEstimate(flops=2 * macs, bytes_accessed=8 * 2**20, transcendentals=4 * T * H),
    )(*args)


def on_device(
    inputs,
    bucket,
    lengths,
    nu_log,
    theta_log,
    gamma_log,
    in_proj,
    out_proj,
    skip,
    norm_gain,
    norm_bias,
    glu_weight,
    glu_bias,
    output_cotangent,
):
    row_count, seq, part = inputs.shape
    width = norm_gain.shape[0]
    chans = nu_log.shape[0]
    R, S = lax.axis_size(ROWS), lax.axis_size(STATE)
    dims = SimpleNamespace(R=R, S=S, T=seq, H=width, W=part)
    assert row_count == S and 2 * chans == LANES and part == LANES and S % 2 == 0 and R % 2 == 0

    outputs, d_norm, gsum, vec = run_block(
        dims,
        inputs,
        output_cotangent,
        in_proj.transpose(1, 2, 0).reshape(2 * chans, width),
        out_proj.reshape(2 * chans, width),
        glu_weight.reshape(2 * width, part),
        bucket,
        lengths,
        nu_log[None],
        theta_log[None],
        gamma_log[None],
        skip[None],
        glu_bias,
        norm_gain[None],
        norm_bias[None],
    )
    return finish(dims, lengths, outputs, d_norm, output_cotangent, gsum, vec)


def finish_kernel(dims, *refs):
    S, T, HB = dims.S, dims.T, dims.H // dims.R
    (lengths, out_in, d_norm, cot, gsum, vec) = refs[:6]
    (out, d_inputs, d_nu, d_theta, d_gamma, d_in, d_out, d_skip, d_gain, d_bias, d_glu, d_glu_bias) = refs[6:]
    out[...] = out_in[...]
    for row in range(S):
        for first in range(0, T, CHUNK):
            lines = slice(first, first + CHUNK)
            place = lax.broadcasted_iota(jnp.int32, (CHUNK, LANES), 0) + first
            direct = jnp.where(place < lengths[row], cot[row, lines, :].astype(F32), 0.0)
            d_inputs[row, lines, :] = d_norm[row, lines, :].astype(F32) + direct
    d_nu[...] = vec[0:1, 0:HALF]
    d_theta[...] = pltpu.roll(vec[0:1, :], HALF, 1)[:, 0:HALF]
    d_gamma[...] = vec[1:2, 0:HALF]
    d_skip[...] = vec[2:3, :]
    d_glu_bias[...] = vec[3:5, :]
    for s in range(S):
        here = slice(s * LANES, (s + 1) * LANES)
        d_gain[:, here] = vec[SUB + s : SUB + s + 1, :]
        d_bias[:, here] = vec[SUB + S + s : SUB + S + s + 1, :]
    both = gsum[:, 0:LANES]
    d_in[pl.ds(0, HB, stride=2), :] = both[:, 0:HALF]
    d_in[pl.ds(1, HB, stride=2), :] = pltpu.roll(both, HALF, 1)[:, 0:HALF]
    d_out[...] = gsum[:, LANES : 2 * LANES].T
    d_glu[pl.ds(0, HB, stride=2), :] = gsum[:, 2 * LANES : 3 * LANES]
    d_glu[pl.ds(1, HB, stride=2), :] = gsum[:, 3 * LANES : 4 * LANES]


def finish(dims, lengths, outputs, d_norm, cot, gsum, vec):
    R, S, T, H, W = dims.R, dims.S, dims.T, dims.H, dims.W
    HB = H // R
    vmem = pl.BlockSpec(memory_space=pltpu.VMEM)
    small = [(1, HALF)] * 3 + [(2 * HB, HALF), (LANES, HB), (1, W), (1, H), (1, H), (2 * HB, W), (2, W)]
    got = pl.pallas_call(
        functools.partial(finish_kernel, dims),
        out_shape=(
            jax.ShapeDtypeStruct((S, T, W), BF16),
            jax.ShapeDtypeStruct((S, T, W), F32),
            *(jax.ShapeDtypeStruct(shape, F32) for shape in small),
        ),
        in_specs=[pl.BlockSpec(memory_space=pltpu.SMEM)] + [vmem] * 5,
        out_specs=(vmem,) * 12,
    )(lengths, outputs, d_norm, cot, gsum, vec)
    out, d_inputs, d_nu, d_theta, d_gamma, d_in, d_out, d_skip, d_gain, d_bias, d_glu, d_glu_bias = got
    return (
        out,
        d_inputs,
        d_nu.reshape(HALF),
        d_theta.reshape(HALF),
        d_gamma.reshape(HALF),
        d_in.reshape(HB, 2, HALF),
        d_out.reshape(2, HALF, HB),
        d_skip.reshape(W),
        d_gain.reshape(H),
        d_bias.reshape(H),
        d_glu.reshape(HB, 2, W),
        d_glu_bias,
    )


def solution(mesh):
    return jax.shard_map(
        on_device,
        mesh=mesh,
        in_specs=(
            P(ROWS, None, STATE),
            P(ROWS),
            P(ROWS),
            P(STATE),
            P(STATE),
            P(STATE),
            P(None, None, STATE),
            P(None, STATE, None),
            P(STATE),
            P(),
            P(),
            P(None, None, STATE),
            P(None, STATE),
            P(ROWS, None, STATE),
        ),
        out_specs=(
            P(ROWS, None, STATE),
            P(ROWS, None, STATE),
            P(STATE),
            P(STATE),
            P(STATE),
            P(ROWS, None, STATE),
            P(None, STATE, ROWS),
            P(STATE),
            P(),
            P(),
            P(ROWS, None, STATE),
            P(None, STATE),
        ),
        check_vma=False,
    )
```

```python
import functools
import math
from types import SimpleNamespace

import jax
import jax.numpy as jnp
from jax import lax
from jax.experimental import pallas as pl
from jax.experimental.pallas import tpu as pltpu
from jax.sharding import PartitionSpec as P

epsilon = 1e-05

F32 = jnp.float32
BF16 = jnp.bfloat16
MESH = pl.DeviceIdType.MESH
ROWS, STATE = "rows", "state"
SUB = 8
LANES = 128
HALF = LANES // 2
CHUNK = 64
SEG = 32
LEVELS = tuple(1 << i for i in range(SEG.bit_length() - 1))

OWN_X, OWN_WIN, OWN_WOUT, OWN_WGLU, OWN_C, OWN_OUT, OWN_DIN, OWN_SMALL = range(8)
PAR_S, X, C, OUT, DIN, SM, SN, W1 = range(8)
SIB, FAR, PEER, FAR_SIB = range(4)
GLU_FAR, GLU_SIB = 1, 4
G1 = W1 + 16
G2 = G1 + 4
AX_X, AX_Y, AX_Z = range(3)


def loop(count, body, unroll=1):
    def step(i, carry):
        body(i)
        return carry

    lax.fori_loop(0, count, step, 0, unroll=unroll)


def nn(a, b):
    return lax.dot_general(a, b, (((1,), (0,)), ((), ())), preferred_element_type=F32)


def nt(a, b):
    return lax.dot_general(a, b, (((1,), (1,)), ((), ())), preferred_element_type=F32)


def tn(a, b):
    return lax.dot_general(a, b, (((0,), (0,)), ((), ())), preferred_element_type=F32)


def cmul(a, b):
    return a[0] * b[0] - a[1] * b[1], a[0] * b[1] + a[1] * b[0]


def conj_mul(a, b):
    return a[0] * b[0] + a[1] * b[1], a[0] * b[1] - a[1] * b[0]


def swap_halves(u, v, low):
    return (
        jnp.where(low, u, pltpu.roll(v, HALF, 1)),
        jnp.where(low, pltpu.roll(u, HALF, 1), v),
    )


def fold(x):
    return jnp.sum(x.reshape(x.shape[0] // SUB, SUB, x.shape[1]), axis=0)


def block_kernel(dims, *refs):
    R, S, T, H, W, gdt = dims.R, dims.S, dims.T, dims.H, dims.W, dims.gdt
    NR, NG, R2, HB, L = R * S, S // 2, R // 2, H // R, T // SEG
    Q = 4 if R % 8 == 0 else 2
    G, NB = Q * S, R // Q
    BITS = T.bit_length()
    (inputs, cot, w_in, w_out, w_glu) = refs[:5]
    vectors = refs[5:14]
    (out_ref, din_ref, gsum, vec) = refs[14:18]
    total = 18 + len(dims.names)
    v = SimpleNamespace(**dict(zip(dims.names, refs[18:total])))
    parts = [
        SimpleNamespace(full=refs[total + 2 * i], r1=refs[total + 2 * i + 1], step=G1 + i, at=i * LANES, routes=[])
        for i in range(4)
    ]
    g_in, g_out, g_lin, g_gate = parts
    total += 8
    for i, (part, axes, first, lines) in enumerate(routes_of(R, H)):
        steps = len(axes)
        route = SimpleNamespace(part=parts[part], axes=axes, first=first, lines=lines, step=G2 + 3 * i)
        route.a = refs[total : total + steps + 1]
        route.r = refs[total + steps + 1 : total + 2 * steps + 1]
        route.last = refs[total + 2 * steps + 1]
        total += 2 * steps + 2
        parts[part].routes.append(route)

    me_r, me_s = lax.axis_index(ROWS), lax.axis_index(STATE)
    me = me_r * S + me_s

    def cols(i, width):
        return pl.ds(pl.multiple_of(i * width, LANES), width)

    def lanes(i):
        return slice(i * LANES, (i + 1) * LANES)

    def rows_of(i):
        return pl.ds(pl.multiple_of(i * CHUNK, CHUNK), CHUNK)

    def wait_bytes(ref, which, arrived):
        pltpu.make_async_copy(ref, ref, (v.received if arrived else v.sent).at[which]).wait()

    def send(src, dst, which, target):
        pltpu.make_async_remote_copy(
            src_ref=src,
            dst_ref=dst,
            send_sem=v.sent.at[which],
            recv_sem=v.received.at[which],
            device_id=target,
            device_id_type=MESH,
        ).start()

    def to_state(src_of, dst, which):
        for j in (2, 3, 1) if S == 4 else range(1, S):
            t = lax.rem(me_s + j, S)
            send(src_of(t), dst, which, {STATE: t})

    sib = me_s + 1 - 2 * lax.rem(me_s, 2)
    far = lax.rem(me_s + NG, S)
    sib_far = lax.rem(sib + NG, S)
    pair_r = me_r + 1 - 2 * lax.rem(me_r, 2)
    group_r = me_r - lax.rem(me_r, Q)
    piece = lax.rem(me_r, Q)
    mine_s = lax.rem(me_s, 2)
    mine_r = lax.rem(me_r, 2)

    def line_block(ref, s, p=None):
        if p is None:
            return ref.at[pl.ds(pl.multiple_of(s * LANES, LANES), LANES), :]
        size = LANES // Q
        return ref.at[pl.ds(pl.multiple_of(s * LANES + p * size, size), size), :]

    def glu_block(ref, s):
        return ref.at[:, :, cols(s, W)]

    def lin_block(ref, s):
        return ref.at[0, :, cols(s, W)]

    def gate_block(ref, s, h):
        return ref.at[1, pl.ds(h * (H // 2), H // 2), cols(s, W)]

    own = [
        (w_glu, v.glu_raw, OWN_WGLU),
        (w_in, line_block(v.win, me_s), OWN_WIN),
        (w_out, line_block(v.wout, me_s), OWN_WOUT),
        (inputs.at[me_s], v.xin.at[:, cols(me_s, W)], OWN_X),
        (cot.at[me_s], v.cin.at[:, cols(me_s, W)], OWN_C),
    ]
    small_in = (v.bucket, v.lengths, v.nu, v.theta, v.gamma, v.skip, v.glu_bias, v.gain, v.bias)
    own += [(a, b, OWN_SMALL + i) for i, (a, b) in enumerate(zip(vectors, small_in))]
    own = {which: pltpu.make_async_copy(a, b, v.here.at[which]) for a, b, which in own}

    barrier = pltpu.get_barrier_semaphore()
    number = piece * S + me_s
    is_gate = (number == 0) & (NB > 1)
    gated = 1 if NB > 1 else 0

    def signal(which, i, rows=None):
        pl.semaphore_signal(
            which,
            inc=1,
            device_id={ROWS: group_r + lax.div(i, S) if rows is None else rows, STATE: lax.rem(i, S)},
            device_id_type=MESH,
        )

    def greet(d, carry):
        i = lax.rem(number + d, G)

        @pl.when(i >= gated)
        def _():
            signal(barrier, i)

        return carry

    lax.fori_loop(1, G, greet, 0)
    for copy in own.values():
        copy.start()
    for i in range(len(vectors)):
        own[OWN_SMALL + i].wait()
    bucket_ref, lengths_ref, nu_ref, theta_ref, gamma_ref, skip_ref, glu_bias_ref, gain_ref, bias_ref = small_in

    par = v.par
    par[...] = jnp.zeros((2 * SUB, LANES), F32)
    par[0:1, 0:HALF] = nu_ref[...]
    par[0:1, HALF:LANES] = theta_ref[...]
    par[1:2, 0:HALF] = gamma_ref[...]
    par[2:3, :] = skip_ref[...]
    par[3:5, :] = glu_bias_ref[...]
    for i in range(S):
        par[SUB + i : SUB + i + 1, :] = jnp.full((1, LANES), bucket_ref[i], jnp.int32).astype(F32)
        par[SUB + S + i : SUB + S + i + 1, :] = jnp.full((1, LANES), lengths_ref[i], jnp.int32).astype(F32)
    v.par_s[me_s] = par[...]

    @pl.when(jnp.logical_not(is_gate))
    def _():
        pl.semaphore_wait(barrier, G - 1)

    if NB > 1:

        @pl.when(number == 1)
        def _():
            signal(v.block_in, jnp.int32(0))

        @pl.when(is_gate)
        def _():
            pl.semaphore_wait(v.block_in, 1)

            def next_gate(d, carry):
                signal(barrier, jnp.int32(0), rows=lax.rem(group_r + d * Q, R))
                return carry

            lax.fori_loop(1, NB, next_gate, 0)

    def pass_on():
        if NB > 1:

            @pl.when(is_gate)
            def _():
                pl.semaphore_wait(barrier, NB - 1)

                def tell(i, carry):
                    signal(v.all_in, i)
                    return carry

                lax.fori_loop(1, G, tell, 0)

    def everyone_in():
        if NB > 1:

            @pl.when(jnp.logical_not(is_gate))
            def _():
                pl.semaphore_wait(v.all_in, 1)

    to_state(lambda t: par, v.par_s.at[me_s], PAR_S)

    def w_send(w, own_block, own_piece):
        send(own_piece, w.block(w.ref, me_s, piece), w.step + FAR, {STATE: far})
        send(own_block, w.block(w.ref, me_s), w.step + SIB, {STATE: sib})

    def w_forward_far(w):
        here = w.block(w.ref, far, piece)
        wait_bytes(here, w.step + FAR, True)
        for j in range(1, Q):
            send(here, here, w.step + PEER, {ROWS: group_r + lax.rem(piece + j, Q)})

    def w_forward_all(w):
        wait_bytes(w.rest, w.step + PEER, True)
        send(w.block(w.ref, far), w.block(w.ref, far), w.step + FAR_SIB, {STATE: sib})

    def w_ready(w):
        wait_bytes(w.block(w.ref, sib), w.step + SIB, True)
        wait_bytes(w.block(w.ref, sib_far), w.step + FAR_SIB, True)

    def w_sent(w):
        wait_bytes(w.block(w.ref, sib), w.step + SIB, False)
        wait_bytes(w.block(w.ref, sib), w.step + FAR_SIB, False)
        wait_bytes(w.block(w.ref, sib, piece), w.step + FAR, False)
        wait_bytes(w.rest, w.step + PEER, False)

    others = pl.ds(0, LANES - LANES // Q)
    wt_in = SimpleNamespace(ref=v.win, block=line_block, step=W1, rest=v.win.at[others, :])
    wt_out = SimpleNamespace(ref=v.wout, block=line_block, step=W1 + 4, rest=v.wout.at[others, :])
    wt_glu = W1 + 8

    def piece_of(ref):
        size = LANES // Q
        return ref.at[pl.ds(pl.multiple_of(piece * size, size), size), :]

    w_send(wt_in, w_in, piece_of(w_in))
    to_state(lambda t: inputs.at[t], v.xin.at[:, cols(me_s, W)], X)
    w_send(wt_out, w_out, piece_of(w_out))
    own[OWN_WGLU].wait()

    def split_glu(i):
        here = rows_of(i)
        v.glu_wide[...] = v.glu_raw[pl.ds(pl.multiple_of(i * 2 * CHUNK, 2 * CHUNK), 2 * CHUNK), :].astype(F32)
        for k in range(2):
            v.wglu[k, here, cols(me_s, W)] = v.glu_wide[pl.ds(k, CHUNK, stride=2), :].astype(BF16)

    loop(H // CHUNK, split_glu)
    glu_own = glu_block(v.wglu, me_s)
    send(glu_own, glu_own, wt_glu + SIB, {STATE: sib})
    first_three = [lin_block(v.wglu, me_s), gate_block(v.wglu, me_s, 0)]
    for i, block in enumerate(first_three):
        send(block, block, wt_glu + GLU_FAR + i, {STATE: far})

    line = lax.broadcasted_iota(jnp.int32, (CHUNK, T), 0)
    place = lax.broadcasted_iota(jnp.int32, (CHUNK, T), 1)

    def orders(i):
        base = pl.multiple_of(i * CHUNK, CHUNK)
        at = line + base
        v.perm[pl.ds(base, CHUNK), :] = (
            place == lax.rem(at, SEG) * L + lax.div(at, SEG)
        ).astype(F32).astype(BF16)
        v.back[pl.ds(base, CHUNK), :] = (
            at == lax.rem(place, SEG) * L + lax.div(place, SEG)
        ).astype(F32).astype(BF16)

    loop(T // CHUNK, orders)

    w_forward_far(wt_in)

    low = lax.broadcasted_iota(jnp.int32, (SEG, LANES), 1) < HALF
    low1 = lax.broadcasted_iota(jnp.int32, (1, LANES), 1) < HALF
    low8 = lax.broadcasted_iota(jnp.int32, (SUB, LANES), 1) < HALF
    seg = lax.broadcasted_iota(jnp.int32, (SEG, LANES), 0)

    wait_bytes(v.par_s.at[pl.ds(0, S - 1)], PAR_S, True)
    par_s = v.par_s
    lam, gam, rate, angle = [], [], [], []
    for a in range(NG):
        nu, theta = swap_halves(par_s[2 * a, 0:1, :], par_s[2 * a + 1, 0:1, :], low1)
        rate.append(jnp.exp(nu))
        angle.append(jnp.exp(theta))
        magnitude = jnp.exp(-rate[a])
        lam.append((magnitude * jnp.cos(angle[a]), magnitude * jnp.sin(angle[a])))
        gam.append(jnp.exp(swap_halves(par_s[2 * a, 1:2, :], par_s[2 * a + 1, 1:2, :], low1)[0]))
    skip = jnp.concatenate([par_s[s, 2:3, :] for s in range(S)], axis=1)
    gain, bias = gain_ref[...], bias_ref[...]
    power = [[(jnp.broadcast_to(l[0], (SUB, LANES)), jnp.broadcast_to(l[1], (SUB, LANES))) for l in lam]]
    for _ in range(BITS - 1):
        power.append([cmul(p, p) for p in power[-1]])
    for b in range(BITS):
        for a in range(NG):
            for c in range(2):
                v.pows[b, a, c] = power[b][a][c]

    def raised(exponent):
        result = [(jnp.ones(exponent.shape, F32), jnp.zeros(exponent.shape, F32)) for _ in range(NG)]
        for b in range(BITS):
            hit = (lax.shift_right_logical(exponent, b) & 1) == 1
            for a in range(NG):
                re, im = cmul(result[a], (v.pows[b, a, 0, 0:1, :], v.pows[b, a, 1, 0:1, :]))
                result[a] = (jnp.where(hit, re, result[a][0]), jnp.where(hit, im, result[a][1]))
        return result

    my_bucket = par[pl.ds(SUB + me_s, 1), :]
    len1 = par[pl.ds(SUB + S + me_s, 1), :].astype(jnp.int32)
    my_len = jnp.broadcast_to(len1, (SEG, LANES))
    seg_pow = raised(jnp.clip(my_len - seg * L, 0, L))
    lead_pow = raised(jnp.minimum(my_len, seg * L))
    tail_pow = raised(jnp.maximum(my_len - (seg + 1) * L, 0))
    for a in range(NG):
        ahead = seg_pow[a]
        behind = seg_pow[a]
        for i, d in enumerate(LEVELS):
            for c in range(2):
                v.hs_f[i, a, c] = jnp.where(seg >= d, ahead[c], 0.0)
                v.hs_b[i, a, c] = jnp.where(seg < SEG - d, behind[c], 0.0)
            ahead = cmul(ahead, (pltpu.roll(ahead[0], d, 0), pltpu.roll(ahead[1], d, 0)))
            behind = cmul(behind, (pltpu.roll(behind[0], SEG - d, 0), pltpu.roll(behind[1], SEG - d, 0)))
        for c in range(2):
            v.lead_pow[a, c] = lead_pow[a][c]
            v.tail_pow[a, c] = tail_pow[a][c]

    def lines_of(p):
        return pl.ds(pl.multiple_of(p * SUB, SUB), SUB)

    FULL = 2 * NG + 1

    def carry_copy(way, source, t):
        return pltpu.make_async_remote_copy(
            src_ref=way.msg.at[pl.ds(0, FULL), :],
            dst_ref=way.chain.at[source, pl.ds(0, FULL), :],
            send_sem=way.sent.at[t],
            recv_sem=way.received.at[source],
            device_id={ROWS: lax.div(t, S), STATE: lax.rem(t, S)},
            device_id_type=MESH,
        )

    def exchange(way, values):
        for a in range(NG):
            for c in range(2):
                way.msg[pl.ds(c * NG + a, 1), :] = values[a][c]
        way.msg[2 * NG : FULL, :] = jnp.where(low1, my_bucket, par[pl.ds(SUB + S + me_s, 1), :])

        def one(i, carry):
            carry_copy(way, me, NR - 1 - i if way.forward else i).start()
            return carry

        lax.fori_loop(0, NR - 1 - me if way.forward else me, one, 0)

    def collect(way):
        def arrive(p, carry):
            carry_copy(way, p, me).wait_recv()
            return carry

        lax.fori_loop(*way.come, arrive, 0)

        def powers(i):
            for j in range(SUB):
                v.row_len[j : j + 1, :] = way.chain[i * SUB + j, 2 * NG : FULL, :]
            both = v.row_len[...]
            turned = pltpu.roll(both, HALF, 1)
            here = jnp.where(low8, both, turned)
            lens = jnp.where(low8, turned, both).astype(jnp.int32)
            p = lax.broadcasted_iota(jnp.int32, (SUB, LANES), 0) + i * SUB
            hit = (here == my_bucket) & (my_bucket > 0.5) & ((p < me) if way.forward else (p > me))
            factor = raised(lens)
            for a in range(NG):
                v.row_pow[a, lines_of(i), :] = jnp.where(hit, factor[a][0], 1.0)
                v.row_pow[NG + a, lines_of(i), :] = jnp.where(hit, factor[a][1], 0.0)
            v.row_hit[lines_of(i), :] = jnp.where(hit, 1.0, 0.0)

        loop(NR // SUB, powers)

        def fold_in(i, carry):
            p = i if way.forward else NR - 1 - i
            hit = v.row_hit[pl.ds(p, 1), :] > 0.5
            new = []
            for a in range(NG):
                factor = (v.row_pow[a, pl.ds(p, 1), :], v.row_pow[NG + a, pl.ds(p, 1), :])
                re, im = cmul(factor, carry[a]) if way.forward else conj_mul(factor, carry[a])
                add = (way.chain[p, a : a + 1, :], way.chain[p, NG + a : NG + a + 1, :])
                new.append((re + jnp.where(hit, add[0], 0.0), im + jnp.where(hit, add[1], 0.0)))
            return tuple(new)

        zero = jnp.zeros((1, LANES), F32)
        return lax.fori_loop(0, me if way.forward else NR - 1 - me, fold_in, tuple((zero, zero) for _ in range(NG)))

    def carries_sent(way):
        def one(t, carry):
            carry_copy(way, me, t).wait_send()
            return carry

        lax.fori_loop(*way.to, one, 0)

    ahead = SimpleNamespace(
        forward=True, msg=v.msg_f, chain=v.chain_f, sent=v.sent_f, received=v.received_f, to=(me + 1, NR), come=(0, me)
    )
    behind = SimpleNamespace(
        forward=False, msg=v.msg_b, chain=v.chain_b, sent=v.sent_b, received=v.received_b, to=(0, me), come=(me + 1, NR)
    )

    pos = lax.broadcasted_iota(jnp.int32, (CHUNK, LANES), 0)
    pos = lax.rem(pos, SEG) * L + lax.div(pos, SEG)

    def valid_of(i, width):
        ok = jnp.where(pos + i * (CHUNK // SEG) < len1, 1.0, 0.0)
        return jnp.concatenate([ok] * (width // LANES), axis=1) if width > LANES else ok

    w_forward_all(wt_in)
    pass_on()

    own[OWN_X].wait()
    wait_bytes(v.xin.at[:, pl.ds(0, (S - 1) * W)], X, True)
    v.x[...] = nn(v.perm[...], v.xin[...])

    def layer_norm(i):
        rows = rows_of(i)
        x = v.x[rows, :]
        centred = x - jnp.mean(x, -1, keepdims=True)
        inverse = lax.rsqrt(jnp.mean(centred * centred, -1, keepdims=True) + epsilon)
        normed = centred * inverse
        v.normed[rows, :] = normed
        v.inverse[rows, :] = jnp.broadcast_to(inverse, (CHUNK, LANES))
        v.mixed_low[rows, :] = (normed * gain + bias).astype(BF16)

    loop(T // CHUNK, layer_norm, unroll=2)
    w_forward_far(wt_out)
    own[OWN_WIN].wait()
    w_ready(wt_in)
    v.wide[...] = nt(v.mixed_low[...], v.win[...])

    lamb = [tuple(jnp.broadcast_to(c, (SEG, LANES)) for c in l) for l in lam]
    gamb = [jnp.broadcast_to(g, (SEG, LANES)) for g in gam]

    def load_c(ref, at):
        return [(ref[at, lanes(a)], ref[at, lanes(NG + a)]) for a in range(NG)]

    def store_c(ref, at, values):
        for a in range(NG):
            ref[at, lanes(a)] = values[a][0]
            ref[at, lanes(NG + a)] = values[a][1]

    def load_g(ref, at):
        return [swap_halves(ref[at, lanes(2 * a)], ref[at, lanes(2 * a + 1)], low) for a in range(NG)]

    def to_g(values):
        return [g for a in range(NG) for g in swap_halves(values[a][0], values[a][1], low)]

    def step_of(k):
        return pl.ds(pl.multiple_of(k * SEG, SEG), SEG)

    zeros = tuple((jnp.zeros((SEG, LANES), F32), jnp.zeros((SEG, LANES), F32)) for _ in range(NG))

    def advance(k, state, proj):
        ok = seg * L + k < my_len
        new = []
        for a in range(NG):
            re, im = cmul(lamb[a], state[a])
            re, im = re + gamb[a] * proj[a][0], im + gamb[a] * proj[a][1]
            new.append((jnp.where(ok, re, state[a][0]), jnp.where(ok, im, state[a][1])))
        return tuple(new)

    def fwd_first(k, state):
        proj = load_g(v.wide, step_of(k))
        store_c(v.proj, step_of(k), proj)
        return advance(k, state, proj)

    ends = lax.fori_loop(0, L, fwd_first, zeros, unroll=4)

    def across(values, table, forward):
        done = []
        for a in range(NG):
            x = values[a]
            for i, d in enumerate(LEVELS):
                shift = d if forward else SEG - d
                other = (pltpu.roll(x[0], shift, 0), pltpu.roll(x[1], shift, 0))
                factor = (table[i, a, 0], table[i, a, 1])
                add = cmul(factor, other) if forward else conj_mul(factor, other)
                x = (x[0] + add[0], x[1] + add[1])
            done.append(x)
        return done

    ends = across(ends, v.hs_f, True)
    everyone_in()
    exchange(ahead, [tuple(x[SEG - 1 : SEG, :] for x in ends[a]) for a in range(NG)])
    before = [
        tuple(jnp.where(seg > 0, pltpu.roll(x, 1, 0), 0.0) for x in ends[a]) for a in range(NG)
    ]
    block = gate_block(v.wglu, me_s, 1)
    send(block, block, wt_glu + GLU_FAR + 2, {STATE: far})
    to_state(lambda t: cot.at[t], v.cin.at[:, cols(me_s, W)], C)
    w_forward_all(wt_out)
    own[OWN_C].wait()
    far_blocks = [lin_block(v.wglu, far), gate_block(v.wglu, far, 0), gate_block(v.wglu, far, 1)]
    for i, block in enumerate(far_blocks):
        wait_bytes(block, wt_glu + GLU_FAR + i, True)
        send(block, block, wt_glu + GLU_SIB + i, {STATE: sib})
    starts = collect(ahead)
    state = []
    for a in range(NG):
        add = cmul((v.lead_pow[a, 0], v.lead_pow[a, 1]), starts[a])
        state.append((before[a][0] + add[0], before[a][1] + add[1]))
    store_c(v.state, pl.ds(0, SEG), state)

    def fwd_second(k, state):
        state = advance(k, state, load_c(v.proj, step_of(k)))
        store_c(v.state, step_of(k + 1), state)
        low_out = to_g([(re, -im) for re, im in state])
        for s in range(S):
            v.state_low[step_of(k), lanes(s)] = low_out[s].astype(BF16)
        return state

    lax.fori_loop(0, L, fwd_second, tuple(state), unroll=4)

    own[OWN_WOUT].wait()
    w_ready(wt_out)
    v.wide[...] = nn(v.state_low[...], v.wout[...])

    def gelu(i):
        rows = rows_of(i)
        mixed_in = v.normed[rows, :] * gain + bias
        mixed = v.wide[rows, :] + skip * mixed_in
        cdf = 0.5 * (1.0 + lax.erf(mixed * (1.0 / math.sqrt(2.0))))
        density = jnp.exp(-0.5 * mixed * mixed) * (1.0 / math.sqrt(2.0 * math.pi))
        v.act[rows, :] = (mixed * cdf).astype(BF16)
        v.dgelu[rows, :] = cdf + mixed * density

    loop(T // CHUNK, gelu, unroll=2)
    wait_bytes(glu_block(v.wglu, sib), wt_glu + SIB, True)
    for i, block in enumerate([lin_block(v.wglu, sib_far), gate_block(v.wglu, sib_far, 0), gate_block(v.wglu, sib_far, 1)]):
        wait_bytes(block, wt_glu + GLU_SIB + i, True)
    for k in range(2):
        v.pre[k] = nn(v.act[...], v.wglu[k])

    def glu(i):
        rows = rows_of(i)
        ok = valid_of(i, W)
        for s in range(S):
            here = slice(s * W, (s + 1) * W)
            linear = v.pre[0, rows, here] + par_s[s, 3:4, :]
            gate = v.pre[1, rows, here] + par_s[s, 4:5, :]
            share = jax.nn.sigmoid(gate)
            value = linear * share
            v.out_low[rows, here] = (ok * (v.x[rows, here] + value)).astype(BF16)
            v.pre[0, rows, here] = ok * share
            v.pre[1, rows, here] = ok * (value * (1.0 - share))

    loop(T // CHUNK, glu, unroll=2)

    def give_back(low_ref, nat, result, own_which):
        nat[...] = nn(v.back[...], low_ref[...]).astype(BF16)
        copy = pltpu.make_async_copy(nat.at[:, cols(me_s, W)], result.at[me_s], v.here.at[own_which])
        copy.start()
        return copy

    def give_to(nat, result, which, t):
        send(nat.at[:, cols(t, W)], result.at[me_s], which, {STATE: t})

    out_copy = give_back(v.out_low, v.out_nat, out_ref, OWN_OUT)
    give_to(v.out_nat, out_ref, OUT, far)
    wait_bytes(v.cin.at[:, pl.ds(0, (S - 1) * W)], C, True)
    v.wide[...] = nn(v.perm[...], v.cin[...])

    def glu_back(i):
        rows = rows_of(i)
        dout = v.wide[rows, :]
        for k in range(2):
            v.d_pre[k, rows, :] = (dout * v.pre[k, rows, :]).astype(BF16)

    loop(T // CHUNK, glu_back, unroll=2)

    R4 = R // 4 if R % 4 == 0 else R // 2
    sizes = {AX_X: NG, AX_Y: 2, AX_Z: 2 if R % 4 == 0 else 1, None: R4}

    def places(r, b):
        return {AX_X: b, AX_Y: lax.rem(r, 2), AX_Z: lax.rem(lax.div(r, 2), sizes[AX_Z]), None: lax.div(r, 2 * sizes[AX_Z])}

    mine = places(me_r, lax.div(me_s, 2))
    partner = {
        AX_X: {STATE: far},
        AX_Y: {ROWS: pair_r},
        AX_Z: {ROWS: me_r + 2 - 4 * mine[AX_Z]},
    }

    def slot(route, r, b):
        at, index = places(r, b), 0
        for axis in route.axes[1:] + route.others:
            index = index * sizes[axis] + at[axis]
        return at[route.axes[0]], index

    def owner(route, n):
        at = dict(mine)
        for axis in reversed(route.others):
            at[axis] = lax.rem(n, sizes[axis])
            n = lax.div(n, sizes[axis])
        return {ROWS: at[AX_Y] + 2 * (at[AX_Z] + sizes[AX_Z] * at[None]), STATE: 2 * at[AX_X] + mine_s}

    for part in parts:
        for route in part.routes:
            route.others = tuple(axis for axis in sizes if axis not in route.axes)
            route.number = 0
            for axis in route.others:
                route.number = route.number * sizes[axis] + mine[axis]

    def first_send(part):
        for b in range(NG):
            send(part.full.at[:, cols(2 * b + 1 - mine_s, LANES)], part.r1.at[b], part.step, {STATE: sib})

    def first_wait(part):
        wait_bytes(part.r1, part.step, True)

    def first_sum(route):
        part = route.part

        def one(r):
            rows = pl.ds(pl.multiple_of(r * HB + route.first, route.lines), route.lines)
            for b in range(NG):
                total = part.full[rows, cols(2 * b + mine_s, LANES)].astype(F32) + part.r1[b, rows, :].astype(F32)
                route.a[0][slot(route, r, b)] = total.astype(gdt)

        loop(R, one, unroll=2)
        pass_half(route, 0)

    def pass_half(route, i):
        axis = route.axes[i]
        send(route.a[i].at[1 - mine[axis]], route.r[i], route.step + i, partner[axis])

    def next_sum(route, i):
        wait_bytes(route.r[i], route.step + i, True)
        count, last = route.r[i].shape[0], i + 1 == len(route.axes)

        def one(n):
            total = route.a[i][mine[route.axes[i]], n].astype(F32) + route.r[i][n].astype(F32)
            to = n if last else (lax.div(n, count // 2), lax.rem(n, count // 2))
            route.a[i + 1][to] = total.astype(gdt)

        loop(count, one, unroll=2)
        if not last:
            pass_half(route, i + 1)
            return
        done = route.a[i + 1]
        route.last[route.number] = done[route.number]

        def give(d, carry):
            n = lax.rem(route.number + d, count)
            send(done.at[n], route.last.at[route.number], route.step + 2, owner(route, n))
            return carry

        lax.fori_loop(1, count, give, 0)

    def last_sum(route):
        count = route.last.shape[0]
        wait_bytes(route.last.at[pl.ds(0, count - 1)], route.step + 2, True)

        def one(n, total):
            return total + route.last[n].astype(F32)

        total = lax.fori_loop(0, count, one, jnp.zeros((route.lines, LANES), F32), unroll=2)
        gsum[route.first : route.first + route.lines, route.part.at : route.part.at + LANES] = total

    def all_sent(part):
        wait_bytes(part.r1, part.step, False)
        for route in part.routes:
            for i in range(len(route.axes)):
                wait_bytes(route.r[i], route.step + i, False)
            wait_bytes(route.last.at[pl.ds(0, route.last.shape[0] - 1)], route.step + 2, False)

    v.wide[...] = nt(v.d_pre[0], v.wglu[0]) + nt(v.d_pre[1], v.wglu[1])

    def gelu_back(i, total):
        rows = rows_of(i)
        d_mixed = v.wide[rows, :] * v.dgelu[rows, :]
        v.d_mixed[rows, :] = d_mixed
        v.d_rec[rows, :] = d_mixed.astype(BF16)
        return total + fold(d_mixed * (v.normed[rows, :] * gain + bias))

    d_skip = lax.fori_loop(0, T // CHUNK, gelu_back, jnp.zeros((SUB, H), F32), unroll=2)
    d_skip = jnp.sum(d_skip, axis=0, keepdims=True)
    v.wide[...] = nt(v.d_rec[...], v.wout[...])
    def retreat(k, source, carry):
        ok = seg * L + k < my_len
        adjoint, new = [], []
        for a in range(NG):
            re, im = source[a][0] + carry[a][0], source[a][1] + carry[a][1]
            adjoint.append((re, im))
            nre, nim = conj_mul(lamb[a], (re, im))
            new.append((jnp.where(ok, nre, re), jnp.where(ok, nim, im)))
        return ok, adjoint, tuple(new)

    def bwd_first(i, carry):
        k = L - 1 - i
        source = [(re, -im) for re, im in load_g(v.wide, step_of(k))]
        store_c(v.source, step_of(k), source)
        return retreat(k, source, carry)[2]

    heads = lax.fori_loop(0, L, bwd_first, zeros, unroll=4)
    heads = across(heads, v.hs_b, False)
    exchange(behind, [tuple(x[0:1, :] for x in heads[a]) for a in range(NG)])
    after = [
        tuple(jnp.where(seg < SEG - 1, pltpu.roll(x, SEG - 1, 0), 0.0) for x in heads[a])
        for a in range(NG)
    ]
    for k, part in ((0, g_lin), (1, g_gate)):
        part.full[...] = tn(v.act[...], v.d_pre[k]).astype(gdt)
        first_send(part)
    g_out.full[...] = tn(v.d_rec[...], v.state_low[...]).astype(gdt)
    first_send(g_out)
    first_wait(g_lin)
    first_sum(g_lin.routes[0])
    first_wait(g_gate)
    first_sum(g_gate.routes[0])
    first_wait(g_out)
    first_sum(g_out.routes[0])
    give_to(v.out_nat, out_ref, OUT, sib)
    give_to(v.out_nat, out_ref, OUT, sib_far)
    ones = jnp.ones((2 * SUB, T), BF16)
    d_bias = [nn(ones, v.d_pre[k])[0:1, :] for k in range(2)]
    omegas = collect(behind)
    carry = []
    for a in range(NG):
        add = conj_mul((v.tail_pow[a, 0], v.tail_pow[a, 1]), omegas[a])
        carry.append((after[a][0] + add[0], after[a][1] + add[1]))

    def bwd_second(i, item):
        k = L - 1 - i
        carry, sums = item
        ok, adjoint, carry = retreat(k, load_c(v.source, step_of(k)), carry)
        previous = load_c(v.state, step_of(k))
        proj = load_c(v.proj, step_of(k))
        new_sums, low_out = [], []
        for a in range(NG):
            re, im = (jnp.where(ok, x, 0.0) for x in adjoint[a])
            dre, dim = conj_mul(previous[a], (re, im))
            dg = re * proj[a][0] + im * proj[a][1]
            new_sums.append(tuple(x + fold(y) for x, y in zip(sums[a], (dre, dim, dg))))
            low_out.append((gamb[a] * re, gamb[a] * im))
        low_out = to_g(low_out)
        for s in range(S):
            v.d_proj[step_of(k), lanes(s)] = low_out[s].astype(BF16)
        return carry, tuple(new_sums)

    zero = jnp.zeros((SUB, LANES), F32)
    _, sums = lax.fori_loop(
        0, L, bwd_second, (tuple(carry), tuple((zero, zero, zero) for _ in range(NG))), unroll=2
    )

    g_in.full[...] = tn(v.mixed_low[...], v.d_proj[...]).astype(gdt)
    first_send(g_in)
    v.wide[...] = nn(v.d_proj[...], v.win[...])
    for part in (g_lin, g_gate, g_out):
        next_sum(part.routes[0], 0)


    def norm_back(i, totals):
        rows = rows_of(i)
        d_mixed_in = v.wide[rows, :] + skip * v.d_mixed[rows, :]
        normed = v.normed[rows, :]
        inverse = jnp.concatenate([v.inverse[rows, :]] * (H // LANES), axis=1)
        g = d_mixed_in * gain
        first = jnp.mean(g, -1, keepdims=True)
        second = jnp.mean(g * normed, -1, keepdims=True)
        v.din_low[rows, :] = (inverse * (g - first - normed * second)).astype(BF16)
        return totals[0] + fold(d_mixed_in * normed), totals[1] + fold(d_mixed_in)

    zero_h = jnp.zeros((SUB, H), F32)
    d_gain, d_nbias = lax.fori_loop(0, T // CHUNK, norm_back, (zero_h, zero_h), unroll=2)
    d_gain = jnp.sum(d_gain, axis=0, keepdims=True)
    d_nbias = jnp.sum(d_nbias, axis=0, keepdims=True)
    small = v.small
    small[...] = jnp.zeros((S, SUB, LANES), F32)
    for a in range(NG):
        sr, si, sg = (jnp.sum(x, axis=0, keepdims=True) for x in sums[a])
        d_nu = -rate[a] * (sr * lam[a][0] + si * lam[a][1])
        d_theta = angle[a] * (si * lam[a][0] - sr * lam[a][1])
        pair = swap_halves(d_nu, d_theta, low1)
        pair_g = swap_halves(gam[a] * sg, jnp.zeros_like(sg), low1)
        for u in range(2):
            small[2 * a + u, 0:1, :] = pair[u]
            small[2 * a + u, 1:2, :] = pair_g[u]
    for s in range(S):
        here = slice(s * W, (s + 1) * W)
        small[s, 2:3, :] = d_skip[:, here]
        small[s, 3:4, :] = d_bias[0][:, here]
        small[s, 4:5, :] = d_bias[1][:, here]
        small[s, 5:6, :] = d_gain[:, here]
        small[s, 6:7, :] = d_nbias[:, here]
    v.small_r[me_s] = small[...]
    to_state(lambda t: small, v.small_r.at[me_s], SM)
    first_wait(g_in)
    for route in g_in.routes:
        first_sum(route)
    for part in (g_lin, g_gate, g_out):
        if len(part.routes[0].axes) > 1:
            next_sum(part.routes[0], 1)

    din_copy = give_back(v.din_low, v.din_nat, din_ref, OWN_DIN)
    for t in (far, sib_far, sib):
        give_to(v.din_nat, din_ref, DIN, t)
    wait_bytes(v.small_r.at[pl.ds(0, S - 1)], SM, True)
    group = v.small_r[0]
    for s in range(1, S):
        group = group + v.small_r[s]
    small2 = v.small2
    v.group[...] = group
    small2[0:SUB, :] = v.group[me_s]
    for s in range(S):
        small2[SUB + s : SUB + s + 1, :] = group[s, 5:6, :]
        small2[SUB + S + s : SUB + S + s + 1, :] = group[s, 6:7, :]
    v.small2_r[me_r] = small2[...]

    def small_rows(d, carry):
        send(small2, v.small2_r.at[me_r], SN, {ROWS: lax.rem(me_r + d, R)})
        return carry

    lax.fori_loop(1, R, small_rows, 0)
    for route in g_in.routes:
        next_sum(route, 0)
    for part in (g_lin, g_gate, g_out):
        last_sum(part.routes[0])
    wait_bytes(v.small2_r.at[pl.ds(0, R - 1)], SN, True)

    def sum_rows(r, total):
        return total + v.small2_r[r]

    vec[...] = lax.fori_loop(0, R, sum_rows, jnp.zeros((2 * SUB, LANES), F32))
    for route in g_in.routes:
        last_sum(route)

    out_copy.wait()
    din_copy.wait()
    wait_bytes(out_ref.at[pl.ds(0, S - 1)], OUT, True)
    wait_bytes(din_ref.at[pl.ds(0, S - 1)], DIN, True)
    wait_bytes(out_ref.at[pl.ds(0, S - 1)], OUT, False)
    wait_bytes(din_ref.at[pl.ds(0, S - 1)], DIN, False)
    wait_bytes(v.par_s.at[pl.ds(0, S - 1)], PAR_S, False)
    wait_bytes(v.xin.at[:, pl.ds(0, (S - 1) * W)], X, False)
    for w in (wt_in, wt_out):
        w_sent(w)
    wait_bytes(glu_own, wt_glu + SIB, False)
    for i, block in enumerate(far_blocks):
        wait_bytes(block, wt_glu + GLU_FAR + i, False)
        wait_bytes(block, wt_glu + GLU_SIB + i, False)
    wait_bytes(v.cin.at[:, pl.ds(0, (S - 1) * W)], C, False)
    carries_sent(ahead)
    carries_sent(behind)
    wait_bytes(v.small_r.at[pl.ds(0, S - 1)], SM, False)
    wait_bytes(v.small2_r.at[pl.ds(0, R - 1)], SN, False)
    for part in parts:
        all_sent(part)


def routes_of(R, H):
    HB = H // R
    if HB % (4 * SUB) == 0:
        routes = [(0, (AX_Y,), 0, HB // 2), (0, (AX_X,), HB // 2, HB // 2)]
    else:
        routes = [(0, (AX_Y,), 0, HB)]
    if R % 4 == 0:
        return routes + [(1, (AX_X, AX_Y), 0, HB), (2, (AX_Y, AX_Z), 0, HB), (3, (AX_Z,), 0, HB)]
    return routes + [(1, (AX_X,), 0, HB), (2, (AX_Y,), 0, HB), (3, (AX_X,), 0, HB)]


def run_block(dims, *args):
    R, S, T, H, W = dims.R, dims.S, dims.T, dims.H, dims.W
    NR, NG, HB = R * S, S // 2, H // R
    CH, levels = S * LANES, len(LEVELS)
    gdt = BF16 if HB % (2 * SUB) == 0 else F32
    dims.gdt = gdt
    bits = T.bit_length()
    shapes = dict(
        xin=((T, H), BF16),
        cin=((T, H), BF16),
        win=((CH, H), BF16),
        wout=((CH, H), BF16),
        wglu=((2, H, H), BF16),
        glu_raw=((2 * H, W), BF16),
        glu_wide=((2 * CHUNK, W), F32),
        perm=((T, T), BF16),
        back=((T, T), BF16),
        nu=((1, HALF), F32),
        theta=((1, HALF), F32),
        gamma=((1, HALF), F32),
        skip=((1, W), F32),
        glu_bias=((2, W), F32),
        gain=((1, H), F32),
        bias=((1, H), F32),
        par=((2 * SUB, LANES), F32),
        par_s=((S, 2 * SUB, LANES), F32),
        pows=((bits, NG, 2, SUB, LANES), F32),
        hs_f=((levels, NG, 2, SEG, LANES), F32),
        hs_b=((levels, NG, 2, SEG, LANES), F32),
        lead_pow=((NG, 2, SEG, LANES), F32),
        tail_pow=((NG, 2, SEG, LANES), F32),
        row_pow=((2 * NG, NR, LANES), F32),
        row_hit=((NR, LANES), F32),
        msg_f=((SUB, LANES), F32),
        msg_b=((SUB, LANES), F32),
        row_len=((SUB, LANES), F32),
        chain_f=((NR, SUB, LANES), F32),
        chain_b=((NR, SUB, LANES), F32),
        x=((T, H), F32),
        normed=((T, H), F32),
        inverse=((T, LANES), F32),
        mixed_low=((T, H), BF16),
        wide=((T, max(H, CH)), F32),
        proj=((T, CH), F32),
        state=((T + SEG, CH), F32),
        state_low=((T, CH), BF16),
        act=((T, H), BF16),
        dgelu=((T, H), F32),
        pre=((2, T, H), F32),
        out_low=((T, H), BF16),
        out_nat=((T, H), BF16),
        d_pre=((2, T, H), BF16),
        d_mixed=((T, H), F32),
        d_rec=((T, H), BF16),
        source=((T, CH), F32),
        d_proj=((T, CH), BF16),
        din_low=((T, H), BF16),
        din_nat=((T, H), BF16),
        small=((S, SUB, LANES), F32),
        small_r=((S, S, SUB, LANES), F32),
        group=((S, SUB, LANES), F32),
        small2=((2 * SUB, LANES), F32),
        small2_r=((R, 2 * SUB, LANES), F32),
    )
    scalars = dict(bucket=(S,), lengths=(S,))
    flags = dict(block_in=1, all_in=1)
    copies = dict(here=OWN_SMALL + 9, sent=G2 + 15, received=G2 + 15, sent_f=NR, received_f=NR, sent_b=NR, received_b=NR)
    dims.names = [*shapes, *scalars, *flags, *copies]
    parts = []
    for _ in range(4):
        parts += [(H, CH), (NG, H, LANES)]
    routes = routes_of(R, H)
    for _, axes, _, lines in routes:
        left = [2 * R >> (i + 1) for i in range(len(axes))]
        parts += [(2, n, lines, LANES) for n in left] + [(left[-1], lines, LANES)]
        parts += [(n, lines, LANES) for n in left] + [(left[-1], lines, LANES)]
    scratch = [pltpu.VMEM(shape, dtype) for shape, dtype in shapes.values()]
    scratch += [pltpu.SMEM(shape, jnp.int32) for shape in scalars.values()]
    scratch += [pltpu.SemaphoreType.REGULAR for _ in flags]
    scratch += [pltpu.SemaphoreType.DMA((n,)) for n in copies.values()]
    scratch += [pltpu.VMEM(shape, gdt) for shape in parts]
    any_spec = pl.BlockSpec(memory_space=pl.ANY)
    vmem = pl.BlockSpec(memory_space=pltpu.VMEM)
    macs = T * H * (2 * CH + 2 * H) * 3 + 4 * T * T * H
    return pl.pallas_call(
        functools.partial(block_kernel, dims),
        out_shape=(
            jax.ShapeDtypeStruct((S, T, W), BF16),
            jax.ShapeDtypeStruct((S, T, W), BF16),
            jax.ShapeDtypeStruct((HB, 4 * LANES), F32),
            jax.ShapeDtypeStruct((2 * SUB, LANES), F32),
        ),
        in_specs=[any_spec] * 14,
        out_specs=(any_spec, any_spec, vmem, vmem),
        scratch_shapes=scratch,
        compiler_params=pltpu.CompilerParams(
            collective_id=0, has_side_effects=True, vmem_limit_bytes=56 * 2**20
        ),
        cost_estimate=pl.CostEstimate(flops=2 * macs, bytes_accessed=8 * 2**20, transcendentals=4 * T * H),
    )(*args)


def on_device(
    inputs,
    bucket,
    lengths,
    nu_log,
    theta_log,
    gamma_log,
    in_proj,
    out_proj,
    skip,
    norm_gain,
    norm_bias,
    glu_weight,
    glu_bias,
    output_cotangent,
):
    row_count, seq, part = inputs.shape
    width = norm_gain.shape[0]
    chans = nu_log.shape[0]
    R, S = lax.axis_size(ROWS), lax.axis_size(STATE)
    dims = SimpleNamespace(R=R, S=S, T=seq, H=width, W=part)
    assert row_count == S and 2 * chans == LANES and part == LANES and S % 2 == 0 and R % 2 == 0

    outputs, d_norm, gsum, vec = run_block(
        dims,
        inputs,
        output_cotangent,
        in_proj.transpose(1, 2, 0).reshape(2 * chans, width),
        out_proj.reshape(2 * chans, width),
        glu_weight.reshape(2 * width, part),
        bucket,
        lengths,
        nu_log[None],
        theta_log[None],
        gamma_log[None],
        skip[None],
        glu_bias,
        norm_gain[None],
        norm_bias[None],
    )
    return finish(dims, lengths, outputs, d_norm, output_cotangent, gsum, vec)


def finish_kernel(dims, *refs):
    S, T, HB = dims.S, dims.T, dims.H // dims.R
    (lengths, out_in, d_norm, cot, gsum, vec) = refs[:6]
    (out, d_inputs, d_nu, d_theta, d_gamma, d_in, d_out, d_skip, d_gain, d_bias, d_glu, d_glu_bias) = refs[6:]
    out[...] = out_in[...]
    for row in range(S):
        for first in range(0, T, CHUNK):
            lines = slice(first, first + CHUNK)
            place = lax.broadcasted_iota(jnp.int32, (CHUNK, LANES), 0) + first
            direct = jnp.where(place < lengths[row], cot[row, lines, :].astype(F32), 0.0)
            d_inputs[row, lines, :] = d_norm[row, lines, :].astype(F32) + direct
    d_nu[...] = vec[0:1, 0:HALF]
    d_theta[...] = pltpu.roll(vec[0:1, :], HALF, 1)[:, 0:HALF]
    d_gamma[...] = vec[1:2, 0:HALF]
    d_skip[...] = vec[2:3, :]
    d_glu_bias[...] = vec[3:5, :]
    for s in range(S):
        here = slice(s * LANES, (s + 1) * LANES)
        d_gain[:, here] = vec[SUB + s : SUB + s + 1, :]
        d_bias[:, here] = vec[SUB + S + s : SUB + S + s + 1, :]
    both = gsum[:, 0:LANES]
    d_in[pl.ds(0, HB, stride=2), :] = both[:, 0:HALF]
    d_in[pl.ds(1, HB, stride=2), :] = pltpu.roll(both, HALF, 1)[:, 0:HALF]
    d_out[...] = gsum[:, LANES : 2 * LANES].T
    d_glu[pl.ds(0, HB, stride=2), :] = gsum[:, 2 * LANES : 3 * LANES]
    d_glu[pl.ds(1, HB, stride=2), :] = gsum[:, 3 * LANES : 4 * LANES]


def finish(dims, lengths, outputs, d_norm, cot, gsum, vec):
    R, S, T, H, W = dims.R, dims.S, dims.T, dims.H, dims.W
    HB = H // R
    vmem = pl.BlockSpec(memory_space=pltpu.VMEM)
    small = [(1, HALF)] * 3 + [(2 * HB, HALF), (LANES, HB), (1, W), (1, H), (1, H), (2 * HB, W), (2, W)]
    got = pl.pallas_call(
        functools.partial(finish_kernel, dims),
        out_shape=(
            jax.ShapeDtypeStruct((S, T, W), BF16),
            jax.ShapeDtypeStruct((S, T, W), F32),
            *(jax.ShapeDtypeStruct(shape, F32) for shape in small),
        ),
        in_specs=[pl.BlockSpec(memory_space=pltpu.SMEM)] + [vmem] * 5,
        out_specs=(vmem,) * 12,
    )(lengths, outputs, d_norm, cot, gsum, vec)
    out, d_inputs, d_nu, d_theta, d_gamma, d_in, d_out, d_skip, d_gain, d_bias, d_glu, d_glu_bias = got
    return (
        out,
        d_inputs,
        d_nu.reshape(HALF),
        d_theta.reshape(HALF),
        d_gamma.reshape(HALF),
        d_in.reshape(HB, 2, HALF),
        d_out.reshape(2, HALF, HB),
        d_skip.reshape(W),
        d_gain.reshape(H),
        d_bias.reshape(H),
        d_glu.reshape(HB, 2, W),
        d_glu_bias,
    )


def solution(mesh):
    return jax.shard_map(
        on_device,
        mesh=mesh,
        in_specs=(
            P(ROWS, None, STATE),
            P(ROWS),
            P(ROWS),
            P(STATE),
            P(STATE),
            P(STATE),
            P(None, None, STATE),
            P(None, STATE, None),
            P(STATE),
            P(),
            P(),
            P(None, None, STATE),
            P(None, STATE),
            P(ROWS, None, STATE),
        ),
        out_specs=(
            P(ROWS, None, STATE),
            P(ROWS, None, STATE),
            P(STATE),
            P(STATE),
            P(STATE),
            P(ROWS, None, STATE),
            P(None, STATE, ROWS),
            P(STATE),
            P(),
            P(),
            P(ROWS, None, STATE),
            P(None, STATE),
        ),
        check_vma=False,
    )
```

```python
import functools
import math
from types import SimpleNamespace

import jax
import jax.numpy as jnp
from jax import lax
from jax.experimental import pallas as pl
from jax.experimental.pallas import tpu as pltpu
from jax.sharding import PartitionSpec as P

epsilon = 1e-05

F32 = jnp.float32
BF16 = jnp.bfloat16
MESH = pl.DeviceIdType.MESH
ROWS, STATE = "rows", "state"
SUB = 8
LANES = 128
HALF = LANES // 2
CHUNK = 64
SEG = 32
LEVELS = tuple(1 << i for i in range(SEG.bit_length() - 1))

OWN_X, OWN_WIN, OWN_WOUT, OWN_WGLU, OWN_C, OWN_OUT, OWN_DIN, OWN_SMALL = range(8)
PAR_S, X, C, OUT, DIN, SM, SN, W1 = range(8)
SIB, FAR, PEER, FAR_SIB = range(4)
GLU_FAR, GLU_SIB = 1, 4
G1 = W1 + 16
G2 = G1 + 4
AX_X, AX_Y, AX_Z = range(3)


def loop(count, body, unroll=1):
    def step(i, carry):
        body(i)
        return carry

    lax.fori_loop(0, count, step, 0, unroll=unroll)


def nn(a, b):
    return lax.dot_general(a, b, (((1,), (0,)), ((), ())), preferred_element_type=F32)


def nt(a, b):
    return lax.dot_general(a, b, (((1,), (1,)), ((), ())), preferred_element_type=F32)


def tn(a, b):
    return lax.dot_general(a, b, (((0,), (0,)), ((), ())), preferred_element_type=F32)


def cmul(a, b):
    return a[0] * b[0] - a[1] * b[1], a[0] * b[1] + a[1] * b[0]


def conj_mul(a, b):
    return a[0] * b[0] + a[1] * b[1], a[0] * b[1] - a[1] * b[0]


def swap_halves(u, v, low):
    return (
        jnp.where(low, u, pltpu.roll(v, HALF, 1)),
        jnp.where(low, pltpu.roll(u, HALF, 1), v),
    )


def fold(x):
    return jnp.sum(x.reshape(x.shape[0] // SUB, SUB, x.shape[1]), axis=0)


def block_kernel(dims, *refs):
    R, S, T, H, W, gdt = dims.R, dims.S, dims.T, dims.H, dims.W, dims.gdt
    NR, NG, R2, HB, L = R * S, S // 2, R // 2, H // R, T // SEG
    Q = 4 if R % 8 == 0 else 2
    G, NB = Q * S, R // Q
    BITS = T.bit_length()
    (inputs, cot, w_in, w_out, w_glu) = refs[:5]
    vectors = refs[5:14]
    (out_ref, din_ref, gsum, vec) = refs[14:18]
    total = 18 + len(dims.names)
    v = SimpleNamespace(**dict(zip(dims.names, refs[18:total])))
    parts = [
        SimpleNamespace(full=refs[total + 2 * i], r1=refs[total + 2 * i + 1], step=G1 + i, at=i * LANES, routes=[])
        for i in range(4)
    ]
    g_in, g_out, g_lin, g_gate = parts
    total += 8
    for i, (part, axes, first, lines) in enumerate(routes_of(R, H)):
        steps = len(axes)
        route = SimpleNamespace(part=parts[part], axes=axes, first=first, lines=lines, step=G2 + 4 * i)
        route.a = refs[total : total + steps + 1]
        route.r = refs[total + steps + 1 : total + 2 * steps + 1]
        route.last = refs[total + 2 * steps + 1]
        total += 2 * steps + 2
        parts[part].routes.append(route)

    me_r, me_s = lax.axis_index(ROWS), lax.axis_index(STATE)
    me = me_r * S + me_s

    def cols(i, width):
        return pl.ds(pl.multiple_of(i * width, LANES), width)

    def lanes(i):
        return slice(i * LANES, (i + 1) * LANES)

    def rows_of(i):
        return pl.ds(pl.multiple_of(i * CHUNK, CHUNK), CHUNK)

    def wait_bytes(ref, which, arrived):
        pltpu.make_async_copy(ref, ref, (v.received if arrived else v.sent).at[which]).wait()

    def send(src, dst, which, target):
        pltpu.make_async_remote_copy(
            src_ref=src,
            dst_ref=dst,
            send_sem=v.sent.at[which],
            recv_sem=v.received.at[which],
            device_id=target,
            device_id_type=MESH,
        ).start()

    def to_state(src_of, dst, which):
        for j in (2, 3, 1) if S == 4 else range(1, S):
            t = lax.rem(me_s + j, S)
            send(src_of(t), dst, which, {STATE: t})

    sib = me_s + 1 - 2 * lax.rem(me_s, 2)
    far = lax.rem(me_s + NG, S)
    sib_far = lax.rem(sib + NG, S)
    pair_r = me_r + 1 - 2 * lax.rem(me_r, 2)
    group_r = me_r - lax.rem(me_r, Q)
    piece = lax.rem(me_r, Q)
    mine_s = lax.rem(me_s, 2)
    mine_r = lax.rem(me_r, 2)

    def line_block(ref, s, p=None):
        if p is None:
            return ref.at[pl.ds(pl.multiple_of(s * LANES, LANES), LANES), :]
        size = LANES // Q
        return ref.at[pl.ds(pl.multiple_of(s * LANES + p * size, size), size), :]

    def glu_block(ref, s):
        return ref.at[:, :, cols(s, W)]

    def lin_block(ref, s):
        return ref.at[0, :, cols(s, W)]

    def gate_block(ref, s, h):
        return ref.at[1, pl.ds(h * (H // 2), H // 2), cols(s, W)]

    own = [
        (w_glu, v.glu_raw, OWN_WGLU),
        (w_in, line_block(v.win, me_s), OWN_WIN),
        (w_out, line_block(v.wout, me_s), OWN_WOUT),
        (inputs.at[me_s], v.xin.at[:, cols(me_s, W)], OWN_X),
        (cot.at[me_s], v.cin.at[:, cols(me_s, W)], OWN_C),
    ]
    small_in = (v.bucket, v.lengths, v.nu, v.theta, v.gamma, v.skip, v.glu_bias, v.gain, v.bias)
    own += [(a, b, OWN_SMALL + i) for i, (a, b) in enumerate(zip(vectors, small_in))]
    own = {which: pltpu.make_async_copy(a, b, v.here.at[which]) for a, b, which in own}

    barrier = pltpu.get_barrier_semaphore()
    number = piece * S + me_s
    is_gate = (number == 0) & (NB > 1)
    gated = 1 if NB > 1 else 0

    def signal(which, i, rows=None):
        pl.semaphore_signal(
            which,
            inc=1,
            device_id={ROWS: group_r + lax.div(i, S) if rows is None else rows, STATE: lax.rem(i, S)},
            device_id_type=MESH,
        )

    for p in range(Q - 1, -1, -1):
        for d in (2, 3, 1, 0) if S == 4 else range(S):
            if (p, d) != (0, 0):
                i = lax.rem(piece + p, Q) * S + lax.rem(me_s + d, S)
                pl.when(i >= gated)(functools.partial(signal, barrier, i))
    for copy in own.values():
        copy.start()
    for i in range(len(vectors)):
        own[OWN_SMALL + i].wait()
    bucket_ref, lengths_ref, nu_ref, theta_ref, gamma_ref, skip_ref, glu_bias_ref, gain_ref, bias_ref = small_in

    par = v.par
    par[...] = jnp.zeros((2 * SUB, LANES), F32)
    par[0:1, 0:HALF] = nu_ref[...]
    par[0:1, HALF:LANES] = theta_ref[...]
    par[1:2, 0:HALF] = gamma_ref[...]
    par[2:3, :] = skip_ref[...]
    par[3:5, :] = glu_bias_ref[...]
    for i in range(S):
        par[SUB + i : SUB + i + 1, :] = jnp.full((1, LANES), bucket_ref[i], jnp.int32).astype(F32)
        par[SUB + S + i : SUB + S + i + 1, :] = jnp.full((1, LANES), lengths_ref[i], jnp.int32).astype(F32)
    v.par_s[me_s] = par[...]

    @pl.when(jnp.logical_not(is_gate))
    def _():
        pl.semaphore_wait(barrier, G - 1)

    if NB > 1:

        @pl.when(number == 1)
        def _():
            signal(v.block_in, jnp.int32(0))

        @pl.when(is_gate)
        def _():
            pl.semaphore_wait(v.block_in, 1)

            def next_gate(d, carry):
                signal(barrier, jnp.int32(0), rows=lax.rem(group_r + d * Q, R))
                return carry

            lax.fori_loop(1, NB, next_gate, 0)

    def pass_on():
        if NB > 1:

            @pl.when(is_gate)
            def _():
                pl.semaphore_wait(barrier, NB - 1)

                def tell(i, carry):
                    signal(v.all_in, i)
                    return carry

                lax.fori_loop(1, G, tell, 0)

    def everyone_in():
        if NB > 1:

            @pl.when(jnp.logical_not(is_gate))
            def _():
                pl.semaphore_wait(v.all_in, 1)

    to_state(lambda t: par, v.par_s.at[me_s], PAR_S)

    def w_send(w, own_block, own_piece):
        send(own_piece, w.block(w.ref, me_s, piece), w.step + FAR, {STATE: far})
        send(own_block, w.block(w.ref, me_s), w.step + SIB, {STATE: sib})

    def w_forward_far(w):
        here = w.block(w.ref, far, piece)
        wait_bytes(here, w.step + FAR, True)
        for j in range(1, Q):
            send(here, here, w.step + PEER, {ROWS: group_r + lax.rem(piece + j, Q)})

    def w_forward_all(w):
        wait_bytes(w.rest, w.step + PEER, True)
        send(w.block(w.ref, far), w.block(w.ref, far), w.step + FAR_SIB, {STATE: sib})

    def w_ready(w):
        wait_bytes(w.block(w.ref, sib), w.step + SIB, True)
        wait_bytes(w.block(w.ref, sib_far), w.step + FAR_SIB, True)

    def w_sent(w):
        wait_bytes(w.block(w.ref, sib), w.step + SIB, False)
        wait_bytes(w.block(w.ref, sib), w.step + FAR_SIB, False)
        wait_bytes(w.block(w.ref, sib, piece), w.step + FAR, False)
        wait_bytes(w.rest, w.step + PEER, False)

    others = pl.ds(0, LANES - LANES // Q)
    wt_in = SimpleNamespace(ref=v.win, block=line_block, step=W1, rest=v.win.at[others, :])
    wt_out = SimpleNamespace(ref=v.wout, block=line_block, step=W1 + 4, rest=v.wout.at[others, :])
    wt_glu = W1 + 8

    def piece_of(ref):
        size = LANES // Q
        return ref.at[pl.ds(pl.multiple_of(piece * size, size), size), :]

    w_send(wt_in, w_in, piece_of(w_in))
    to_state(lambda t: inputs.at[t], v.xin.at[:, cols(me_s, W)], X)
    w_send(wt_out, w_out, piece_of(w_out))
    own[OWN_WGLU].wait()

    def split_glu(i):
        here = rows_of(i)
        v.glu_wide[...] = v.glu_raw[pl.ds(pl.multiple_of(i * 2 * CHUNK, 2 * CHUNK), 2 * CHUNK), :].astype(F32)
        for k in range(2):
            v.wglu[k, here, cols(me_s, W)] = v.glu_wide[pl.ds(k, CHUNK, stride=2), :].astype(BF16)

    loop(H // CHUNK, split_glu)
    glu_own = glu_block(v.wglu, me_s)
    send(glu_own, glu_own, wt_glu + SIB, {STATE: sib})
    first_three = [lin_block(v.wglu, me_s), gate_block(v.wglu, me_s, 0)]
    for i, block in enumerate(first_three):
        send(block, block, wt_glu + GLU_FAR + i, {STATE: far})

    line = lax.broadcasted_iota(jnp.int32, (CHUNK, T), 0)
    place = lax.broadcasted_iota(jnp.int32, (CHUNK, T), 1)

    def orders(i):
        base = pl.multiple_of(i * CHUNK, CHUNK)
        at = line + base
        v.perm[pl.ds(base, CHUNK), :] = (
            place == lax.rem(at, SEG) * L + lax.div(at, SEG)
        ).astype(F32).astype(BF16)
        v.back[pl.ds(base, CHUNK), :] = (
            at == lax.rem(place, SEG) * L + lax.div(place, SEG)
        ).astype(F32).astype(BF16)
        v.eye[pl.ds(base, CHUNK), :] = (place == at).astype(F32).astype(BF16)

    loop(T // CHUNK, orders)

    w_forward_far(wt_in)

    low = lax.broadcasted_iota(jnp.int32, (SEG, LANES), 1) < HALF
    low1 = lax.broadcasted_iota(jnp.int32, (1, LANES), 1) < HALF
    seg = lax.broadcasted_iota(jnp.int32, (SEG, LANES), 0)

    wait_bytes(v.par_s.at[pl.ds(0, S - 1)], PAR_S, True)
    par_s = v.par_s
    lam, gam, rate, angle = [], [], [], []
    for a in range(NG):
        nu, theta = swap_halves(par_s[2 * a, 0:1, :], par_s[2 * a + 1, 0:1, :], low1)
        rate.append(jnp.exp(nu))
        angle.append(jnp.exp(theta))
        magnitude = jnp.exp(-rate[a])
        lam.append((magnitude * jnp.cos(angle[a]), magnitude * jnp.sin(angle[a])))
        gam.append(jnp.exp(swap_halves(par_s[2 * a, 1:2, :], par_s[2 * a + 1, 1:2, :], low1)[0]))
    skip = jnp.concatenate([par_s[s, 2:3, :] for s in range(S)], axis=1)
    gain, bias = gain_ref[...], bias_ref[...]
    power = [[(jnp.broadcast_to(l[0], (SUB, LANES)), jnp.broadcast_to(l[1], (SUB, LANES))) for l in lam]]
    for _ in range(BITS - 1):
        power.append([cmul(p, p) for p in power[-1]])
    for b in range(BITS):
        for a in range(NG):
            for c in range(2):
                v.pows[b, a, c] = power[b][a][c]

    def raised(exponent):
        result = [(jnp.ones(exponent.shape, F32), jnp.zeros(exponent.shape, F32)) for _ in range(NG)]
        for b in range(BITS):
            hit = (lax.shift_right_logical(exponent, b) & 1) == 1
            for a in range(NG):
                re, im = cmul(result[a], (v.pows[b, a, 0, 0:1, :], v.pows[b, a, 1, 0:1, :]))
                result[a] = (jnp.where(hit, re, result[a][0]), jnp.where(hit, im, result[a][1]))
        return result

    my_bucket = par[pl.ds(SUB + me_s, 1), :]
    len1 = par[pl.ds(SUB + S + me_s, 1), :].astype(jnp.int32)
    my_len = jnp.broadcast_to(len1, (SEG, LANES))
    seg_pow = raised(jnp.clip(my_len - seg * L, 0, L))
    lead_pow = raised(jnp.minimum(my_len, seg * L))
    tail_pow = raised(jnp.maximum(my_len - (seg + 1) * L, 0))
    for a in range(NG):
        ahead = seg_pow[a]
        behind = seg_pow[a]
        for i, d in enumerate(LEVELS):
            for c in range(2):
                v.hs_f[i, a, c] = jnp.where(seg >= d, ahead[c], 0.0)
                v.hs_b[i, a, c] = jnp.where(seg < SEG - d, behind[c], 0.0)
            ahead = cmul(ahead, (pltpu.roll(ahead[0], d, 0), pltpu.roll(ahead[1], d, 0)))
            behind = cmul(behind, (pltpu.roll(behind[0], SEG - d, 0), pltpu.roll(behind[1], SEG - d, 0)))
        for c in range(2):
            v.lead_pow[a, c] = lead_pow[a][c]
            v.tail_pow[a, c] = tail_pow[a][c]

    def lines_of(p):
        return pl.ds(pl.multiple_of(p * SUB, SUB), SUB)

    FULL = 2 * NG + 1

    def carry_copy(way, source, t):
        return pltpu.make_async_remote_copy(
            src_ref=way.msg.at[pl.ds(0, FULL), :],
            dst_ref=way.chain.at[source, pl.ds(0, FULL), :],
            send_sem=way.sent.at[t],
            recv_sem=way.received.at[source],
            device_id={ROWS: lax.div(t, S), STATE: lax.rem(t, S)},
            device_id_type=MESH,
        )

    def exchange(way, values):
        for a in range(NG):
            for c in range(2):
                way.msg[pl.ds(c * NG + a, 1), :] = values[a][c]
        way.msg[2 * NG : FULL, :] = jnp.where(low1, my_bucket, par[pl.ds(SUB + S + me_s, 1), :])

        def one(i, carry):
            carry_copy(way, me, NR - 1 - i if way.forward else i).start()
            return carry

        lax.fori_loop(0, NR - 1 - me if way.forward else me, one, 0)

    group = min(NR, 4 * SUB)
    low_g = lax.broadcasted_iota(jnp.int32, (group, LANES), 1) < HALF

    def collect(way):
        def arrive(p, carry):
            carry_copy(way, p, me).wait_recv()
            return carry

        lax.fori_loop(*way.come, arrive, 0)

        def powers(i):
            for j in range(group):
                v.row_len[j : j + 1, :] = way.chain[i * group + j, 2 * NG : FULL, :]
            both = v.row_len[0:group, :]
            turned = pltpu.roll(both, HALF, 1)
            here = jnp.where(low_g, both, turned)
            lens = jnp.where(low_g, turned, both).astype(jnp.int32)
            p = lax.broadcasted_iota(jnp.int32, (group, LANES), 0) + i * group
            hit = (here == my_bucket) & (my_bucket > 0.5) & ((p < me) if way.forward else (p > me))
            factor = raised(lens)
            at = pl.ds(pl.multiple_of(i * group, SUB), group)
            for a in range(NG):
                v.row_pow[a, at, :] = jnp.where(hit, factor[a][0], 1.0)
                v.row_pow[NG + a, at, :] = jnp.where(hit, factor[a][1], 0.0)
            v.row_hit[at, :] = jnp.where(hit, 1.0, 0.0)

        loop(NR // group, powers)

        run = NR // 4

        def fold_in(i, carry):
            after = []
            for q in range(4):
                p = q * run + (i if way.forward else run - 1 - i)
                hit = v.row_hit[pl.ds(p, 1), :] > 0.5
                new = []
                for a in range(NG):
                    factor = (v.row_pow[a, pl.ds(p, 1), :], v.row_pow[NG + a, pl.ds(p, 1), :])
                    total, product = carry[q][a]
                    re, im = cmul(factor, total) if way.forward else conj_mul(factor, total)
                    add = (way.chain[p, a : a + 1, :], way.chain[p, NG + a : NG + a + 1, :])
                    total = (re + jnp.where(hit, add[0], 0.0), im + jnp.where(hit, add[1], 0.0))
                    new.append((total, cmul(factor, product)))
                after.append(tuple(new))
            return tuple(after)

        zero, one = jnp.zeros((1, LANES), F32), jnp.ones((1, LANES), F32)
        first = tuple(tuple(((zero, zero), (one, zero)) for _ in range(NG)) for _ in range(4))
        runs = lax.fori_loop(0, run, fold_in, first, unroll=2)
        result = []
        for a in range(NG):
            total = (zero, zero)
            for q in range(4) if way.forward else range(3, -1, -1):
                moved = cmul(runs[q][a][1], total) if way.forward else conj_mul(runs[q][a][1], total)
                total = (moved[0] + runs[q][a][0][0], moved[1] + runs[q][a][0][1])
            result.append(total)
        return result

    def carries_sent(way):
        def one(t, carry):
            carry_copy(way, me, t).wait_send()
            return carry

        lax.fori_loop(*way.to, one, 0)

    ahead = SimpleNamespace(
        forward=True, msg=v.msg_f, chain=v.chain_f, sent=v.sent_f, received=v.received_f, to=(me + 1, NR), come=(0, me)
    )
    behind = SimpleNamespace(
        forward=False, msg=v.msg_b, chain=v.chain_b, sent=v.sent_b, received=v.received_b, to=(0, me), come=(me + 1, NR)
    )

    pos = lax.broadcasted_iota(jnp.int32, (CHUNK, LANES), 0)
    pos = lax.rem(pos, SEG) * L + lax.div(pos, SEG)

    def valid_of(i, width):
        ok = jnp.where(pos + i * (CHUNK // SEG) < len1, 1.0, 0.0)
        return jnp.concatenate([ok] * (width // LANES), axis=1) if width > LANES else ok

    w_forward_all(wt_in)
    pass_on()

    own[OWN_X].wait()
    wait_bytes(v.xin.at[:, pl.ds(0, (S - 1) * W)], X, True)
    v.x[...] = nn(v.perm[...], v.xin[...])

    def layer_norm(i):
        rows = rows_of(i)
        x = v.x[rows, :]
        centred = x - jnp.mean(x, -1, keepdims=True)
        inverse = lax.rsqrt(jnp.mean(centred * centred, -1, keepdims=True) + epsilon)
        normed = centred * inverse
        v.normed[rows, :] = normed
        v.inverse[rows, :] = jnp.broadcast_to(inverse, (CHUNK, LANES))
        v.mixed_low[rows, :] = (normed * gain + bias).astype(BF16)

    loop(T // CHUNK, layer_norm, unroll=2)
    w_forward_far(wt_out)
    own[OWN_WIN].wait()
    w_ready(wt_in)
    v.wide[...] = nt(v.mixed_low[...], v.win[...])

    lamb = [tuple(jnp.broadcast_to(c, (SEG, LANES)) for c in l) for l in lam]
    gamb = [jnp.broadcast_to(g, (SEG, LANES)) for g in gam]

    def load_c(ref, at):
        return [(ref[at, lanes(a)], ref[at, lanes(NG + a)]) for a in range(NG)]

    def store_c(ref, at, values):
        for a in range(NG):
            ref[at, lanes(a)] = values[a][0]
            ref[at, lanes(NG + a)] = values[a][1]

    def load_g(ref, at):
        return [swap_halves(ref[at, lanes(2 * a)], ref[at, lanes(2 * a + 1)], low) for a in range(NG)]

    def to_g(values):
        return [g for a in range(NG) for g in swap_halves(values[a][0], values[a][1], low)]

    def step_of(k):
        return pl.ds(pl.multiple_of(k * SEG, SEG), SEG)

    zeros = tuple((jnp.zeros((SEG, LANES), F32), jnp.zeros((SEG, LANES), F32)) for _ in range(NG))

    def advance(k, state, proj):
        ok = seg * L + k < my_len
        new = []
        for a in range(NG):
            re, im = cmul(lamb[a], state[a])
            re, im = re + gamb[a] * proj[a][0], im + gamb[a] * proj[a][1]
            new.append((jnp.where(ok, re, state[a][0]), jnp.where(ok, im, state[a][1])))
        return tuple(new)

    def fwd_first(k, state):
        proj = load_g(v.wide, step_of(k))
        store_c(v.proj, step_of(k), proj)
        return advance(k, state, proj)

    ends = lax.fori_loop(0, L, fwd_first, zeros, unroll=4)

    def across(values, table, forward):
        done = []
        for a in range(NG):
            x = values[a]
            for i, d in enumerate(LEVELS):
                shift = d if forward else SEG - d
                other = (pltpu.roll(x[0], shift, 0), pltpu.roll(x[1], shift, 0))
                factor = (table[i, a, 0], table[i, a, 1])
                add = cmul(factor, other) if forward else conj_mul(factor, other)
                x = (x[0] + add[0], x[1] + add[1])
            done.append(x)
        return done

    ends = across(ends, v.hs_f, True)
    everyone_in()
    exchange(ahead, [tuple(x[SEG - 1 : SEG, :] for x in ends[a]) for a in range(NG)])
    before = [
        tuple(jnp.where(seg > 0, pltpu.roll(x, 1, 0), 0.0) for x in ends[a]) for a in range(NG)
    ]
    block = gate_block(v.wglu, me_s, 1)
    send(block, block, wt_glu + GLU_FAR + 2, {STATE: far})
    to_state(lambda t: cot.at[t], v.cin.at[:, cols(me_s, W)], C)
    w_forward_all(wt_out)
    own[OWN_C].wait()
    far_blocks = [lin_block(v.wglu, far), gate_block(v.wglu, far, 0), gate_block(v.wglu, far, 1)]
    for i, block in enumerate(far_blocks):
        wait_bytes(block, wt_glu + GLU_FAR + i, True)
        send(block, block, wt_glu + GLU_SIB + i, {STATE: sib})
    v.mixed_t[...] = nt(v.eye[...], v.mixed_low[...]).astype(BF16)
    starts = collect(ahead)
    state = []
    for a in range(NG):
        add = cmul((v.lead_pow[a, 0], v.lead_pow[a, 1]), starts[a])
        state.append((before[a][0] + add[0], before[a][1] + add[1]))
    store_c(v.state, pl.ds(0, SEG), state)

    def fwd_second(k, state):
        state = advance(k, state, load_c(v.proj, step_of(k)))
        store_c(v.state, step_of(k + 1), state)
        low_out = to_g([(re, -im) for re, im in state])
        for s in range(S):
            v.state_low[step_of(k), lanes(s)] = low_out[s].astype(BF16)
        return state

    lax.fori_loop(0, L, fwd_second, tuple(state), unroll=4)

    own[OWN_WOUT].wait()
    w_ready(wt_out)
    v.wide[...] = nn(v.state_low[...], v.wout[...])

    def gelu(i):
        rows = rows_of(i)
        mixed_in = v.normed[rows, :] * gain + bias
        mixed = v.wide[rows, :] + skip * mixed_in
        cdf = 0.5 * (1.0 + lax.erf(mixed * (1.0 / math.sqrt(2.0))))
        density = jnp.exp(-0.5 * mixed * mixed) * (1.0 / math.sqrt(2.0 * math.pi))
        v.act[rows, :] = (mixed * cdf).astype(BF16)
        v.dgelu[rows, :] = cdf + mixed * density

    loop(T // CHUNK, gelu, unroll=2)
    wait_bytes(glu_block(v.wglu, sib), wt_glu + SIB, True)
    for i, block in enumerate([lin_block(v.wglu, sib_far), gate_block(v.wglu, sib_far, 0), gate_block(v.wglu, sib_far, 1)]):
        wait_bytes(block, wt_glu + GLU_SIB + i, True)
    for k in range(2):
        v.pre[k] = nn(v.act[...], v.wglu[k])

    def glu(i):
        rows = rows_of(i)
        ok = valid_of(i, W)
        for s in range(S):
            here = slice(s * W, (s + 1) * W)
            linear = v.pre[0, rows, here] + par_s[s, 3:4, :]
            gate = v.pre[1, rows, here] + par_s[s, 4:5, :]
            share = jax.nn.sigmoid(gate)
            value = linear * share
            v.out_low[rows, here] = (ok * (v.x[rows, here] + value)).astype(BF16)
            v.pre[0, rows, here] = ok * share
            v.pre[1, rows, here] = ok * (value * (1.0 - share))

    loop(T // CHUNK, glu, unroll=2)

    def give_back(low_ref, nat, result, own_which):
        nat[...] = nn(v.back[...], low_ref[...]).astype(BF16)
        copy = pltpu.make_async_copy(nat.at[:, cols(me_s, W)], result.at[me_s], v.here.at[own_which])
        copy.start()
        return copy

    def give_to(nat, result, which, t):
        send(nat.at[:, cols(t, W)], result.at[me_s], which, {STATE: t})

    out_copy = give_back(v.out_low, v.out_nat, out_ref, OWN_OUT)
    give_to(v.out_nat, out_ref, OUT, far)
    v.act_t[...] = nt(v.eye[...], v.act[...]).astype(BF16)
    wait_bytes(v.cin.at[:, pl.ds(0, (S - 1) * W)], C, True)
    v.wide[...] = nn(v.perm[...], v.cin[...])

    def glu_back(i):
        rows = rows_of(i)
        dout = v.wide[rows, :]
        for k in range(2):
            v.d_pre[k, rows, :] = (dout * v.pre[k, rows, :]).astype(BF16)

    loop(T // CHUNK, glu_back, unroll=2)

    R4 = R // 4 if R % 4 == 0 else R // 2
    sizes = {AX_X: NG, AX_Y: 2, AX_Z: 2 if R % 4 == 0 else 1, None: R4}

    def places(r, b):
        return {AX_X: b, AX_Y: lax.rem(r, 2), AX_Z: lax.rem(lax.div(r, 2), sizes[AX_Z]), None: lax.div(r, 2 * sizes[AX_Z])}

    mine = places(me_r, lax.div(me_s, 2))
    partner = {
        AX_X: {STATE: far},
        AX_Y: {ROWS: pair_r},
        AX_Z: {ROWS: me_r + 2 - 4 * mine[AX_Z]},
    }

    def slot(route, r, b):
        at, index = places(r, b), 0
        for axis in route.axes[1:] + route.others:
            index = index * sizes[axis] + at[axis]
        return at[route.axes[0]], index

    def owner(route, n):
        at = dict(mine)
        for axis in reversed(route.others):
            at[axis] = lax.rem(n, sizes[axis])
            n = lax.div(n, sizes[axis])
        return {ROWS: at[AX_Y] + 2 * (at[AX_Z] + sizes[AX_Z] * at[None]), STATE: 2 * at[AX_X] + mine_s}

    for part in parts:
        for route in part.routes:
            route.others = tuple(axis for axis in sizes if axis not in route.axes)
            route.number = 0
            for axis in route.others:
                route.number = route.number * sizes[axis] + mine[axis]

    def first_send(part):
        for b in range(NG):
            send(part.full.at[:, cols(2 * b + 1 - mine_s, LANES)], part.r1.at[b], part.step, {STATE: sib})

    def first_wait(part):
        wait_bytes(part.r1, part.step, True)

    def first_sum(route):
        part = route.part

        def one(r):
            rows = pl.ds(pl.multiple_of(r * HB + route.first, route.lines), route.lines)
            for b in range(NG):
                total = part.full[rows, cols(2 * b + mine_s, LANES)].astype(F32) + part.r1[b, rows, :].astype(F32)
                route.a[0][slot(route, r, b)] = total.astype(gdt)

        loop(R, one, unroll=2)
        pass_half(route, 0)

    def pass_half(route, i):
        axis = route.axes[i]
        send(route.a[i].at[1 - mine[axis]], route.r[i], route.step + i, partner[axis])

    def next_sum(route, i):
        wait_bytes(route.r[i], route.step + i, True)
        count, last = route.r[i].shape[0], i + 1 == len(route.axes)

        def one(n):
            total = route.a[i][mine[route.axes[i]], n].astype(F32) + route.r[i][n].astype(F32)
            to = n if last else (lax.div(n, count // 2), lax.rem(n, count // 2))
            route.a[i + 1][to] = total.astype(gdt)

        loop(count, one, unroll=2)
        if not last:
            pass_half(route, i + 1)
            return
        done = route.a[i + 1]
        route.last[route.number] = done[route.number]

        def give(d, carry):
            n = lax.rem(route.number + d, count)
            send(done.at[n], route.last.at[route.number], route.step + len(route.axes), owner(route, n))
            return carry

        lax.fori_loop(1, count, give, 0)

    def last_sum(route):
        count = route.last.shape[0]
        if count > 1:
            wait_bytes(route.last.at[pl.ds(0, count - 1)], route.step + len(route.axes), True)

        def one(n, total):
            return total + route.last[n].astype(F32)

        total = lax.fori_loop(0, count, one, jnp.zeros((route.lines, LANES), F32), unroll=2)
        gsum[route.first : route.first + route.lines, route.part.at : route.part.at + LANES] = total

    def all_sent(part):
        wait_bytes(part.r1, part.step, False)
        for route in part.routes:
            for i in range(len(route.axes)):
                wait_bytes(route.r[i], route.step + i, False)
            if route.last.shape[0] > 1:
                wait_bytes(route.last.at[pl.ds(0, route.last.shape[0] - 1)], route.step + len(route.axes), False)

    def glu_first():
        for part in (g_lin, g_gate):
            first_wait(part)
            first_sum(part.routes[0])

    def glu_next():
        for part in (g_lin, g_gate):
            next_sum(part.routes[0], 0)

    first_half, second_half = me_r < R // 2, me_r >= R // 2
    for k, part in ((0, g_lin), (1, g_gate)):
        part.full[...] = nn(v.act_t[...], v.d_pre[k]).astype(gdt)
        first_send(part)
    v.wide[...] = nt(v.d_pre[0], v.wglu[0]) + nt(v.d_pre[1], v.wglu[1])

    def gelu_back(i, total):
        rows = rows_of(i)
        d_mixed = v.wide[rows, :] * v.dgelu[rows, :]
        v.d_mixed[rows, :] = d_mixed
        v.d_rec[rows, :] = d_mixed.astype(BF16)
        return total + fold(d_mixed * (v.normed[rows, :] * gain + bias))

    d_skip = lax.fori_loop(0, T // CHUNK, gelu_back, jnp.zeros((SUB, H), F32), unroll=2)
    d_skip = jnp.sum(d_skip, axis=0, keepdims=True)
    pl.when(first_half)(glu_first)
    v.wide[...] = nt(v.d_rec[...], v.wout[...])
    def retreat(k, source, carry):
        ok = seg * L + k < my_len
        adjoint, new = [], []
        for a in range(NG):
            re, im = source[a][0] + carry[a][0], source[a][1] + carry[a][1]
            adjoint.append((re, im))
            nre, nim = conj_mul(lamb[a], (re, im))
            new.append((jnp.where(ok, nre, re), jnp.where(ok, nim, im)))
        return ok, adjoint, tuple(new)

    def bwd_first(i, carry):
        k = L - 1 - i
        source = [(re, -im) for re, im in load_g(v.wide, step_of(k))]
        store_c(v.source, step_of(k), source)
        return retreat(k, source, carry)[2]

    heads = lax.fori_loop(0, L, bwd_first, zeros, unroll=4)
    heads = across(heads, v.hs_b, False)
    exchange(behind, [tuple(x[0:1, :] for x in heads[a]) for a in range(NG)])
    after = [
        tuple(jnp.where(seg < SEG - 1, pltpu.roll(x, SEG - 1, 0), 0.0) for x in heads[a])
        for a in range(NG)
    ]
    pl.when(second_half)(glu_first)
    g_out.full[...] = tn(v.d_rec[...], v.state_low[...]).astype(gdt)
    first_send(g_out)
    ones = jnp.ones((2 * SUB, T), BF16)
    d_bias = [nn(ones, v.d_pre[k])[0:1, :] for k in range(2)]
    first_wait(g_out)
    first_sum(g_out.routes[0])
    give_to(v.out_nat, out_ref, OUT, sib)
    give_to(v.out_nat, out_ref, OUT, sib_far)
    pl.when(first_half)(glu_next)
    omegas = collect(behind)
    carry = []
    for a in range(NG):
        add = conj_mul((v.tail_pow[a, 0], v.tail_pow[a, 1]), omegas[a])
        carry.append((after[a][0] + add[0], after[a][1] + add[1]))

    def bwd_second(i, item):
        k = L - 1 - i
        carry, sums = item
        ok, adjoint, carry = retreat(k, load_c(v.source, step_of(k)), carry)
        previous = load_c(v.state, step_of(k))
        proj = load_c(v.proj, step_of(k))
        new_sums, low_out = [], []
        for a in range(NG):
            re, im = (jnp.where(ok, x, 0.0) for x in adjoint[a])
            dre, dim = conj_mul(previous[a], (re, im))
            dg = re * proj[a][0] + im * proj[a][1]
            new_sums.append(tuple(x + fold(y) for x, y in zip(sums[a], (dre, dim, dg))))
            low_out.append((gamb[a] * re, gamb[a] * im))
        low_out = to_g(low_out)
        for s in range(S):
            v.d_proj[step_of(k), lanes(s)] = low_out[s].astype(BF16)
        return carry, tuple(new_sums)

    zero = jnp.zeros((SUB, LANES), F32)
    _, sums = lax.fori_loop(
        0, L, bwd_second, (tuple(carry), tuple((zero, zero, zero) for _ in range(NG))), unroll=2
    )

    g_in.full[...] = nn(v.mixed_t[...], v.d_proj[...]).astype(gdt)
    first_send(g_in)
    v.wide[...] = nn(v.d_proj[...], v.win[...])
    pl.when(second_half)(glu_next)
    next_sum(g_out.routes[0], 0)


    def norm_back(i, totals):
        rows = rows_of(i)
        d_mixed_in = v.wide[rows, :] + skip * v.d_mixed[rows, :]
        normed = v.normed[rows, :]
        inverse = jnp.concatenate([v.inverse[rows, :]] * (H // LANES), axis=1)
        g = d_mixed_in * gain
        first = jnp.mean(g, -1, keepdims=True)
        second = jnp.mean(g * normed, -1, keepdims=True)
        v.din_low[rows, :] = (inverse * (g - first - normed * second)).astype(BF16)
        return totals[0] + fold(d_mixed_in * normed), totals[1] + fold(d_mixed_in)

    zero_h = jnp.zeros((SUB, H), F32)
    d_gain, d_nbias = lax.fori_loop(0, T // CHUNK, norm_back, (zero_h, zero_h), unroll=2)
    d_gain = jnp.sum(d_gain, axis=0, keepdims=True)
    d_nbias = jnp.sum(d_nbias, axis=0, keepdims=True)
    small = v.small
    small[...] = jnp.zeros((S, SUB, LANES), F32)
    for a in range(NG):
        sr, si, sg = (jnp.sum(x, axis=0, keepdims=True) for x in sums[a])
        d_nu = -rate[a] * (sr * lam[a][0] + si * lam[a][1])
        d_theta = angle[a] * (si * lam[a][0] - sr * lam[a][1])
        pair = swap_halves(d_nu, d_theta, low1)
        pair_g = swap_halves(gam[a] * sg, jnp.zeros_like(sg), low1)
        for u in range(2):
            small[2 * a + u, 0:1, :] = pair[u]
            small[2 * a + u, 1:2, :] = pair_g[u]
    for s in range(S):
        here = slice(s * W, (s + 1) * W)
        small[s, 2:3, :] = d_skip[:, here]
        small[s, 3:4, :] = d_bias[0][:, here]
        small[s, 4:5, :] = d_bias[1][:, here]
        small[s, 5:6, :] = d_gain[:, here]
        small[s, 6:7, :] = d_nbias[:, here]
    v.small_r[me_s] = small[...]
    to_state(lambda t: small, v.small_r.at[me_s], SM)
    first_wait(g_in)
    for route in g_in.routes:
        first_sum(route)
    if len(g_gate.routes[0].axes) > 1:
        next_sum(g_gate.routes[0], 1)
    din_copy = give_back(v.din_low, v.din_nat, din_ref, OWN_DIN)
    for t in (far, sib):
        give_to(v.din_nat, din_ref, DIN, t)
    if len(g_out.routes[0].axes) > 1:
        next_sum(g_out.routes[0], 1)
    for route in g_in.routes:
        next_sum(route, 0)
    give_to(v.din_nat, din_ref, DIN, sib_far)
    wait_bytes(v.small_r.at[pl.ds(0, S - 1)], SM, True)
    group = v.small_r[0]
    for s in range(1, S):
        group = group + v.small_r[s]
    small2 = v.small2
    v.group[...] = group
    small2[0:SUB, :] = v.group[me_s]
    for s in range(S):
        small2[SUB + s : SUB + s + 1, :] = group[s, 5:6, :]
        small2[SUB + S + s : SUB + S + s + 1, :] = group[s, 6:7, :]
    v.small2_r[me_r] = small2[...]

    def small_rows(d, carry):
        send(small2, v.small2_r.at[me_r], SN, {ROWS: lax.rem(me_r + d, R)})
        return carry

    lax.fori_loop(1, R, small_rows, 0)
    for part in (g_lin, g_gate, g_out):
        last_sum(part.routes[0])
    wait_bytes(v.small2_r.at[pl.ds(0, R - 1)], SN, True)

    def sum_rows(r, total):
        return total + v.small2_r[r]

    vec[...] = lax.fori_loop(0, R, sum_rows, jnp.zeros((2 * SUB, LANES), F32))
    for route in g_in.routes:
        last_sum(route)

    out_copy.wait()
    din_copy.wait()
    wait_bytes(out_ref.at[pl.ds(0, S - 1)], OUT, True)
    wait_bytes(din_ref.at[pl.ds(0, S - 1)], DIN, True)
    wait_bytes(out_ref.at[pl.ds(0, S - 1)], OUT, False)
    wait_bytes(din_ref.at[pl.ds(0, S - 1)], DIN, False)
    wait_bytes(v.par_s.at[pl.ds(0, S - 1)], PAR_S, False)
    wait_bytes(v.xin.at[:, pl.ds(0, (S - 1) * W)], X, False)
    for w in (wt_in, wt_out):
        w_sent(w)
    wait_bytes(glu_own, wt_glu + SIB, False)
    for i, block in enumerate(far_blocks):
        wait_bytes(block, wt_glu + GLU_FAR + i, False)
        wait_bytes(block, wt_glu + GLU_SIB + i, False)
    wait_bytes(v.cin.at[:, pl.ds(0, (S - 1) * W)], C, False)
    carries_sent(ahead)
    carries_sent(behind)
    wait_bytes(v.small_r.at[pl.ds(0, S - 1)], SM, False)
    wait_bytes(v.small2_r.at[pl.ds(0, R - 1)], SN, False)
    for part in parts:
        all_sent(part)


def routes_of(R, H):
    HB = H // R
    if HB % (4 * SUB) == 0:
        routes = [(0, (AX_Y,), 0, HB // 2), (0, (AX_Z if R % 4 == 0 else AX_X,), HB // 2, HB // 2)]
    else:
        routes = [(0, (AX_Y,), 0, HB)]
    if R % 4 == 0:
        return routes + [(1, (AX_X, AX_Y), 0, HB), (2, (AX_Y,), 0, HB), (3, (AX_Z, AX_Y), 0, HB)]
    return routes + [(1, (AX_X,), 0, HB), (2, (AX_Y,), 0, HB), (3, (AX_X,), 0, HB)]


def run_block(dims, *args):
    R, S, T, H, W = dims.R, dims.S, dims.T, dims.H, dims.W
    NR, NG, HB = R * S, S // 2, H // R
    CH, levels = S * LANES, len(LEVELS)
    gdt = BF16 if HB % (2 * SUB) == 0 else F32
    dims.gdt = gdt
    bits = T.bit_length()
    shapes = dict(
        xin=((T, H), BF16),
        cin=((T, H), BF16),
        win=((CH, H), BF16),
        wout=((CH, H), BF16),
        wglu=((2, H, H), BF16),
        glu_raw=((2 * H, W), BF16),
        glu_wide=((2 * CHUNK, W), F32),
        perm=((T, T), BF16),
        back=((T, T), BF16),
        eye=((T, T), BF16),
        mixed_t=((H, T), BF16),
        act_t=((H, T), BF16),
        nu=((1, HALF), F32),
        theta=((1, HALF), F32),
        gamma=((1, HALF), F32),
        skip=((1, W), F32),
        glu_bias=((2, W), F32),
        gain=((1, H), F32),
        bias=((1, H), F32),
        par=((2 * SUB, LANES), F32),
        par_s=((S, 2 * SUB, LANES), F32),
        pows=((bits, NG, 2, SUB, LANES), F32),
        hs_f=((levels, NG, 2, SEG, LANES), F32),
        hs_b=((levels, NG, 2, SEG, LANES), F32),
        lead_pow=((NG, 2, SEG, LANES), F32),
        tail_pow=((NG, 2, SEG, LANES), F32),
        row_pow=((2 * NG, NR, LANES), F32),
        row_hit=((NR, LANES), F32),
        msg_f=((SUB, LANES), F32),
        msg_b=((SUB, LANES), F32),
        row_len=((4 * SUB, LANES), F32),
        chain_f=((NR, SUB, LANES), F32),
        chain_b=((NR, SUB, LANES), F32),
        x=((T, H), F32),
        normed=((T, H), F32),
        inverse=((T, LANES), F32),
        mixed_low=((T, H), BF16),
        wide=((T, max(H, CH)), F32),
        proj=((T, CH), F32),
        state=((T + SEG, CH), F32),
        state_low=((T, CH), BF16),
        act=((T, H), BF16),
        dgelu=((T, H), F32),
        pre=((2, T, H), F32),
        out_low=((T, H), BF16),
        out_nat=((T, H), BF16),
        d_pre=((2, T, H), BF16),
        d_mixed=((T, H), F32),
        d_rec=((T, H), BF16),
        source=((T, CH), F32),
        d_proj=((T, CH), BF16),
        din_low=((T, H), BF16),
        din_nat=((T, H), BF16),
        small=((S, SUB, LANES), F32),
        small_r=((S, S, SUB, LANES), F32),
        group=((S, SUB, LANES), F32),
        small2=((2 * SUB, LANES), F32),
        small2_r=((R, 2 * SUB, LANES), F32),
    )
    scalars = dict(bucket=(S,), lengths=(S,))
    flags = dict(block_in=1, all_in=1)
    copies = dict(here=OWN_SMALL + 9, sent=G2 + 20, received=G2 + 20, sent_f=NR, received_f=NR, sent_b=NR, received_b=NR)
    dims.names = [*shapes, *scalars, *flags, *copies]
    parts = []
    for _ in range(4):
        parts += [(H, CH), (NG, H, LANES)]
    routes = routes_of(R, H)
    for _, axes, _, lines in routes:
        left = [2 * R >> (i + 1) for i in range(len(axes))]
        parts += [(2, n, lines, LANES) for n in left] + [(left[-1], lines, LANES)]
        parts += [(n, lines, LANES) for n in left] + [(left[-1], lines, LANES)]
    scratch = [pltpu.VMEM(shape, dtype) for shape, dtype in shapes.values()]
    scratch += [pltpu.SMEM(shape, jnp.int32) for shape in scalars.values()]
    scratch += [pltpu.SemaphoreType.REGULAR for _ in flags]
    scratch += [pltpu.SemaphoreType.DMA((n,)) for n in copies.values()]
    scratch += [pltpu.VMEM(shape, gdt) for shape in parts]
    any_spec = pl.BlockSpec(memory_space=pl.ANY)
    vmem = pl.BlockSpec(memory_space=pltpu.VMEM)
    macs = T * H * (2 * CH + 2 * H) * 3 + 4 * T * T * H
    return pl.pallas_call(
        functools.partial(block_kernel, dims),
        out_shape=(
            jax.ShapeDtypeStruct((S, T, W), BF16),
            jax.ShapeDtypeStruct((S, T, W), BF16),
            jax.ShapeDtypeStruct((HB, 4 * LANES), F32),
            jax.ShapeDtypeStruct((2 * SUB, LANES), F32),
        ),
        in_specs=[any_spec] * 14,
        out_specs=(any_spec, any_spec, vmem, vmem),
        scratch_shapes=scratch,
        compiler_params=pltpu.CompilerParams(
            collective_id=0, has_side_effects=True, vmem_limit_bytes=56 * 2**20
        ),
        cost_estimate=pl.CostEstimate(flops=2 * macs, bytes_accessed=8 * 2**20, transcendentals=4 * T * H),
    )(*args)


def on_device(
    inputs,
    bucket,
    lengths,
    nu_log,
    theta_log,
    gamma_log,
    in_proj,
    out_proj,
    skip,
    norm_gain,
    norm_bias,
    glu_weight,
    glu_bias,
    output_cotangent,
):
    row_count, seq, part = inputs.shape
    width = norm_gain.shape[0]
    chans = nu_log.shape[0]
    R, S = lax.axis_size(ROWS), lax.axis_size(STATE)
    dims = SimpleNamespace(R=R, S=S, T=seq, H=width, W=part)
    assert row_count == S and 2 * chans == LANES and part == LANES and S % 2 == 0 and R % 2 == 0

    outputs, d_norm, gsum, vec = run_block(
        dims,
        inputs,
        output_cotangent,
        in_proj.transpose(1, 2, 0).reshape(2 * chans, width),
        out_proj.reshape(2 * chans, width),
        glu_weight.reshape(2 * width, part),
        bucket,
        lengths,
        nu_log[None],
        theta_log[None],
        gamma_log[None],
        skip[None],
        glu_bias,
        norm_gain[None],
        norm_bias[None],
    )
    return finish(dims, lengths, outputs, d_norm, output_cotangent, gsum, vec)


def finish_kernel(dims, *refs):
    S, T, HB = dims.S, dims.T, dims.H // dims.R
    (lengths, out_in, d_norm, cot, gsum, vec) = refs[:6]
    (out, d_inputs, d_nu, d_theta, d_gamma, d_in, d_out, d_skip, d_gain, d_bias, d_glu, d_glu_bias) = refs[6:]
    out[...] = out_in[...]
    for row in range(S):
        for first in range(0, T, CHUNK):
            lines = slice(first, first + CHUNK)
            place = lax.broadcasted_iota(jnp.int32, (CHUNK, LANES), 0) + first
            direct = jnp.where(place < lengths[row], cot[row, lines, :].astype(F32), 0.0)
            d_inputs[row, lines, :] = d_norm[row, lines, :].astype(F32) + direct
    d_nu[...] = vec[0:1, 0:HALF]
    d_theta[...] = pltpu.roll(vec[0:1, :], HALF, 1)[:, 0:HALF]
    d_gamma[...] = vec[1:2, 0:HALF]
    d_skip[...] = vec[2:3, :]
    d_glu_bias[...] = vec[3:5, :]
    for s in range(S):
        here = slice(s * LANES, (s + 1) * LANES)
        d_gain[:, here] = vec[SUB + s : SUB + s + 1, :]
        d_bias[:, here] = vec[SUB + S + s : SUB + S + s + 1, :]
    both = gsum[:, 0:LANES]
    d_in[pl.ds(0, HB, stride=2), :] = both[:, 0:HALF]
    d_in[pl.ds(1, HB, stride=2), :] = pltpu.roll(both, HALF, 1)[:, 0:HALF]
    d_out[...] = gsum[:, LANES : 2 * LANES].T
    d_glu[pl.ds(0, HB, stride=2), :] = gsum[:, 2 * LANES : 3 * LANES]
    d_glu[pl.ds(1, HB, stride=2), :] = gsum[:, 3 * LANES : 4 * LANES]


def finish(dims, lengths, outputs, d_norm, cot, gsum, vec):
    R, S, T, H, W = dims.R, dims.S, dims.T, dims.H, dims.W
    HB = H // R
    vmem = pl.BlockSpec(memory_space=pltpu.VMEM)
    small = [(1, HALF)] * 3 + [(2 * HB, HALF), (LANES, HB), (1, W), (1, H), (1, H), (2 * HB, W), (2, W)]
    got = pl.pallas_call(
        functools.partial(finish_kernel, dims),
        out_shape=(
            jax.ShapeDtypeStruct((S, T, W), BF16),
            jax.ShapeDtypeStruct((S, T, W), F32),
            *(jax.ShapeDtypeStruct(shape, F32) for shape in small),
        ),
        in_specs=[pl.BlockSpec(memory_space=pltpu.SMEM)] + [vmem] * 5,
        out_specs=(vmem,) * 12,
    )(lengths, outputs, d_norm, cot, gsum, vec)
    out, d_inputs, d_nu, d_theta, d_gamma, d_in, d_out, d_skip, d_gain, d_bias, d_glu, d_glu_bias = got
    return (
        out,
        d_inputs,
        d_nu.reshape(HALF),
        d_theta.reshape(HALF),
        d_gamma.reshape(HALF),
        d_in.reshape(HB, 2, HALF),
        d_out.reshape(2, HALF, HB),
        d_skip.reshape(W),
        d_gain.reshape(H),
        d_bias.reshape(H),
        d_glu.reshape(HB, 2, W),
        d_glu_bias,
    )


def solution(mesh):
    return jax.shard_map(
        on_device,
        mesh=mesh,
        in_specs=(
            P(ROWS, None, STATE),
            P(ROWS),
            P(ROWS),
            P(STATE),
            P(STATE),
            P(STATE),
            P(None, None, STATE),
            P(None, STATE, None),
            P(STATE),
            P(),
            P(),
            P(None, None, STATE),
            P(None, STATE),
            P(ROWS, None, STATE),
        ),
        out_specs=(
            P(ROWS, None, STATE),
            P(ROWS, None, STATE),
            P(STATE),
            P(STATE),
            P(STATE),
            P(ROWS, None, STATE),
            P(None, STATE, ROWS),
            P(STATE),
            P(),
            P(),
            P(ROWS, None, STATE),
            P(None, STATE),
        ),
        check_vma=False,
    )
```

```python
import functools
import math
from types import SimpleNamespace

import jax
import jax.numpy as jnp
from jax import lax
from jax.experimental import pallas as pl
from jax.experimental.pallas import tpu as pltpu
from jax.sharding import PartitionSpec as P

epsilon = 1e-05

F32 = jnp.float32
BF16 = jnp.bfloat16
MESH = pl.DeviceIdType.MESH
ROWS, STATE = "rows", "state"
SUB = 8
LANES = 128
HALF = LANES // 2
CHUNK = 64
SEG = 32
LEVELS = tuple(1 << i for i in range(SEG.bit_length() - 1))

OWN_X, OWN_WIN, OWN_WOUT, OWN_WGLU, OWN_C, OWN_OUT, OWN_DIN, OWN_SMALL = range(8)
OWN_WIN_G = OWN_SMALL + 9
PAR_S, X, C, OUT, DIN, SM, SN, W1 = range(8)
SIB, FAR, PEER, FAR_SIB = range(4)
GLU_FAR, GLU_SIB = 1, 4
G1 = W1 + 19
G2 = G1 + 4
AX_X, AX_Y, AX_Z = range(3)


def loop(count, body, unroll=1):
    def step(i, carry):
        body(i)
        return carry

    lax.fori_loop(0, count, step, 0, unroll=unroll)


def nn(a, b):
    return lax.dot_general(a, b, (((1,), (0,)), ((), ())), preferred_element_type=F32)


def nt(a, b):
    return lax.dot_general(a, b, (((1,), (1,)), ((), ())), preferred_element_type=F32)


def tn(a, b):
    return lax.dot_general(a, b, (((0,), (0,)), ((), ())), preferred_element_type=F32)


def cmul(a, b):
    return a[0] * b[0] - a[1] * b[1], a[0] * b[1] + a[1] * b[0]


def conj_mul(a, b):
    return a[0] * b[0] + a[1] * b[1], a[0] * b[1] - a[1] * b[0]


def swap_halves(u, v, low):
    return (
        jnp.where(low, u, pltpu.roll(v, HALF, 1)),
        jnp.where(low, pltpu.roll(u, HALF, 1), v),
    )


def fold(x):
    return jnp.sum(x.reshape(x.shape[0] // SUB, SUB, x.shape[1]), axis=0)


def block_kernel(dims, *refs):
    R, S, T, H, W, gdt = dims.R, dims.S, dims.T, dims.H, dims.W, dims.gdt
    NR, NG, R2, HB, L = R * S, S // 2, R // 2, H // R, T // SEG
    Q = 4 if R % 8 == 0 else 2
    G, NB = Q * S, R // Q
    BITS, CH = T.bit_length(), S * LANES
    (inputs, cot, w_in, w_out, w_glu) = refs[:5]
    vectors = refs[5:14]
    (out_ref, din_ref, gsum, vec) = refs[14:18]
    total = 18 + len(dims.names)
    v = SimpleNamespace(**dict(zip(dims.names, refs[18:total])))
    parts = [
        SimpleNamespace(full=refs[total + 2 * i], r1=refs[total + 2 * i + 1], step=G1 + i, at=i * LANES, routes=[])
        for i in range(4)
    ]
    g_in, g_out, g_lin, g_gate = parts
    total += 8
    for i, (part, axes, first, lines) in enumerate(routes_of(R, H)):
        steps = len(axes)
        route = SimpleNamespace(part=parts[part], axes=axes, first=first, lines=lines, step=G2 + 4 * i)
        route.a = refs[total : total + steps + 1]
        route.r = refs[total + steps + 1 : total + 2 * steps + 1]
        route.last = refs[total + 2 * steps + 1]
        total += 2 * steps + 2
        parts[part].routes.append(route)

    me_r, me_s = lax.axis_index(ROWS), lax.axis_index(STATE)
    me = me_r * S + me_s

    def cols(i, width):
        return pl.ds(pl.multiple_of(i * width, LANES), width)

    def lanes(i):
        return slice(i * LANES, (i + 1) * LANES)

    def rows_of(i):
        return pl.ds(pl.multiple_of(i * CHUNK, CHUNK), CHUNK)

    def wait_bytes(ref, which, arrived):
        pltpu.make_async_copy(ref, ref, (v.received if arrived else v.sent).at[which]).wait()

    def send(src, dst, which, target):
        pltpu.make_async_remote_copy(
            src_ref=src,
            dst_ref=dst,
            send_sem=v.sent.at[which],
            recv_sem=v.received.at[which],
            device_id=target,
            device_id_type=MESH,
        ).start()

    def to_state(src_of, dst, which):
        for j in (2, 3, 1) if S == 4 else range(1, S):
            t = lax.rem(me_s + j, S)
            send(src_of(t), dst, which, {STATE: t})

    sib = me_s + 1 - 2 * lax.rem(me_s, 2)
    far = lax.rem(me_s + NG, S)
    sib_far = lax.rem(sib + NG, S)
    pair_r = me_r + 1 - 2 * lax.rem(me_r, 2)
    group_r = me_r - lax.rem(me_r, Q)
    piece = lax.rem(me_r, Q)
    mine_s = lax.rem(me_s, 2)
    mine_r = lax.rem(me_r, 2)

    def line_block(ref, s, p=None):
        size = HALF if p is None else HALF // Q
        first = s * HALF if p is None else s * HALF + p * size
        return ref.at[:, pl.ds(pl.multiple_of(first, size), size), :]

    def glu_block(ref, s):
        return ref.at[:, :, cols(s, W)]

    def lin_block(ref, s):
        return ref.at[0, :, cols(s, W)]

    def gate_block(ref, s, h):
        return ref.at[1, pl.ds(h * (H // 2), H // 2), cols(s, W)]

    def last_block(ref, s, p=None):
        size = H // 2 if p is None else H // 2 // Q
        first = H // 2 if p is None else H // 2 + p * size
        return ref.at[1, pl.ds(pl.multiple_of(first, size), size), cols(s, W)]

    own = [
        (w_glu, v.glu_raw, OWN_WGLU),
        (w_in, line_block(v.win, me_s), OWN_WIN),
        (w_out, line_block(v.wout, me_s), OWN_WOUT),
        (inputs.at[me_s], v.xin.at[:, cols(me_s, W)], OWN_X),
        (cot.at[me_s], v.cin.at[:, cols(me_s, W)], OWN_C),
    ]
    small_in = (v.bucket, v.lengths, v.nu, v.theta, v.gamma, v.skip, v.glu_bias, v.gain, v.bias)
    own += [(a, b, OWN_SMALL + i) for i, (a, b) in enumerate(zip(vectors, small_in))]
    own = {which: pltpu.make_async_copy(a, b, v.here.at[which]) for a, b, which in own}

    barrier = pltpu.get_barrier_semaphore()
    number = piece * S + me_s
    is_gate = (number == 0) & (NB > 1)
    gated = 1 if NB > 1 else 0

    def signal(which, i, rows=None):
        pl.semaphore_signal(
            which,
            inc=1,
            device_id={ROWS: group_r + lax.div(i, S) if rows is None else rows, STATE: lax.rem(i, S)},
            device_id_type=MESH,
        )

    for p in range(Q - 1, -1, -1):
        for d in (2, 3, 1, 0) if S == 4 else range(S):
            if (p, d) != (0, 0):
                i = lax.rem(piece + p, Q) * S + lax.rem(me_s + d, S)
                pl.when(i >= gated)(functools.partial(signal, barrier, i))
    for copy in own.values():
        copy.start()
    for i in range(len(vectors)):
        own[OWN_SMALL + i].wait()
    bucket_ref, lengths_ref, nu_ref, theta_ref, gamma_ref, skip_ref, glu_bias_ref, gain_ref, bias_ref = small_in

    par = v.par
    par[...] = jnp.zeros((2 * SUB, LANES), F32)
    par[0:1, 0:HALF] = nu_ref[...]
    par[0:1, HALF:LANES] = theta_ref[...]
    par[1:2, 0:HALF] = gamma_ref[...]
    par[2:3, :] = skip_ref[...]
    par[3:5, :] = glu_bias_ref[...]
    for i in range(S):
        par[SUB + i : SUB + i + 1, :] = jnp.full((1, LANES), bucket_ref[i], jnp.int32).astype(F32)
        par[SUB + S + i : SUB + S + i + 1, :] = jnp.full((1, LANES), lengths_ref[i], jnp.int32).astype(F32)
    v.par_s[me_s] = par[...]

    @pl.when(jnp.logical_not(is_gate))
    def _():
        pl.semaphore_wait(barrier, G - 1)

    if NB > 1:

        @pl.when(number == 1)
        def _():
            signal(v.block_in, jnp.int32(0))

        @pl.when(is_gate)
        def _():
            pl.semaphore_wait(v.block_in, 1)

            def next_gate(d, carry):
                signal(barrier, jnp.int32(0), rows=lax.rem(group_r + d * Q, R))
                return carry

            lax.fori_loop(1, NB, next_gate, 0)

    def pass_on():
        if NB > 1:

            @pl.when(is_gate)
            def _():
                pl.semaphore_wait(barrier, NB - 1)

                def tell(i, carry):
                    signal(v.all_in, i)
                    return carry

                lax.fori_loop(1, G, tell, 0)

    def everyone_in():
        if NB > 1:

            @pl.when(jnp.logical_not(is_gate))
            def _():
                pl.semaphore_wait(v.all_in, 1)

    to_state(lambda t: par, v.par_s.at[me_s], PAR_S)

    def w_send(w, own_block, own_piece):
        send(own_piece, w.block(w.ref, me_s, piece), w.step + FAR, {STATE: far})
        send(own_block, w.block(w.ref, me_s), w.step + SIB, {STATE: sib})

    def w_forward_far(w):
        here = w.block(w.ref, far, piece)
        wait_bytes(here, w.step + FAR, True)
        for j in range(1, Q):
            send(here, here, w.step + PEER, {ROWS: group_r + lax.rem(piece + j, Q)})

    def w_forward_all(w):
        wait_bytes(w.rest, w.step + PEER, True)
        send(w.block(w.ref, far), w.block(w.ref, far), w.step + FAR_SIB, {STATE: sib})

    def w_ready(w):
        wait_bytes(w.block(w.ref, sib), w.step + SIB, True)
        wait_bytes(w.block(w.ref, sib_far), w.step + FAR_SIB, True)

    def w_sent(w):
        wait_bytes(w.block(w.ref, sib), w.step + SIB, False)
        wait_bytes(w.block(w.ref, sib), w.step + FAR_SIB, False)
        wait_bytes(w.block(w.ref, sib, piece), w.step + FAR, False)
        wait_bytes(w.rest, w.step + PEER, False)

    others = pl.ds(0, HALF - HALF // Q)
    wt_in = SimpleNamespace(ref=v.win, block=line_block, step=W1, rest=v.win.at[:, others, :])
    wt_out = SimpleNamespace(ref=v.wout, block=line_block, step=W1 + 4, rest=v.wout.at[:, others, :])
    wt_glu = W1 + 8
    wt_last = SimpleNamespace(
        ref=v.wglu, block=last_block, step=W1 + 15, rest=v.wglu.at[1, pl.ds(0, H // 2 - H // 2 // Q), pl.ds(0, W)]
    )

    def piece_of(ref):
        size = HALF // Q
        return ref.at[:, pl.ds(pl.multiple_of(piece * size, size), size), :]

    w_send(wt_in, w_in, piece_of(w_in))
    w_send(wt_out, w_out, piece_of(w_out))
    for t in (far, sib):
        send(inputs.at[t], v.xin.at[:, cols(me_s, W)], X, {STATE: t})
    own[OWN_WGLU].wait()

    def split_glu(i):
        here = rows_of(i)
        v.glu_wide[...] = v.glu_raw[pl.ds(pl.multiple_of(i * 2 * CHUNK, 2 * CHUNK), 2 * CHUNK), :].astype(F32)
        for k in range(2):
            v.wglu[k, here, cols(me_s, W)] = v.glu_wide[pl.ds(k, CHUNK, stride=2), :].astype(BF16)

    loop(H // CHUNK, split_glu)
    block = last_block(v.wglu, me_s, piece)
    send(block, block, wt_last.step + FAR, {STATE: far})
    send(inputs.at[sib_far], v.xin.at[:, cols(me_s, W)], X, {STATE: sib_far})
    glu_own = glu_block(v.wglu, me_s)
    send(glu_own, glu_own, wt_glu + SIB, {STATE: sib})
    first_three = [lin_block(v.wglu, me_s), gate_block(v.wglu, me_s, 0)]
    for i, block in enumerate(first_three):
        send(block, block, wt_glu + GLU_FAR + i, {STATE: far})

    line = lax.broadcasted_iota(jnp.int32, (CHUNK, T), 0)
    place = lax.broadcasted_iota(jnp.int32, (CHUNK, T), 1)

    def orders(i):
        base = pl.multiple_of(i * CHUNK, CHUNK)
        at = line + base
        v.perm[pl.ds(base, CHUNK), :] = (
            place == lax.rem(at, SEG) * L + lax.div(at, SEG)
        ).astype(F32).astype(BF16)
        v.back[pl.ds(base, CHUNK), :] = (
            at == lax.rem(place, SEG) * L + lax.div(place, SEG)
        ).astype(F32).astype(BF16)
        v.eye[pl.ds(base, CHUNK), :] = (place == at).astype(F32).astype(BF16)

    loop(T // CHUNK, orders)
    channel = lax.broadcasted_iota(jnp.int32, (CHUNK, CH), 0)
    goes_to = lax.broadcasted_iota(jnp.int32, (CHUNK, CH), 1)
    taken = (
        (lax.rem(lax.div(goes_to, HALF), 2) * S + lax.div(goes_to, LANES)) * HALF + lax.rem(goes_to, HALF)
    )

    def shard_order(i):
        base = pl.multiple_of(i * CHUNK, CHUNK)
        v.by_shard[pl.ds(base, CHUNK), :] = (taken == channel + base).astype(F32).astype(BF16)

    loop(CH // CHUNK, shard_order)

    w_forward_far(wt_in)
    w_forward_far(wt_out)

    low = lax.broadcasted_iota(jnp.int32, (SEG, LANES), 1) < HALF
    low1 = lax.broadcasted_iota(jnp.int32, (1, LANES), 1) < HALF
    seg = lax.broadcasted_iota(jnp.int32, (SEG, LANES), 0)

    wait_bytes(v.par_s.at[pl.ds(0, S - 1)], PAR_S, True)
    par_s = v.par_s
    lam, gam, rate, angle = [], [], [], []
    for a in range(NG):
        nu, theta = swap_halves(par_s[2 * a, 0:1, :], par_s[2 * a + 1, 0:1, :], low1)
        rate.append(jnp.exp(nu))
        angle.append(jnp.exp(theta))
        magnitude = jnp.exp(-rate[a])
        lam.append((magnitude * jnp.cos(angle[a]), magnitude * jnp.sin(angle[a])))
        gam.append(jnp.exp(swap_halves(par_s[2 * a, 1:2, :], par_s[2 * a + 1, 1:2, :], low1)[0]))
    skip = jnp.concatenate([par_s[s, 2:3, :] for s in range(S)], axis=1)
    gain, bias = gain_ref[...], bias_ref[...]
    power = [[(jnp.broadcast_to(l[0], (SUB, LANES)), jnp.broadcast_to(l[1], (SUB, LANES))) for l in lam]]
    for _ in range(BITS - 1):
        power.append([cmul(p, p) for p in power[-1]])
    for b in range(BITS):
        for a in range(NG):
            for c in range(2):
                v.pows[b, a, c] = power[b][a][c]

    def raised(exponent):
        result = [(jnp.ones(exponent.shape, F32), jnp.zeros(exponent.shape, F32)) for _ in range(NG)]
        for b in range(BITS):
            hit = (lax.shift_right_logical(exponent, b) & 1) == 1
            for a in range(NG):
                re, im = cmul(result[a], (v.pows[b, a, 0, 0:1, :], v.pows[b, a, 1, 0:1, :]))
                result[a] = (jnp.where(hit, re, result[a][0]), jnp.where(hit, im, result[a][1]))
        return result

    my_bucket = par[pl.ds(SUB + me_s, 1), :]
    len1 = par[pl.ds(SUB + S + me_s, 1), :].astype(jnp.int32)
    my_len = jnp.broadcast_to(len1, (SEG, LANES))
    seg_pow = raised(jnp.clip(my_len - seg * L, 0, L))
    lead_pow = raised(jnp.minimum(my_len, seg * L))
    tail_pow = raised(jnp.maximum(my_len - (seg + 1) * L, 0))
    for a in range(NG):
        ahead = seg_pow[a]
        behind = seg_pow[a]
        for i, d in enumerate(LEVELS):
            for c in range(2):
                v.hs_f[i, a, c] = jnp.where(seg >= d, ahead[c], 0.0)
                v.hs_b[i, a, c] = jnp.where(seg < SEG - d, behind[c], 0.0)
            ahead = cmul(ahead, (pltpu.roll(ahead[0], d, 0), pltpu.roll(ahead[1], d, 0)))
            behind = cmul(behind, (pltpu.roll(behind[0], SEG - d, 0), pltpu.roll(behind[1], SEG - d, 0)))
        for c in range(2):
            v.lead_pow[a, c] = lead_pow[a][c]
            v.tail_pow[a, c] = tail_pow[a][c]

    def lines_of(p):
        return pl.ds(pl.multiple_of(p * SUB, SUB), SUB)

    FULL = 2 * NG + 1

    def carry_copy(way, source, t):
        return pltpu.make_async_remote_copy(
            src_ref=way.msg.at[pl.ds(0, FULL), :],
            dst_ref=way.chain.at[source, pl.ds(0, FULL), :],
            send_sem=way.sent.at[t],
            recv_sem=way.received.at[source],
            device_id={ROWS: lax.div(t, S), STATE: lax.rem(t, S)},
            device_id_type=MESH,
        )

    def exchange(way, values):
        for a in range(NG):
            for c in range(2):
                way.msg[pl.ds(c * NG + a, 1), :] = values[a][c]
        way.msg[2 * NG : FULL, :] = jnp.where(low1, my_bucket, par[pl.ds(SUB + S + me_s, 1), :])

        def one(i, carry):
            carry_copy(way, me, NR - 1 - i if way.forward else i).start()
            return carry

        lax.fori_loop(0, NR - 1 - me if way.forward else me, one, 0)

    group = min(NR, 4 * SUB)
    low_g = lax.broadcasted_iota(jnp.int32, (group, LANES), 1) < HALF

    def collect(way):
        def arrive(p, carry):
            carry_copy(way, p, me).wait_recv()
            return carry

        lax.fori_loop(*way.come, arrive, 0)

        def powers(i):
            for j in range(group):
                v.row_len[j : j + 1, :] = way.chain[i * group + j, 2 * NG : FULL, :]
            both = v.row_len[0:group, :]
            turned = pltpu.roll(both, HALF, 1)
            here = jnp.where(low_g, both, turned)
            lens = jnp.where(low_g, turned, both).astype(jnp.int32)
            p = lax.broadcasted_iota(jnp.int32, (group, LANES), 0) + i * group
            hit = (here == my_bucket) & (my_bucket > 0.5) & ((p < me) if way.forward else (p > me))
            factor = raised(lens)
            at = pl.ds(pl.multiple_of(i * group, SUB), group)
            for a in range(NG):
                v.row_pow[a, at, :] = jnp.where(hit, factor[a][0], 1.0)
                v.row_pow[NG + a, at, :] = jnp.where(hit, factor[a][1], 0.0)
            v.row_hit[at, :] = jnp.where(hit, 1.0, 0.0)

        loop(NR // group, powers)

        run = NR // 4

        def fold_in(i, carry):
            after = []
            for q in range(4):
                p = q * run + (i if way.forward else run - 1 - i)
                hit = v.row_hit[pl.ds(p, 1), :] > 0.5
                new = []
                for a in range(NG):
                    factor = (v.row_pow[a, pl.ds(p, 1), :], v.row_pow[NG + a, pl.ds(p, 1), :])
                    total, product = carry[q][a]
                    re, im = cmul(factor, total) if way.forward else conj_mul(factor, total)
                    add = (way.chain[p, a : a + 1, :], way.chain[p, NG + a : NG + a + 1, :])
                    total = (re + jnp.where(hit, add[0], 0.0), im + jnp.where(hit, add[1], 0.0))
                    new.append((total, cmul(factor, product)))
                after.append(tuple(new))
            return tuple(after)

        zero, one = jnp.zeros((1, LANES), F32), jnp.ones((1, LANES), F32)
        first = tuple(tuple(((zero, zero), (one, zero)) for _ in range(NG)) for _ in range(4))
        runs = lax.fori_loop(0, run, fold_in, first, unroll=2)
        result = []
        for a in range(NG):
            total = (zero, zero)
            for q in range(4) if way.forward else range(3, -1, -1):
                moved = cmul(runs[q][a][1], total) if way.forward else conj_mul(runs[q][a][1], total)
                total = (moved[0] + runs[q][a][0][0], moved[1] + runs[q][a][0][1])
            result.append(total)
        return result

    def carries_sent(way):
        def one(t, carry):
            carry_copy(way, me, t).wait_send()
            return carry

        lax.fori_loop(*way.to, one, 0)

    ahead = SimpleNamespace(
        forward=True, msg=v.msg_f, chain=v.chain_f, sent=v.sent_f, received=v.received_f, to=(me + 1, NR), come=(0, me)
    )
    behind = SimpleNamespace(
        forward=False, msg=v.msg_b, chain=v.chain_b, sent=v.sent_b, received=v.received_b, to=(0, me), come=(me + 1, NR)
    )

    pos = lax.broadcasted_iota(jnp.int32, (CHUNK, LANES), 0)
    pos = lax.rem(pos, SEG) * L + lax.div(pos, SEG)

    def valid_of(i, width):
        ok = jnp.where(pos + i * (CHUNK // SEG) < len1, 1.0, 0.0)
        return jnp.concatenate([ok] * (width // LANES), axis=1) if width > LANES else ok

    w_forward_all(wt_in)
    w_forward_all(wt_out)
    w_forward_far(wt_last)
    pass_on()

    own[OWN_X].wait()
    wait_bytes(v.xin.at[:, pl.ds(0, (S - 1) * W)], X, True)
    v.x[...] = nn(v.perm[...], v.xin[...])

    def layer_norm(i):
        rows = rows_of(i)
        x = v.x[rows, :]
        centred = x - jnp.mean(x, -1, keepdims=True)
        inverse = lax.rsqrt(jnp.mean(centred * centred, -1, keepdims=True) + epsilon)
        normed = centred * inverse
        v.normed[rows, :] = normed
        v.inverse[rows, :] = jnp.broadcast_to(inverse, (CHUNK, LANES))
        v.mixed_low[rows, :] = (normed * gain + bias).astype(BF16)

    loop(T // CHUNK, layer_norm, unroll=4)
    own[OWN_WIN].wait()
    w_ready(wt_in)
    v.proj[...] = nt(v.mixed_low[...], v.win[...].reshape(CH, H))
    by_shard = [
        pltpu.make_async_copy(line_block(v.win, s), v.win_g.at[s], v.here.at[OWN_WIN_G + s]) for s in range(S)
    ]
    for copy in by_shard:
        copy.start()

    lamb = [tuple(jnp.broadcast_to(c, (SEG, LANES)) for c in l) for l in lam]
    gamb = [jnp.broadcast_to(g, (SEG, LANES)) for g in gam]

    def load_c(ref, at):
        return [(ref[at, lanes(a)], ref[at, lanes(NG + a)]) for a in range(NG)]

    def store_c(ref, at, values):
        for a in range(NG):
            ref[at, lanes(a)] = values[a][0]
            ref[at, lanes(NG + a)] = values[a][1]

    def to_g(values):
        return [g for a in range(NG) for g in swap_halves(values[a][0], values[a][1], low)]

    def step_of(k):
        return pl.ds(pl.multiple_of(k * SEG, SEG), SEG)

    zeros = tuple((jnp.zeros((SEG, LANES), F32), jnp.zeros((SEG, LANES), F32)) for _ in range(NG))

    def advance(k, state, proj):
        ok = seg * L + k < my_len
        new = []
        for a in range(NG):
            re, im = cmul(lamb[a], state[a])
            re, im = re + gamb[a] * proj[a][0], im + gamb[a] * proj[a][1]
            new.append((jnp.where(ok, re, state[a][0]), jnp.where(ok, im, state[a][1])))
        return tuple(new)

    def fwd_first(k, state):
        return advance(k, state, load_c(v.proj, step_of(k)))

    ends = lax.fori_loop(0, L, fwd_first, zeros, unroll=4)

    def across(values, table, forward):
        done = []
        for a in range(NG):
            x = values[a]
            for i, d in enumerate(LEVELS):
                shift = d if forward else SEG - d
                other = (pltpu.roll(x[0], shift, 0), pltpu.roll(x[1], shift, 0))
                factor = (table[i, a, 0], table[i, a, 1])
                add = cmul(factor, other) if forward else conj_mul(factor, other)
                x = (x[0] + add[0], x[1] + add[1])
            done.append(x)
        return done

    ends = across(ends, v.hs_f, True)
    everyone_in()
    exchange(ahead, [tuple(x[SEG - 1 : SEG, :] for x in ends[a]) for a in range(NG)])
    before = [
        tuple(jnp.where(seg > 0, pltpu.roll(x, 1, 0), 0.0) for x in ends[a]) for a in range(NG)
    ]
    to_state(lambda t: cot.at[t], v.cin.at[:, cols(me_s, W)], C)
    own[OWN_C].wait()
    far_blocks = [lin_block(v.wglu, far), gate_block(v.wglu, far, 0)]
    for i, block in enumerate(far_blocks):
        wait_bytes(block, wt_glu + GLU_FAR + i, True)
        send(block, block, wt_glu + GLU_SIB + i, {STATE: sib})
    w_forward_all(wt_last)
    v.mixed_t[...] = nt(v.eye[...], v.mixed_low[...]).astype(BF16)
    starts = collect(ahead)
    state = []
    for a in range(NG):
        add = cmul((v.lead_pow[a, 0], v.lead_pow[a, 1]), starts[a])
        state.append((before[a][0] + add[0], before[a][1] + add[1]))
    store_c(v.state, pl.ds(0, SEG), state)

    def fwd_second(k, state):
        state = advance(k, state, load_c(v.proj, step_of(k)))
        store_c(v.state, step_of(k + 1), state)
        for a in range(NG):
            v.state_low[step_of(k), lanes(a)] = state[a][0].astype(BF16)
            v.state_low[step_of(k), lanes(NG + a)] = (-state[a][1]).astype(BF16)
        return state

    lax.fori_loop(0, L, fwd_second, tuple(state), unroll=4)

    own[OWN_WOUT].wait()
    w_ready(wt_out)
    v.wide[...] = nn(v.state_low[...], v.wout[...].reshape(CH, H))

    def gelu(i):
        rows = rows_of(i)
        mixed_in = v.normed[rows, :] * gain + bias
        mixed = v.wide[rows, :] + skip * mixed_in
        cdf = 0.5 * (1.0 + lax.erf(mixed * (1.0 / math.sqrt(2.0))))
        density = jnp.exp(-0.5 * mixed * mixed) * (1.0 / math.sqrt(2.0 * math.pi))
        v.act[rows, :] = (mixed * cdf).astype(BF16)
        v.dgelu[rows, :] = cdf + mixed * density

    loop(T // CHUNK, gelu, unroll=4)
    wait_bytes(glu_block(v.wglu, sib), wt_glu + SIB, True)
    for i, block in enumerate([lin_block(v.wglu, sib_far), gate_block(v.wglu, sib_far, 0)]):
        wait_bytes(block, wt_glu + GLU_SIB + i, True)
    wait_bytes(last_block(v.wglu, sib_far), wt_last.step + FAR_SIB, True)
    for k in range(2):
        v.pre[k] = nn(v.act[...], v.wglu[k])

    def glu(i):
        rows = rows_of(i)
        ok = valid_of(i, W)
        for s in range(S):
            here = slice(s * W, (s + 1) * W)
            linear = v.pre[0, rows, here] + par_s[s, 3:4, :]
            gate = v.pre[1, rows, here] + par_s[s, 4:5, :]
            share = jax.nn.sigmoid(gate)
            value = linear * share
            v.out_low[rows, here] = (ok * (v.x[rows, here] + value)).astype(BF16)
            v.pre[0, rows, here] = ok * share
            v.pre[1, rows, here] = ok * (value * (1.0 - share))

    loop(T // CHUNK, glu, unroll=4)

    def give_back(low_ref, nat, result, own_which):
        nat[...] = nn(v.back[...], low_ref[...]).astype(BF16)
        copy = pltpu.make_async_copy(nat.at[:, cols(me_s, W)], result.at[me_s], v.here.at[own_which])
        copy.start()
        return copy

    def give_to(nat, result, which, t):
        send(nat.at[:, cols(t, W)], result.at[me_s], which, {STATE: t})

    out_copy = give_back(v.out_low, v.out_nat, out_ref, OWN_OUT)
    give_to(v.out_nat, out_ref, OUT, far)
    v.act_t[...] = nt(v.eye[...], v.act[...]).astype(BF16)
    wait_bytes(v.cin.at[:, pl.ds(0, (S - 1) * W)], C, True)
    v.wide[...] = nn(v.perm[...], v.cin[...])

    def glu_back(i):
        rows = rows_of(i)
        dout = v.wide[rows, :]
        for k in range(2):
            v.d_pre[k, rows, :] = (dout * v.pre[k, rows, :]).astype(BF16)

    loop(T // CHUNK, glu_back, unroll=4)

    R4 = R // 4 if R % 4 == 0 else R // 2
    sizes = {None: R4, AX_X: NG, AX_Y: 2, AX_Z: 2 if R % 4 == 0 else 1}

    def places(r, b):
        return {AX_X: b, AX_Y: lax.rem(r, 2), AX_Z: lax.rem(lax.div(r, 2), sizes[AX_Z]), None: lax.div(r, 2 * sizes[AX_Z])}

    mine = places(me_r, lax.div(me_s, 2))
    partner = {
        AX_X: {STATE: far},
        AX_Y: {ROWS: pair_r},
        AX_Z: {ROWS: me_r + 2 - 4 * mine[AX_Z]},
    }

    def slot(route, r, b):
        at, index = places(r, b), 0
        for axis in route.axes[1:] + route.others:
            index = index * sizes[axis] + at[axis]
        return at[route.axes[0]], index

    def owner(route, n):
        at = dict(mine)
        for axis in reversed(route.others):
            at[axis] = lax.rem(n, sizes[axis])
            n = lax.div(n, sizes[axis])
        return {ROWS: at[AX_Y] + 2 * (at[AX_Z] + sizes[AX_Z] * at[None]), STATE: 2 * at[AX_X] + mine_s}

    for part in parts:
        for route in part.routes:
            route.others = tuple(axis for axis in sizes if axis not in route.axes)
            route.number = 0
            for axis in route.others:
                route.number = route.number * sizes[axis] + mine[axis]

    def first_send(part):
        for b in range(NG):
            send(part.full.at[:, cols(2 * b + 1 - mine_s, LANES)], part.r1.at[b], part.step, {STATE: sib})

    def first_wait(part):
        wait_bytes(part.r1, part.step, True)

    def first_sum(route):
        part = route.part

        def one(r):
            rows = pl.ds(pl.multiple_of(r * HB + route.first, route.lines), route.lines)
            for b in range(NG):
                total = part.full[rows, cols(2 * b + mine_s, LANES)].astype(F32) + part.r1[b, rows, :].astype(F32)
                route.a[0][slot(route, r, b)] = total.astype(gdt)

        loop(R, one, unroll=4)
        pass_half(route, 0)

    def pass_half(route, i):
        axis = route.axes[i]
        send(route.a[i].at[1 - mine[axis]], route.r[i], route.step + i, partner[axis])

    def next_sum(route, i):
        wait_bytes(route.r[i], route.step + i, True)
        count, last = route.r[i].shape[0], i + 1 == len(route.axes)

        def one(n):
            total = route.a[i][mine[route.axes[i]], n].astype(F32) + route.r[i][n].astype(F32)
            to = n if last else (lax.div(n, count // 2), lax.rem(n, count // 2))
            route.a[i + 1][to] = total.astype(gdt)

        loop(count, one, unroll=4)
        if not last:
            pass_half(route, i + 1)
            return
        done = route.a[i + 1]
        route.last[route.number] = done[route.number]

        def give(d, carry):
            n = d + jnp.where(d >= route.number, 1, 0)
            send(done.at[n], route.last.at[route.number], route.step + len(route.axes), owner(route, n))
            return carry

        lax.fori_loop(0, count - 1, give, 0)

    def last_sum(route):
        count = route.last.shape[0]
        if count > 1:
            wait_bytes(route.last.at[pl.ds(0, count - 1)], route.step + len(route.axes), True)

        def one(n, total):
            return total + route.last[n].astype(F32)

        total = lax.fori_loop(0, count, one, jnp.zeros((route.lines, LANES), F32), unroll=4)
        gsum[route.first : route.first + route.lines, route.part.at : route.part.at + LANES] = total

    def all_sent(part):
        wait_bytes(part.r1, part.step, False)
        for route in part.routes:
            for i in range(len(route.axes)):
                wait_bytes(route.r[i], route.step + i, False)
            if route.last.shape[0] > 1:
                wait_bytes(route.last.at[pl.ds(0, route.last.shape[0] - 1)], route.step + len(route.axes), False)

    def glu_first():
        for part in (g_lin, g_gate):
            first_wait(part)
            first_sum(part.routes[0])

    def glu_next():
        for part in (g_lin, g_gate):
            next_sum(part.routes[0], 0)

    first_half, second_half = me_r < R // 2, me_r >= R // 2
    for k, part in ((0, g_lin), (1, g_gate)):
        part.full[...] = nn(v.act_t[...], v.d_pre[k]).astype(gdt)
        first_send(part)
    v.wide[...] = nt(v.d_pre[0], v.wglu[0]) + nt(v.d_pre[1], v.wglu[1])

    def gelu_back(i, total):
        rows = rows_of(i)
        d_mixed = v.wide[rows, :] * v.dgelu[rows, :]
        v.d_mixed[rows, :] = d_mixed
        v.d_rec[rows, :] = d_mixed.astype(BF16)
        return total + fold(d_mixed * (v.normed[rows, :] * gain + bias))

    d_skip = lax.fori_loop(0, T // CHUNK, gelu_back, jnp.zeros((SUB, H), F32), unroll=4)
    d_skip = jnp.sum(d_skip, axis=0, keepdims=True)
    pl.when(first_half)(glu_first)
    v.source[...] = nt(v.d_rec[...], v.wout[...].reshape(CH, H))
    def retreat(k, source, carry):
        ok = seg * L + k < my_len
        adjoint, new = [], []
        for a in range(NG):
            re, im = carry[a][0] + source[a][0], carry[a][1] - source[a][1]
            adjoint.append((re, im))
            nre, nim = conj_mul(lamb[a], (re, im))
            new.append((jnp.where(ok, nre, re), jnp.where(ok, nim, im)))
        return ok, adjoint, tuple(new)

    def bwd_first(i, carry):
        k = L - 1 - i
        return retreat(k, load_c(v.source, step_of(k)), carry)[2]

    heads = lax.fori_loop(0, L, bwd_first, zeros, unroll=4)
    heads = across(heads, v.hs_b, False)
    exchange(behind, [tuple(x[0:1, :] for x in heads[a]) for a in range(NG)])
    give_to(v.out_nat, out_ref, OUT, sib)
    give_to(v.out_nat, out_ref, OUT, sib_far)
    after = [
        tuple(jnp.where(seg < SEG - 1, pltpu.roll(x, SEG - 1, 0), 0.0) for x in heads[a])
        for a in range(NG)
    ]
    pl.when(second_half)(glu_first)
    v.state_g[...] = nn(v.state_low[...], v.by_shard[...]).astype(BF16)
    g_out.full[...] = tn(v.d_rec[...], v.state_g[...]).astype(gdt)
    first_send(g_out)
    ones = jnp.ones((2 * SUB, T), BF16)
    d_bias = [nn(ones, v.d_pre[k])[0:1, :] for k in range(2)]
    first_wait(g_out)
    first_sum(g_out.routes[0])
    pl.when(first_half)(glu_next)
    omegas = collect(behind)
    carry = []
    for a in range(NG):
        add = conj_mul((v.tail_pow[a, 0], v.tail_pow[a, 1]), omegas[a])
        carry.append((after[a][0] + add[0], after[a][1] + add[1]))

    def bwd_second(i, item):
        k = L - 1 - i
        carry, sums = item
        ok, adjoint, carry = retreat(k, load_c(v.source, step_of(k)), carry)
        previous = load_c(v.state, step_of(k))
        proj = load_c(v.proj, step_of(k))
        new_sums, low_out = [], []
        for a in range(NG):
            re, im = (jnp.where(ok, x, 0.0) for x in adjoint[a])
            dre, dim = conj_mul(previous[a], (re, im))
            dg = re * proj[a][0] + im * proj[a][1]
            new_sums.append(tuple(x + fold(y) for x, y in zip(sums[a], (dre, dim, dg))))
            low_out.append((gamb[a] * re, gamb[a] * im))
        low_out = to_g(low_out)
        for s in range(S):
            v.d_proj[step_of(k), lanes(s)] = low_out[s].astype(BF16)
        return carry, tuple(new_sums)

    zero = jnp.zeros((SUB, LANES), F32)
    _, sums = lax.fori_loop(
        0, L, bwd_second, (tuple(carry), tuple((zero, zero, zero) for _ in range(NG))), unroll=2
    )

    g_in.full[...] = nn(v.mixed_t[...], v.d_proj[...]).astype(gdt)
    first_send(g_in)
    for copy in by_shard:
        copy.wait()
    v.wide[...] = nn(v.d_proj[...], v.win_g[...].reshape(CH, H))
    pl.when(second_half)(glu_next)

    def norm_back(i, totals):
        rows = rows_of(i)
        d_mixed_in = v.wide[rows, :] + skip * v.d_mixed[rows, :]
        normed = v.normed[rows, :]
        inverse = jnp.concatenate([v.inverse[rows, :]] * (H // LANES), axis=1)
        g = d_mixed_in * gain
        first = jnp.mean(g, -1, keepdims=True)
        second = jnp.mean(g * normed, -1, keepdims=True)
        v.din_low[rows, :] = (inverse * (g - first - normed * second)).astype(BF16)
        return totals[0] + fold(d_mixed_in * normed), totals[1] + fold(d_mixed_in)

    zero_h = jnp.zeros((SUB, H), F32)
    d_gain, d_nbias = lax.fori_loop(0, T // CHUNK, norm_back, (zero_h, zero_h), unroll=4)
    d_gain = jnp.sum(d_gain, axis=0, keepdims=True)
    d_nbias = jnp.sum(d_nbias, axis=0, keepdims=True)
    small = v.small
    small[...] = jnp.zeros((S, SUB, LANES), F32)
    for a in range(NG):
        sr, si, sg = (jnp.sum(x, axis=0, keepdims=True) for x in sums[a])
        d_nu = -rate[a] * (sr * lam[a][0] + si * lam[a][1])
        d_theta = angle[a] * (si * lam[a][0] - sr * lam[a][1])
        pair = swap_halves(d_nu, d_theta, low1)
        pair_g = swap_halves(gam[a] * sg, jnp.zeros_like(sg), low1)
        for u in range(2):
            small[2 * a + u, 0:1, :] = pair[u]
            small[2 * a + u, 1:2, :] = pair_g[u]
    for s in range(S):
        here = slice(s * W, (s + 1) * W)
        small[s, 2:3, :] = d_skip[:, here]
        small[s, 3:4, :] = d_bias[0][:, here]
        small[s, 4:5, :] = d_bias[1][:, here]
        small[s, 5:6, :] = d_gain[:, here]
        small[s, 6:7, :] = d_nbias[:, here]
    v.small_r[me_s] = small[...]
    to_state(lambda t: small, v.small_r.at[me_s], SM)
    first_wait(g_in)
    for route in g_in.routes:
        first_sum(route)
    next_sum(g_out.routes[0], 0)
    din_copy = give_back(v.din_low, v.din_nat, din_ref, OWN_DIN)
    for t in (far, sib):
        give_to(v.din_nat, din_ref, DIN, t)
    if len(g_gate.routes[0].axes) > 1:
        next_sum(g_gate.routes[0], 1)
    wait_bytes(v.small_r.at[pl.ds(0, S - 1)], SM, True)
    group = v.small_r[0]
    for s in range(1, S):
        group = group + v.small_r[s]
    small2 = v.small2
    v.group[...] = group
    small2[0:SUB, :] = v.group[me_s]
    for s in range(S):
        small2[SUB + s : SUB + s + 1, :] = group[s, 5:6, :]
        small2[SUB + S + s : SUB + S + s + 1, :] = group[s, 6:7, :]
    v.small2_r[me_r] = small2[...]

    def small_rows(d, carry):
        send(small2, v.small2_r.at[me_r], SN, {ROWS: d + jnp.where(d >= me_r, 1, 0)})
        return carry

    lax.fori_loop(0, R - 1, small_rows, 0)
    for route in g_in.routes:
        next_sum(route, 0)
    give_to(v.din_nat, din_ref, DIN, sib_far)
    if len(g_out.routes[0].axes) > 1:
        next_sum(g_out.routes[0], 1)
    for part in (g_lin, g_gate, g_out):
        last_sum(part.routes[0])
    wait_bytes(v.small2_r.at[pl.ds(0, R - 1)], SN, True)

    def sum_rows(r, total):
        return total + v.small2_r[r]

    vec[...] = lax.fori_loop(0, R, sum_rows, jnp.zeros((2 * SUB, LANES), F32))
    for route in g_in.routes:
        last_sum(route)

    out_copy.wait()
    din_copy.wait()
    wait_bytes(out_ref.at[pl.ds(0, S - 1)], OUT, True)
    wait_bytes(din_ref.at[pl.ds(0, S - 1)], DIN, True)
    wait_bytes(out_ref.at[pl.ds(0, S - 1)], OUT, False)
    wait_bytes(din_ref.at[pl.ds(0, S - 1)], DIN, False)
    wait_bytes(v.par_s.at[pl.ds(0, S - 1)], PAR_S, False)
    wait_bytes(v.xin.at[:, pl.ds(0, (S - 1) * W)], X, False)
    for w in (wt_in, wt_out):
        w_sent(w)
    wait_bytes(glu_own, wt_glu + SIB, False)
    for i, block in enumerate(far_blocks):
        wait_bytes(block, wt_glu + GLU_FAR + i, False)
        wait_bytes(block, wt_glu + GLU_SIB + i, False)
    wait_bytes(last_block(v.wglu, far), wt_last.step + FAR_SIB, False)
    wait_bytes(last_block(v.wglu, far, piece), wt_last.step + FAR, False)
    wait_bytes(wt_last.rest, wt_last.step + PEER, False)
    wait_bytes(v.cin.at[:, pl.ds(0, (S - 1) * W)], C, False)
    carries_sent(ahead)
    carries_sent(behind)
    wait_bytes(v.small_r.at[pl.ds(0, S - 1)], SM, False)
    wait_bytes(v.small2_r.at[pl.ds(0, R - 1)], SN, False)
    for part in parts:
        all_sent(part)


def routes_of(R, H):
    HB = H // R
    if HB % (4 * SUB) == 0:
        routes = [(0, (AX_Y,), 0, HB // 2), (0, (AX_Z if R % 4 == 0 else AX_X,), HB // 2, HB // 2)]
    else:
        routes = [(0, (AX_Y,), 0, HB)]
    if R % 4 == 0:
        return routes + [(1, (AX_X, AX_Y), 0, HB), (2, (AX_Y,), 0, HB), (3, (AX_Z, AX_Y), 0, HB)]
    return routes + [(1, (AX_X,), 0, HB), (2, (AX_Y,), 0, HB), (3, (AX_X,), 0, HB)]


def run_block(dims, *args):
    R, S, T, H, W = dims.R, dims.S, dims.T, dims.H, dims.W
    NR, NG, HB = R * S, S // 2, H // R
    CH, levels = S * LANES, len(LEVELS)
    gdt = BF16 if HB % (2 * SUB) == 0 else F32
    dims.gdt = gdt
    bits = T.bit_length()
    shapes = dict(
        xin=((T, H), BF16),
        cin=((T, H), BF16),
        win=((2, S * HALF, H), BF16),
        wout=((2, S * HALF, H), BF16),
        win_g=((S, 2, HALF, H), BF16),
        by_shard=((CH, CH), BF16),
        state_g=((T, CH), BF16),
        wglu=((2, H, H), BF16),
        glu_raw=((2 * H, W), BF16),
        glu_wide=((2 * CHUNK, W), F32),
        perm=((T, T), BF16),
        back=((T, T), BF16),
        eye=((T, T), BF16),
        mixed_t=((H, T), BF16),
        act_t=((H, T), BF16),
        nu=((1, HALF), F32),
        theta=((1, HALF), F32),
        gamma=((1, HALF), F32),
        skip=((1, W), F32),
        glu_bias=((2, W), F32),
        gain=((1, H), F32),
        bias=((1, H), F32),
        par=((2 * SUB, LANES), F32),
        par_s=((S, 2 * SUB, LANES), F32),
        pows=((bits, NG, 2, SUB, LANES), F32),
        hs_f=((levels, NG, 2, SEG, LANES), F32),
        hs_b=((levels, NG, 2, SEG, LANES), F32),
        lead_pow=((NG, 2, SEG, LANES), F32),
        tail_pow=((NG, 2, SEG, LANES), F32),
        row_pow=((2 * NG, NR, LANES), F32),
        row_hit=((NR, LANES), F32),
        msg_f=((SUB, LANES), F32),
        msg_b=((SUB, LANES), F32),
        row_len=((4 * SUB, LANES), F32),
        chain_f=((NR, SUB, LANES), F32),
        chain_b=((NR, SUB, LANES), F32),
        x=((T, H), F32),
        normed=((T, H), F32),
        inverse=((T, LANES), F32),
        mixed_low=((T, H), BF16),
        wide=((T, max(H, CH)), F32),
        proj=((T, CH), F32),
        state=((T + SEG, CH), F32),
        state_low=((T, CH), BF16),
        act=((T, H), BF16),
        dgelu=((T, H), F32),
        pre=((2, T, H), F32),
        out_low=((T, H), BF16),
        out_nat=((T, H), BF16),
        d_pre=((2, T, H), BF16),
        d_mixed=((T, H), F32),
        d_rec=((T, H), BF16),
        source=((T, CH), F32),
        d_proj=((T, CH), BF16),
        din_low=((T, H), BF16),
        din_nat=((T, H), BF16),
        small=((S, SUB, LANES), F32),
        small_r=((S, S, SUB, LANES), F32),
        group=((S, SUB, LANES), F32),
        small2=((2 * SUB, LANES), F32),
        small2_r=((R, 2 * SUB, LANES), F32),
    )
    scalars = dict(bucket=(S,), lengths=(S,))
    flags = dict(block_in=1, all_in=1)
    copies = dict(here=OWN_WIN_G + S, sent=G2 + 20, received=G2 + 20, sent_f=NR, received_f=NR, sent_b=NR, received_b=NR)
    dims.names = [*shapes, *scalars, *flags, *copies]
    parts = []
    for _ in range(4):
        parts += [(H, CH), (NG, H, LANES)]
    routes = routes_of(R, H)
    for _, axes, _, lines in routes:
        left = [2 * R >> (i + 1) for i in range(len(axes))]
        parts += [(2, n, lines, LANES) for n in left] + [(left[-1], lines, LANES)]
        parts += [(n, lines, LANES) for n in left] + [(left[-1], lines, LANES)]
    scratch = [pltpu.VMEM(shape, dtype) for shape, dtype in shapes.values()]
    scratch += [pltpu.SMEM(shape, jnp.int32) for shape in scalars.values()]
    scratch += [pltpu.SemaphoreType.REGULAR for _ in flags]
    scratch += [pltpu.SemaphoreType.DMA((n,)) for n in copies.values()]
    scratch += [pltpu.VMEM(shape, gdt) for shape in parts]
    any_spec = pl.BlockSpec(memory_space=pl.ANY)
    vmem = pl.BlockSpec(memory_space=pltpu.VMEM)
    macs = T * H * (2 * CH + 2 * H) * 3 + 4 * T * T * H
    return pl.pallas_call(
        functools.partial(block_kernel, dims),
        out_shape=(
            jax.ShapeDtypeStruct((S, T, W), BF16),
            jax.ShapeDtypeStruct((S, T, W), BF16),
            jax.ShapeDtypeStruct((HB, 4 * LANES), F32),
            jax.ShapeDtypeStruct((2 * SUB, LANES), F32),
        ),
        in_specs=[any_spec] * 14,
        out_specs=(any_spec, any_spec, vmem, vmem),
        scratch_shapes=scratch,
        compiler_params=pltpu.CompilerParams(
            collective_id=0, has_side_effects=True, vmem_limit_bytes=56 * 2**20
        ),
        cost_estimate=pl.CostEstimate(flops=2 * macs, bytes_accessed=8 * 2**20, transcendentals=4 * T * H),
    )(*args)


def on_device(
    inputs,
    bucket,
    lengths,
    nu_log,
    theta_log,
    gamma_log,
    in_proj,
    out_proj,
    skip,
    norm_gain,
    norm_bias,
    glu_weight,
    glu_bias,
    output_cotangent,
):
    row_count, seq, part = inputs.shape
    width = norm_gain.shape[0]
    chans = nu_log.shape[0]
    R, S = lax.axis_size(ROWS), lax.axis_size(STATE)
    dims = SimpleNamespace(R=R, S=S, T=seq, H=width, W=part)
    assert row_count == S and 2 * chans == LANES and part == LANES and S % 2 == 0 and R % 2 == 0

    outputs, d_norm, gsum, vec = run_block(
        dims,
        inputs,
        output_cotangent,
        in_proj.transpose(1, 2, 0),
        out_proj,
        glu_weight.reshape(2 * width, part),
        bucket,
        lengths,
        nu_log[None],
        theta_log[None],
        gamma_log[None],
        skip[None],
        glu_bias,
        norm_gain[None],
        norm_bias[None],
    )
    return finish(dims, lengths, outputs, d_norm, output_cotangent, gsum, vec)


def finish_kernel(dims, *refs):
    S, T, HB = dims.S, dims.T, dims.H // dims.R
    (lengths, out_in, d_norm, cot, gsum, vec) = refs[:6]
    (out, d_inputs, d_nu, d_theta, d_gamma, d_in, d_out, d_skip, d_gain, d_bias, d_glu, d_glu_bias) = refs[6:]
    out[...] = out_in[...]
    for row in range(S):
        for first in range(0, T, CHUNK):
            lines = slice(first, first + CHUNK)
            place = lax.broadcasted_iota(jnp.int32, (CHUNK, LANES), 0) + first
            direct = jnp.where(place < lengths[row], cot[row, lines, :].astype(F32), 0.0)
            d_inputs[row, lines, :] = d_norm[row, lines, :].astype(F32) + direct
    d_nu[...] = vec[0:1, 0:HALF]
    d_theta[...] = pltpu.roll(vec[0:1, :], HALF, 1)[:, 0:HALF]
    d_gamma[...] = vec[1:2, 0:HALF]
    d_skip[...] = vec[2:3, :]
    d_glu_bias[...] = vec[3:5, :]
    for s in range(S):
        here = slice(s * LANES, (s + 1) * LANES)
        d_gain[:, here] = vec[SUB + s : SUB + s + 1, :]
        d_bias[:, here] = vec[SUB + S + s : SUB + S + s + 1, :]
    both = gsum[:, 0:LANES]
    d_in[pl.ds(0, HB, stride=2), :] = both[:, 0:HALF]
    d_in[pl.ds(1, HB, stride=2), :] = pltpu.roll(both, HALF, 1)[:, 0:HALF]
    d_out[...] = gsum[:, LANES : 2 * LANES].T
    d_glu[pl.ds(0, HB, stride=2), :] = gsum[:, 2 * LANES : 3 * LANES]
    d_glu[pl.ds(1, HB, stride=2), :] = gsum[:, 3 * LANES : 4 * LANES]


def finish(dims, lengths, outputs, d_norm, cot, gsum, vec):
    R, S, T, H, W = dims.R, dims.S, dims.T, dims.H, dims.W
    HB = H // R
    vmem = pl.BlockSpec(memory_space=pltpu.VMEM)
    small = [(1, HALF)] * 3 + [(2 * HB, HALF), (LANES, HB), (1, W), (1, H), (1, H), (2 * HB, W), (2, W)]
    got = pl.pallas_call(
        functools.partial(finish_kernel, dims),
        out_shape=(
            jax.ShapeDtypeStruct((S, T, W), BF16),
            jax.ShapeDtypeStruct((S, T, W), F32),
            *(jax.ShapeDtypeStruct(shape, F32) for shape in small),
        ),
        in_specs=[pl.BlockSpec(memory_space=pltpu.SMEM)] + [vmem] * 5,
        out_specs=(vmem,) * 12,
    )(lengths, outputs, d_norm, cot, gsum, vec)
    out, d_inputs, d_nu, d_theta, d_gamma, d_in, d_out, d_skip, d_gain, d_bias, d_glu, d_glu_bias = got
    return (
        out,
        d_inputs,
        d_nu.reshape(HALF),
        d_theta.reshape(HALF),
        d_gamma.reshape(HALF),
        d_in.reshape(HB, 2, HALF),
        d_out.reshape(2, HALF, HB),
        d_skip.reshape(W),
        d_gain.reshape(H),
        d_bias.reshape(H),
        d_glu.reshape(HB, 2, W),
        d_glu_bias,
    )


def solution(mesh):
    return jax.shard_map(
        on_device,
        mesh=mesh,
        in_specs=(
            P(ROWS, None, STATE),
            P(ROWS),
            P(ROWS),
            P(STATE),
            P(STATE),
            P(STATE),
            P(None, None, STATE),
            P(None, STATE, None),
            P(STATE),
            P(),
            P(),
            P(None, None, STATE),
            P(None, STATE),
            P(ROWS, None, STATE),
        ),
        out_specs=(
            P(ROWS, None, STATE),
            P(ROWS, None, STATE),
            P(STATE),
            P(STATE),
            P(STATE),
            P(ROWS, None, STATE),
            P(None, STATE, ROWS),
            P(STATE),
            P(),
            P(),
            P(ROWS, None, STATE),
            P(None, STATE),
        ),
        check_vma=False,
    )
```

```python
import functools
import math
from types import SimpleNamespace

import jax
import jax.numpy as jnp
from jax import lax
from jax.experimental import pallas as pl
from jax.experimental.pallas import tpu as pltpu
from jax.sharding import PartitionSpec as P

epsilon = 1e-05

F32 = jnp.float32
BF16 = jnp.bfloat16
MESH = pl.DeviceIdType.MESH
ROWS, STATE = "rows", "state"
SUB = 8
LANES = 128
HALF = LANES // 2
CHUNK = 64
SEG = 32
LEVELS = tuple(1 << i for i in range(SEG.bit_length() - 1))

OWN_X, OWN_WIN, OWN_WOUT, OWN_WGLU, OWN_C, OWN_OUT, OWN_DIN, OWN_SMALL = range(8)
OWN_WIN_G = OWN_SMALL + 9
PAR_S, INFO, INFO_ALL, X, C, OUT, DIN, SM, SN, SB, W1 = range(11)
SIB, FAR, PEER, FAR_SIB = range(4)
GLU_FAR, GLU_SIB = 1, 4
G1 = W1 + 19
G2 = G1 + 4
AX_X, AX_Y, AX_Z = range(3)


def loop(count, body, unroll=1):
    def step(i, carry):
        body(i)
        return carry

    lax.fori_loop(0, count, step, 0, unroll=unroll)


def nn(a, b):
    return lax.dot_general(a, b, (((1,), (0,)), ((), ())), preferred_element_type=F32)


def nt(a, b):
    return lax.dot_general(a, b, (((1,), (1,)), ((), ())), preferred_element_type=F32)


def tn(a, b):
    return lax.dot_general(a, b, (((0,), (0,)), ((), ())), preferred_element_type=F32)


def cmul(a, b):
    return a[0] * b[0] - a[1] * b[1], a[0] * b[1] + a[1] * b[0]


def conj_mul(a, b):
    return a[0] * b[0] + a[1] * b[1], a[0] * b[1] - a[1] * b[0]


def swap_halves(u, v, low):
    return (
        jnp.where(low, u, pltpu.roll(v, HALF, 1)),
        jnp.where(low, pltpu.roll(u, HALF, 1), v),
    )


def fold(x):
    return jnp.sum(x.reshape(x.shape[0] // SUB, SUB, x.shape[1]), axis=0)


def block_kernel(dims, *refs):
    R, S, T, H, W, gdt = dims.R, dims.S, dims.T, dims.H, dims.W, dims.gdt
    NR, NG, R2, HB, L = R * S, S // 2, R // 2, H // R, T // SEG
    Q = 4 if R % 8 == 0 else 2
    G, NB = Q * S, R // Q
    BITS, CH = T.bit_length(), S * LANES
    (inputs, cot, w_in, w_out, w_glu) = refs[:5]
    vectors = refs[5:14]
    (out_ref, din_ref, gsum, vec) = refs[14:18]
    total = 18 + len(dims.names)
    v = SimpleNamespace(**dict(zip(dims.names, refs[18:total])))
    parts = [
        SimpleNamespace(full=refs[total + 2 * i], r1=refs[total + 2 * i + 1], step=G1 + i, at=i * LANES, routes=[])
        for i in range(4)
    ]
    g_in, g_out, g_lin, g_gate = parts
    total += 8
    for i, (part, axes, first, lines) in enumerate(routes_of(R, H)):
        steps = len(axes)
        route = SimpleNamespace(part=parts[part], axes=axes, first=first, lines=lines, step=G2 + 4 * i)
        route.a = refs[total : total + steps + 1]
        route.r = refs[total + steps + 1 : total + 2 * steps + 1]
        route.last = refs[total + 2 * steps + 1]
        total += 2 * steps + 2
        parts[part].routes.append(route)

    me_r, me_s = lax.axis_index(ROWS), lax.axis_index(STATE)
    me = me_r * S + me_s

    def cols(i, width):
        return pl.ds(pl.multiple_of(i * width, LANES), width)

    def lanes(i):
        return slice(i * LANES, (i + 1) * LANES)

    def rows_of(i):
        return pl.ds(pl.multiple_of(i * CHUNK, CHUNK), CHUNK)

    def wait_bytes(ref, which, arrived):
        pltpu.make_async_copy(ref, ref, (v.received if arrived else v.sent).at[which]).wait()

    def send(src, dst, which, target):
        pltpu.make_async_remote_copy(
            src_ref=src,
            dst_ref=dst,
            send_sem=v.sent.at[which],
            recv_sem=v.received.at[which],
            device_id=target,
            device_id_type=MESH,
        ).start()

    def to_state(src_of, dst, which):
        for j in (2, 3, 1) if S == 4 else range(1, S):
            t = lax.rem(me_s + j, S)
            send(src_of(t), dst, which, {STATE: t})

    sib = me_s + 1 - 2 * lax.rem(me_s, 2)
    far = lax.rem(me_s + NG, S)
    sib_far = lax.rem(sib + NG, S)
    pair_r = me_r + 1 - 2 * lax.rem(me_r, 2)
    group_r = me_r - lax.rem(me_r, Q)
    piece = lax.rem(me_r, Q)
    mine_s = lax.rem(me_s, 2)
    mine_r = lax.rem(me_r, 2)

    def line_block(ref, s, p=None):
        size = HALF if p is None else HALF // Q
        first = s * HALF if p is None else s * HALF + p * size
        return ref.at[:, pl.ds(pl.multiple_of(first, size), size), :]

    def glu_block(ref, s):
        return ref.at[:, :, cols(s, W)]

    def lin_block(ref, s):
        return ref.at[0, :, cols(s, W)]

    def gate_block(ref, s, h):
        return ref.at[1, pl.ds(h * (H // 2), H // 2), cols(s, W)]

    def last_block(ref, s, p=None):
        size = H // 2 if p is None else H // 2 // Q
        first = H // 2 if p is None else H // 2 + p * size
        return ref.at[1, pl.ds(pl.multiple_of(first, size), size), cols(s, W)]

    own = [
        (w_glu, v.glu_raw, OWN_WGLU),
        (w_in, line_block(v.win, me_s), OWN_WIN),
        (w_out, line_block(v.wout, me_s), OWN_WOUT),
        (inputs.at[me_s], v.xin.at[:, cols(me_s, W)], OWN_X),
        (cot.at[me_s], v.cin.at[:, cols(me_s, W)], OWN_C),
    ]
    small_in = (v.bucket, v.lengths, v.nu, v.theta, v.gamma, v.skip, v.glu_bias, v.gain, v.bias)
    own += [(a, b, OWN_SMALL + i) for i, (a, b) in enumerate(zip(vectors, small_in))]
    own = {which: pltpu.make_async_copy(a, b, v.here.at[which]) for a, b, which in own}

    barrier = pltpu.get_barrier_semaphore()
    number = piece * S + me_s
    is_gate = (number == 0) & (NB > 1)
    gated = 1 if NB > 1 else 0

    def signal(which, i, rows=None):
        pl.semaphore_signal(
            which,
            inc=1,
            device_id={ROWS: group_r + lax.div(i, S) if rows is None else rows, STATE: lax.rem(i, S)},
            device_id_type=MESH,
        )

    v.chain_f[...] = jnp.zeros((NR, 2 * NG, LANES), F32)
    v.chain_b[...] = jnp.zeros((NR, 2 * NG, LANES), F32)

    for p in range(Q - 1, -1, -1):
        for d in (2, 3, 1, 0) if S == 4 else range(S):
            if (p, d) != (0, 0):
                i = lax.rem(piece + p, Q) * S + lax.rem(me_s + d, S)
                pl.when(i >= gated)(functools.partial(signal, barrier, i))
    for copy in own.values():
        copy.start()
    for i in range(len(vectors)):
        own[OWN_SMALL + i].wait()
    bucket_ref, lengths_ref, nu_ref, theta_ref, gamma_ref, skip_ref, glu_bias_ref, gain_ref, bias_ref = small_in

    par = v.par
    par[...] = jnp.zeros((2 * SUB, LANES), F32)
    par[0:1, 0:HALF] = nu_ref[...]
    par[0:1, HALF:LANES] = theta_ref[...]
    par[1:2, 0:HALF] = gamma_ref[...]
    par[2:3, :] = skip_ref[...]
    par[3:5, :] = glu_bias_ref[...]
    for i in range(S):
        par[SUB + i : SUB + i + 1, :] = jnp.full((1, LANES), bucket_ref[i], jnp.int32).astype(F32)
        par[SUB + S + i : SUB + S + i + 1, :] = jnp.full((1, LANES), lengths_ref[i], jnp.int32).astype(F32)
        v.info[me_r, i : i + 1, :] = jnp.where(
            lax.broadcasted_iota(jnp.int32, (1, LANES), 1) < HALF,
            par[SUB + i : SUB + i + 1, :],
            par[SUB + S + i : SUB + S + i + 1, :],
        )
    v.par_s[me_s] = par[...]

    @pl.when(jnp.logical_not(is_gate))
    def _():
        pl.semaphore_wait(barrier, G - 1)

    if NB > 1:

        @pl.when(number == 1)
        def _():
            signal(v.block_in, jnp.int32(0))

        @pl.when(is_gate)
        def _():
            pl.semaphore_wait(v.block_in, 1)

            def next_gate(d, carry):
                signal(barrier, jnp.int32(0), rows=lax.rem(group_r + d * Q, R))
                return carry

            lax.fori_loop(1, NB, next_gate, 0)

    def pass_on():
        if NB > 1:

            @pl.when(is_gate)
            def _():
                pl.semaphore_wait(barrier, NB - 1)

                def tell(i, carry):
                    signal(v.all_in, i)
                    return carry

                lax.fori_loop(1, G, tell, 0)

    def everyone_in():
        if NB > 1:

            @pl.when(jnp.logical_not(is_gate))
            def _():
                pl.semaphore_wait(v.all_in, 1)

    to_state(lambda t: par, v.par_s.at[me_s], PAR_S)
    for j in range(1, Q):
        send(v.info.at[me_r], v.info.at[me_r], INFO, {ROWS: group_r + lax.rem(piece + j, Q)})

    def w_send(w, own_block, own_piece):
        send(own_piece, w.block(w.ref, me_s, piece), w.step + FAR, {STATE: far})
        send(own_block, w.block(w.ref, me_s), w.step + SIB, {STATE: sib})

    def w_forward_far(w):
        here = w.block(w.ref, far, piece)
        wait_bytes(here, w.step + FAR, True)
        for j in range(1, Q):
            send(here, here, w.step + PEER, {ROWS: group_r + lax.rem(piece + j, Q)})

    def w_forward_all(w):
        wait_bytes(w.rest, w.step + PEER, True)
        send(w.block(w.ref, far), w.block(w.ref, far), w.step + FAR_SIB, {STATE: sib})

    def w_ready(w):
        wait_bytes(w.block(w.ref, sib), w.step + SIB, True)
        wait_bytes(w.block(w.ref, sib_far), w.step + FAR_SIB, True)

    def w_sent(w):
        wait_bytes(w.block(w.ref, sib), w.step + SIB, False)
        wait_bytes(w.block(w.ref, sib), w.step + FAR_SIB, False)
        wait_bytes(w.block(w.ref, sib, piece), w.step + FAR, False)
        wait_bytes(w.rest, w.step + PEER, False)

    others = pl.ds(0, HALF - HALF // Q)
    wt_in = SimpleNamespace(ref=v.win, block=line_block, step=W1, rest=v.win.at[:, others, :])
    wt_out = SimpleNamespace(ref=v.wout, block=line_block, step=W1 + 4, rest=v.wout.at[:, others, :])
    wt_glu = W1 + 8
    wt_last = SimpleNamespace(
        ref=v.wglu, block=last_block, step=W1 + 15, rest=v.wglu.at[1, pl.ds(0, H // 2 - H // 2 // Q), pl.ds(0, W)]
    )

    def piece_of(ref):
        size = HALF // Q
        return ref.at[:, pl.ds(pl.multiple_of(piece * size, size), size), :]

    w_send(wt_in, w_in, piece_of(w_in))
    w_send(wt_out, w_out, piece_of(w_out))
    for t in (far, sib):
        send(inputs.at[t], v.xin.at[:, cols(me_s, W)], X, {STATE: t})
    own[OWN_WGLU].wait()

    def split_glu(i):
        here = rows_of(i)
        v.glu_wide[...] = v.glu_raw[pl.ds(pl.multiple_of(i * 2 * CHUNK, 2 * CHUNK), 2 * CHUNK), :].astype(F32)
        for k in range(2):
            v.wglu[k, here, cols(me_s, W)] = v.glu_wide[pl.ds(k, CHUNK, stride=2), :].astype(BF16)

    loop(H // CHUNK, split_glu)
    block = last_block(v.wglu, me_s, piece)
    send(block, block, wt_last.step + FAR, {STATE: far})
    send(inputs.at[sib_far], v.xin.at[:, cols(me_s, W)], X, {STATE: sib_far})
    glu_own = glu_block(v.wglu, me_s)
    send(glu_own, glu_own, wt_glu + SIB, {STATE: sib})
    first_three = [lin_block(v.wglu, me_s), gate_block(v.wglu, me_s, 0)]
    for i, block in enumerate(first_three):
        send(block, block, wt_glu + GLU_FAR + i, {STATE: far})

    line = lax.broadcasted_iota(jnp.int32, (CHUNK, T), 0)
    place = lax.broadcasted_iota(jnp.int32, (CHUNK, T), 1)

    def orders(i):
        base = pl.multiple_of(i * CHUNK, CHUNK)
        at = line + base
        v.perm[pl.ds(base, CHUNK), :] = (
            place == lax.rem(at, SEG) * L + lax.div(at, SEG)
        ).astype(F32).astype(BF16)
        v.back[pl.ds(base, CHUNK), :] = (
            at == lax.rem(place, SEG) * L + lax.div(place, SEG)
        ).astype(F32).astype(BF16)
        v.eye[pl.ds(base, CHUNK), :] = (place == at).astype(F32).astype(BF16)

    loop(T // CHUNK, orders)
    channel = lax.broadcasted_iota(jnp.int32, (CHUNK, CH), 0)
    goes_to = lax.broadcasted_iota(jnp.int32, (CHUNK, CH), 1)
    taken = (
        (lax.rem(lax.div(goes_to, HALF), 2) * S + lax.div(goes_to, LANES)) * HALF + lax.rem(goes_to, HALF)
    )

    def shard_order(i):
        base = pl.multiple_of(i * CHUNK, CHUNK)
        v.by_shard[pl.ds(base, CHUNK), :] = (taken == channel + base).astype(F32).astype(BF16)

    loop(CH // CHUNK, shard_order)

    w_forward_far(wt_in)
    w_forward_far(wt_out)

    low = lax.broadcasted_iota(jnp.int32, (SEG, LANES), 1) < HALF
    low1 = lax.broadcasted_iota(jnp.int32, (1, LANES), 1) < HALF
    seg = lax.broadcasted_iota(jnp.int32, (SEG, LANES), 0)

    wait_bytes(v.par_s.at[pl.ds(0, S - 1)], PAR_S, True)
    par_s = v.par_s
    lam, gam, rate, angle = [], [], [], []
    for a in range(NG):
        nu, theta = swap_halves(par_s[2 * a, 0:1, :], par_s[2 * a + 1, 0:1, :], low1)
        rate.append(jnp.exp(nu))
        angle.append(jnp.exp(theta))
        magnitude = jnp.exp(-rate[a])
        lam.append((magnitude * jnp.cos(angle[a]), magnitude * jnp.sin(angle[a])))
        gam.append(jnp.exp(swap_halves(par_s[2 * a, 1:2, :], par_s[2 * a + 1, 1:2, :], low1)[0]))
    skip = jnp.concatenate([par_s[s, 2:3, :] for s in range(S)], axis=1)
    gain, bias = gain_ref[...], bias_ref[...]
    power = [[(jnp.broadcast_to(l[0], (SUB, LANES)), jnp.broadcast_to(l[1], (SUB, LANES))) for l in lam]]
    for _ in range(BITS - 1):
        power.append([cmul(p, p) for p in power[-1]])
    for b in range(BITS):
        for a in range(NG):
            for c in range(2):
                v.pows[b, a, c] = power[b][a][c]

    def raised(exponent):
        result = [(jnp.ones(exponent.shape, F32), jnp.zeros(exponent.shape, F32)) for _ in range(NG)]
        for b in range(BITS):
            hit = (lax.shift_right_logical(exponent, b) & 1) == 1
            for a in range(NG):
                re, im = cmul(result[a], (v.pows[b, a, 0, 0:1, :], v.pows[b, a, 1, 0:1, :]))
                result[a] = (jnp.where(hit, re, result[a][0]), jnp.where(hit, im, result[a][1]))
        return result

    my_bucket = par[pl.ds(SUB + me_s, 1), :]
    len1 = par[pl.ds(SUB + S + me_s, 1), :].astype(jnp.int32)
    my_len = jnp.broadcast_to(len1, (SEG, LANES))
    seg_pow = raised(jnp.clip(my_len - seg * L, 0, L))
    lead_pow = raised(jnp.minimum(my_len, seg * L))
    tail_pow = raised(jnp.maximum(my_len - (seg + 1) * L, 0))
    for a in range(NG):
        ahead = seg_pow[a]
        behind = seg_pow[a]
        for i, d in enumerate(LEVELS):
            for c in range(2):
                v.hs_f[i, a, c] = jnp.where(seg >= d, ahead[c], 0.0)
                v.hs_b[i, a, c] = jnp.where(seg < SEG - d, behind[c], 0.0)
            ahead = cmul(ahead, (pltpu.roll(ahead[0], d, 0), pltpu.roll(ahead[1], d, 0)))
            behind = cmul(behind, (pltpu.roll(behind[0], SEG - d, 0), pltpu.roll(behind[1], SEG - d, 0)))
        for c in range(2):
            v.lead_pow[a, c] = lead_pow[a][c]
            v.tail_pow[a, c] = tail_pow[a][c]

    def lines_of(p):
        return pl.ds(pl.multiple_of(p * SUB, SUB), SUB)

    def carry_copy(way, source, t):
        return pltpu.make_async_remote_copy(
            src_ref=way.msg,
            dst_ref=way.chain.at[source],
            send_sem=way.sent.at[t],
            recv_sem=way.received.at[source],
            device_id={ROWS: lax.div(t, S), STATE: lax.rem(t, S)},
            device_id_type=MESH,
        )

    def exchange(way, values):
        for a in range(NG):
            for c in range(2):
                way.msg[pl.ds(c * NG + a, 1), :] = values[a][c]

        def one(i, carry):
            carry_copy(way, me, NR - 1 - i if way.forward else i).start()
            return carry

        lax.fori_loop(0, NR - 1 - me if way.forward else me, one, 0)

    group = min(NR, 4 * SUB)
    low_g = lax.broadcasted_iota(jnp.int32, (group, LANES), 1) < HALF

    def weigh(way):
        def powers(i):
            for j in range(group // S):
                v.row_len[j * S : (j + 1) * S, :] = v.info[i * (group // S) + j]
            both = v.row_len[0:group, :]
            turned = pltpu.roll(both, HALF, 1)
            here = jnp.where(low_g, both, turned)
            lens = jnp.where(low_g, turned, both).astype(jnp.int32)
            p = lax.broadcasted_iota(jnp.int32, (group, LANES), 0) + i * group
            hit = (here == my_bucket) & (my_bucket > 0.5) & ((p < me) if way.forward else (p > me))
            factor = raised(lens)
            at = pl.ds(pl.multiple_of(i * group, SUB), group)
            for a in range(NG):
                v.row_pow[a, at, :] = jnp.where(hit, factor[a][0], 1.0)
                v.row_pow[NG + a, at, :] = jnp.where(hit, factor[a][1], 0.0)
            v.row_hit[at, :] = jnp.where(hit, 1.0, 0.0)

        loop(NR // group, powers)

        def one(i, run):
            p = NR - 1 - i if way.forward else i
            hit = v.row_hit[pl.ds(p, 1), :]
            after = []
            for a in range(NG):
                for c in range(2):
                    for k in range(2):
                        way.weight[c, p, k * NG + a : k * NG + a + 1, :] = hit * run[a][c]
                after.append(cmul((v.row_pow[a, pl.ds(p, 1), :], v.row_pow[NG + a, pl.ds(p, 1), :]), run[a]))
            return tuple(after)

        first = tuple((jnp.ones((1, LANES), F32), jnp.zeros((1, LANES), F32)) for _ in range(NG))
        lax.fori_loop(0, NR, one, first, unroll=4)

    def collect(way):
        def arrive(p, carry):
            carry_copy(way, p, me).wait_recv()
            return carry

        lax.fori_loop(*way.come, arrive, 0)

        def some(i, sums):
            at = pl.ds(i * group, group)
            x = way.chain[at]
            return tuple(sums[c] + jnp.sum(way.weight[c, at] * x, axis=0) for c in range(2))

        zero = jnp.zeros((2 * NG, LANES), F32)
        x, y = lax.fori_loop(0, NR // group, some, (zero, zero))
        sign = 1.0 if way.forward else -1.0
        return [
            (x[a : a + 1] - sign * y[NG + a : NG + a + 1], x[NG + a : NG + a + 1] + sign * y[a : a + 1])
            for a in range(NG)
        ]

    def carries_sent(way):
        def one(t, carry):
            carry_copy(way, me, t).wait_send()
            return carry

        lax.fori_loop(*way.to, one, 0)

    ahead = SimpleNamespace(
        forward=True, msg=v.msg_f, chain=v.chain_f, sent=v.sent_f, received=v.received_f,
        weight=v.weight_f, to=(me + 1, NR), come=(0, me),
    )
    behind = SimpleNamespace(
        forward=False, msg=v.msg_b, chain=v.chain_b, sent=v.sent_b, received=v.received_b,
        weight=v.weight_b, to=(0, me), come=(me + 1, NR),
    )

    pos = lax.broadcasted_iota(jnp.int32, (CHUNK, LANES), 0)
    pos = lax.rem(pos, SEG) * L + lax.div(pos, SEG)

    def valid_of(i, width):
        ok = jnp.where(pos + i * (CHUNK // SEG) < len1, 1.0, 0.0)
        return jnp.concatenate([ok] * (width // LANES), axis=1) if width > LANES else ok

    pass_on()
    w_forward_all(wt_in)
    w_forward_all(wt_out)
    w_forward_far(wt_last)
    wait_bytes(v.info.at[pl.ds(0, Q - 1)], INFO, True)

    own[OWN_X].wait()
    wait_bytes(v.xin.at[:, pl.ds(0, (S - 1) * W)], X, True)
    v.x[...] = nn(v.perm[...], v.xin[...])

    def layer_norm(i):
        rows = rows_of(i)
        x = v.x[rows, :]
        centred = x - jnp.mean(x, -1, keepdims=True)
        inverse = lax.rsqrt(jnp.mean(centred * centred, -1, keepdims=True) + epsilon)
        normed = centred * inverse
        v.normed[rows, :] = normed
        v.inverse[rows, :] = jnp.broadcast_to(inverse, (CHUNK, LANES))
        v.mixed_low[rows, :] = (normed * gain + bias).astype(BF16)

    loop(T // CHUNK, layer_norm, unroll=4)
    own[OWN_WIN].wait()
    w_ready(wt_in)
    v.proj[...] = nt(v.mixed_low[...], v.win[...].reshape(CH, H))
    everyone_in()
    mine_q = v.info.at[pl.ds(pl.multiple_of(group_r, Q), Q)]

    def info_to(d, carry):
        send(mine_q, mine_q, INFO_ALL, {ROWS: lax.rem(me_r + d * Q, R)})
        return carry

    if NB > 1:
        lax.fori_loop(1, NB, info_to, 0)
    by_shard = [
        pltpu.make_async_copy(line_block(v.win, s), v.win_g.at[s], v.here.at[OWN_WIN_G + s]) for s in range(S)
    ]
    for copy in by_shard:
        copy.start()

    lamb = [tuple(jnp.broadcast_to(c, (SEG, LANES)) for c in l) for l in lam]
    gamb = [jnp.broadcast_to(g, (SEG, LANES)) for g in gam]

    def load_c(ref, at):
        return [(ref[at, lanes(a)], ref[at, lanes(NG + a)]) for a in range(NG)]

    def store_c(ref, at, values):
        for a in range(NG):
            ref[at, lanes(a)] = values[a][0]
            ref[at, lanes(NG + a)] = values[a][1]

    def to_g(values):
        return [g for a in range(NG) for g in swap_halves(values[a][0], values[a][1], low)]

    def step_of(k):
        return pl.ds(pl.multiple_of(k * SEG, SEG), SEG)

    zeros = tuple((jnp.zeros((SEG, LANES), F32), jnp.zeros((SEG, LANES), F32)) for _ in range(NG))

    def advance(k, state, proj):
        ok = seg * L + k < my_len
        new = []
        for a in range(NG):
            re, im = cmul(lamb[a], state[a])
            re, im = re + gamb[a] * proj[a][0], im + gamb[a] * proj[a][1]
            new.append((jnp.where(ok, re, state[a][0]), jnp.where(ok, im, state[a][1])))
        return tuple(new)

    def fwd_first(k, state):
        return advance(k, state, load_c(v.proj, step_of(k)))

    ends = lax.fori_loop(0, L, fwd_first, zeros, unroll=4)

    def across(values, table, forward):
        done = []
        for a in range(NG):
            x = values[a]
            for i, d in enumerate(LEVELS):
                shift = d if forward else SEG - d
                other = (pltpu.roll(x[0], shift, 0), pltpu.roll(x[1], shift, 0))
                factor = (table[i, a, 0], table[i, a, 1])
                add = cmul(factor, other) if forward else conj_mul(factor, other)
                x = (x[0] + add[0], x[1] + add[1])
            done.append(x)
        return done

    ends = across(ends, v.hs_f, True)
    exchange(ahead, [tuple(x[SEG - 1 : SEG, :] for x in ends[a]) for a in range(NG)])
    before = [
        tuple(jnp.where(seg > 0, pltpu.roll(x, 1, 0), 0.0) for x in ends[a]) for a in range(NG)
    ]
    to_state(lambda t: cot.at[t], v.cin.at[:, cols(me_s, W)], C)
    own[OWN_C].wait()
    far_blocks = [lin_block(v.wglu, far), gate_block(v.wglu, far, 0)]
    for i, block in enumerate(far_blocks):
        wait_bytes(block, wt_glu + GLU_FAR + i, True)
        send(block, block, wt_glu + GLU_SIB + i, {STATE: sib})
    w_forward_all(wt_last)
    v.mixed_t[...] = nt(v.eye[...], v.mixed_low[...]).astype(BF16)
    if NB > 1:
        wait_bytes(v.info.at[pl.ds(0, R - Q)], INFO_ALL, True)
    weigh(ahead)
    starts = collect(ahead)
    state = []
    for a in range(NG):
        add = cmul((v.lead_pow[a, 0], v.lead_pow[a, 1]), starts[a])
        state.append((before[a][0] + add[0], before[a][1] + add[1]))
    store_c(v.state, pl.ds(0, SEG), state)

    def fwd_second(k, state):
        state = advance(k, state, load_c(v.proj, step_of(k)))
        store_c(v.state, step_of(k + 1), state)
        for a in range(NG):
            v.state_low[step_of(k), lanes(a)] = state[a][0].astype(BF16)
            v.state_low[step_of(k), lanes(NG + a)] = (-state[a][1]).astype(BF16)
        return state

    lax.fori_loop(0, L, fwd_second, tuple(state), unroll=4)

    own[OWN_WOUT].wait()
    w_ready(wt_out)
    v.wide[...] = nn(v.state_low[...], v.wout[...].reshape(CH, H))

    def gelu(i):
        rows = rows_of(i)
        mixed_in = v.normed[rows, :] * gain + bias
        mixed = v.wide[rows, :] + skip * mixed_in
        cdf = 0.5 * (1.0 + lax.erf(mixed * (1.0 / math.sqrt(2.0))))
        density = jnp.exp(-0.5 * mixed * mixed) * (1.0 / math.sqrt(2.0 * math.pi))
        v.act[rows, :] = (mixed * cdf).astype(BF16)
        v.dgelu[rows, :] = cdf + mixed * density

    loop(T // CHUNK, gelu, unroll=4)
    wait_bytes(glu_block(v.wglu, sib), wt_glu + SIB, True)
    for i, block in enumerate([lin_block(v.wglu, sib_far), gate_block(v.wglu, sib_far, 0)]):
        wait_bytes(block, wt_glu + GLU_SIB + i, True)
    wait_bytes(last_block(v.wglu, sib_far), wt_last.step + FAR_SIB, True)
    for k in range(2):
        v.pre[k] = nn(v.act[...], v.wglu[k])

    def glu(i):
        rows = rows_of(i)
        ok = valid_of(i, W)
        for s in range(S):
            here = slice(s * W, (s + 1) * W)
            linear = v.pre[0, rows, here] + par_s[s, 3:4, :]
            gate = v.pre[1, rows, here] + par_s[s, 4:5, :]
            share = jax.nn.sigmoid(gate)
            value = linear * share
            v.out_low[rows, here] = (ok * (v.x[rows, here] + value)).astype(BF16)
            v.pre[0, rows, here] = ok * share
            v.pre[1, rows, here] = ok * (value * (1.0 - share))

    loop(T // CHUNK, glu, unroll=4)

    def give_back(low_ref, nat, result, own_which):
        nat[...] = nn(v.back[...], low_ref[...]).astype(BF16)
        copy = pltpu.make_async_copy(nat.at[:, cols(me_s, W)], result.at[me_s], v.here.at[own_which])
        copy.start()
        return copy

    def give_to(nat, result, which, t):
        send(nat.at[:, cols(t, W)], result.at[me_s], which, {STATE: t})

    out_copy = give_back(v.out_low, v.out_nat, out_ref, OWN_OUT)
    give_to(v.out_nat, out_ref, OUT, far)
    v.act_t[...] = nt(v.eye[...], v.act[...]).astype(BF16)
    wait_bytes(v.cin.at[:, pl.ds(0, (S - 1) * W)], C, True)
    v.wide[...] = nn(v.perm[...], v.cin[...])

    def glu_back(i):
        rows = rows_of(i)
        dout = v.wide[rows, :]
        for k in range(2):
            v.d_pre[k, rows, :] = (dout * v.pre[k, rows, :]).astype(BF16)

    loop(T // CHUNK, glu_back, unroll=4)

    R4 = R // 4 if R % 4 == 0 else R // 2
    sizes = {None: R4, AX_X: NG, AX_Y: 2, AX_Z: 2 if R % 4 == 0 else 1}

    def places(r, b):
        return {AX_X: b, AX_Y: lax.rem(r, 2), AX_Z: lax.rem(lax.div(r, 2), sizes[AX_Z]), None: lax.div(r, 2 * sizes[AX_Z])}

    mine = places(me_r, lax.div(me_s, 2))
    partner = {
        AX_X: {STATE: far},
        AX_Y: {ROWS: pair_r},
        AX_Z: {ROWS: me_r + 2 - 4 * mine[AX_Z]},
    }

    def slot(route, r, b):
        at, index = places(r, b), 0
        for axis in route.axes[1:] + route.others:
            index = index * sizes[axis] + at[axis]
        return at[route.axes[0]], index

    def owner(route, n):
        at = dict(mine)
        for axis in reversed(route.others):
            at[axis] = lax.rem(n, sizes[axis])
            n = lax.div(n, sizes[axis])
        return {ROWS: at[AX_Y] + 2 * (at[AX_Z] + sizes[AX_Z] * at[None]), STATE: 2 * at[AX_X] + mine_s}

    for part in parts:
        for route in part.routes:
            route.others = tuple(axis for axis in sizes if axis not in route.axes)
            route.number = 0
            for axis in route.others:
                route.number = route.number * sizes[axis] + mine[axis]

    def first_send(part):
        for b in range(NG):
            send(part.full.at[:, cols(2 * b + 1 - mine_s, LANES)], part.r1.at[b], part.step, {STATE: sib})

    def first_wait(part):
        wait_bytes(part.r1, part.step, True)

    def first_sum(route):
        part = route.part

        def one(r):
            rows = pl.ds(pl.multiple_of(r * HB + route.first, route.lines), route.lines)
            for b in range(NG):
                total = part.full[rows, cols(2 * b + mine_s, LANES)].astype(F32) + part.r1[b, rows, :].astype(F32)
                route.a[0][slot(route, r, b)] = total.astype(gdt)

        loop(R, one, unroll=4)
        pass_half(route, 0)

    def pass_half(route, i):
        axis = route.axes[i]
        send(route.a[i].at[1 - mine[axis]], route.r[i], route.step + i, partner[axis])

    def next_sum(route, i):
        wait_bytes(route.r[i], route.step + i, True)
        count, last = route.r[i].shape[0], i + 1 == len(route.axes)

        def one(n):
            total = route.a[i][mine[route.axes[i]], n].astype(F32) + route.r[i][n].astype(F32)
            to = n if last else (lax.div(n, count // 2), lax.rem(n, count // 2))
            route.a[i + 1][to] = total.astype(gdt)

        loop(count, one, unroll=4)
        if not last:
            pass_half(route, i + 1)
            return
        done = route.a[i + 1]
        route.last[route.number] = done[route.number]

        def give(d, carry):
            n = d + jnp.where(d >= route.number, 1, 0)
            send(done.at[n], route.last.at[route.number], route.step + len(route.axes), owner(route, n))
            return carry

        lax.fori_loop(0, count - 1, give, 0)

    def last_sum(route):
        count = route.last.shape[0]
        if count > 1:
            wait_bytes(route.last.at[pl.ds(0, count - 1)], route.step + len(route.axes), True)

        def one(n, total):
            return total + route.last[n].astype(F32)

        total = lax.fori_loop(0, count, one, jnp.zeros((route.lines, LANES), F32), unroll=4)
        gsum[route.first : route.first + route.lines, route.part.at : route.part.at + LANES] = total

    def all_sent(part):
        wait_bytes(part.r1, part.step, False)
        for route in part.routes:
            for i in range(len(route.axes)):
                wait_bytes(route.r[i], route.step + i, False)
            if route.last.shape[0] > 1:
                wait_bytes(route.last.at[pl.ds(0, route.last.shape[0] - 1)], route.step + len(route.axes), False)

    def glu_first():
        for part in (g_lin, g_gate):
            first_wait(part)
            first_sum(part.routes[0])

    def glu_next():
        for part in (g_lin, g_gate):
            next_sum(part.routes[0], 0)

    v.wide[...] = nt(v.d_pre[0], v.wglu[0]) + nt(v.d_pre[1], v.wglu[1])

    def gelu_back(i, total):
        rows = rows_of(i)
        d_mixed = v.wide[rows, :] * v.dgelu[rows, :]
        v.d_mixed[rows, :] = d_mixed
        v.d_rec[rows, :] = d_mixed.astype(BF16)
        return total + fold(d_mixed * (v.normed[rows, :] * gain + bias))

    d_skip = lax.fori_loop(0, T // CHUNK, gelu_back, jnp.zeros((SUB, H), F32), unroll=4)
    d_skip = jnp.sum(d_skip, axis=0, keepdims=True)
    v.source[...] = nt(v.d_rec[...], v.wout[...].reshape(CH, H))
    def retreat(k, source, carry):
        ok = seg * L + k < my_len
        adjoint, new = [], []
        for a in range(NG):
            re, im = carry[a][0] + source[a][0], carry[a][1] - source[a][1]
            adjoint.append((re, im))
            nre, nim = conj_mul(lamb[a], (re, im))
            new.append((jnp.where(ok, nre, re), jnp.where(ok, nim, im)))
        return ok, adjoint, tuple(new)

    def bwd_first(i, carry):
        k = L - 1 - i
        return retreat(k, load_c(v.source, step_of(k)), carry)[2]

    heads = lax.fori_loop(0, L, bwd_first, zeros, unroll=4)
    heads = across(heads, v.hs_b, False)
    exchange(behind, [tuple(x[0:1, :] for x in heads[a]) for a in range(NG)])
    give_to(v.out_nat, out_ref, OUT, sib)
    give_to(v.out_nat, out_ref, OUT, sib_far)
    after = [
        tuple(jnp.where(seg < SEG - 1, pltpu.roll(x, SEG - 1, 0), 0.0) for x in heads[a])
        for a in range(NG)
    ]
    for k, part in ((0, g_lin), (1, g_gate)):
        part.full[...] = nn(v.act_t[...], v.d_pre[k]).astype(gdt)
        first_send(part)
    glu_first()
    v.state_g[...] = nn(v.state_low[...], v.by_shard[...]).astype(BF16)
    g_out.full[...] = tn(v.d_rec[...], v.state_g[...]).astype(gdt)
    first_send(g_out)
    ones = jnp.ones((2 * SUB, T), BF16)
    d_bias = [nn(ones, v.d_pre[k])[0:1, :] for k in range(2)]
    first_wait(g_out)
    first_sum(g_out.routes[0])
    weigh(behind)
    omegas = collect(behind)
    carry = []
    for a in range(NG):
        add = conj_mul((v.tail_pow[a, 0], v.tail_pow[a, 1]), omegas[a])
        carry.append((after[a][0] + add[0], after[a][1] + add[1]))

    def bwd_second(i, item):
        k = L - 1 - i
        carry, sums = item
        ok, adjoint, carry = retreat(k, load_c(v.source, step_of(k)), carry)
        previous = load_c(v.state, step_of(k))
        proj = load_c(v.proj, step_of(k))
        new_sums, low_out = [], []
        for a in range(NG):
            re, im = (jnp.where(ok, x, 0.0) for x in adjoint[a])
            dre, dim = conj_mul(previous[a], (re, im))
            dg = re * proj[a][0] + im * proj[a][1]
            new_sums.append(tuple(x + fold(y) for x, y in zip(sums[a], (dre, dim, dg))))
            low_out.append((gamb[a] * re, gamb[a] * im))
        low_out = to_g(low_out)
        for s in range(S):
            v.d_proj[step_of(k), lanes(s)] = low_out[s].astype(BF16)
        return carry, tuple(new_sums)

    zero = jnp.zeros((SUB, LANES), F32)
    _, sums = lax.fori_loop(
        0, L, bwd_second, (tuple(carry), tuple((zero, zero, zero) for _ in range(NG))), unroll=2
    )

    g_in.full[...] = nn(v.mixed_t[...], v.d_proj[...]).astype(gdt)
    first_send(g_in)
    for copy in by_shard:
        copy.wait()
    v.wide[...] = nn(v.d_proj[...], v.win_g[...].reshape(CH, H))
    glu_next()

    def norm_back(i, totals):
        rows = rows_of(i)
        d_mixed_in = v.wide[rows, :] + skip * v.d_mixed[rows, :]
        normed = v.normed[rows, :]
        inverse = jnp.concatenate([v.inverse[rows, :]] * (H // LANES), axis=1)
        g = d_mixed_in * gain
        first = jnp.mean(g, -1, keepdims=True)
        second = jnp.mean(g * normed, -1, keepdims=True)
        v.din_low[rows, :] = (inverse * (g - first - normed * second)).astype(BF16)
        return totals[0] + fold(d_mixed_in * normed), totals[1] + fold(d_mixed_in)

    zero_h = jnp.zeros((SUB, H), F32)
    d_gain, d_nbias = lax.fori_loop(0, T // CHUNK, norm_back, (zero_h, zero_h), unroll=4)
    d_gain = jnp.sum(d_gain, axis=0, keepdims=True)
    d_nbias = jnp.sum(d_nbias, axis=0, keepdims=True)
    small = v.small
    small[...] = jnp.zeros((S, SUB, LANES), F32)
    for a in range(NG):
        sr, si, sg = (jnp.sum(x, axis=0, keepdims=True) for x in sums[a])
        d_nu = -rate[a] * (sr * lam[a][0] + si * lam[a][1])
        d_theta = angle[a] * (si * lam[a][0] - sr * lam[a][1])
        pair = swap_halves(d_nu, d_theta, low1)
        pair_g = swap_halves(gam[a] * sg, jnp.zeros_like(sg), low1)
        for u in range(2):
            small[2 * a + u, 0:1, :] = pair[u]
            small[2 * a + u, 1:2, :] = pair_g[u]
    for s in range(S):
        here = slice(s * W, (s + 1) * W)
        small[s, 2:3, :] = d_skip[:, here]
        small[s, 3:4, :] = d_bias[0][:, here]
        small[s, 4:5, :] = d_bias[1][:, here]
        small[s, 5:6, :] = d_gain[:, here]
        small[s, 6:7, :] = d_nbias[:, here]
    v.small_r[me_s] = small[...]
    to_state(lambda t: small, v.small_r.at[me_s], SM)
    first_wait(g_in)
    for route in g_in.routes:
        first_sum(route)
    next_sum(g_out.routes[0], 0)
    din_copy = give_back(v.din_low, v.din_nat, din_ref, OWN_DIN)
    for t in (far, sib):
        give_to(v.din_nat, din_ref, DIN, t)
    if len(g_gate.routes[0].axes) > 1:
        next_sum(g_gate.routes[0], 1)
    wait_bytes(v.small_r.at[pl.ds(0, S - 1)], SM, True)
    group = v.small_r[0]
    for s in range(1, S):
        group = group + v.small_r[s]
    small2 = v.small2
    v.group[...] = group
    small2[0:SUB, :] = v.group[me_s]
    for s in range(S):
        small2[SUB + s : SUB + s + 1, :] = group[s, 5:6, :]
        small2[SUB + S + s : SUB + S + s + 1, :] = group[s, 6:7, :]
    v.small2_r[piece] = small2[...]
    for j in range(1, Q):
        send(small2, v.small2_r.at[piece], SN, {ROWS: group_r + lax.rem(piece + j, Q)})
    for route in g_in.routes:
        next_sum(route, 0)
    give_to(v.din_nat, din_ref, DIN, sib_far)
    wait_bytes(v.small2_r.at[pl.ds(0, Q - 1)], SN, True)
    small3 = v.small2_r[0]
    for j in range(1, Q):
        small3 = small3 + v.small2_r[j]
    block = lax.div(me_r, Q)
    v.small3_r[block] = small3

    def small_blocks(d, carry):
        send(v.small3_r.at[block], v.small3_r.at[block], SB, {ROWS: lax.rem(me_r + d * Q, R)})
        return carry

    lax.fori_loop(1, NB, small_blocks, 0)
    if len(g_out.routes[0].axes) > 1:
        next_sum(g_out.routes[0], 1)
    for part in (g_lin, g_gate, g_out):
        last_sum(part.routes[0])
    if NB > 1:
        wait_bytes(v.small3_r.at[pl.ds(0, NB - 1)], SB, True)
    total = v.small3_r[0]
    for i in range(1, NB):
        total = total + v.small3_r[i]
    vec[...] = total
    for route in g_in.routes:
        last_sum(route)

    out_copy.wait()
    din_copy.wait()
    wait_bytes(out_ref.at[pl.ds(0, S - 1)], OUT, True)
    wait_bytes(din_ref.at[pl.ds(0, S - 1)], DIN, True)
    wait_bytes(out_ref.at[pl.ds(0, S - 1)], OUT, False)
    wait_bytes(din_ref.at[pl.ds(0, S - 1)], DIN, False)
    wait_bytes(v.par_s.at[pl.ds(0, S - 1)], PAR_S, False)
    wait_bytes(v.info.at[pl.ds(0, Q - 1)], INFO, False)
    if NB > 1:
        wait_bytes(v.info.at[pl.ds(0, R - Q)], INFO_ALL, False)
    wait_bytes(v.xin.at[:, pl.ds(0, (S - 1) * W)], X, False)
    for w in (wt_in, wt_out):
        w_sent(w)
    wait_bytes(glu_own, wt_glu + SIB, False)
    for i, block in enumerate(far_blocks):
        wait_bytes(block, wt_glu + GLU_FAR + i, False)
        wait_bytes(block, wt_glu + GLU_SIB + i, False)
    wait_bytes(last_block(v.wglu, far), wt_last.step + FAR_SIB, False)
    wait_bytes(last_block(v.wglu, far, piece), wt_last.step + FAR, False)
    wait_bytes(wt_last.rest, wt_last.step + PEER, False)
    wait_bytes(v.cin.at[:, pl.ds(0, (S - 1) * W)], C, False)
    carries_sent(ahead)
    carries_sent(behind)
    wait_bytes(v.small_r.at[pl.ds(0, S - 1)], SM, False)
    wait_bytes(v.small2_r.at[pl.ds(0, Q - 1)], SN, False)
    if NB > 1:
        wait_bytes(v.small3_r.at[pl.ds(0, NB - 1)], SB, False)
    for part in parts:
        all_sent(part)


def routes_of(R, H):
    HB = H // R
    if HB % (4 * SUB) == 0:
        routes = [(0, (AX_Y,), 0, HB // 2), (0, (AX_Z if R % 4 == 0 else AX_X,), HB // 2, HB // 2)]
    else:
        routes = [(0, (AX_Y,), 0, HB)]
    if R % 4 == 0:
        return routes + [(1, (AX_X, AX_Y), 0, HB), (2, (AX_Y,), 0, HB), (3, (AX_Z, AX_Y), 0, HB)]
    return routes + [(1, (AX_X,), 0, HB), (2, (AX_Y,), 0, HB), (3, (AX_X,), 0, HB)]


def run_block(dims, *args):
    R, S, T, H, W = dims.R, dims.S, dims.T, dims.H, dims.W
    NR, NG, HB = R * S, S // 2, H // R
    CH, levels = S * LANES, len(LEVELS)
    gdt = BF16 if HB % (2 * SUB) == 0 else F32
    dims.gdt = gdt
    bits = T.bit_length()
    shapes = dict(
        xin=((T, H), BF16),
        cin=((T, H), BF16),
        win=((2, S * HALF, H), BF16),
        wout=((2, S * HALF, H), BF16),
        win_g=((S, 2, HALF, H), BF16),
        by_shard=((CH, CH), BF16),
        state_g=((T, CH), BF16),
        wglu=((2, H, H), BF16),
        glu_raw=((2 * H, W), BF16),
        glu_wide=((2 * CHUNK, W), F32),
        perm=((T, T), BF16),
        back=((T, T), BF16),
        eye=((T, T), BF16),
        mixed_t=((H, T), BF16),
        act_t=((H, T), BF16),
        nu=((1, HALF), F32),
        theta=((1, HALF), F32),
        gamma=((1, HALF), F32),
        skip=((1, W), F32),
        glu_bias=((2, W), F32),
        gain=((1, H), F32),
        bias=((1, H), F32),
        par=((2 * SUB, LANES), F32),
        par_s=((S, 2 * SUB, LANES), F32),
        pows=((bits, NG, 2, SUB, LANES), F32),
        hs_f=((levels, NG, 2, SEG, LANES), F32),
        hs_b=((levels, NG, 2, SEG, LANES), F32),
        lead_pow=((NG, 2, SEG, LANES), F32),
        tail_pow=((NG, 2, SEG, LANES), F32),
        row_pow=((2 * NG, NR, LANES), F32),
        row_hit=((NR, LANES), F32),
        row_len=((4 * SUB, LANES), F32),
        info=((R, S, LANES), F32),
        msg_f=((2 * NG, LANES), F32),
        msg_b=((2 * NG, LANES), F32),
        chain_f=((NR, 2 * NG, LANES), F32),
        chain_b=((NR, 2 * NG, LANES), F32),
        weight_f=((2, NR, 2 * NG, LANES), F32),
        weight_b=((2, NR, 2 * NG, LANES), F32),
        x=((T, H), F32),
        normed=((T, H), F32),
        inverse=((T, LANES), F32),
        mixed_low=((T, H), BF16),
        wide=((T, max(H, CH)), F32),
        proj=((T, CH), F32),
        state=((T + SEG, CH), F32),
        state_low=((T, CH), BF16),
        act=((T, H), BF16),
        dgelu=((T, H), F32),
        pre=((2, T, H), F32),
        out_low=((T, H), BF16),
        out_nat=((T, H), BF16),
        d_pre=((2, T, H), BF16),
        d_mixed=((T, H), F32),
        d_rec=((T, H), BF16),
        source=((T, CH), F32),
        d_proj=((T, CH), BF16),
        din_low=((T, H), BF16),
        din_nat=((T, H), BF16),
        small=((S, SUB, LANES), F32),
        small_r=((S, S, SUB, LANES), F32),
        group=((S, SUB, LANES), F32),
        small2=((2 * SUB, LANES), F32),
        small2_r=((4, 2 * SUB, LANES), F32),
        small3_r=((R // 2, 2 * SUB, LANES), F32),
    )
    scalars = dict(bucket=(S,), lengths=(S,))
    flags = dict(block_in=1, all_in=1)
    copies = dict(here=OWN_WIN_G + S, sent=G2 + 20, received=G2 + 20, sent_f=NR, received_f=NR, sent_b=NR, received_b=NR)
    dims.names = [*shapes, *scalars, *flags, *copies]
    parts = []
    for _ in range(4):
        parts += [(H, CH), (NG, H, LANES)]
    routes = routes_of(R, H)
    for _, axes, _, lines in routes:
        left = [2 * R >> (i + 1) for i in range(len(axes))]
        parts += [(2, n, lines, LANES) for n in left] + [(left[-1], lines, LANES)]
        parts += [(n, lines, LANES) for n in left] + [(left[-1], lines, LANES)]
    scratch = [pltpu.VMEM(shape, dtype) for shape, dtype in shapes.values()]
    scratch += [pltpu.SMEM(shape, jnp.int32) for shape in scalars.values()]
    scratch += [pltpu.SemaphoreType.REGULAR for _ in flags]
    scratch += [pltpu.SemaphoreType.DMA((n,)) for n in copies.values()]
    scratch += [pltpu.VMEM(shape, gdt) for shape in parts]
    any_spec = pl.BlockSpec(memory_space=pl.ANY)
    vmem = pl.BlockSpec(memory_space=pltpu.VMEM)
    macs = T * H * (2 * CH + 2 * H) * 3 + 4 * T * T * H
    return pl.pallas_call(
        functools.partial(block_kernel, dims),
        out_shape=(
            jax.ShapeDtypeStruct((S, T, W), BF16),
            jax.ShapeDtypeStruct((S, T, W), BF16),
            jax.ShapeDtypeStruct((HB, 4 * LANES), F32),
            jax.ShapeDtypeStruct((2 * SUB, LANES), F32),
        ),
        in_specs=[any_spec] * 14,
        out_specs=(any_spec, any_spec, vmem, vmem),
        scratch_shapes=scratch,
        compiler_params=pltpu.CompilerParams(
            collective_id=0, has_side_effects=True, vmem_limit_bytes=56 * 2**20
        ),
        cost_estimate=pl.CostEstimate(flops=2 * macs, bytes_accessed=8 * 2**20, transcendentals=4 * T * H),
    )(*args)


def on_device(
    inputs,
    bucket,
    lengths,
    nu_log,
    theta_log,
    gamma_log,
    in_proj,
    out_proj,
    skip,
    norm_gain,
    norm_bias,
    glu_weight,
    glu_bias,
    output_cotangent,
):
    row_count, seq, part = inputs.shape
    width = norm_gain.shape[0]
    chans = nu_log.shape[0]
    R, S = lax.axis_size(ROWS), lax.axis_size(STATE)
    dims = SimpleNamespace(R=R, S=S, T=seq, H=width, W=part)
    assert row_count == S and 2 * chans == LANES and part == LANES and S % 2 == 0 and R % 2 == 0

    outputs, d_norm, gsum, vec = run_block(
        dims,
        inputs,
        output_cotangent,
        in_proj.transpose(1, 2, 0),
        out_proj,
        glu_weight.reshape(2 * width, part),
        bucket,
        lengths,
        nu_log[None],
        theta_log[None],
        gamma_log[None],
        skip[None],
        glu_bias,
        norm_gain[None],
        norm_bias[None],
    )
    return finish(dims, lengths, outputs, d_norm, output_cotangent, gsum, vec)


def finish_kernel(dims, *refs):
    S, T, HB = dims.S, dims.T, dims.H // dims.R
    (lengths, out_in, d_norm, cot, gsum, vec) = refs[:6]
    (out, d_inputs, d_nu, d_theta, d_gamma, d_in, d_out, d_skip, d_gain, d_bias, d_glu, d_glu_bias) = refs[6:]
    out[...] = out_in[...]
    for row in range(S):
        for first in range(0, T, CHUNK):
            lines = slice(first, first + CHUNK)
            place = lax.broadcasted_iota(jnp.int32, (CHUNK, LANES), 0) + first
            direct = jnp.where(place < lengths[row], cot[row, lines, :].astype(F32), 0.0)
            d_inputs[row, lines, :] = d_norm[row, lines, :].astype(F32) + direct
    d_nu[...] = vec[0:1, 0:HALF]
    d_theta[...] = pltpu.roll(vec[0:1, :], HALF, 1)[:, 0:HALF]
    d_gamma[...] = vec[1:2, 0:HALF]
    d_skip[...] = vec[2:3, :]
    d_glu_bias[...] = vec[3:5, :]
    for s in range(S):
        here = slice(s * LANES, (s + 1) * LANES)
        d_gain[:, here] = vec[SUB + s : SUB + s + 1, :]
        d_bias[:, here] = vec[SUB + S + s : SUB + S + s + 1, :]
    both = gsum[:, 0:LANES]
    d_in[pl.ds(0, HB, stride=2), :] = both[:, 0:HALF]
    d_in[pl.ds(1, HB, stride=2), :] = pltpu.roll(both, HALF, 1)[:, 0:HALF]
    d_out[...] = gsum[:, LANES : 2 * LANES].T
    d_glu[pl.ds(0, HB, stride=2), :] = gsum[:, 2 * LANES : 3 * LANES]
    d_glu[pl.ds(1, HB, stride=2), :] = gsum[:, 3 * LANES : 4 * LANES]


def finish(dims, lengths, outputs, d_norm, cot, gsum, vec):
    R, S, T, H, W = dims.R, dims.S, dims.T, dims.H, dims.W
    HB = H // R
    vmem = pl.BlockSpec(memory_space=pltpu.VMEM)
    small = [(1, HALF)] * 3 + [(2 * HB, HALF), (LANES, HB), (1, W), (1, H), (1, H), (2 * HB, W), (2, W)]
    got = pl.pallas_call(
        functools.partial(finish_kernel, dims),
        out_shape=(
            jax.ShapeDtypeStruct((S, T, W), BF16),
            jax.ShapeDtypeStruct((S, T, W), F32),
            *(jax.ShapeDtypeStruct(shape, F32) for shape in small),
        ),
        in_specs=[pl.BlockSpec(memory_space=pltpu.SMEM)] + [vmem] * 5,
        out_specs=(vmem,) * 12,
    )(lengths, outputs, d_norm, cot, gsum, vec)
    out, d_inputs, d_nu, d_theta, d_gamma, d_in, d_out, d_skip, d_gain, d_bias, d_glu, d_glu_bias = got
    return (
        out,
        d_inputs,
        d_nu.reshape(HALF),
        d_theta.reshape(HALF),
        d_gamma.reshape(HALF),
        d_in.reshape(HB, 2, HALF),
        d_out.reshape(2, HALF, HB),
        d_skip.reshape(W),
        d_gain.reshape(H),
        d_bias.reshape(H),
        d_glu.reshape(HB, 2, W),
        d_glu_bias,
    )


def solution(mesh):
    return jax.shard_map(
        on_device,
        mesh=mesh,
        in_specs=(
            P(ROWS, None, STATE),
            P(ROWS),
            P(ROWS),
            P(STATE),
            P(STATE),
            P(STATE),
            P(None, None, STATE),
            P(None, STATE, None),
            P(STATE),
            P(),
            P(),
            P(None, None, STATE),
            P(None, STATE),
            P(ROWS, None, STATE),
        ),
        out_specs=(
            P(ROWS, None, STATE),
            P(ROWS, None, STATE),
            P(STATE),
            P(STATE),
            P(STATE),
            P(ROWS, None, STATE),
            P(None, STATE, ROWS),
            P(STATE),
            P(),
            P(),
            P(ROWS, None, STATE),
            P(None, STATE),
        ),
        check_vma=False,
    )
```

```python
import functools
import math
from types import SimpleNamespace

import jax
import jax.numpy as jnp
from jax import lax
from jax.experimental import pallas as pl
from jax.experimental.pallas import tpu as pltpu
from jax.sharding import PartitionSpec as P

epsilon = 1e-05

F32 = jnp.float32
BF16 = jnp.bfloat16
MESH = pl.DeviceIdType.MESH
ROWS, STATE = "rows", "state"
SUB = 8
LANES = 128
HALF = LANES // 2
CHUNK = 128
SEG = 32
LEVELS = tuple(1 << i for i in range(SEG.bit_length() - 1))

OWN_X, OWN_WIN, OWN_WOUT, OWN_WGLU, OWN_C, OWN_OUT, OWN_DIN, OWN_SMALL = range(8)
OWN_WIN_G = OWN_SMALL + 9
PAR_S, INFO, INFO_ALL, X, C, OUT, DIN, SM, SN, SB, W1 = range(11)
SIB, FAR, PEER, FAR_SIB = range(4)
GLU_FAR, GLU_SIB = 1, 4
G1 = W1 + 19
G2 = G1 + 4
AX_X, AX_Y, AX_Z = range(3)


def loop(count, body, unroll=1):
    def step(i, carry):
        body(i)
        return carry

    lax.fori_loop(0, count, step, 0, unroll=unroll)


def nn(a, b):
    return lax.dot_general(a, b, (((1,), (0,)), ((), ())), preferred_element_type=F32)


def nt(a, b):
    return lax.dot_general(a, b, (((1,), (1,)), ((), ())), preferred_element_type=F32)


def tn(a, b):
    return lax.dot_general(a, b, (((0,), (0,)), ((), ())), preferred_element_type=F32)


def cmul(a, b):
    return a[0] * b[0] - a[1] * b[1], a[0] * b[1] + a[1] * b[0]


def conj_mul(a, b):
    return a[0] * b[0] + a[1] * b[1], a[0] * b[1] - a[1] * b[0]


def swap_halves(u, v, low):
    return (
        jnp.where(low, u, pltpu.roll(v, HALF, 1)),
        jnp.where(low, pltpu.roll(u, HALF, 1), v),
    )


def fold(x):
    return jnp.sum(x.reshape(x.shape[0] // SUB, SUB, x.shape[1]), axis=0)


def block_kernel(dims, *refs):
    R, S, T, H, W, gdt = dims.R, dims.S, dims.T, dims.H, dims.W, dims.gdt
    NR, NG, R2, HB, L = R * S, S // 2, R // 2, H // R, T // SEG
    Q = 4 if R % 8 == 0 else 2
    G, NB = Q * S, R // Q
    BITS, CH = T.bit_length(), S * LANES
    (inputs, cot, w_in, w_out, w_glu) = refs[:5]
    vectors = refs[5:14]
    (out_ref, din_ref, gsum, vec) = refs[14:18]
    total = 18 + len(dims.names)
    v = SimpleNamespace(**dict(zip(dims.names, refs[18:total])))
    parts = [
        SimpleNamespace(full=refs[total + 2 * i], r1=refs[total + 2 * i + 1], step=G1 + i, at=i * LANES, routes=[])
        for i in range(4)
    ]
    g_in, g_out, g_lin, g_gate = parts
    total += 8
    for i, (part, axes, first, lines) in enumerate(routes_of(R, H)):
        steps = len(axes)
        route = SimpleNamespace(part=parts[part], axes=axes, first=first, lines=lines, step=G2 + 4 * i)
        route.a = refs[total : total + steps + 1]
        route.r = refs[total + steps + 1 : total + 2 * steps + 1]
        route.last = refs[total + 2 * steps + 1]
        total += 2 * steps + 2
        parts[part].routes.append(route)

    me_r, me_s = lax.axis_index(ROWS), lax.axis_index(STATE)
    me = me_r * S + me_s

    def cols(i, width):
        return pl.ds(pl.multiple_of(i * width, LANES), width)

    def lanes(i):
        return slice(i * LANES, (i + 1) * LANES)

    def rows_of(i):
        return pl.ds(pl.multiple_of(i * CHUNK, CHUNK), CHUNK)

    def wait_bytes(ref, which, arrived):
        pltpu.make_async_copy(ref, ref, (v.received if arrived else v.sent).at[which]).wait()

    def send(src, dst, which, target):
        pltpu.make_async_remote_copy(
            src_ref=src,
            dst_ref=dst,
            send_sem=v.sent.at[which],
            recv_sem=v.received.at[which],
            device_id=target,
            device_id_type=MESH,
        ).start()

    def to_state(src_of, dst, which):
        for j in (2, 3, 1) if S == 4 else range(1, S):
            t = lax.rem(me_s + j, S)
            send(src_of(t), dst, which, {STATE: t})

    sib = me_s + 1 - 2 * lax.rem(me_s, 2)
    far = lax.rem(me_s + NG, S)
    sib_far = lax.rem(sib + NG, S)
    pair_r = me_r + 1 - 2 * lax.rem(me_r, 2)
    group_r = me_r - lax.rem(me_r, Q)
    piece = lax.rem(me_r, Q)
    mine_s = lax.rem(me_s, 2)
    mine_r = lax.rem(me_r, 2)

    def line_block(ref, s, p=None):
        size = HALF if p is None else HALF // Q
        first = s * HALF if p is None else s * HALF + p * size
        return ref.at[:, pl.ds(pl.multiple_of(first, size), size), :]

    def glu_block(ref, s):
        return ref.at[:, :, cols(s, W)]

    def lin_block(ref, s):
        return ref.at[0, :, cols(s, W)]

    def gate_block(ref, s, h):
        return ref.at[1, pl.ds(h * (H // 2), H // 2), cols(s, W)]

    def last_block(ref, s, p=None):
        size = H // 2 if p is None else H // 2 // Q
        first = H // 2 if p is None else H // 2 + p * size
        return ref.at[1, pl.ds(pl.multiple_of(first, size), size), cols(s, W)]

    own = [
        (w_glu, v.glu_raw, OWN_WGLU),
        (w_in, line_block(v.win, me_s), OWN_WIN),
        (w_out, line_block(v.wout, me_s), OWN_WOUT),
        (inputs.at[me_s], v.xin.at[:, cols(me_s, W)], OWN_X),
        (cot.at[me_s], v.cin.at[:, cols(me_s, W)], OWN_C),
    ]
    small_in = (v.bucket, v.lengths, v.nu, v.theta, v.gamma, v.skip, v.glu_bias, v.gain, v.bias)
    own += [(a, b, OWN_SMALL + i) for i, (a, b) in enumerate(zip(vectors, small_in))]
    own = {which: pltpu.make_async_copy(a, b, v.here.at[which]) for a, b, which in own}

    barrier = pltpu.get_barrier_semaphore()
    number = piece * S + me_s
    is_gate = (number == 0) & (NB > 1)
    gated = 1 if NB > 1 else 0

    def signal(which, i, rows=None):
        pl.semaphore_signal(
            which,
            inc=1,
            device_id={ROWS: group_r + lax.div(i, S) if rows is None else rows, STATE: lax.rem(i, S)},
            device_id_type=MESH,
        )

    for p in range(Q - 1, -1, -1):
        for d in (2, 3, 1, 0) if S == 4 else range(S):
            if (p, d) != (0, 0):
                i = lax.rem(piece + p, Q) * S + lax.rem(me_s + d, S)
                pl.when(i >= gated)(functools.partial(signal, barrier, i))
    for copy in own.values():
        copy.start()
    for i in range(len(vectors)):
        own[OWN_SMALL + i].wait()
    bucket_ref, lengths_ref, nu_ref, theta_ref, gamma_ref, skip_ref, glu_bias_ref, gain_ref, bias_ref = small_in

    par = v.par
    par[...] = jnp.zeros((2 * SUB, LANES), F32)
    par[0:1, 0:HALF] = nu_ref[...]
    par[0:1, HALF:LANES] = theta_ref[...]
    par[1:2, 0:HALF] = gamma_ref[...]
    par[2:3, :] = skip_ref[...]
    par[3:5, :] = glu_bias_ref[...]
    for i in range(S):
        par[SUB + i : SUB + i + 1, :] = jnp.full((1, LANES), bucket_ref[i], jnp.int32).astype(F32)
        par[SUB + S + i : SUB + S + i + 1, :] = jnp.full((1, LANES), lengths_ref[i], jnp.int32).astype(F32)
        v.info[me_r, i : i + 1, :] = jnp.where(
            lax.broadcasted_iota(jnp.int32, (1, LANES), 1) < HALF,
            par[SUB + i : SUB + i + 1, :],
            par[SUB + S + i : SUB + S + i + 1, :],
        )
    v.par_s[me_s] = par[...]

    @pl.when(jnp.logical_not(is_gate))
    def _():
        pl.semaphore_wait(barrier, G - 1)

    if NB > 1:

        @pl.when(number == 1)
        def _():
            signal(v.block_in, jnp.int32(0))

        @pl.when(is_gate)
        def _():
            pl.semaphore_wait(v.block_in, 1)

            def next_gate(d, carry):
                signal(barrier, jnp.int32(0), rows=lax.rem(group_r + d * Q, R))
                return carry

            lax.fori_loop(1, NB, next_gate, 0)

    def pass_on():
        if NB > 1:

            @pl.when(is_gate)
            def _():
                pl.semaphore_wait(barrier, NB - 1)

                def tell(i, carry):
                    signal(v.all_in, i)
                    return carry

                lax.fori_loop(1, G, tell, 0)

    def everyone_in():
        if NB > 1:

            @pl.when(jnp.logical_not(is_gate))
            def _():
                pl.semaphore_wait(v.all_in, 1)

    to_state(lambda t: par, v.par_s.at[me_s], PAR_S)
    for j in range(1, Q):
        send(v.info.at[me_r], v.info.at[me_r], INFO, {ROWS: group_r + lax.rem(piece + j, Q)})

    def w_send(w, own_block, own_piece):
        send(own_piece, w.block(w.ref, me_s, piece), w.step + FAR, {STATE: far})
        send(own_block, w.block(w.ref, me_s), w.step + SIB, {STATE: sib})

    def w_forward_far(w):
        here = w.block(w.ref, far, piece)
        wait_bytes(here, w.step + FAR, True)
        for j in range(1, Q):
            send(here, here, w.step + PEER, {ROWS: group_r + lax.rem(piece + j, Q)})

    def w_forward_all(w):
        wait_bytes(w.rest, w.step + PEER, True)
        send(w.block(w.ref, far), w.block(w.ref, far), w.step + FAR_SIB, {STATE: sib})

    def w_ready(w):
        wait_bytes(w.block(w.ref, sib), w.step + SIB, True)
        wait_bytes(w.block(w.ref, sib_far), w.step + FAR_SIB, True)

    def w_sent(w):
        wait_bytes(w.block(w.ref, sib), w.step + SIB, False)
        wait_bytes(w.block(w.ref, sib), w.step + FAR_SIB, False)
        wait_bytes(w.block(w.ref, sib, piece), w.step + FAR, False)
        wait_bytes(w.rest, w.step + PEER, False)

    others = pl.ds(0, HALF - HALF // Q)
    wt_in = SimpleNamespace(ref=v.win, block=line_block, step=W1, rest=v.win.at[:, others, :])
    wt_out = SimpleNamespace(ref=v.wout, block=line_block, step=W1 + 4, rest=v.wout.at[:, others, :])
    wt_glu = W1 + 8
    wt_last = SimpleNamespace(
        ref=v.wglu, block=last_block, step=W1 + 15, rest=v.wglu.at[1, pl.ds(0, H // 2 - H // 2 // Q), pl.ds(0, W)]
    )

    def piece_of(ref):
        size = HALF // Q
        return ref.at[:, pl.ds(pl.multiple_of(piece * size, size), size), :]

    w_send(wt_in, w_in, piece_of(w_in))
    w_send(wt_out, w_out, piece_of(w_out))
    for t in (far, sib):
        send(inputs.at[t], v.xin.at[:, cols(me_s, W)], X, {STATE: t})
    own[OWN_WGLU].wait()

    def split_glu(i):
        here = rows_of(i)
        v.glu_wide[...] = v.glu_raw[pl.ds(pl.multiple_of(i * 2 * CHUNK, 2 * CHUNK), 2 * CHUNK), :].astype(F32)
        for k in range(2):
            v.wglu[k, here, cols(me_s, W)] = v.glu_wide[pl.ds(k, CHUNK, stride=2), :].astype(BF16)

    loop(H // CHUNK, split_glu)
    block = last_block(v.wglu, me_s, piece)
    send(block, block, wt_last.step + FAR, {STATE: far})
    send(inputs.at[sib_far], v.xin.at[:, cols(me_s, W)], X, {STATE: sib_far})
    glu_own = glu_block(v.wglu, me_s)
    send(glu_own, glu_own, wt_glu + SIB, {STATE: sib})
    first_three = [lin_block(v.wglu, me_s), gate_block(v.wglu, me_s, 0)]
    for i, block in enumerate(first_three):
        send(block, block, wt_glu + GLU_FAR + i, {STATE: far})

    line = lax.broadcasted_iota(jnp.int32, (CHUNK, T), 0)
    place = lax.broadcasted_iota(jnp.int32, (CHUNK, T), 1)

    def orders(i):
        base = pl.multiple_of(i * CHUNK, CHUNK)
        at = line + base
        v.perm[pl.ds(base, CHUNK), :] = (
            place == lax.rem(at, SEG) * L + lax.div(at, SEG)
        ).astype(F32).astype(BF16)
        v.back[pl.ds(base, CHUNK), :] = (
            at == lax.rem(place, SEG) * L + lax.div(place, SEG)
        ).astype(F32).astype(BF16)
        v.eye[pl.ds(base, CHUNK), :] = (place == at).astype(F32).astype(BF16)

    loop(T // CHUNK, orders)
    channel = lax.broadcasted_iota(jnp.int32, (CHUNK, CH), 0)
    goes_to = lax.broadcasted_iota(jnp.int32, (CHUNK, CH), 1)
    taken = (
        (lax.rem(lax.div(goes_to, HALF), 2) * S + lax.div(goes_to, LANES)) * HALF + lax.rem(goes_to, HALF)
    )

    def shard_order(i):
        base = pl.multiple_of(i * CHUNK, CHUNK)
        v.by_shard[pl.ds(base, CHUNK), :] = (taken == channel + base).astype(F32).astype(BF16)

    loop(CH // CHUNK, shard_order)

    w_forward_far(wt_in)
    w_forward_far(wt_out)

    low = lax.broadcasted_iota(jnp.int32, (SEG, LANES), 1) < HALF
    low1 = lax.broadcasted_iota(jnp.int32, (1, LANES), 1) < HALF
    seg = lax.broadcasted_iota(jnp.int32, (SEG, LANES), 0)

    wait_bytes(v.par_s.at[pl.ds(0, S - 1)], PAR_S, True)
    par_s = v.par_s
    lam, gam, rate, angle = [], [], [], []
    for a in range(NG):
        nu, theta = swap_halves(par_s[2 * a, 0:1, :], par_s[2 * a + 1, 0:1, :], low1)
        rate.append(jnp.exp(nu))
        angle.append(jnp.exp(theta))
        magnitude = jnp.exp(-rate[a])
        lam.append((magnitude * jnp.cos(angle[a]), magnitude * jnp.sin(angle[a])))
        gam.append(jnp.exp(swap_halves(par_s[2 * a, 1:2, :], par_s[2 * a + 1, 1:2, :], low1)[0]))
    skip = jnp.concatenate([par_s[s, 2:3, :] for s in range(S)], axis=1)
    gain, bias = gain_ref[...], bias_ref[...]
    power = [[(jnp.broadcast_to(l[0], (SUB, LANES)), jnp.broadcast_to(l[1], (SUB, LANES))) for l in lam]]
    for _ in range(BITS - 1):
        power.append([cmul(p, p) for p in power[-1]])
    for b in range(BITS):
        for a in range(NG):
            for c in range(2):
                v.pows[b, a, c] = power[b][a][c]

    def raised(exponent):
        result = [(jnp.ones(exponent.shape, F32), jnp.zeros(exponent.shape, F32)) for _ in range(NG)]
        for b in range(BITS):
            hit = (lax.shift_right_logical(exponent, b) & 1) == 1
            for a in range(NG):
                re, im = cmul(result[a], (v.pows[b, a, 0, 0:1, :], v.pows[b, a, 1, 0:1, :]))
                result[a] = (jnp.where(hit, re, result[a][0]), jnp.where(hit, im, result[a][1]))
        return result

    my_bucket = par[pl.ds(SUB + me_s, 1), :]
    len1 = par[pl.ds(SUB + S + me_s, 1), :].astype(jnp.int32)
    my_len = jnp.broadcast_to(len1, (SEG, LANES))
    seg_pow = raised(jnp.clip(my_len - seg * L, 0, L))
    lead_pow = raised(jnp.minimum(my_len, seg * L))
    tail_pow = raised(jnp.maximum(my_len - (seg + 1) * L, 0))
    for a in range(NG):
        ahead = seg_pow[a]
        behind = seg_pow[a]
        for i, d in enumerate(LEVELS):
            for c in range(2):
                v.hs_f[i, a, c] = jnp.where(seg >= d, ahead[c], 0.0)
                v.hs_b[i, a, c] = jnp.where(seg < SEG - d, behind[c], 0.0)
            ahead = cmul(ahead, (pltpu.roll(ahead[0], d, 0), pltpu.roll(ahead[1], d, 0)))
            behind = cmul(behind, (pltpu.roll(behind[0], SEG - d, 0), pltpu.roll(behind[1], SEG - d, 0)))
        for c in range(2):
            v.lead_pow[a, c] = lead_pow[a][c]
            v.tail_pow[a, c] = tail_pow[a][c]

    def lines_of(p):
        return pl.ds(pl.multiple_of(p * SUB, SUB), SUB)

    def carry_copy(way, source, t):
        return pltpu.make_async_remote_copy(
            src_ref=way.msg,
            dst_ref=way.chain.at[source],
            send_sem=way.sent.at[t],
            recv_sem=way.received.at[source],
            device_id={ROWS: lax.div(t, S), STATE: lax.rem(t, S)},
            device_id_type=MESH,
        )

    def exchange(way, values):
        for a in range(NG):
            for c in range(2):
                way.msg[pl.ds(c * NG + a, 1), :] = values[a][c]

        def one(i, carry):
            carry_copy(way, me, me + 1 + i if way.forward else me - 1 - i).start()
            return carry

        lax.fori_loop(0, NR - 1 - me if way.forward else me, one, 0)

    group = min(NR, 4 * SUB)
    low_g = lax.broadcasted_iota(jnp.int32, (group, LANES), 1) < HALF

    def weigh(way):
        def powers(i):
            for j in range(group // S):
                v.row_len[j * S : (j + 1) * S, :] = v.info[i * (group // S) + j]
            both = v.row_len[0:group, :]
            turned = pltpu.roll(both, HALF, 1)
            here = jnp.where(low_g, both, turned)
            lens = jnp.where(low_g, turned, both).astype(jnp.int32)
            p = lax.broadcasted_iota(jnp.int32, (group, LANES), 0) + i * group
            hit = (here == my_bucket) & (my_bucket > 0.5) & ((p < me) if way.forward else (p > me))
            factor = raised(lens)
            at = pl.ds(pl.multiple_of(i * group, SUB), group)
            for a in range(NG):
                v.row_pow[a, at, :] = jnp.where(hit, factor[a][0], 1.0)
                v.row_pow[NG + a, at, :] = jnp.where(hit, factor[a][1], 0.0)
            v.row_hit[at, :] = jnp.where(hit, 1.0, 0.0)

        loop(NR // group, powers)

        def one(i, run):
            p = NR - 1 - i if way.forward else i
            hit = v.row_hit[pl.ds(p, 1), :]
            after = []
            for a in range(NG):
                for c in range(2):
                    for k in range(2):
                        way.weight[c, p, k * NG + a : k * NG + a + 1, :] = hit * run[a][c]
                after.append(cmul((v.row_pow[a, pl.ds(p, 1), :], v.row_pow[NG + a, pl.ds(p, 1), :]), run[a]))
            return tuple(after)

        first = tuple((jnp.ones((1, LANES), F32), jnp.zeros((1, LANES), F32)) for _ in range(NG))
        lax.fori_loop(0, NR, one, first, unroll=4)

    def collect(way):
        def arrive(p, carry):
            carry_copy(way, p, me).wait_recv()
            return carry

        lax.fori_loop(*way.come, arrive, 0)

        def some(i, sums):
            at = pl.ds(i * group, group)
            x = way.chain[at]
            return tuple(
                sums[c] + jnp.sum(jnp.where(way.weight[c, at] == 0.0, 0.0, way.weight[c, at] * x), axis=0)
                for c in range(2)
            )

        zero = jnp.zeros((2 * NG, LANES), F32)
        x, y = lax.fori_loop(0, NR // group, some, (zero, zero))
        sign = 1.0 if way.forward else -1.0
        return [
            (x[a : a + 1] - sign * y[NG + a : NG + a + 1], x[NG + a : NG + a + 1] + sign * y[a : a + 1])
            for a in range(NG)
        ]

    def carries_sent(way):
        def one(t, carry):
            carry_copy(way, me, t).wait_send()
            return carry

        lax.fori_loop(*way.to, one, 0)

    ahead = SimpleNamespace(
        forward=True, msg=v.msg_f, chain=v.chain_f, sent=v.sent_f, received=v.received_f,
        weight=v.weight_f, to=(me + 1, NR), come=(0, me),
    )
    behind = SimpleNamespace(
        forward=False, msg=v.msg_b, chain=v.chain_b, sent=v.sent_b, received=v.received_b,
        weight=v.weight_b, to=(0, me), come=(me + 1, NR),
    )

    pos = lax.broadcasted_iota(jnp.int32, (CHUNK, LANES), 0)
    pos = lax.rem(pos, SEG) * L + lax.div(pos, SEG)

    def valid_of(i, width):
        ok = jnp.where(pos + i * (CHUNK // SEG) < len1, 1.0, 0.0)
        return jnp.concatenate([ok] * (width // LANES), axis=1) if width > LANES else ok

    pass_on()
    w_forward_all(wt_in)
    w_forward_all(wt_out)
    w_forward_far(wt_last)
    wait_bytes(v.info.at[pl.ds(0, Q - 1)], INFO, True)

    own[OWN_X].wait()
    wait_bytes(v.xin.at[:, pl.ds(0, (S - 1) * W)], X, True)
    v.x[...] = nn(v.perm[...], v.xin[...])

    def layer_norm(i):
        rows = rows_of(i)
        x = v.x[rows, :]
        centred = x - jnp.mean(x, -1, keepdims=True)
        inverse = lax.rsqrt(jnp.mean(centred * centred, -1, keepdims=True) + epsilon)
        normed = centred * inverse
        v.normed[rows, :] = normed
        v.inverse[rows, :] = jnp.broadcast_to(inverse, (CHUNK, LANES))
        v.mixed_low[rows, :] = (normed * gain + bias).astype(BF16)

    loop(T // CHUNK, layer_norm, unroll=4)
    own[OWN_WIN].wait()
    w_ready(wt_in)
    v.proj[...] = nt(v.mixed_low[...], v.win[...].reshape(CH, H))
    everyone_in()
    mine_q = v.info.at[pl.ds(pl.multiple_of(group_r, Q), Q)]

    def info_to(d, carry):
        send(mine_q, mine_q, INFO_ALL, {ROWS: lax.rem(me_r + d * Q, R)})
        return carry

    if NB > 1:
        lax.fori_loop(1, NB, info_to, 0)
    by_shard = [
        pltpu.make_async_copy(line_block(v.win, s), v.win_g.at[s], v.here.at[OWN_WIN_G + s]) for s in range(S)
    ]
    for copy in by_shard:
        copy.start()

    lamb = [tuple(jnp.broadcast_to(c, (SEG, LANES)) for c in l) for l in lam]
    gamb = [jnp.broadcast_to(g, (SEG, LANES)) for g in gam]

    def load_c(ref, at):
        return [(ref[at, lanes(a)], ref[at, lanes(NG + a)]) for a in range(NG)]

    def store_c(ref, at, values):
        for a in range(NG):
            ref[at, lanes(a)] = values[a][0]
            ref[at, lanes(NG + a)] = values[a][1]

    def to_g(values):
        return [g for a in range(NG) for g in swap_halves(values[a][0], values[a][1], low)]

    def step_of(k):
        return pl.ds(pl.multiple_of(k * SEG, SEG), SEG)

    zeros = tuple((jnp.zeros((SEG, LANES), F32), jnp.zeros((SEG, LANES), F32)) for _ in range(NG))

    def advance(k, state, proj):
        ok = seg * L + k < my_len
        new = []
        for a in range(NG):
            re, im = cmul(lamb[a], state[a])
            re, im = re + gamb[a] * proj[a][0], im + gamb[a] * proj[a][1]
            new.append((jnp.where(ok, re, state[a][0]), jnp.where(ok, im, state[a][1])))
        return tuple(new)

    def fwd_first(k, state):
        return advance(k, state, load_c(v.proj, step_of(k)))

    ends = lax.fori_loop(0, L, fwd_first, zeros, unroll=4)

    def across(values, table, forward):
        done = []
        for a in range(NG):
            x = values[a]
            for i, d in enumerate(LEVELS):
                shift = d if forward else SEG - d
                other = (pltpu.roll(x[0], shift, 0), pltpu.roll(x[1], shift, 0))
                factor = (table[i, a, 0], table[i, a, 1])
                add = cmul(factor, other) if forward else conj_mul(factor, other)
                x = (x[0] + add[0], x[1] + add[1])
            done.append(x)
        return done

    ends = across(ends, v.hs_f, True)
    exchange(ahead, [tuple(x[SEG - 1 : SEG, :] for x in ends[a]) for a in range(NG)])
    before = [
        tuple(jnp.where(seg > 0, pltpu.roll(x, 1, 0), 0.0) for x in ends[a]) for a in range(NG)
    ]
    to_state(lambda t: cot.at[t], v.cin.at[:, cols(me_s, W)], C)
    own[OWN_C].wait()
    far_blocks = [lin_block(v.wglu, far), gate_block(v.wglu, far, 0)]
    for i, block in enumerate(far_blocks):
        wait_bytes(block, wt_glu + GLU_FAR + i, True)
        send(block, block, wt_glu + GLU_SIB + i, {STATE: sib})
    w_forward_all(wt_last)
    v.mixed_t[...] = nt(v.eye[...], v.mixed_low[...]).astype(BF16)
    if NB > 1:
        wait_bytes(v.info.at[pl.ds(0, R - Q)], INFO_ALL, True)
    weigh(ahead)
    starts = collect(ahead)
    state = []
    for a in range(NG):
        add = cmul((v.lead_pow[a, 0], v.lead_pow[a, 1]), starts[a])
        state.append((before[a][0] + add[0], before[a][1] + add[1]))
    store_c(v.state, pl.ds(0, SEG), state)

    def fwd_second(k, state):
        state = advance(k, state, load_c(v.proj, step_of(k)))
        store_c(v.state, step_of(k + 1), state)
        for a in range(NG):
            v.state_low[step_of(k), lanes(a)] = state[a][0].astype(BF16)
            v.state_low[step_of(k), lanes(NG + a)] = (-state[a][1]).astype(BF16)
        return state

    lax.fori_loop(0, L, fwd_second, tuple(state), unroll=4)

    own[OWN_WOUT].wait()
    w_ready(wt_out)
    v.wide[...] = nn(v.state_low[...], v.wout[...].reshape(CH, H))

    def gelu(i):
        rows = rows_of(i)
        mixed_in = v.normed[rows, :] * gain + bias
        mixed = v.wide[rows, :] + skip * mixed_in
        cdf = 0.5 * (1.0 + lax.erf(mixed * (1.0 / math.sqrt(2.0))))
        density = jnp.exp(-0.5 * mixed * mixed) * (1.0 / math.sqrt(2.0 * math.pi))
        v.act[rows, :] = (mixed * cdf).astype(BF16)
        v.dgelu[rows, :] = cdf + mixed * density

    loop(T // CHUNK, gelu, unroll=4)
    wait_bytes(glu_block(v.wglu, sib), wt_glu + SIB, True)
    for i, block in enumerate([lin_block(v.wglu, sib_far), gate_block(v.wglu, sib_far, 0)]):
        wait_bytes(block, wt_glu + GLU_SIB + i, True)
    wait_bytes(last_block(v.wglu, sib_far), wt_last.step + FAR_SIB, True)
    for k in range(2):
        v.pre[k] = nn(v.act[...], v.wglu[k])

    def glu(i):
        rows = rows_of(i)
        ok = valid_of(i, W)
        for s in range(S):
            here = slice(s * W, (s + 1) * W)
            linear = v.pre[0, rows, here] + par_s[s, 3:4, :]
            gate = v.pre[1, rows, here] + par_s[s, 4:5, :]
            share = jax.nn.sigmoid(gate)
            value = linear * share
            v.out_low[rows, here] = (ok * (v.x[rows, here] + value)).astype(BF16)
            v.pre[0, rows, here] = ok * share
            v.pre[1, rows, here] = ok * (value * (1.0 - share))

    loop(T // CHUNK, glu, unroll=4)

    def give_back(low_ref, nat, result, own_which):
        nat[...] = nn(v.back[...], low_ref[...]).astype(BF16)
        copy = pltpu.make_async_copy(nat.at[:, cols(me_s, W)], result.at[me_s], v.here.at[own_which])
        copy.start()
        return copy

    def give_to(nat, result, which, t):
        send(nat.at[:, cols(t, W)], result.at[me_s], which, {STATE: t})

    out_copy = give_back(v.out_low, v.out_nat, out_ref, OWN_OUT)
    give_to(v.out_nat, out_ref, OUT, far)
    give_to(v.out_nat, out_ref, OUT, sib)
    give_to(v.out_nat, out_ref, OUT, sib_far)
    v.act_t[...] = nt(v.eye[...], v.act[...]).astype(BF16)
    wait_bytes(v.cin.at[:, pl.ds(0, (S - 1) * W)], C, True)
    v.wide[...] = nn(v.perm[...], v.cin[...])

    def glu_back(i):
        rows = rows_of(i)
        dout = v.wide[rows, :]
        for k in range(2):
            v.d_pre[k, rows, :] = (dout * v.pre[k, rows, :]).astype(BF16)

    loop(T // CHUNK, glu_back, unroll=4)

    R4 = R // 4 if R % 4 == 0 else R // 2
    sizes = {None: R4, AX_X: NG, AX_Y: 2, AX_Z: 2 if R % 4 == 0 else 1}

    def places(r, b):
        return {AX_X: b, AX_Y: lax.rem(r, 2), AX_Z: lax.rem(lax.div(r, 2), sizes[AX_Z]), None: lax.div(r, 2 * sizes[AX_Z])}

    mine = places(me_r, lax.div(me_s, 2))
    partner = {
        AX_X: {STATE: far},
        AX_Y: {ROWS: pair_r},
        AX_Z: {ROWS: me_r + 2 - 4 * mine[AX_Z]},
    }

    def slot(route, r, b):
        at, index = places(r, b), 0
        for axis in route.axes[1:] + route.others:
            index = index * sizes[axis] + at[axis]
        return at[route.axes[0]], index

    def owner(route, n):
        at = dict(mine)
        for axis in reversed(route.others):
            at[axis] = lax.rem(n, sizes[axis])
            n = lax.div(n, sizes[axis])
        return {ROWS: at[AX_Y] + 2 * (at[AX_Z] + sizes[AX_Z] * at[None]), STATE: 2 * at[AX_X] + mine_s}

    for part in parts:
        for route in part.routes:
            route.others = tuple(axis for axis in sizes if axis not in route.axes)
            route.number = 0
            for axis in route.others:
                route.number = route.number * sizes[axis] + mine[axis]

    def first_send(part):
        for b in range(NG):
            send(part.full.at[:, cols(2 * b + 1 - mine_s, LANES)], part.r1.at[b], part.step, {STATE: sib})

    def first_wait(part):
        wait_bytes(part.r1, part.step, True)

    def first_sum(route):
        part = route.part

        def one(r):
            rows = pl.ds(pl.multiple_of(r * HB + route.first, route.lines), route.lines)
            for b in range(NG):
                total = part.full[rows, cols(2 * b + mine_s, LANES)].astype(F32) + part.r1[b, rows, :].astype(F32)
                route.a[0][slot(route, r, b)] = total.astype(gdt)

        loop(R, one, unroll=4)
        pass_half(route, 0)

    def pass_half(route, i):
        axis = route.axes[i]
        send(route.a[i].at[1 - mine[axis]], route.r[i], route.step + i, partner[axis])

    def next_sum(route, i):
        wait_bytes(route.r[i], route.step + i, True)
        count, last = route.r[i].shape[0], i + 1 == len(route.axes)

        def one(n):
            total = route.a[i][mine[route.axes[i]], n].astype(F32) + route.r[i][n].astype(F32)
            to = n if last else (lax.div(n, count // 2), lax.rem(n, count // 2))
            route.a[i + 1][to] = total.astype(gdt)

        loop(count, one, unroll=4)
        if not last:
            pass_half(route, i + 1)
            return
        done = route.a[i + 1]
        route.last[route.number] = done[route.number]

        def give(d, carry):
            n = d + jnp.where(d >= route.number, 1, 0)
            send(done.at[n], route.last.at[route.number], route.step + len(route.axes), owner(route, n))
            return carry

        lax.fori_loop(0, count - 1, give, 0)

    def last_sum(route):
        count = route.last.shape[0]
        if count > 1:
            wait_bytes(route.last.at[pl.ds(0, count - 1)], route.step + len(route.axes), True)

        def one(n, total):
            return total + route.last[n].astype(F32)

        total = lax.fori_loop(0, count, one, jnp.zeros((route.lines, LANES), F32), unroll=4)
        gsum[route.first : route.first + route.lines, route.part.at : route.part.at + LANES] = total

    def all_sent(part):
        wait_bytes(part.r1, part.step, False)
        for route in part.routes:
            for i in range(len(route.axes)):
                wait_bytes(route.r[i], route.step + i, False)
            if route.last.shape[0] > 1:
                wait_bytes(route.last.at[pl.ds(0, route.last.shape[0] - 1)], route.step + len(route.axes), False)

    def glu_first():
        for part in (g_lin, g_gate):
            first_wait(part)
            first_sum(part.routes[0])

    def glu_next():
        for part in (g_lin, g_gate):
            next_sum(part.routes[0], 0)

    v.wide[...] = nt(v.d_pre[0], v.wglu[0]) + nt(v.d_pre[1], v.wglu[1])

    def gelu_back(i, total):
        rows = rows_of(i)
        d_mixed = v.wide[rows, :] * v.dgelu[rows, :]
        v.d_mixed[rows, :] = d_mixed
        v.d_rec[rows, :] = d_mixed.astype(BF16)
        return total + fold(d_mixed * (v.normed[rows, :] * gain + bias))

    d_skip = lax.fori_loop(0, T // CHUNK, gelu_back, jnp.zeros((SUB, H), F32), unroll=4)
    d_skip = jnp.sum(d_skip, axis=0, keepdims=True)
    v.source[...] = nt(v.d_rec[...], v.wout[...].reshape(CH, H))
    def retreat(k, source, carry):
        ok = seg * L + k < my_len
        adjoint, new = [], []
        for a in range(NG):
            re, im = carry[a][0] + source[a][0], carry[a][1] - source[a][1]
            adjoint.append((re, im))
            nre, nim = conj_mul(lamb[a], (re, im))
            new.append((jnp.where(ok, nre, re), jnp.where(ok, nim, im)))
        return ok, adjoint, tuple(new)

    def bwd_first(i, carry):
        k = L - 1 - i
        return retreat(k, load_c(v.source, step_of(k)), carry)[2]

    heads = lax.fori_loop(0, L, bwd_first, zeros, unroll=4)
    heads = across(heads, v.hs_b, False)
    exchange(behind, [tuple(x[0:1, :] for x in heads[a]) for a in range(NG)])
    after = [
        tuple(jnp.where(seg < SEG - 1, pltpu.roll(x, SEG - 1, 0), 0.0) for x in heads[a])
        for a in range(NG)
    ]
    for k, part in ((0, g_lin), (1, g_gate)):
        part.full[...] = nn(v.act_t[...], v.d_pre[k]).astype(gdt)
        first_send(part)
    glu_first()
    v.state_g[...] = nn(v.state_low[...], v.by_shard[...]).astype(BF16)
    g_out.full[...] = tn(v.d_rec[...], v.state_g[...]).astype(gdt)
    first_send(g_out)
    ones = jnp.ones((2 * SUB, T), BF16)
    d_bias = [nn(ones, v.d_pre[k])[0:1, :] for k in range(2)]
    first_wait(g_out)
    first_sum(g_out.routes[0])
    weigh(behind)
    omegas = collect(behind)
    carry = []
    for a in range(NG):
        add = conj_mul((v.tail_pow[a, 0], v.tail_pow[a, 1]), omegas[a])
        carry.append((after[a][0] + add[0], after[a][1] + add[1]))

    def bwd_second(i, item):
        k = L - 1 - i
        carry, sums = item
        ok, adjoint, carry = retreat(k, load_c(v.source, step_of(k)), carry)
        previous = load_c(v.state, step_of(k))
        proj = load_c(v.proj, step_of(k))
        new_sums, low_out = [], []
        for a in range(NG):
            re, im = (jnp.where(ok, x, 0.0) for x in adjoint[a])
            dre, dim = conj_mul(previous[a], (re, im))
            dg = re * proj[a][0] + im * proj[a][1]
            new_sums.append(tuple(x + fold(y) for x, y in zip(sums[a], (dre, dim, dg))))
            low_out.append((gamb[a] * re, gamb[a] * im))
        low_out = to_g(low_out)
        for s in range(S):
            v.d_proj[step_of(k), lanes(s)] = low_out[s].astype(BF16)
        return carry, tuple(new_sums)

    zero = jnp.zeros((SUB, LANES), F32)
    _, sums = lax.fori_loop(
        0, L, bwd_second, (tuple(carry), tuple((zero, zero, zero) for _ in range(NG))), unroll=2
    )

    g_in.full[...] = nn(v.mixed_t[...], v.d_proj[...]).astype(gdt)
    first_send(g_in)
    for copy in by_shard:
        copy.wait()
    v.wide[...] = nn(v.d_proj[...], v.win_g[...].reshape(CH, H))
    glu_next()

    def norm_back(i, totals):
        rows = rows_of(i)
        d_mixed_in = v.wide[rows, :] + skip * v.d_mixed[rows, :]
        normed = v.normed[rows, :]
        inverse = jnp.concatenate([v.inverse[rows, :]] * (H // LANES), axis=1)
        g = d_mixed_in * gain
        first = jnp.mean(g, -1, keepdims=True)
        second = jnp.mean(g * normed, -1, keepdims=True)
        v.din_low[rows, :] = (inverse * (g - first - normed * second)).astype(BF16)
        return totals[0] + fold(d_mixed_in * normed), totals[1] + fold(d_mixed_in)

    zero_h = jnp.zeros((SUB, H), F32)
    d_gain, d_nbias = lax.fori_loop(0, T // CHUNK, norm_back, (zero_h, zero_h), unroll=4)
    d_gain = jnp.sum(d_gain, axis=0, keepdims=True)
    d_nbias = jnp.sum(d_nbias, axis=0, keepdims=True)
    small = v.small
    small[...] = jnp.zeros((S, SUB, LANES), F32)
    for a in range(NG):
        sr, si, sg = (jnp.sum(x, axis=0, keepdims=True) for x in sums[a])
        d_nu = -rate[a] * (sr * lam[a][0] + si * lam[a][1])
        d_theta = angle[a] * (si * lam[a][0] - sr * lam[a][1])
        pair = swap_halves(d_nu, d_theta, low1)
        pair_g = swap_halves(gam[a] * sg, jnp.zeros_like(sg), low1)
        for u in range(2):
            small[2 * a + u, 0:1, :] = pair[u]
            small[2 * a + u, 1:2, :] = pair_g[u]
    for s in range(S):
        here = slice(s * W, (s + 1) * W)
        small[s, 2:3, :] = d_skip[:, here]
        small[s, 3:4, :] = d_bias[0][:, here]
        small[s, 4:5, :] = d_bias[1][:, here]
        small[s, 5:6, :] = d_gain[:, here]
        small[s, 6:7, :] = d_nbias[:, here]
    v.small_r[me_s] = small[...]
    to_state(lambda t: small, v.small_r.at[me_s], SM)
    first_wait(g_in)
    for route in g_in.routes:
        first_sum(route)
    next_sum(g_out.routes[0], 0)
    din_copy = give_back(v.din_low, v.din_nat, din_ref, OWN_DIN)
    for t in (far, sib):
        give_to(v.din_nat, din_ref, DIN, t)
    if len(g_gate.routes[0].axes) > 1:
        next_sum(g_gate.routes[0], 1)
    wait_bytes(v.small_r.at[pl.ds(0, S - 1)], SM, True)
    group = v.small_r[0]
    for s in range(1, S):
        group = group + v.small_r[s]
    small2 = v.small2
    v.group[...] = group
    small2[0:SUB, :] = v.group[me_s]
    for s in range(S):
        small2[SUB + s : SUB + s + 1, :] = group[s, 5:6, :]
        small2[SUB + S + s : SUB + S + s + 1, :] = group[s, 6:7, :]
    v.small2_r[piece] = small2[...]
    for j in range(1, Q):
        send(small2, v.small2_r.at[piece], SN, {ROWS: group_r + lax.rem(piece + j, Q)})
    for route in g_in.routes:
        next_sum(route, 0)
    give_to(v.din_nat, din_ref, DIN, sib_far)
    wait_bytes(v.small2_r.at[pl.ds(0, Q - 1)], SN, True)
    small3 = v.small2_r[0]
    for j in range(1, Q):
        small3 = small3 + v.small2_r[j]
    block = lax.div(me_r, Q)
    v.small3_r[block] = small3

    def small_blocks(d, carry):
        send(v.small3_r.at[block], v.small3_r.at[block], SB, {ROWS: lax.rem(me_r + d * Q, R)})
        return carry

    lax.fori_loop(1, NB, small_blocks, 0)
    if len(g_out.routes[0].axes) > 1:
        next_sum(g_out.routes[0], 1)
    for part in (g_lin, g_gate, g_out):
        last_sum(part.routes[0])
    if NB > 1:
        wait_bytes(v.small3_r.at[pl.ds(0, NB - 1)], SB, True)
    total = v.small3_r[0]
    for i in range(1, NB):
        total = total + v.small3_r[i]
    vec[...] = total
    for route in g_in.routes:
        last_sum(route)

    out_copy.wait()
    din_copy.wait()
    wait_bytes(out_ref.at[pl.ds(0, S - 1)], OUT, True)
    wait_bytes(din_ref.at[pl.ds(0, S - 1)], DIN, True)
    wait_bytes(out_ref.at[pl.ds(0, S - 1)], OUT, False)
    wait_bytes(din_ref.at[pl.ds(0, S - 1)], DIN, False)
    wait_bytes(v.par_s.at[pl.ds(0, S - 1)], PAR_S, False)
    wait_bytes(v.info.at[pl.ds(0, Q - 1)], INFO, False)
    if NB > 1:
        wait_bytes(v.info.at[pl.ds(0, R - Q)], INFO_ALL, False)
    wait_bytes(v.xin.at[:, pl.ds(0, (S - 1) * W)], X, False)
    for w in (wt_in, wt_out):
        w_sent(w)
    wait_bytes(glu_own, wt_glu + SIB, False)
    for i, block in enumerate(far_blocks):
        wait_bytes(block, wt_glu + GLU_FAR + i, False)
        wait_bytes(block, wt_glu + GLU_SIB + i, False)
    wait_bytes(last_block(v.wglu, far), wt_last.step + FAR_SIB, False)
    wait_bytes(last_block(v.wglu, far, piece), wt_last.step + FAR, False)
    wait_bytes(wt_last.rest, wt_last.step + PEER, False)
    wait_bytes(v.cin.at[:, pl.ds(0, (S - 1) * W)], C, False)
    carries_sent(ahead)
    carries_sent(behind)
    wait_bytes(v.small_r.at[pl.ds(0, S - 1)], SM, False)
    wait_bytes(v.small2_r.at[pl.ds(0, Q - 1)], SN, False)
    if NB > 1:
        wait_bytes(v.small3_r.at[pl.ds(0, NB - 1)], SB, False)
    for part in parts:
        all_sent(part)


def routes_of(R, H):
    HB = H // R
    if HB % (4 * SUB) == 0:
        routes = [(0, (AX_Y,), 0, HB // 2), (0, (AX_Z if R % 4 == 0 else AX_X,), HB // 2, HB // 2)]
    else:
        routes = [(0, (AX_Y,), 0, HB)]
    if R % 4 == 0:
        return routes + [(1, (AX_X, AX_Y), 0, HB), (2, (AX_Y,), 0, HB), (3, (AX_Z, AX_Y), 0, HB)]
    return routes + [(1, (AX_X,), 0, HB), (2, (AX_Y,), 0, HB), (3, (AX_X,), 0, HB)]


def run_block(dims, *args):
    R, S, T, H, W = dims.R, dims.S, dims.T, dims.H, dims.W
    NR, NG, HB = R * S, S // 2, H // R
    CH, levels = S * LANES, len(LEVELS)
    gdt = BF16 if HB % (2 * SUB) == 0 else F32
    dims.gdt = gdt
    bits = T.bit_length()
    shapes = dict(
        xin=((T, H), BF16),
        cin=((T, H), BF16),
        win=((2, S * HALF, H), BF16),
        wout=((2, S * HALF, H), BF16),
        win_g=((S, 2, HALF, H), BF16),
        by_shard=((CH, CH), BF16),
        state_g=((T, CH), BF16),
        wglu=((2, H, H), BF16),
        glu_raw=((2 * H, W), BF16),
        glu_wide=((2 * CHUNK, W), F32),
        perm=((T, T), BF16),
        back=((T, T), BF16),
        eye=((T, T), BF16),
        mixed_t=((H, T), BF16),
        act_t=((H, T), BF16),
        nu=((1, HALF), F32),
        theta=((1, HALF), F32),
        gamma=((1, HALF), F32),
        skip=((1, W), F32),
        glu_bias=((2, W), F32),
        gain=((1, H), F32),
        bias=((1, H), F32),
        par=((2 * SUB, LANES), F32),
        par_s=((S, 2 * SUB, LANES), F32),
        pows=((bits, NG, 2, SUB, LANES), F32),
        hs_f=((levels, NG, 2, SEG, LANES), F32),
        hs_b=((levels, NG, 2, SEG, LANES), F32),
        lead_pow=((NG, 2, SEG, LANES), F32),
        tail_pow=((NG, 2, SEG, LANES), F32),
        row_pow=((2 * NG, NR, LANES), F32),
        row_hit=((NR, LANES), F32),
        row_len=((4 * SUB, LANES), F32),
        info=((R, S, LANES), F32),
        msg_f=((2 * NG, LANES), F32),
        msg_b=((2 * NG, LANES), F32),
        chain_f=((NR, 2 * NG, LANES), F32),
        chain_b=((NR, 2 * NG, LANES), F32),
        weight_f=((2, NR, 2 * NG, LANES), F32),
        weight_b=((2, NR, 2 * NG, LANES), F32),
        x=((T, H), F32),
        normed=((T, H), F32),
        inverse=((T, LANES), F32),
        mixed_low=((T, H), BF16),
        wide=((T, max(H, CH)), F32),
        proj=((T, CH), F32),
        state=((T + SEG, CH), F32),
        state_low=((T, CH), BF16),
        act=((T, H), BF16),
        dgelu=((T, H), F32),
        pre=((2, T, H), F32),
        out_low=((T, H), BF16),
        out_nat=((T, H), BF16),
        d_pre=((2, T, H), BF16),
        d_mixed=((T, H), F32),
        d_rec=((T, H), BF16),
        source=((T, CH), F32),
        d_proj=((T, CH), BF16),
        din_low=((T, H), BF16),
        din_nat=((T, H), BF16),
        small=((S, SUB, LANES), F32),
        small_r=((S, S, SUB, LANES), F32),
        group=((S, SUB, LANES), F32),
        small2=((2 * SUB, LANES), F32),
        small2_r=((4, 2 * SUB, LANES), F32),
        small3_r=((R // 2, 2 * SUB, LANES), F32),
    )
    scalars = dict(bucket=(S,), lengths=(S,))
    flags = dict(block_in=1, all_in=1)
    copies = dict(here=OWN_WIN_G + S, sent=G2 + 20, received=G2 + 20, sent_f=NR, received_f=NR, sent_b=NR, received_b=NR)
    dims.names = [*shapes, *scalars, *flags, *copies]
    parts = []
    for _ in range(4):
        parts += [(H, CH), (NG, H, LANES)]
    routes = routes_of(R, H)
    for _, axes, _, lines in routes:
        left = [2 * R >> (i + 1) for i in range(len(axes))]
        parts += [(2, n, lines, LANES) for n in left] + [(left[-1], lines, LANES)]
        parts += [(n, lines, LANES) for n in left] + [(left[-1], lines, LANES)]
    scratch = [pltpu.VMEM(shape, dtype) for shape, dtype in shapes.values()]
    scratch += [pltpu.SMEM(shape, jnp.int32) for shape in scalars.values()]
    scratch += [pltpu.SemaphoreType.REGULAR for _ in flags]
    scratch += [pltpu.SemaphoreType.DMA((n,)) for n in copies.values()]
    scratch += [pltpu.VMEM(shape, gdt) for shape in parts]
    any_spec = pl.BlockSpec(memory_space=pl.ANY)
    vmem = pl.BlockSpec(memory_space=pltpu.VMEM)
    macs = T * H * (2 * CH + 2 * H) * 3 + 4 * T * T * H
    return pl.pallas_call(
        functools.partial(block_kernel, dims),
        out_shape=(
            jax.ShapeDtypeStruct((S, T, W), BF16),
            jax.ShapeDtypeStruct((S, T, W), BF16),
            jax.ShapeDtypeStruct((HB, 4 * LANES), F32),
            jax.ShapeDtypeStruct((2 * SUB, LANES), F32),
        ),
        in_specs=[any_spec] * 14,
        out_specs=(any_spec, any_spec, vmem, vmem),
        scratch_shapes=scratch,
        compiler_params=pltpu.CompilerParams(
            collective_id=0, has_side_effects=True, vmem_limit_bytes=56 * 2**20
        ),
        cost_estimate=pl.CostEstimate(flops=2 * macs, bytes_accessed=8 * 2**20, transcendentals=4 * T * H),
    )(*args)


def on_device(
    inputs,
    bucket,
    lengths,
    nu_log,
    theta_log,
    gamma_log,
    in_proj,
    out_proj,
    skip,
    norm_gain,
    norm_bias,
    glu_weight,
    glu_bias,
    output_cotangent,
):
    row_count, seq, part = inputs.shape
    width = norm_gain.shape[0]
    chans = nu_log.shape[0]
    R, S = lax.axis_size(ROWS), lax.axis_size(STATE)
    dims = SimpleNamespace(R=R, S=S, T=seq, H=width, W=part)
    assert row_count == S and 2 * chans == LANES and part == LANES and S % 2 == 0 and R % 2 == 0

    outputs, d_norm, gsum, vec = run_block(
        dims,
        inputs,
        output_cotangent,
        in_proj.transpose(1, 2, 0),
        out_proj,
        glu_weight.reshape(2 * width, part),
        bucket,
        lengths,
        nu_log[None],
        theta_log[None],
        gamma_log[None],
        skip[None],
        glu_bias,
        norm_gain[None],
        norm_bias[None],
    )
    return finish(dims, lengths, outputs, d_norm, output_cotangent, gsum, vec)


def finish_kernel(dims, *refs):
    S, T, HB = dims.S, dims.T, dims.H // dims.R
    (lengths, out_in, d_norm, cot, gsum, vec) = refs[:6]
    (out, d_inputs, d_nu, d_theta, d_gamma, d_in, d_out, d_skip, d_gain, d_bias, d_glu, d_glu_bias) = refs[6:]
    out[...] = out_in[...]
    for row in range(S):
        for first in range(0, T, CHUNK):
            lines = slice(first, first + CHUNK)
            place = lax.broadcasted_iota(jnp.int32, (CHUNK, LANES), 0) + first
            direct = jnp.where(place < lengths[row], cot[row, lines, :].astype(F32), 0.0)
            d_inputs[row, lines, :] = d_norm[row, lines, :].astype(F32) + direct
    d_nu[...] = vec[0:1, 0:HALF]
    d_theta[...] = pltpu.roll(vec[0:1, :], HALF, 1)[:, 0:HALF]
    d_gamma[...] = vec[1:2, 0:HALF]
    d_skip[...] = vec[2:3, :]
    d_glu_bias[...] = vec[3:5, :]
    for s in range(S):
        here = slice(s * LANES, (s + 1) * LANES)
        d_gain[:, here] = vec[SUB + s : SUB + s + 1, :]
        d_bias[:, here] = vec[SUB + S + s : SUB + S + s + 1, :]
    both = gsum[:, 0:LANES]
    d_in[pl.ds(0, HB, stride=2), :] = both[:, 0:HALF]
    d_in[pl.ds(1, HB, stride=2), :] = pltpu.roll(both, HALF, 1)[:, 0:HALF]
    d_out[...] = gsum[:, LANES : 2 * LANES].T
    d_glu[pl.ds(0, HB, stride=2), :] = gsum[:, 2 * LANES : 3 * LANES]
    d_glu[pl.ds(1, HB, stride=2), :] = gsum[:, 3 * LANES : 4 * LANES]


def finish(dims, lengths, outputs, d_norm, cot, gsum, vec):
    R, S, T, H, W = dims.R, dims.S, dims.T, dims.H, dims.W
    HB = H // R
    vmem = pl.BlockSpec(memory_space=pltpu.VMEM)
    small = [(1, HALF)] * 3 + [(2 * HB, HALF), (LANES, HB), (1, W), (1, H), (1, H), (2 * HB, W), (2, W)]
    got = pl.pallas_call(
        functools.partial(finish_kernel, dims),
        out_shape=(
            jax.ShapeDtypeStruct((S, T, W), BF16),
            jax.ShapeDtypeStruct((S, T, W), F32),
            *(jax.ShapeDtypeStruct(shape, F32) for shape in small),
        ),
        in_specs=[pl.BlockSpec(memory_space=pltpu.SMEM)] + [vmem] * 5,
        out_specs=(vmem,) * 12,
    )(lengths, outputs, d_norm, cot, gsum, vec)
    out, d_inputs, d_nu, d_theta, d_gamma, d_in, d_out, d_skip, d_gain, d_bias, d_glu, d_glu_bias = got
    return (
        out,
        d_inputs,
        d_nu.reshape(HALF),
        d_theta.reshape(HALF),
        d_gamma.reshape(HALF),
        d_in.reshape(HB, 2, HALF),
        d_out.reshape(2, HALF, HB),
        d_skip.reshape(W),
        d_gain.reshape(H),
        d_bias.reshape(H),
        d_glu.reshape(HB, 2, W),
        d_glu_bias,
    )


def solution(mesh):
    return jax.shard_map(
        on_device,
        mesh=mesh,
        in_specs=(
            P(ROWS, None, STATE),
            P(ROWS),
            P(ROWS),
            P(STATE),
            P(STATE),
            P(STATE),
            P(None, None, STATE),
            P(None, STATE, None),
            P(STATE),
            P(),
            P(),
            P(None, None, STATE),
            P(None, STATE),
            P(ROWS, None, STATE),
        ),
        out_specs=(
            P(ROWS, None, STATE),
            P(ROWS, None, STATE),
            P(STATE),
            P(STATE),
            P(STATE),
            P(ROWS, None, STATE),
            P(None, STATE, ROWS),
            P(STATE),
            P(),
            P(),
            P(ROWS, None, STATE),
            P(None, STATE),
        ),
        check_vma=False,
    )
```

```python
import functools
import math
from types import SimpleNamespace

import jax
import jax.numpy as jnp
from jax import lax
from jax.experimental import pallas as pl
from jax.experimental.pallas import tpu as pltpu
from jax.sharding import PartitionSpec as P

epsilon = 1e-05

F32 = jnp.float32
BF16 = jnp.bfloat16
MESH = pl.DeviceIdType.MESH
ROWS, STATE = "rows", "state"
SUB = 8
LANES = 128
HALF = LANES // 2
CHUNK = 128
SEG = 32
LEVELS = tuple(1 << i for i in range(SEG.bit_length() - 1))

OWN_X, OWN_WIN, OWN_WOUT, OWN_WGLU, OWN_C, OWN_OUT, OWN_DIN, OWN_SMALL = range(8)
OWN_WIN_G = OWN_SMALL + 9
PAR_S, INFO, INFO_ALL, X, C, OUT, DIN, SM, SN, SB, W1 = range(11)
SIB, FAR, PEER, FAR_SIB = range(4)
GLU_FAR, GLU_SIB = 1, 4
G1 = W1 + 19
G2 = G1 + 4
AX_X, AX_Y, AX_Z = range(3)


def loop(count, body, unroll=1):
    def step(i, carry):
        body(i)
        return carry

    lax.fori_loop(0, count, step, 0, unroll=unroll)


def nn(a, b):
    return lax.dot_general(a, b, (((1,), (0,)), ((), ())), preferred_element_type=F32)


def nt(a, b):
    return lax.dot_general(a, b, (((1,), (1,)), ((), ())), preferred_element_type=F32)


def tn(a, b):
    return lax.dot_general(a, b, (((0,), (0,)), ((), ())), preferred_element_type=F32)


def cmul(a, b):
    return a[0] * b[0] - a[1] * b[1], a[0] * b[1] + a[1] * b[0]


def conj_mul(a, b):
    return a[0] * b[0] + a[1] * b[1], a[0] * b[1] - a[1] * b[0]


def swap_halves(u, v, low):
    return (
        jnp.where(low, u, pltpu.roll(v, HALF, 1)),
        jnp.where(low, pltpu.roll(u, HALF, 1), v),
    )


def fold(x):
    return jnp.sum(x.reshape(x.shape[0] // SUB, SUB, x.shape[1]), axis=0)


def block_kernel(dims, *refs):
    R, S, T, H, W, gdt = dims.R, dims.S, dims.T, dims.H, dims.W, dims.gdt
    NR, NG, R2, HB, L = R * S, S // 2, R // 2, H // R, T // SEG
    Q = 4 if R % 8 == 0 else 2
    G, NB = Q * S, R // Q
    BITS, CH = T.bit_length(), S * LANES
    (inputs, cot, w_in, w_out, w_glu) = refs[:5]
    vectors = refs[5:14]
    (out_ref, din_ref, gsum, vec) = refs[14:18]
    total = 18 + len(dims.names)
    v = SimpleNamespace(**dict(zip(dims.names, refs[18:total])))
    parts = [
        SimpleNamespace(full=refs[total + 2 * i], r1=refs[total + 2 * i + 1], step=G1 + i, at=i * LANES, routes=[])
        for i in range(4)
    ]
    g_in, g_out, g_lin, g_gate = parts
    total += 8
    for i, (part, axes, first, lines) in enumerate(routes_of(R, H)):
        steps = len(axes)
        route = SimpleNamespace(part=parts[part], axes=axes, first=first, lines=lines, step=G2 + 4 * i)
        route.a = refs[total : total + steps + 1]
        route.r = refs[total + steps + 1 : total + 2 * steps + 1]
        route.last = refs[total + 2 * steps + 1]
        total += 2 * steps + 2
        parts[part].routes.append(route)

    me_r, me_s = lax.axis_index(ROWS), lax.axis_index(STATE)
    me = me_r * S + me_s

    def cols(i, width):
        return pl.ds(pl.multiple_of(i * width, LANES), width)

    def lanes(i):
        return slice(i * LANES, (i + 1) * LANES)

    def rows_of(i):
        return pl.ds(pl.multiple_of(i * CHUNK, CHUNK), CHUNK)

    def wait_bytes(ref, which, arrived):
        pltpu.make_async_copy(ref, ref, (v.received if arrived else v.sent).at[which]).wait()

    def send(src, dst, which, target):
        pltpu.make_async_remote_copy(
            src_ref=src,
            dst_ref=dst,
            send_sem=v.sent.at[which],
            recv_sem=v.received.at[which],
            device_id=target,
            device_id_type=MESH,
        ).start()

    def to_state(src_of, dst, which):
        for j in (2, 3, 1) if S == 4 else range(1, S):
            t = lax.rem(me_s + j, S)
            send(src_of(t), dst, which, {STATE: t})

    sib = me_s + 1 - 2 * lax.rem(me_s, 2)
    far = lax.rem(me_s + NG, S)
    sib_far = lax.rem(sib + NG, S)
    pair_r = me_r + 1 - 2 * lax.rem(me_r, 2)
    group_r = me_r - lax.rem(me_r, Q)
    piece = lax.rem(me_r, Q)
    mine_s = lax.rem(me_s, 2)
    mine_r = lax.rem(me_r, 2)

    def line_block(ref, s, p=None):
        size = HALF if p is None else HALF // Q
        first = s * HALF if p is None else s * HALF + p * size
        return ref.at[:, pl.ds(pl.multiple_of(first, size), size), :]

    def glu_block(ref, s):
        return ref.at[:, :, cols(s, W)]

    def lin_block(ref, s):
        return ref.at[0, :, cols(s, W)]

    def gate_block(ref, s, h):
        return ref.at[1, pl.ds(h * (H // 2), H // 2), cols(s, W)]

    def last_block(ref, s, p=None):
        size = H // 2 if p is None else H // 2 // Q
        first = H // 2 if p is None else H // 2 + p * size
        return ref.at[1, pl.ds(pl.multiple_of(first, size), size), cols(s, W)]

    own = [
        (w_glu, v.glu_raw, OWN_WGLU),
        (w_in, line_block(v.win, me_s), OWN_WIN),
        (w_out, line_block(v.wout, me_s), OWN_WOUT),
        (inputs.at[me_s], v.xin.at[:, cols(me_s, W)], OWN_X),
        (cot.at[me_s], v.cin.at[:, cols(me_s, W)], OWN_C),
    ]
    small_in = (v.bucket, v.lengths, v.nu, v.theta, v.gamma, v.skip, v.glu_bias, v.gain, v.bias)
    own += [(a, b, OWN_SMALL + i) for i, (a, b) in enumerate(zip(vectors, small_in))]
    own = {which: pltpu.make_async_copy(a, b, v.here.at[which]) for a, b, which in own}

    barrier = pltpu.get_barrier_semaphore()
    number = piece * S + me_s
    is_gate = (number == 0) & (NB > 1)
    gated = 1 if NB > 1 else 0

    def signal(which, i, rows=None):
        pl.semaphore_signal(
            which,
            inc=1,
            device_id={ROWS: group_r + lax.div(i, S) if rows is None else rows, STATE: lax.rem(i, S)},
            device_id_type=MESH,
        )

    for p in range(Q - 1, -1, -1):
        for d in (2, 3, 1, 0) if S == 4 else range(S):
            if (p, d) != (0, 0):
                i = lax.rem(piece + p, Q) * S + lax.rem(me_s + d, S)
                pl.when(i >= gated)(functools.partial(signal, barrier, i))
    for copy in own.values():
        copy.start()
    for i in range(len(vectors)):
        own[OWN_SMALL + i].wait()
    bucket_ref, lengths_ref, nu_ref, theta_ref, gamma_ref, skip_ref, glu_bias_ref, gain_ref, bias_ref = small_in

    par = v.par
    par[...] = jnp.zeros((2 * SUB, LANES), F32)
    par[0:1, 0:HALF] = nu_ref[...]
    par[0:1, HALF:LANES] = theta_ref[...]
    par[1:2, 0:HALF] = gamma_ref[...]
    par[2:3, :] = skip_ref[...]
    par[3:5, :] = glu_bias_ref[...]
    for i in range(S):
        par[SUB + i : SUB + i + 1, :] = jnp.full((1, LANES), bucket_ref[i], jnp.int32).astype(F32)
        par[SUB + S + i : SUB + S + i + 1, :] = jnp.full((1, LANES), lengths_ref[i], jnp.int32).astype(F32)
        v.info[me_r, i : i + 1, :] = jnp.where(
            lax.broadcasted_iota(jnp.int32, (1, LANES), 1) < HALF,
            par[SUB + i : SUB + i + 1, :],
            par[SUB + S + i : SUB + S + i + 1, :],
        )
    v.par_s[me_s] = par[...]

    @pl.when(jnp.logical_not(is_gate))
    def _():
        pl.semaphore_wait(barrier, G - 1)

    if NB > 1:

        @pl.when(number == 1)
        def _():
            signal(v.block_in, jnp.int32(0))

        @pl.when(is_gate)
        def _():
            pl.semaphore_wait(v.block_in, 1)

            def next_gate(d, carry):
                signal(barrier, jnp.int32(0), rows=lax.rem(group_r + d * Q, R))
                return carry

            lax.fori_loop(1, NB, next_gate, 0)

    def pass_on():
        if NB > 1:

            @pl.when(is_gate)
            def _():
                pl.semaphore_wait(barrier, NB - 1)

                def tell(i, carry):
                    signal(v.all_in, i)
                    return carry

                lax.fori_loop(1, G, tell, 0)

    def everyone_in():
        if NB > 1:

            @pl.when(jnp.logical_not(is_gate))
            def _():
                pl.semaphore_wait(v.all_in, 1)

    to_state(lambda t: par, v.par_s.at[me_s], PAR_S)
    for j in range(1, Q):
        send(v.info.at[me_r], v.info.at[me_r], INFO, {ROWS: group_r + lax.rem(piece + j, Q)})

    def w_send(w, own_block, own_piece):
        send(own_piece, w.block(w.ref, me_s, piece), w.step + FAR, {STATE: far})
        send(own_block, w.block(w.ref, me_s), w.step + SIB, {STATE: sib})

    def w_forward_far(w):
        here = w.block(w.ref, far, piece)
        wait_bytes(here, w.step + FAR, True)
        for j in range(1, Q):
            send(here, here, w.step + PEER, {ROWS: group_r + lax.rem(piece + j, Q)})

    def w_forward_all(w):
        wait_bytes(w.rest, w.step + PEER, True)
        send(w.block(w.ref, far), w.block(w.ref, far), w.step + FAR_SIB, {STATE: sib})

    def w_ready(w):
        wait_bytes(w.block(w.ref, sib), w.step + SIB, True)
        wait_bytes(w.block(w.ref, sib_far), w.step + FAR_SIB, True)

    def w_sent(w):
        wait_bytes(w.block(w.ref, sib), w.step + SIB, False)
        wait_bytes(w.block(w.ref, sib), w.step + FAR_SIB, False)
        wait_bytes(w.block(w.ref, sib, piece), w.step + FAR, False)
        wait_bytes(w.rest, w.step + PEER, False)

    others = pl.ds(0, HALF - HALF // Q)
    wt_in = SimpleNamespace(ref=v.win, block=line_block, step=W1, rest=v.win.at[:, others, :])
    wt_out = SimpleNamespace(ref=v.wout, block=line_block, step=W1 + 4, rest=v.wout.at[:, others, :])
    wt_glu = W1 + 8
    wt_last = SimpleNamespace(
        ref=v.wglu, block=last_block, step=W1 + 15, rest=v.wglu.at[1, pl.ds(0, H // 2 - H // 2 // Q), pl.ds(0, W)]
    )

    def piece_of(ref):
        size = HALF // Q
        return ref.at[:, pl.ds(pl.multiple_of(piece * size, size), size), :]

    w_send(wt_in, w_in, piece_of(w_in))
    w_send(wt_out, w_out, piece_of(w_out))
    for t in (far, sib):
        send(inputs.at[t], v.xin.at[:, cols(me_s, W)], X, {STATE: t})
    own[OWN_WGLU].wait()

    def split_glu(i):
        here = rows_of(i)
        v.glu_wide[...] = v.glu_raw[pl.ds(pl.multiple_of(i * 2 * CHUNK, 2 * CHUNK), 2 * CHUNK), :].astype(F32)
        for k in range(2):
            v.wglu[k, here, cols(me_s, W)] = v.glu_wide[pl.ds(k, CHUNK, stride=2), :].astype(BF16)

    loop(H // CHUNK, split_glu)
    block = last_block(v.wglu, me_s, piece)
    send(block, block, wt_last.step + FAR, {STATE: far})
    send(inputs.at[sib_far], v.xin.at[:, cols(me_s, W)], X, {STATE: sib_far})
    glu_own = glu_block(v.wglu, me_s)
    send(glu_own, glu_own, wt_glu + SIB, {STATE: sib})
    first_three = [lin_block(v.wglu, me_s), gate_block(v.wglu, me_s, 0)]
    for i, block in enumerate(first_three):
        send(block, block, wt_glu + GLU_FAR + i, {STATE: far})

    line = lax.broadcasted_iota(jnp.int32, (CHUNK, T), 0)
    place = lax.broadcasted_iota(jnp.int32, (CHUNK, T), 1)

    def orders(i):
        base = pl.multiple_of(i * CHUNK, CHUNK)
        at = line + base
        v.perm[pl.ds(base, CHUNK), :] = (
            place == lax.rem(at, SEG) * L + lax.div(at, SEG)
        ).astype(F32).astype(BF16)
        v.back[pl.ds(base, CHUNK), :] = (
            at == lax.rem(place, SEG) * L + lax.div(place, SEG)
        ).astype(F32).astype(BF16)
        v.eye[pl.ds(base, CHUNK), :] = (place == at).astype(F32).astype(BF16)

    loop(T // CHUNK, orders)
    channel = lax.broadcasted_iota(jnp.int32, (CHUNK, CH), 0)
    goes_to = lax.broadcasted_iota(jnp.int32, (CHUNK, CH), 1)
    taken = (
        (lax.rem(lax.div(goes_to, HALF), 2) * S + lax.div(goes_to, LANES)) * HALF + lax.rem(goes_to, HALF)
    )

    def shard_order(i):
        base = pl.multiple_of(i * CHUNK, CHUNK)
        v.by_shard[pl.ds(base, CHUNK), :] = (taken == channel + base).astype(F32).astype(BF16)

    loop(CH // CHUNK, shard_order)

    w_forward_far(wt_in)
    w_forward_far(wt_out)

    low = lax.broadcasted_iota(jnp.int32, (SEG, LANES), 1) < HALF
    low1 = lax.broadcasted_iota(jnp.int32, (1, LANES), 1) < HALF
    seg = lax.broadcasted_iota(jnp.int32, (SEG, LANES), 0)

    wait_bytes(v.par_s.at[pl.ds(0, S - 1)], PAR_S, True)
    par_s = v.par_s
    lam, gam, rate, angle = [], [], [], []
    for a in range(NG):
        nu, theta = swap_halves(par_s[2 * a, 0:1, :], par_s[2 * a + 1, 0:1, :], low1)
        rate.append(jnp.exp(nu))
        angle.append(jnp.exp(theta))
        magnitude = jnp.exp(-rate[a])
        lam.append((magnitude * jnp.cos(angle[a]), magnitude * jnp.sin(angle[a])))
        gam.append(jnp.exp(swap_halves(par_s[2 * a, 1:2, :], par_s[2 * a + 1, 1:2, :], low1)[0]))
    skip = jnp.concatenate([par_s[s, 2:3, :] for s in range(S)], axis=1)
    gain, bias = gain_ref[...], bias_ref[...]
    power = [[(jnp.broadcast_to(l[0], (SUB, LANES)), jnp.broadcast_to(l[1], (SUB, LANES))) for l in lam]]
    for _ in range(BITS - 1):
        power.append([cmul(p, p) for p in power[-1]])
    for b in range(BITS):
        for a in range(NG):
            for c in range(2):
                v.pows[b, a, c] = power[b][a][c]

    def raised(exponent):
        result = [(jnp.ones(exponent.shape, F32), jnp.zeros(exponent.shape, F32)) for _ in range(NG)]
        for b in range(BITS):
            hit = (lax.shift_right_logical(exponent, b) & 1) == 1
            for a in range(NG):
                re, im = cmul(result[a], (v.pows[b, a, 0, 0:1, :], v.pows[b, a, 1, 0:1, :]))
                result[a] = (jnp.where(hit, re, result[a][0]), jnp.where(hit, im, result[a][1]))
        return result

    my_bucket = par[pl.ds(SUB + me_s, 1), :]
    len1 = par[pl.ds(SUB + S + me_s, 1), :].astype(jnp.int32)
    my_len = jnp.broadcast_to(len1, (SEG, LANES))
    seg_pow = raised(jnp.clip(my_len - seg * L, 0, L))
    lead_pow = raised(jnp.minimum(my_len, seg * L))
    tail_pow = raised(jnp.maximum(my_len - (seg + 1) * L, 0))
    for a in range(NG):
        ahead = seg_pow[a]
        behind = seg_pow[a]
        for i, d in enumerate(LEVELS):
            for c in range(2):
                v.hs_f[i, a, c] = jnp.where(seg >= d, ahead[c], 0.0)
                v.hs_b[i, a, c] = jnp.where(seg < SEG - d, behind[c], 0.0)
            ahead = cmul(ahead, (pltpu.roll(ahead[0], d, 0), pltpu.roll(ahead[1], d, 0)))
            behind = cmul(behind, (pltpu.roll(behind[0], SEG - d, 0), pltpu.roll(behind[1], SEG - d, 0)))
        for c in range(2):
            v.lead_pow[a, c] = lead_pow[a][c]
            v.tail_pow[a, c] = tail_pow[a][c]

    def lines_of(p):
        return pl.ds(pl.multiple_of(p * SUB, SUB), SUB)

    def carry_copy(way, source, t):
        return pltpu.make_async_remote_copy(
            src_ref=way.msg,
            dst_ref=way.chain.at[source],
            send_sem=way.sent.at[t],
            recv_sem=way.received.at[source],
            device_id={ROWS: lax.div(t, S), STATE: lax.rem(t, S)},
            device_id_type=MESH,
        )

    def exchange(way, values):
        for a in range(NG):
            for c in range(2):
                way.msg[pl.ds(c * NG + a, 1), :] = values[a][c]

        def one(i, carry):
            carry_copy(way, me, me + 1 + i if way.forward else me - 1 - i).start()
            return carry

        lax.fori_loop(0, NR - 1 - me if way.forward else me, one, 0)

    group = min(NR, 4 * SUB)
    low_g = lax.broadcasted_iota(jnp.int32, (group, LANES), 1) < HALF

    def weigh(way):
        def powers(i):
            for j in range(group // S):
                v.row_len[j * S : (j + 1) * S, :] = v.info[i * (group // S) + j]
            both = v.row_len[0:group, :]
            turned = pltpu.roll(both, HALF, 1)
            here = jnp.where(low_g, both, turned)
            lens = jnp.where(low_g, turned, both).astype(jnp.int32)
            p = lax.broadcasted_iota(jnp.int32, (group, LANES), 0) + i * group
            hit = (here == my_bucket) & (my_bucket > 0.5) & ((p < me) if way.forward else (p > me))
            factor = raised(lens)
            at = pl.ds(pl.multiple_of(i * group, SUB), group)
            for a in range(NG):
                v.row_pow[a, at, :] = jnp.where(hit, factor[a][0], 1.0)
                v.row_pow[NG + a, at, :] = jnp.where(hit, factor[a][1], 0.0)
            v.row_hit[at, :] = jnp.where(hit, 1.0, 0.0)

        loop(NR // group, powers)

        def one(i, run):
            p = NR - 1 - i if way.forward else i
            hit = v.row_hit[pl.ds(p, 1), :]
            after = []
            for a in range(NG):
                for c in range(2):
                    for k in range(2):
                        way.weight[c, p, k * NG + a : k * NG + a + 1, :] = hit * run[a][c]
                after.append(cmul((v.row_pow[a, pl.ds(p, 1), :], v.row_pow[NG + a, pl.ds(p, 1), :]), run[a]))
            return tuple(after)

        first = tuple((jnp.ones((1, LANES), F32), jnp.zeros((1, LANES), F32)) for _ in range(NG))
        lax.fori_loop(0, NR, one, first, unroll=4)

    def collect(way):
        def arrive(p, carry):
            carry_copy(way, p, me).wait_recv()
            return carry

        lax.fori_loop(*way.come, arrive, 0)

        def some(i, sums):
            at = pl.ds(i * group, group)
            x = way.chain[at]
            return tuple(
                sums[c] + jnp.sum(jnp.where(way.weight[c, at] == 0.0, 0.0, way.weight[c, at] * x), axis=0)
                for c in range(2)
            )

        zero = jnp.zeros((2 * NG, LANES), F32)
        x, y = lax.fori_loop(0, NR // group, some, (zero, zero))
        sign = 1.0 if way.forward else -1.0
        return [
            (x[a : a + 1] - sign * y[NG + a : NG + a + 1], x[NG + a : NG + a + 1] + sign * y[a : a + 1])
            for a in range(NG)
        ]

    def carries_sent(way):
        def one(t, carry):
            carry_copy(way, me, t).wait_send()
            return carry

        lax.fori_loop(*way.to, one, 0)

    ahead = SimpleNamespace(
        forward=True, msg=v.msg_f, chain=v.chain_f, sent=v.sent_f, received=v.received_f,
        weight=v.weight_f, to=(me + 1, NR), come=(0, me),
    )
    behind = SimpleNamespace(
        forward=False, msg=v.msg_b, chain=v.chain_b, sent=v.sent_b, received=v.received_b,
        weight=v.weight_b, to=(0, me), come=(me + 1, NR),
    )

    pos = lax.broadcasted_iota(jnp.int32, (CHUNK, LANES), 0)
    pos = lax.rem(pos, SEG) * L + lax.div(pos, SEG)

    def valid_of(i, width):
        ok = jnp.where(pos + i * (CHUNK // SEG) < len1, 1.0, 0.0)
        return jnp.concatenate([ok] * (width // LANES), axis=1) if width > LANES else ok

    pass_on()
    w_forward_all(wt_in)
    w_forward_all(wt_out)
    w_forward_far(wt_last)
    wait_bytes(v.info.at[pl.ds(0, Q - 1)], INFO, True)

    own[OWN_X].wait()
    wait_bytes(v.xin.at[:, pl.ds(0, (S - 1) * W)], X, True)
    v.x[...] = nn(v.perm[...], v.xin[...])

    def layer_norm(i):
        rows = rows_of(i)
        x = v.x[rows, :]
        centred = x - jnp.mean(x, -1, keepdims=True)
        inverse = lax.rsqrt(jnp.mean(centred * centred, -1, keepdims=True) + epsilon)
        normed = centred * inverse
        v.normed[rows, :] = normed
        v.inverse[rows, :] = jnp.broadcast_to(inverse, (CHUNK, LANES))
        v.mixed_low[rows, :] = (normed * gain + bias).astype(BF16)

    loop(T // CHUNK, layer_norm, unroll=4)
    own[OWN_WIN].wait()
    w_ready(wt_in)
    v.proj[...] = nt(v.mixed_low[...], v.win[...].reshape(CH, H))
    everyone_in()
    mine_q = v.info.at[pl.ds(pl.multiple_of(group_r, Q), Q)]

    def info_to(d, carry):
        send(mine_q, mine_q, INFO_ALL, {ROWS: lax.rem(me_r + d * Q, R)})
        return carry

    if NB > 1:
        lax.fori_loop(1, NB, info_to, 0)
    by_shard = [
        pltpu.make_async_copy(line_block(v.win, s), v.win_g.at[s], v.here.at[OWN_WIN_G + s]) for s in range(S)
    ]
    for copy in by_shard:
        copy.start()

    lamb = [tuple(jnp.broadcast_to(c, (SEG, LANES)) for c in l) for l in lam]
    gamb = [jnp.broadcast_to(g, (SEG, LANES)) for g in gam]

    def load_c(ref, at):
        return [(ref[at, lanes(a)], ref[at, lanes(NG + a)]) for a in range(NG)]

    def store_c(ref, at, values):
        for a in range(NG):
            ref[at, lanes(a)] = values[a][0]
            ref[at, lanes(NG + a)] = values[a][1]

    def to_g(values):
        return [g for a in range(NG) for g in swap_halves(values[a][0], values[a][1], low)]

    def step_of(k):
        return pl.ds(pl.multiple_of(k * SEG, SEG), SEG)

    zeros = tuple((jnp.zeros((SEG, LANES), F32), jnp.zeros((SEG, LANES), F32)) for _ in range(NG))

    def advance(k, state, proj):
        ok = seg * L + k < my_len
        new = []
        for a in range(NG):
            re, im = cmul(lamb[a], state[a])
            re, im = re + gamb[a] * proj[a][0], im + gamb[a] * proj[a][1]
            new.append((jnp.where(ok, re, state[a][0]), jnp.where(ok, im, state[a][1])))
        return tuple(new)

    def fwd_first(k, state):
        return advance(k, state, load_c(v.proj, step_of(k)))

    ends = lax.fori_loop(0, L, fwd_first, zeros, unroll=4)

    def across(values, table, forward):
        done = []
        for a in range(NG):
            x = values[a]
            for i, d in enumerate(LEVELS):
                shift = d if forward else SEG - d
                other = (pltpu.roll(x[0], shift, 0), pltpu.roll(x[1], shift, 0))
                factor = (table[i, a, 0], table[i, a, 1])
                add = cmul(factor, other) if forward else conj_mul(factor, other)
                x = (x[0] + add[0], x[1] + add[1])
            done.append(x)
        return done

    ends = across(ends, v.hs_f, True)
    exchange(ahead, [tuple(x[SEG - 1 : SEG, :] for x in ends[a]) for a in range(NG)])
    before = [
        tuple(jnp.where(seg > 0, pltpu.roll(x, 1, 0), 0.0) for x in ends[a]) for a in range(NG)
    ]
    to_state(lambda t: cot.at[t], v.cin.at[:, cols(me_s, W)], C)
    own[OWN_C].wait()
    far_blocks = [lin_block(v.wglu, far), gate_block(v.wglu, far, 0)]
    for i, block in enumerate(far_blocks):
        wait_bytes(block, wt_glu + GLU_FAR + i, True)
        send(block, block, wt_glu + GLU_SIB + i, {STATE: sib})
    w_forward_all(wt_last)
    v.mixed_t[...] = nt(v.eye[...], v.mixed_low[...]).astype(BF16)
    if NB > 1:
        wait_bytes(v.info.at[pl.ds(0, R - Q)], INFO_ALL, True)
    weigh(ahead)
    starts = collect(ahead)
    state = []
    for a in range(NG):
        add = cmul((v.lead_pow[a, 0], v.lead_pow[a, 1]), starts[a])
        state.append((before[a][0] + add[0], before[a][1] + add[1]))
    store_c(v.state, pl.ds(0, SEG), state)

    def fwd_second(k, state):
        state = advance(k, state, load_c(v.proj, step_of(k)))
        store_c(v.state, step_of(k + 1), state)
        for a in range(NG):
            v.state_low[step_of(k), lanes(a)] = state[a][0].astype(BF16)
            v.state_low[step_of(k), lanes(NG + a)] = (-state[a][1]).astype(BF16)
        return state

    lax.fori_loop(0, L, fwd_second, tuple(state), unroll=4)

    own[OWN_WOUT].wait()
    w_ready(wt_out)
    v.wide[...] = nn(v.state_low[...], v.wout[...].reshape(CH, H))

    def gelu(i):
        rows = rows_of(i)
        mixed_in = v.normed[rows, :] * gain + bias
        mixed = v.wide[rows, :] + skip * mixed_in
        cdf = 0.5 * (1.0 + lax.erf(mixed * (1.0 / math.sqrt(2.0))))
        density = jnp.exp(-0.5 * mixed * mixed) * (1.0 / math.sqrt(2.0 * math.pi))
        v.act[rows, :] = (mixed * cdf).astype(BF16)
        v.dgelu[rows, :] = cdf + mixed * density

    loop(T // CHUNK, gelu, unroll=4)
    wait_bytes(glu_block(v.wglu, sib), wt_glu + SIB, True)
    for i, block in enumerate([lin_block(v.wglu, sib_far), gate_block(v.wglu, sib_far, 0)]):
        wait_bytes(block, wt_glu + GLU_SIB + i, True)
    wait_bytes(last_block(v.wglu, sib_far), wt_last.step + FAR_SIB, True)
    for k in range(2):
        v.pre[k] = nn(v.act[...], v.wglu[k])

    def glu(i):
        rows = rows_of(i)
        ok = valid_of(i, W)
        for s in range(S):
            here = slice(s * W, (s + 1) * W)
            linear = v.pre[0, rows, here] + par_s[s, 3:4, :]
            gate = v.pre[1, rows, here] + par_s[s, 4:5, :]
            share = jax.nn.sigmoid(gate)
            value = linear * share
            v.out_low[rows, here] = (ok * (v.x[rows, here] + value)).astype(BF16)
            v.pre[0, rows, here] = ok * share
            v.pre[1, rows, here] = ok * (value * (1.0 - share))

    loop(T // CHUNK, glu, unroll=4)

    def give_back(low_ref, nat, result, own_which):
        nat[...] = nn(v.back[...], low_ref[...]).astype(BF16)
        copy = pltpu.make_async_copy(nat.at[:, cols(me_s, W)], result.at[me_s], v.here.at[own_which])
        copy.start()
        return copy

    def give_to(nat, result, which, t):
        send(nat.at[:, cols(t, W)], result.at[me_s], which, {STATE: t})

    out_copy = give_back(v.out_low, v.out_nat, out_ref, OWN_OUT)
    give_to(v.out_nat, out_ref, OUT, far)
    give_to(v.out_nat, out_ref, OUT, sib)
    give_to(v.out_nat, out_ref, OUT, sib_far)
    weigh(behind)
    v.act_t[...] = nt(v.eye[...], v.act[...]).astype(BF16)
    v.state_g[...] = nn(v.state_low[...], v.by_shard[...]).astype(BF16)
    wait_bytes(v.cin.at[:, pl.ds(0, (S - 1) * W)], C, True)
    v.wide[...] = nn(v.perm[...], v.cin[...])

    def glu_back(i):
        rows = rows_of(i)
        dout = v.wide[rows, :]
        for k in range(2):
            v.d_pre[k, rows, :] = (dout * v.pre[k, rows, :]).astype(BF16)

    loop(T // CHUNK, glu_back, unroll=4)

    R4 = R // 4 if R % 4 == 0 else R // 2
    sizes = {None: R4, AX_X: NG, AX_Y: 2, AX_Z: 2 if R % 4 == 0 else 1}

    def places(r, b):
        return {AX_X: b, AX_Y: lax.rem(r, 2), AX_Z: lax.rem(lax.div(r, 2), sizes[AX_Z]), None: lax.div(r, 2 * sizes[AX_Z])}

    mine = places(me_r, lax.div(me_s, 2))
    partner = {
        AX_X: {STATE: far},
        AX_Y: {ROWS: pair_r},
        AX_Z: {ROWS: me_r + 2 - 4 * mine[AX_Z]},
    }

    def slot(route, r, b):
        at, index = places(r, b), 0
        for axis in route.axes[1:] + route.others:
            index = index * sizes[axis] + at[axis]
        return at[route.axes[0]], index

    def owner(route, n):
        at = dict(mine)
        for axis in reversed(route.others):
            at[axis] = lax.rem(n, sizes[axis])
            n = lax.div(n, sizes[axis])
        return {ROWS: at[AX_Y] + 2 * (at[AX_Z] + sizes[AX_Z] * at[None]), STATE: 2 * at[AX_X] + mine_s}

    for part in parts:
        for route in part.routes:
            route.others = tuple(axis for axis in sizes if axis not in route.axes)
            route.number = 0
            for axis in route.others:
                route.number = route.number * sizes[axis] + mine[axis]

    def first_send(part):
        for b in range(NG):
            send(part.full.at[:, cols(2 * b + 1 - mine_s, LANES)], part.r1.at[b], part.step, {STATE: sib})

    def first_wait(part):
        wait_bytes(part.r1, part.step, True)

    def first_sum(route):
        part = route.part

        def one(r):
            rows = pl.ds(pl.multiple_of(r * HB + route.first, route.lines), route.lines)
            for b in range(NG):
                total = part.full[rows, cols(2 * b + mine_s, LANES)].astype(F32) + part.r1[b, rows, :].astype(F32)
                route.a[0][slot(route, r, b)] = total.astype(gdt)

        loop(R, one, unroll=4)
        pass_half(route, 0)

    def pass_half(route, i):
        axis = route.axes[i]
        send(route.a[i].at[1 - mine[axis]], route.r[i], route.step + i, partner[axis])

    def next_sum(route, i):
        wait_bytes(route.r[i], route.step + i, True)
        count, last = route.r[i].shape[0], i + 1 == len(route.axes)

        def one(n):
            total = route.a[i][mine[route.axes[i]], n].astype(F32) + route.r[i][n].astype(F32)
            to = n if last else (lax.div(n, count // 2), lax.rem(n, count // 2))
            route.a[i + 1][to] = total.astype(gdt)

        loop(count, one, unroll=4)
        if not last:
            pass_half(route, i + 1)
            return
        done = route.a[i + 1]
        route.last[route.number] = done[route.number]

        def give(d, carry):
            n = d + jnp.where(d >= route.number, 1, 0)
            send(done.at[n], route.last.at[route.number], route.step + len(route.axes), owner(route, n))
            return carry

        lax.fori_loop(0, count - 1, give, 0)

    def last_sum(route):
        count = route.last.shape[0]
        if count > 1:
            wait_bytes(route.last.at[pl.ds(0, count - 1)], route.step + len(route.axes), True)

        def one(n, total):
            return total + route.last[n].astype(F32)

        total = lax.fori_loop(0, count, one, jnp.zeros((route.lines, LANES), F32), unroll=4)
        gsum[route.first : route.first + route.lines, route.part.at : route.part.at + LANES] = total

    def all_sent(part):
        wait_bytes(part.r1, part.step, False)
        for route in part.routes:
            for i in range(len(route.axes)):
                wait_bytes(route.r[i], route.step + i, False)
            if route.last.shape[0] > 1:
                wait_bytes(route.last.at[pl.ds(0, route.last.shape[0] - 1)], route.step + len(route.axes), False)

    def glu_first():
        for part in (g_lin, g_gate):
            first_wait(part)
            first_sum(part.routes[0])

    def glu_next():
        for part in (g_lin, g_gate):
            next_sum(part.routes[0], 0)

    v.wide[...] = nt(v.d_pre[0], v.wglu[0]) + nt(v.d_pre[1], v.wglu[1])

    def gelu_back(i, total):
        rows = rows_of(i)
        d_mixed = v.wide[rows, :] * v.dgelu[rows, :]
        v.d_mixed[rows, :] = d_mixed
        v.d_rec[rows, :] = d_mixed.astype(BF16)
        return total + fold(d_mixed * (v.normed[rows, :] * gain + bias))

    d_skip = lax.fori_loop(0, T // CHUNK, gelu_back, jnp.zeros((SUB, H), F32), unroll=4)
    d_skip = jnp.sum(d_skip, axis=0, keepdims=True)
    v.source[...] = nt(v.d_rec[...], v.wout[...].reshape(CH, H))
    def retreat(k, source, carry):
        ok = seg * L + k < my_len
        adjoint, new = [], []
        for a in range(NG):
            re, im = carry[a][0] + source[a][0], carry[a][1] - source[a][1]
            adjoint.append((re, im))
            nre, nim = conj_mul(lamb[a], (re, im))
            new.append((jnp.where(ok, nre, re), jnp.where(ok, nim, im)))
        return ok, adjoint, tuple(new)

    def bwd_first(i, carry):
        k = L - 1 - i
        return retreat(k, load_c(v.source, step_of(k)), carry)[2]

    heads = lax.fori_loop(0, L, bwd_first, zeros, unroll=4)
    heads = across(heads, v.hs_b, False)
    exchange(behind, [tuple(x[0:1, :] for x in heads[a]) for a in range(NG)])
    after = [
        tuple(jnp.where(seg < SEG - 1, pltpu.roll(x, SEG - 1, 0), 0.0) for x in heads[a])
        for a in range(NG)
    ]
    for k, part in ((0, g_lin), (1, g_gate)):
        part.full[...] = nn(v.act_t[...], v.d_pre[k]).astype(gdt)
        first_send(part)
    g_out.full[...] = tn(v.d_rec[...], v.state_g[...]).astype(gdt)
    first_send(g_out)
    glu_first()
    first_wait(g_out)
    first_sum(g_out.routes[0])
    omegas = collect(behind)
    carry = []
    for a in range(NG):
        add = conj_mul((v.tail_pow[a, 0], v.tail_pow[a, 1]), omegas[a])
        carry.append((after[a][0] + add[0], after[a][1] + add[1]))

    def bwd_second(i, item):
        k = L - 1 - i
        carry, sums = item
        ok, adjoint, carry = retreat(k, load_c(v.source, step_of(k)), carry)
        previous = load_c(v.state, step_of(k))
        proj = load_c(v.proj, step_of(k))
        new_sums, low_out = [], []
        for a in range(NG):
            re, im = (jnp.where(ok, x, 0.0) for x in adjoint[a])
            dre, dim = conj_mul(previous[a], (re, im))
            dg = re * proj[a][0] + im * proj[a][1]
            new_sums.append(tuple(x + fold(y) for x, y in zip(sums[a], (dre, dim, dg))))
            low_out.append((gamb[a] * re, gamb[a] * im))
        low_out = to_g(low_out)
        for s in range(S):
            v.d_proj[step_of(k), lanes(s)] = low_out[s].astype(BF16)
        return carry, tuple(new_sums)

    zero = jnp.zeros((SUB, LANES), F32)
    _, sums = lax.fori_loop(
        0, L, bwd_second, (tuple(carry), tuple((zero, zero, zero) for _ in range(NG))), unroll=2
    )

    g_in.full[...] = nn(v.mixed_t[...], v.d_proj[...]).astype(gdt)
    first_send(g_in)
    for copy in by_shard:
        copy.wait()
    v.wide[...] = nn(v.d_proj[...], v.win_g[...].reshape(CH, H))
    glu_next()

    def norm_back(i, totals):
        rows = rows_of(i)
        d_mixed_in = v.wide[rows, :] + skip * v.d_mixed[rows, :]
        normed = v.normed[rows, :]
        inverse = jnp.concatenate([v.inverse[rows, :]] * (H // LANES), axis=1)
        g = d_mixed_in * gain
        first = jnp.mean(g, -1, keepdims=True)
        second = jnp.mean(g * normed, -1, keepdims=True)
        v.din_low[rows, :] = (inverse * (g - first - normed * second)).astype(BF16)
        return totals[0] + fold(d_mixed_in * normed), totals[1] + fold(d_mixed_in)

    zero_h = jnp.zeros((SUB, H), F32)
    d_gain, d_nbias = lax.fori_loop(0, T // CHUNK, norm_back, (zero_h, zero_h), unroll=4)
    d_gain = jnp.sum(d_gain, axis=0, keepdims=True)
    d_nbias = jnp.sum(d_nbias, axis=0, keepdims=True)
    ones = jnp.ones((2 * SUB, T), BF16)
    d_bias = [nn(ones, v.d_pre[k])[0:1, :] for k in range(2)]
    small = v.small
    small[...] = jnp.zeros((S, SUB, LANES), F32)
    for a in range(NG):
        sr, si, sg = (jnp.sum(x, axis=0, keepdims=True) for x in sums[a])
        d_nu = -rate[a] * (sr * lam[a][0] + si * lam[a][1])
        d_theta = angle[a] * (si * lam[a][0] - sr * lam[a][1])
        pair = swap_halves(d_nu, d_theta, low1)
        pair_g = swap_halves(gam[a] * sg, jnp.zeros_like(sg), low1)
        for u in range(2):
            small[2 * a + u, 0:1, :] = pair[u]
            small[2 * a + u, 1:2, :] = pair_g[u]
    for s in range(S):
        here = slice(s * W, (s + 1) * W)
        small[s, 2:3, :] = d_skip[:, here]
        small[s, 3:4, :] = d_bias[0][:, here]
        small[s, 4:5, :] = d_bias[1][:, here]
        small[s, 5:6, :] = d_gain[:, here]
        small[s, 6:7, :] = d_nbias[:, here]
    v.small_r[me_s] = small[...]
    to_state(lambda t: small, v.small_r.at[me_s], SM)
    first_wait(g_in)
    for route in g_in.routes:
        first_sum(route)
    next_sum(g_out.routes[0], 0)
    din_copy = give_back(v.din_low, v.din_nat, din_ref, OWN_DIN)
    for t in (far, sib):
        give_to(v.din_nat, din_ref, DIN, t)
    if len(g_gate.routes[0].axes) > 1:
        next_sum(g_gate.routes[0], 1)
    wait_bytes(v.small_r.at[pl.ds(0, S - 1)], SM, True)
    group = v.small_r[0]
    for s in range(1, S):
        group = group + v.small_r[s]
    small2 = v.small2
    v.group[...] = group
    small2[0:SUB, :] = v.group[me_s]
    for s in range(S):
        small2[SUB + s : SUB + s + 1, :] = group[s, 5:6, :]
        small2[SUB + S + s : SUB + S + s + 1, :] = group[s, 6:7, :]
    v.small2_r[piece] = small2[...]
    for j in range(1, Q):
        send(small2, v.small2_r.at[piece], SN, {ROWS: group_r + lax.rem(piece + j, Q)})
    for route in g_in.routes:
        next_sum(route, 0)
    give_to(v.din_nat, din_ref, DIN, sib_far)
    wait_bytes(v.small2_r.at[pl.ds(0, Q - 1)], SN, True)
    small3 = v.small2_r[0]
    for j in range(1, Q):
        small3 = small3 + v.small2_r[j]
    block = lax.div(me_r, Q)
    v.small3_r[block] = small3

    def small_blocks(d, carry):
        send(v.small3_r.at[block], v.small3_r.at[block], SB, {ROWS: lax.rem(me_r + d * Q, R)})
        return carry

    lax.fori_loop(1, NB, small_blocks, 0)
    if len(g_out.routes[0].axes) > 1:
        next_sum(g_out.routes[0], 1)
    for part in (g_lin, g_gate, g_out):
        last_sum(part.routes[0])
    if NB > 1:
        wait_bytes(v.small3_r.at[pl.ds(0, NB - 1)], SB, True)
    total = v.small3_r[0]
    for i in range(1, NB):
        total = total + v.small3_r[i]
    vec[...] = total
    for route in g_in.routes:
        last_sum(route)

    out_copy.wait()
    din_copy.wait()
    wait_bytes(out_ref.at[pl.ds(0, S - 1)], OUT, True)
    wait_bytes(din_ref.at[pl.ds(0, S - 1)], DIN, True)
    wait_bytes(out_ref.at[pl.ds(0, S - 1)], OUT, False)
    wait_bytes(din_ref.at[pl.ds(0, S - 1)], DIN, False)
    wait_bytes(v.par_s.at[pl.ds(0, S - 1)], PAR_S, False)
    wait_bytes(v.info.at[pl.ds(0, Q - 1)], INFO, False)
    if NB > 1:
        wait_bytes(v.info.at[pl.ds(0, R - Q)], INFO_ALL, False)
    wait_bytes(v.xin.at[:, pl.ds(0, (S - 1) * W)], X, False)
    for w in (wt_in, wt_out):
        w_sent(w)
    wait_bytes(glu_own, wt_glu + SIB, False)
    for i, block in enumerate(far_blocks):
        wait_bytes(block, wt_glu + GLU_FAR + i, False)
        wait_bytes(block, wt_glu + GLU_SIB + i, False)
    wait_bytes(last_block(v.wglu, far), wt_last.step + FAR_SIB, False)
    wait_bytes(last_block(v.wglu, far, piece), wt_last.step + FAR, False)
    wait_bytes(wt_last.rest, wt_last.step + PEER, False)
    wait_bytes(v.cin.at[:, pl.ds(0, (S - 1) * W)], C, False)
    carries_sent(ahead)
    carries_sent(behind)
    wait_bytes(v.small_r.at[pl.ds(0, S - 1)], SM, False)
    wait_bytes(v.small2_r.at[pl.ds(0, Q - 1)], SN, False)
    if NB > 1:
        wait_bytes(v.small3_r.at[pl.ds(0, NB - 1)], SB, False)
    for part in parts:
        all_sent(part)


def routes_of(R, H):
    HB = H // R
    if HB % (4 * SUB) == 0:
        routes = [(0, (AX_Y,), 0, HB // 2), (0, (AX_Z if R % 4 == 0 else AX_X,), HB // 2, HB // 2)]
    else:
        routes = [(0, (AX_Y,), 0, HB)]
    if R % 4 == 0:
        return routes + [(1, (AX_X, AX_Y), 0, HB), (2, (AX_Y,), 0, HB), (3, (AX_Z, AX_Y), 0, HB)]
    return routes + [(1, (AX_X,), 0, HB), (2, (AX_Y,), 0, HB), (3, (AX_X,), 0, HB)]


def run_block(dims, *args):
    R, S, T, H, W = dims.R, dims.S, dims.T, dims.H, dims.W
    NR, NG, HB = R * S, S // 2, H // R
    CH, levels = S * LANES, len(LEVELS)
    gdt = BF16 if HB % (2 * SUB) == 0 else F32
    dims.gdt = gdt
    bits = T.bit_length()
    shapes = dict(
        xin=((T, H), BF16),
        cin=((T, H), BF16),
        win=((2, S * HALF, H), BF16),
        wout=((2, S * HALF, H), BF16),
        win_g=((S, 2, HALF, H), BF16),
        by_shard=((CH, CH), BF16),
        state_g=((T, CH), BF16),
        wglu=((2, H, H), BF16),
        glu_raw=((2 * H, W), BF16),
        glu_wide=((2 * CHUNK, W), F32),
        perm=((T, T), BF16),
        back=((T, T), BF16),
        eye=((T, T), BF16),
        mixed_t=((H, T), BF16),
        act_t=((H, T), BF16),
        nu=((1, HALF), F32),
        theta=((1, HALF), F32),
        gamma=((1, HALF), F32),
        skip=((1, W), F32),
        glu_bias=((2, W), F32),
        gain=((1, H), F32),
        bias=((1, H), F32),
        par=((2 * SUB, LANES), F32),
        par_s=((S, 2 * SUB, LANES), F32),
        pows=((bits, NG, 2, SUB, LANES), F32),
        hs_f=((levels, NG, 2, SEG, LANES), F32),
        hs_b=((levels, NG, 2, SEG, LANES), F32),
        lead_pow=((NG, 2, SEG, LANES), F32),
        tail_pow=((NG, 2, SEG, LANES), F32),
        row_pow=((2 * NG, NR, LANES), F32),
        row_hit=((NR, LANES), F32),
        row_len=((4 * SUB, LANES), F32),
        info=((R, S, LANES), F32),
        msg_f=((2 * NG, LANES), F32),
        msg_b=((2 * NG, LANES), F32),
        chain_f=((NR, 2 * NG, LANES), F32),
        chain_b=((NR, 2 * NG, LANES), F32),
        weight_f=((2, NR, 2 * NG, LANES), F32),
        weight_b=((2, NR, 2 * NG, LANES), F32),
        x=((T, H), F32),
        normed=((T, H), F32),
        inverse=((T, LANES), F32),
        mixed_low=((T, H), BF16),
        wide=((T, max(H, CH)), F32),
        proj=((T, CH), F32),
        state=((T + SEG, CH), F32),
        state_low=((T, CH), BF16),
        act=((T, H), BF16),
        dgelu=((T, H), F32),
        pre=((2, T, H), F32),
        out_low=((T, H), BF16),
        out_nat=((T, H), BF16),
        d_pre=((2, T, H), BF16),
        d_mixed=((T, H), F32),
        d_rec=((T, H), BF16),
        source=((T, CH), F32),
        d_proj=((T, CH), BF16),
        din_low=((T, H), BF16),
        din_nat=((T, H), BF16),
        small=((S, SUB, LANES), F32),
        small_r=((S, S, SUB, LANES), F32),
        group=((S, SUB, LANES), F32),
        small2=((2 * SUB, LANES), F32),
        small2_r=((4, 2 * SUB, LANES), F32),
        small3_r=((R // 2, 2 * SUB, LANES), F32),
    )
    scalars = dict(bucket=(S,), lengths=(S,))
    flags = dict(block_in=1, all_in=1)
    copies = dict(here=OWN_WIN_G + S, sent=G2 + 20, received=G2 + 20, sent_f=NR, received_f=NR, sent_b=NR, received_b=NR)
    dims.names = [*shapes, *scalars, *flags, *copies]
    parts = []
    for _ in range(4):
        parts += [(H, CH), (NG, H, LANES)]
    routes = routes_of(R, H)
    for _, axes, _, lines in routes:
        left = [2 * R >> (i + 1) for i in range(len(axes))]
        parts += [(2, n, lines, LANES) for n in left] + [(left[-1], lines, LANES)]
        parts += [(n, lines, LANES) for n in left] + [(left[-1], lines, LANES)]
    scratch = [pltpu.VMEM(shape, dtype) for shape, dtype in shapes.values()]
    scratch += [pltpu.SMEM(shape, jnp.int32) for shape in scalars.values()]
    scratch += [pltpu.SemaphoreType.REGULAR for _ in flags]
    scratch += [pltpu.SemaphoreType.DMA((n,)) for n in copies.values()]
    scratch += [pltpu.VMEM(shape, gdt) for shape in parts]
    any_spec = pl.BlockSpec(memory_space=pl.ANY)
    vmem = pl.BlockSpec(memory_space=pltpu.VMEM)
    macs = T * H * (2 * CH + 2 * H) * 3 + 4 * T * T * H
    return pl.pallas_call(
        functools.partial(block_kernel, dims),
        out_shape=(
            jax.ShapeDtypeStruct((S, T, W), BF16),
            jax.ShapeDtypeStruct((S, T, W), BF16),
            jax.ShapeDtypeStruct((HB, 4 * LANES), F32),
            jax.ShapeDtypeStruct((2 * SUB, LANES), F32),
        ),
        in_specs=[any_spec] * 14,
        out_specs=(any_spec, any_spec, vmem, vmem),
        scratch_shapes=scratch,
        compiler_params=pltpu.CompilerParams(
            collective_id=0, has_side_effects=True, vmem_limit_bytes=56 * 2**20
        ),
        cost_estimate=pl.CostEstimate(flops=2 * macs, bytes_accessed=8 * 2**20, transcendentals=4 * T * H),
    )(*args)


def on_device(
    inputs,
    bucket,
    lengths,
    nu_log,
    theta_log,
    gamma_log,
    in_proj,
    out_proj,
    skip,
    norm_gain,
    norm_bias,
    glu_weight,
    glu_bias,
    output_cotangent,
):
    row_count, seq, part = inputs.shape
    width = norm_gain.shape[0]
    chans = nu_log.shape[0]
    R, S = lax.axis_size(ROWS), lax.axis_size(STATE)
    dims = SimpleNamespace(R=R, S=S, T=seq, H=width, W=part)
    assert row_count == S and 2 * chans == LANES and part == LANES and S % 2 == 0 and R % 2 == 0

    outputs, d_norm, gsum, vec = run_block(
        dims,
        inputs,
        output_cotangent,
        in_proj.transpose(1, 2, 0),
        out_proj,
        glu_weight.reshape(2 * width, part),
        bucket,
        lengths,
        nu_log[None],
        theta_log[None],
        gamma_log[None],
        skip[None],
        glu_bias,
        norm_gain[None],
        norm_bias[None],
    )
    return finish(dims, lengths, outputs, d_norm, output_cotangent, gsum, vec)


def finish_kernel(dims, *refs):
    S, T, HB = dims.S, dims.T, dims.H // dims.R
    (lengths, out_in, d_norm, cot, gsum, vec) = refs[:6]
    (out, d_inputs, d_nu, d_theta, d_gamma, d_in, d_out, d_skip, d_gain, d_bias, d_glu, d_glu_bias) = refs[6:]
    out[...] = out_in[...]
    for row in range(S):
        for first in range(0, T, CHUNK):
            lines = slice(first, first + CHUNK)
            place = lax.broadcasted_iota(jnp.int32, (CHUNK, LANES), 0) + first
            direct = jnp.where(place < lengths[row], cot[row, lines, :].astype(F32), 0.0)
            d_inputs[row, lines, :] = d_norm[row, lines, :].astype(F32) + direct
    d_nu[...] = vec[0:1, 0:HALF]
    d_theta[...] = pltpu.roll(vec[0:1, :], HALF, 1)[:, 0:HALF]
    d_gamma[...] = vec[1:2, 0:HALF]
    d_skip[...] = vec[2:3, :]
    d_glu_bias[...] = vec[3:5, :]
    for s in range(S):
        here = slice(s * LANES, (s + 1) * LANES)
        d_gain[:, here] = vec[SUB + s : SUB + s + 1, :]
        d_bias[:, here] = vec[SUB + S + s : SUB + S + s + 1, :]
    both = gsum[:, 0:LANES]
    d_in[pl.ds(0, HB, stride=2), :] = both[:, 0:HALF]
    d_in[pl.ds(1, HB, stride=2), :] = pltpu.roll(both, HALF, 1)[:, 0:HALF]
    d_out[...] = gsum[:, LANES : 2 * LANES].T
    d_glu[pl.ds(0, HB, stride=2), :] = gsum[:, 2 * LANES : 3 * LANES]
    d_glu[pl.ds(1, HB, stride=2), :] = gsum[:, 3 * LANES : 4 * LANES]


def finish(dims, lengths, outputs, d_norm, cot, gsum, vec):
    R, S, T, H, W = dims.R, dims.S, dims.T, dims.H, dims.W
    HB = H // R
    vmem = pl.BlockSpec(memory_space=pltpu.VMEM)
    small = [(1, HALF)] * 3 + [(2 * HB, HALF), (LANES, HB), (1, W), (1, H), (1, H), (2 * HB, W), (2, W)]
    got = pl.pallas_call(
        functools.partial(finish_kernel, dims),
        out_shape=(
            jax.ShapeDtypeStruct((S, T, W), BF16),
            jax.ShapeDtypeStruct((S, T, W), F32),
            *(jax.ShapeDtypeStruct(shape, F32) for shape in small),
        ),
        in_specs=[pl.BlockSpec(memory_space=pltpu.SMEM)] + [vmem] * 5,
        out_specs=(vmem,) * 12,
    )(lengths, outputs, d_norm, cot, gsum, vec)
    out, d_inputs, d_nu, d_theta, d_gamma, d_in, d_out, d_skip, d_gain, d_bias, d_glu, d_glu_bias = got
    return (
        out,
        d_inputs,
        d_nu.reshape(HALF),
        d_theta.reshape(HALF),
        d_gamma.reshape(HALF),
        d_in.reshape(HB, 2, HALF),
        d_out.reshape(2, HALF, HB),
        d_skip.reshape(W),
        d_gain.reshape(H),
        d_bias.reshape(H),
        d_glu.reshape(HB, 2, W),
        d_glu_bias,
    )


def solution(mesh):
    return jax.shard_map(
        on_device,
        mesh=mesh,
        in_specs=(
            P(ROWS, None, STATE),
            P(ROWS),
            P(ROWS),
            P(STATE),
            P(STATE),
            P(STATE),
            P(None, None, STATE),
            P(None, STATE, None),
            P(STATE),
            P(),
            P(),
            P(None, None, STATE),
            P(None, STATE),
            P(ROWS, None, STATE),
        ),
        out_specs=(
            P(ROWS, None, STATE),
            P(ROWS, None, STATE),
            P(STATE),
            P(STATE),
            P(STATE),
            P(ROWS, None, STATE),
            P(None, STATE, ROWS),
            P(STATE),
            P(),
            P(),
            P(ROWS, None, STATE),
            P(None, STATE),
        ),
        check_vma=False,
    )
```

```python
import functools
import math
from types import SimpleNamespace

import jax
import jax.numpy as jnp
from jax import lax
from jax.experimental import pallas as pl
from jax.experimental.pallas import tpu as pltpu
from jax.sharding import PartitionSpec as P

epsilon = 1e-05

F32 = jnp.float32
BF16 = jnp.bfloat16
MESH = pl.DeviceIdType.MESH
ROWS, STATE = "rows", "state"
SUB = 8
LANES = 128
HALF = LANES // 2
CHUNK = 128
SEG = 32
LEVELS = tuple(1 << i for i in range(SEG.bit_length() - 1))

OWN_X, OWN_WIN, OWN_WOUT, OWN_WGLU, OWN_C, OWN_OUT, OWN_DIN, OWN_SMALL = range(8)
OWN_WIN_G = OWN_SMALL + 9
PAR_S, INFO, INFO_ALL, X, C, OUT, DIN, SM, SN, SB, W1 = range(11)
SIB, FAR, PEER, FAR_SIB = range(4)
GLU_FAR, GLU_SIB = 1, 4
G1 = W1 + 19
G2 = G1 + 4
AX_X, AX_Y, AX_Z = range(3)


def loop(count, body, unroll=1):
    def step(i, carry):
        body(i)
        return carry

    lax.fori_loop(0, count, step, 0, unroll=unroll)


def nn(a, b):
    return lax.dot_general(a, b, (((1,), (0,)), ((), ())), preferred_element_type=F32)


def nt(a, b):
    return lax.dot_general(a, b, (((1,), (1,)), ((), ())), preferred_element_type=F32)


def tn(a, b):
    return lax.dot_general(a, b, (((0,), (0,)), ((), ())), preferred_element_type=F32)


def cmul(a, b):
    return a[0] * b[0] - a[1] * b[1], a[0] * b[1] + a[1] * b[0]


def conj_mul(a, b):
    return a[0] * b[0] + a[1] * b[1], a[0] * b[1] - a[1] * b[0]


def swap_halves(u, v, low):
    return (
        jnp.where(low, u, pltpu.roll(v, HALF, 1)),
        jnp.where(low, pltpu.roll(u, HALF, 1), v),
    )


def fold(x):
    return jnp.sum(x.reshape(x.shape[0] // SUB, SUB, x.shape[1]), axis=0)


def block_kernel(dims, *refs):
    R, S, T, H, W, gdt = dims.R, dims.S, dims.T, dims.H, dims.W, dims.gdt
    NR, NG, R2, HB, L = R * S, S // 2, R // 2, H // R, T // SEG
    Q = 4 if R % 8 == 0 else 2
    G, NB = Q * S, R // Q
    BITS, CH = T.bit_length(), S * LANES
    (inputs, cot, w_in, w_out, w_glu) = refs[:5]
    vectors = refs[5:14]
    (out_ref, din_ref, gsum, vec) = refs[14:18]
    total = 18 + len(dims.names)
    v = SimpleNamespace(**dict(zip(dims.names, refs[18:total])))
    parts = [
        SimpleNamespace(full=refs[total + 2 * i], r1=refs[total + 2 * i + 1], step=G1 + i, at=i * LANES, routes=[])
        for i in range(4)
    ]
    g_in, g_out, g_lin, g_gate = parts
    total += 8
    for i, (part, axes, first, lines) in enumerate(routes_of(R, H)):
        steps = len(axes)
        route = SimpleNamespace(part=parts[part], axes=axes, first=first, lines=lines, step=G2 + 4 * i)
        route.a = refs[total : total + steps + 1]
        route.r = refs[total + steps + 1 : total + 2 * steps + 1]
        route.last = refs[total + 2 * steps + 1]
        total += 2 * steps + 2
        parts[part].routes.append(route)

    me_r, me_s = lax.axis_index(ROWS), lax.axis_index(STATE)
    me = me_r * S + me_s

    def cols(i, width):
        return pl.ds(pl.multiple_of(i * width, LANES), width)

    def lanes(i):
        return slice(i * LANES, (i + 1) * LANES)

    def rows_of(i):
        return pl.ds(pl.multiple_of(i * CHUNK, CHUNK), CHUNK)

    def wait_bytes(ref, which, arrived):
        pltpu.make_async_copy(ref, ref, (v.received if arrived else v.sent).at[which]).wait()

    def send(src, dst, which, target):
        pltpu.make_async_remote_copy(
            src_ref=src,
            dst_ref=dst,
            send_sem=v.sent.at[which],
            recv_sem=v.received.at[which],
            device_id=target,
            device_id_type=MESH,
        ).start()

    def to_state(src_of, dst, which):
        for j in (2, 3, 1) if S == 4 else range(1, S):
            t = lax.rem(me_s + j, S)
            send(src_of(t), dst, which, {STATE: t})

    sib = me_s + 1 - 2 * lax.rem(me_s, 2)
    far = lax.rem(me_s + NG, S)
    sib_far = lax.rem(sib + NG, S)
    pair_r = me_r + 1 - 2 * lax.rem(me_r, 2)
    group_r = me_r - lax.rem(me_r, Q)
    piece = lax.rem(me_r, Q)
    mine_s = lax.rem(me_s, 2)
    mine_r = lax.rem(me_r, 2)

    def line_block(ref, s, p=None):
        size = HALF if p is None else HALF // Q
        first = s * HALF if p is None else s * HALF + p * size
        return ref.at[:, pl.ds(pl.multiple_of(first, size), size), :]

    def glu_block(ref, s):
        return ref.at[:, :, cols(s, W)]

    def lin_block(ref, s):
        return ref.at[0, :, cols(s, W)]

    def gate_block(ref, s, h):
        return ref.at[1, pl.ds(h * (H // 2), H // 2), cols(s, W)]

    def last_block(ref, s, p=None):
        size = H // 2 if p is None else H // 2 // Q
        first = H // 2 if p is None else H // 2 + p * size
        return ref.at[1, pl.ds(pl.multiple_of(first, size), size), cols(s, W)]

    own = [
        (w_glu, v.glu_raw, OWN_WGLU),
        (w_in, line_block(v.win, me_s), OWN_WIN),
        (w_out, line_block(v.wout, me_s), OWN_WOUT),
        (inputs.at[me_s], v.xin.at[:, cols(me_s, W)], OWN_X),
        (cot.at[me_s], v.cin.at[:, cols(me_s, W)], OWN_C),
    ]
    small_in = (v.bucket, v.lengths, v.nu, v.theta, v.gamma, v.skip, v.glu_bias, v.gain, v.bias)
    own += [(a, b, OWN_SMALL + i) for i, (a, b) in enumerate(zip(vectors, small_in))]
    own = {which: pltpu.make_async_copy(a, b, v.here.at[which]) for a, b, which in own}

    barrier = pltpu.get_barrier_semaphore()
    number = piece * S + me_s
    is_gate = (number == 0) & (NB > 1)
    gated = 1 if NB > 1 else 0

    def signal(which, i, rows=None):
        pl.semaphore_signal(
            which,
            inc=1,
            device_id={ROWS: group_r + lax.div(i, S) if rows is None else rows, STATE: lax.rem(i, S)},
            device_id_type=MESH,
        )

    for p in range(Q - 1, -1, -1):
        for d in (2, 3, 1, 0) if S == 4 else range(S):
            if (p, d) != (0, 0):
                i = lax.rem(piece + p, Q) * S + lax.rem(me_s + d, S)
                pl.when(i >= gated)(functools.partial(signal, barrier, i))
    for copy in own.values():
        copy.start()
    for i in range(len(vectors)):
        own[OWN_SMALL + i].wait()
    bucket_ref, lengths_ref, nu_ref, theta_ref, gamma_ref, skip_ref, glu_bias_ref, gain_ref, bias_ref = small_in

    par = v.par
    par[...] = jnp.zeros((2 * SUB, LANES), F32)
    par[0:1, 0:HALF] = nu_ref[...]
    par[0:1, HALF:LANES] = theta_ref[...]
    par[1:2, 0:HALF] = gamma_ref[...]
    par[2:3, :] = skip_ref[...]
    par[3:5, :] = glu_bias_ref[...]
    for i in range(S):
        par[SUB + i : SUB + i + 1, :] = jnp.full((1, LANES), bucket_ref[i], jnp.int32).astype(F32)
        par[SUB + S + i : SUB + S + i + 1, :] = jnp.full((1, LANES), lengths_ref[i], jnp.int32).astype(F32)
        v.info[me_r, i : i + 1, :] = jnp.where(
            lax.broadcasted_iota(jnp.int32, (1, LANES), 1) < HALF,
            par[SUB + i : SUB + i + 1, :],
            par[SUB + S + i : SUB + S + i + 1, :],
        )
    v.par_s[me_s] = par[...]

    @pl.when(jnp.logical_not(is_gate))
    def _():
        pl.semaphore_wait(barrier, G - 1)

    if NB > 1:

        @pl.when(number == 1)
        def _():
            signal(v.block_in, jnp.int32(0))

        @pl.when(is_gate)
        def _():
            pl.semaphore_wait(v.block_in, 1)

            def next_gate(d, carry):
                signal(barrier, jnp.int32(0), rows=lax.rem(group_r + d * Q, R))
                return carry

            lax.fori_loop(1, NB, next_gate, 0)

    def pass_on():
        if NB > 1:

            @pl.when(is_gate)
            def _():
                pl.semaphore_wait(barrier, NB - 1)

                def tell(i, carry):
                    signal(v.all_in, i)
                    return carry

                lax.fori_loop(1, G, tell, 0)

    def everyone_in():
        if NB > 1:

            @pl.when(jnp.logical_not(is_gate))
            def _():
                pl.semaphore_wait(v.all_in, 1)

    to_state(lambda t: par, v.par_s.at[me_s], PAR_S)
    for j in range(1, Q):
        send(v.info.at[me_r], v.info.at[me_r], INFO, {ROWS: group_r + lax.rem(piece + j, Q)})

    def w_send(w, own_block, own_piece):
        send(own_piece, w.block(w.ref, me_s, piece), w.step + FAR, {STATE: far})
        send(own_block, w.block(w.ref, me_s), w.step + SIB, {STATE: sib})

    def w_forward_far(w):
        here = w.block(w.ref, far, piece)
        wait_bytes(here, w.step + FAR, True)
        for j in range(1, Q):
            send(here, here, w.step + PEER, {ROWS: group_r + lax.rem(piece + j, Q)})

    def w_forward_all(w):
        wait_bytes(w.rest, w.step + PEER, True)
        send(w.block(w.ref, far), w.block(w.ref, far), w.step + FAR_SIB, {STATE: sib})

    def w_ready(w):
        wait_bytes(w.block(w.ref, sib), w.step + SIB, True)
        wait_bytes(w.block(w.ref, sib_far), w.step + FAR_SIB, True)

    def w_sent(w):
        wait_bytes(w.block(w.ref, sib), w.step + SIB, False)
        wait_bytes(w.block(w.ref, sib), w.step + FAR_SIB, False)
        wait_bytes(w.block(w.ref, sib, piece), w.step + FAR, False)
        wait_bytes(w.rest, w.step + PEER, False)

    others = pl.ds(0, HALF - HALF // Q)
    wt_in = SimpleNamespace(ref=v.win, block=line_block, step=W1, rest=v.win.at[:, others, :])
    wt_out = SimpleNamespace(ref=v.wout, block=line_block, step=W1 + 4, rest=v.wout.at[:, others, :])
    wt_glu = W1 + 8
    wt_last = SimpleNamespace(
        ref=v.wglu, block=last_block, step=W1 + 15, rest=v.wglu.at[1, pl.ds(0, H // 2 - H // 2 // Q), pl.ds(0, W)]
    )

    def piece_of(ref):
        size = HALF // Q
        return ref.at[:, pl.ds(pl.multiple_of(piece * size, size), size), :]

    w_send(wt_in, w_in, piece_of(w_in))
    w_send(wt_out, w_out, piece_of(w_out))
    for t in (far, sib):
        send(inputs.at[t], v.xin.at[:, cols(me_s, W)], X, {STATE: t})
    own[OWN_WGLU].wait()

    def split_glu(i):
        here = rows_of(i)
        v.glu_wide[...] = v.glu_raw[pl.ds(pl.multiple_of(i * 2 * CHUNK, 2 * CHUNK), 2 * CHUNK), :].astype(F32)
        for k in range(2):
            v.wglu[k, here, cols(me_s, W)] = v.glu_wide[pl.ds(k, CHUNK, stride=2), :].astype(BF16)

    loop(H // CHUNK, split_glu)
    block = last_block(v.wglu, me_s, piece)
    send(block, block, wt_last.step + FAR, {STATE: far})
    send(inputs.at[sib_far], v.xin.at[:, cols(me_s, W)], X, {STATE: sib_far})
    glu_own = glu_block(v.wglu, me_s)
    send(glu_own, glu_own, wt_glu + SIB, {STATE: sib})
    first_three = [lin_block(v.wglu, me_s), gate_block(v.wglu, me_s, 0)]
    for i, block in enumerate(first_three):
        send(block, block, wt_glu + GLU_FAR + i, {STATE: far})

    line = lax.broadcasted_iota(jnp.int32, (CHUNK, T), 0)
    place = lax.broadcasted_iota(jnp.int32, (CHUNK, T), 1)

    def orders(i):
        base = pl.multiple_of(i * CHUNK, CHUNK)
        at = line + base
        v.perm[pl.ds(base, CHUNK), :] = (
            place == lax.rem(at, SEG) * L + lax.div(at, SEG)
        ).astype(F32).astype(BF16)
        v.back[pl.ds(base, CHUNK), :] = (
            at == lax.rem(place, SEG) * L + lax.div(place, SEG)
        ).astype(F32).astype(BF16)
        v.eye[pl.ds(base, CHUNK), :] = (place == at).astype(F32).astype(BF16)

    loop(T // CHUNK, orders)
    channel = lax.broadcasted_iota(jnp.int32, (CHUNK, CH), 0)
    goes_to = lax.broadcasted_iota(jnp.int32, (CHUNK, CH), 1)
    taken = (
        (lax.rem(lax.div(goes_to, HALF), 2) * S + lax.div(goes_to, LANES)) * HALF + lax.rem(goes_to, HALF)
    )

    def shard_order(i):
        base = pl.multiple_of(i * CHUNK, CHUNK)
        v.by_shard[pl.ds(base, CHUNK), :] = (taken == channel + base).astype(F32).astype(BF16)

    loop(CH // CHUNK, shard_order)

    w_forward_far(wt_in)
    w_forward_far(wt_out)

    low = lax.broadcasted_iota(jnp.int32, (SEG, LANES), 1) < HALF
    low1 = lax.broadcasted_iota(jnp.int32, (1, LANES), 1) < HALF
    seg = lax.broadcasted_iota(jnp.int32, (SEG, LANES), 0)

    wait_bytes(v.par_s.at[pl.ds(0, S - 1)], PAR_S, True)
    par_s = v.par_s
    lam, gam, rate, angle = [], [], [], []
    for a in range(NG):
        nu, theta = swap_halves(par_s[2 * a, 0:1, :], par_s[2 * a + 1, 0:1, :], low1)
        rate.append(jnp.exp(nu))
        angle.append(jnp.exp(theta))
        magnitude = jnp.exp(-rate[a])
        lam.append((magnitude * jnp.cos(angle[a]), magnitude * jnp.sin(angle[a])))
        gam.append(jnp.exp(swap_halves(par_s[2 * a, 1:2, :], par_s[2 * a + 1, 1:2, :], low1)[0]))
    skip = jnp.concatenate([par_s[s, 2:3, :] for s in range(S)], axis=1)
    gain, bias = gain_ref[...], bias_ref[...]
    power = [[(jnp.broadcast_to(l[0], (SUB, LANES)), jnp.broadcast_to(l[1], (SUB, LANES))) for l in lam]]
    for _ in range(BITS - 1):
        power.append([cmul(p, p) for p in power[-1]])
    for b in range(BITS):
        for a in range(NG):
            for c in range(2):
                v.pows[b, a, c] = power[b][a][c]

    def raised(exponent):
        result = [(jnp.ones(exponent.shape, F32), jnp.zeros(exponent.shape, F32)) for _ in range(NG)]
        for b in range(BITS):
            hit = (lax.shift_right_logical(exponent, b) & 1) == 1
            for a in range(NG):
                re, im = cmul(result[a], (v.pows[b, a, 0, 0:1, :], v.pows[b, a, 1, 0:1, :]))
                result[a] = (jnp.where(hit, re, result[a][0]), jnp.where(hit, im, result[a][1]))
        return result

    my_bucket = par[pl.ds(SUB + me_s, 1), :]
    len1 = par[pl.ds(SUB + S + me_s, 1), :].astype(jnp.int32)
    my_len = jnp.broadcast_to(len1, (SEG, LANES))
    seg_pow = raised(jnp.clip(my_len - seg * L, 0, L))
    lead_pow = raised(jnp.minimum(my_len, seg * L))
    tail_pow = raised(jnp.maximum(my_len - (seg + 1) * L, 0))
    for a in range(NG):
        ahead = seg_pow[a]
        behind = seg_pow[a]
        for i, d in enumerate(LEVELS):
            for c in range(2):
                v.hs_f[i, a, c] = jnp.where(seg >= d, ahead[c], 0.0)
                v.hs_b[i, a, c] = jnp.where(seg < SEG - d, behind[c], 0.0)
            ahead = cmul(ahead, (pltpu.roll(ahead[0], d, 0), pltpu.roll(ahead[1], d, 0)))
            behind = cmul(behind, (pltpu.roll(behind[0], SEG - d, 0), pltpu.roll(behind[1], SEG - d, 0)))
        for c in range(2):
            v.lead_pow[a, c] = lead_pow[a][c]
            v.tail_pow[a, c] = tail_pow[a][c]

    def lines_of(p):
        return pl.ds(pl.multiple_of(p * SUB, SUB), SUB)

    def carry_copy(way, source, t):
        return pltpu.make_async_remote_copy(
            src_ref=way.msg,
            dst_ref=way.chain.at[source],
            send_sem=way.sent.at[t],
            recv_sem=way.received.at[source],
            device_id={ROWS: lax.div(t, S), STATE: lax.rem(t, S)},
            device_id_type=MESH,
        )

    def exchange(way, values):
        for a in range(NG):
            for c in range(2):
                way.msg[pl.ds(c * NG + a, 1), :] = values[a][c]

        def one(i, carry):
            carry_copy(way, me, me + 1 + i if way.forward else me - 1 - i).start()
            return carry

        lax.fori_loop(0, NR - 1 - me if way.forward else me, one, 0)

    group = min(NR, 4 * SUB)
    low_g = lax.broadcasted_iota(jnp.int32, (group, LANES), 1) < HALF

    def weigh(way):
        def powers(i):
            for j in range(group // S):
                v.row_len[j * S : (j + 1) * S, :] = v.info[i * (group // S) + j]
            both = v.row_len[0:group, :]
            turned = pltpu.roll(both, HALF, 1)
            here = jnp.where(low_g, both, turned)
            lens = jnp.where(low_g, turned, both).astype(jnp.int32)
            p = lax.broadcasted_iota(jnp.int32, (group, LANES), 0) + i * group
            hit = (here == my_bucket) & (my_bucket > 0.5) & ((p < me) if way.forward else (p > me))
            factor = raised(lens)
            at = pl.ds(pl.multiple_of(i * group, SUB), group)
            for a in range(NG):
                v.row_pow[a, at, :] = jnp.where(hit, factor[a][0], 1.0)
                v.row_pow[NG + a, at, :] = jnp.where(hit, factor[a][1], 0.0)
            v.row_hit[at, :] = jnp.where(hit, 1.0, 0.0)

        loop(NR // group, powers)

        def one(i, run):
            p = NR - 1 - i if way.forward else i
            hit = v.row_hit[pl.ds(p, 1), :]
            after = []
            for a in range(NG):
                for c in range(2):
                    for k in range(2):
                        way.weight[c, p, k * NG + a : k * NG + a + 1, :] = hit * run[a][c]
                after.append(cmul((v.row_pow[a, pl.ds(p, 1), :], v.row_pow[NG + a, pl.ds(p, 1), :]), run[a]))
            return tuple(after)

        first = tuple((jnp.ones((1, LANES), F32), jnp.zeros((1, LANES), F32)) for _ in range(NG))
        lax.fori_loop(0, NR, one, first, unroll=4)

    def collect(way):
        def arrive(p, carry):
            carry_copy(way, p, me).wait_recv()
            return carry

        lax.fori_loop(*way.come, arrive, 0)

        def some(i, sums):
            at = pl.ds(i * group, group)
            x = way.chain[at]
            return tuple(
                sums[c] + jnp.sum(jnp.where(way.weight[c, at] == 0.0, 0.0, way.weight[c, at] * x), axis=0)
                for c in range(2)
            )

        zero = jnp.zeros((2 * NG, LANES), F32)
        x, y = lax.fori_loop(0, NR // group, some, (zero, zero))
        sign = 1.0 if way.forward else -1.0
        return [
            (x[a : a + 1] - sign * y[NG + a : NG + a + 1], x[NG + a : NG + a + 1] + sign * y[a : a + 1])
            for a in range(NG)
        ]

    def carries_sent(way):
        def one(t, carry):
            carry_copy(way, me, t).wait_send()
            return carry

        lax.fori_loop(*way.to, one, 0)

    ahead = SimpleNamespace(
        forward=True, msg=v.msg_f, chain=v.chain_f, sent=v.sent_f, received=v.received_f,
        weight=v.weight_f, to=(me + 1, NR), come=(0, me),
    )
    behind = SimpleNamespace(
        forward=False, msg=v.msg_b, chain=v.chain_b, sent=v.sent_b, received=v.received_b,
        weight=v.weight_b, to=(0, me), come=(me + 1, NR),
    )

    pos = lax.broadcasted_iota(jnp.int32, (CHUNK, LANES), 0)
    pos = lax.rem(pos, SEG) * L + lax.div(pos, SEG)

    def valid_of(i, width):
        ok = jnp.where(pos + i * (CHUNK // SEG) < len1, 1.0, 0.0)
        return jnp.concatenate([ok] * (width // LANES), axis=1) if width > LANES else ok

    pass_on()
    w_forward_all(wt_in)
    w_forward_all(wt_out)
    w_forward_far(wt_last)
    wait_bytes(v.info.at[pl.ds(0, Q - 1)], INFO, True)

    own[OWN_X].wait()
    wait_bytes(v.xin.at[:, pl.ds(0, (S - 1) * W)], X, True)
    v.x[...] = nn(v.perm[...], v.xin[...])

    def layer_norm(i):
        rows = rows_of(i)
        x = v.x[rows, :]
        centred = x - jnp.mean(x, -1, keepdims=True)
        inverse = lax.rsqrt(jnp.mean(centred * centred, -1, keepdims=True) + epsilon)
        normed = centred * inverse
        v.normed[rows, :] = normed
        v.inverse[rows, :] = jnp.broadcast_to(inverse, (CHUNK, LANES))
        v.mixed_low[rows, :] = (normed * gain + bias).astype(BF16)

    loop(T // CHUNK, layer_norm, unroll=4)
    own[OWN_WIN].wait()
    w_ready(wt_in)
    v.proj[...] = nt(v.mixed_low[...], v.win[...].reshape(CH, H))
    everyone_in()
    mine_q = v.info.at[pl.ds(pl.multiple_of(group_r, Q), Q)]

    def info_to(d, carry):
        send(mine_q, mine_q, INFO_ALL, {ROWS: lax.rem(me_r + d * Q, R)})
        return carry

    if NB > 1:
        lax.fori_loop(1, NB, info_to, 0)
    by_shard = [
        pltpu.make_async_copy(line_block(v.win, s), v.win_g.at[s], v.here.at[OWN_WIN_G + s]) for s in range(S)
    ]
    for copy in by_shard:
        copy.start()

    lamb = [tuple(jnp.broadcast_to(c, (SEG, LANES)) for c in l) for l in lam]
    gamb = [jnp.broadcast_to(g, (SEG, LANES)) for g in gam]

    def load_c(ref, at):
        return [(ref[at, lanes(a)], ref[at, lanes(NG + a)]) for a in range(NG)]

    def store_c(ref, at, values):
        for a in range(NG):
            ref[at, lanes(a)] = values[a][0]
            ref[at, lanes(NG + a)] = values[a][1]

    def to_g(values):
        return [g for a in range(NG) for g in swap_halves(values[a][0], values[a][1], low)]

    def step_of(k):
        return pl.ds(pl.multiple_of(k * SEG, SEG), SEG)

    zeros = tuple((jnp.zeros((SEG, LANES), F32), jnp.zeros((SEG, LANES), F32)) for _ in range(NG))

    def advance(k, state, proj):
        ok = seg * L + k < my_len
        new = []
        for a in range(NG):
            re, im = cmul(lamb[a], state[a])
            re, im = re + gamb[a] * proj[a][0], im + gamb[a] * proj[a][1]
            new.append((jnp.where(ok, re, state[a][0]), jnp.where(ok, im, state[a][1])))
        return tuple(new)

    def fwd_first(k, state):
        return advance(k, state, load_c(v.proj, step_of(k)))

    ends = lax.fori_loop(0, L, fwd_first, zeros, unroll=4)

    def across(values, table, forward):
        done = []
        for a in range(NG):
            x = values[a]
            for i, d in enumerate(LEVELS):
                shift = d if forward else SEG - d
                other = (pltpu.roll(x[0], shift, 0), pltpu.roll(x[1], shift, 0))
                factor = (table[i, a, 0], table[i, a, 1])
                add = cmul(factor, other) if forward else conj_mul(factor, other)
                x = (x[0] + add[0], x[1] + add[1])
            done.append(x)
        return done

    ends = across(ends, v.hs_f, True)
    exchange(ahead, [tuple(x[SEG - 1 : SEG, :] for x in ends[a]) for a in range(NG)])
    before = [
        tuple(jnp.where(seg > 0, pltpu.roll(x, 1, 0), 0.0) for x in ends[a]) for a in range(NG)
    ]
    to_state(lambda t: cot.at[t], v.cin.at[:, cols(me_s, W)], C)
    own[OWN_C].wait()
    far_blocks = [lin_block(v.wglu, far), gate_block(v.wglu, far, 0)]
    for i, block in enumerate(far_blocks):
        wait_bytes(block, wt_glu + GLU_FAR + i, True)
        send(block, block, wt_glu + GLU_SIB + i, {STATE: sib})
    w_forward_all(wt_last)
    v.mixed_t[...] = nt(v.eye[...], v.mixed_low[...]).astype(BF16)
    if NB > 1:
        wait_bytes(v.info.at[pl.ds(0, R - Q)], INFO_ALL, True)
    weigh(ahead)
    starts = collect(ahead)
    state = []
    for a in range(NG):
        add = cmul((v.lead_pow[a, 0], v.lead_pow[a, 1]), starts[a])
        state.append((before[a][0] + add[0], before[a][1] + add[1]))
    store_c(v.state, pl.ds(0, SEG), state)

    def fwd_second(k, state):
        state = advance(k, state, load_c(v.proj, step_of(k)))
        store_c(v.state, step_of(k + 1), state)
        for a in range(NG):
            v.state_low[step_of(k), lanes(a)] = state[a][0].astype(BF16)
            v.state_low[step_of(k), lanes(NG + a)] = (-state[a][1]).astype(BF16)
        return state

    lax.fori_loop(0, L, fwd_second, tuple(state), unroll=4)

    own[OWN_WOUT].wait()
    w_ready(wt_out)
    v.wide[...] = nn(v.state_low[...], v.wout[...].reshape(CH, H))

    def gelu(i):
        rows = rows_of(i)
        mixed_in = v.normed[rows, :] * gain + bias
        mixed = v.wide[rows, :] + skip * mixed_in
        cdf = 0.5 * (1.0 + lax.erf(mixed * (1.0 / math.sqrt(2.0))))
        density = jnp.exp(-0.5 * mixed * mixed) * (1.0 / math.sqrt(2.0 * math.pi))
        v.act[rows, :] = (mixed * cdf).astype(BF16)
        v.dgelu[rows, :] = cdf + mixed * density

    loop(T // CHUNK, gelu, unroll=4)
    wait_bytes(glu_block(v.wglu, sib), wt_glu + SIB, True)
    for i, block in enumerate([lin_block(v.wglu, sib_far), gate_block(v.wglu, sib_far, 0)]):
        wait_bytes(block, wt_glu + GLU_SIB + i, True)
    wait_bytes(last_block(v.wglu, sib_far), wt_last.step + FAR_SIB, True)
    for k in range(2):
        v.pre[k] = nn(v.act[...], v.wglu[k])

    def glu(i):
        rows = rows_of(i)
        ok = valid_of(i, W)
        for s in range(S):
            here = slice(s * W, (s + 1) * W)
            linear = v.pre[0, rows, here] + par_s[s, 3:4, :]
            gate = v.pre[1, rows, here] + par_s[s, 4:5, :]
            share = jax.nn.sigmoid(gate)
            value = linear * share
            v.out_low[rows, here] = (ok * (v.x[rows, here] + value)).astype(BF16)
            v.pre[0, rows, here] = ok * share
            v.pre[1, rows, here] = ok * (value * (1.0 - share))

    loop(T // CHUNK, glu, unroll=4)

    def give_back(low_ref, nat, result, own_which):
        nat[...] = nn(v.back[...], low_ref[...]).astype(BF16)
        copy = pltpu.make_async_copy(nat.at[:, cols(me_s, W)], result.at[me_s], v.here.at[own_which])
        copy.start()
        return copy

    def give_to(nat, result, which, t):
        send(nat.at[:, cols(t, W)], result.at[me_s], which, {STATE: t})

    out_copy = give_back(v.out_low, v.out_nat, out_ref, OWN_OUT)
    give_to(v.out_nat, out_ref, OUT, far)
    give_to(v.out_nat, out_ref, OUT, sib)
    give_to(v.out_nat, out_ref, OUT, sib_far)
    weigh(behind)
    v.act_t[...] = nt(v.eye[...], v.act[...]).astype(BF16)
    v.state_g[...] = nn(v.state_low[...], v.by_shard[...]).astype(BF16)
    wait_bytes(v.cin.at[:, pl.ds(0, (S - 1) * W)], C, True)
    v.wide[...] = nn(v.perm[...], v.cin[...])

    def glu_back(i):
        rows = rows_of(i)
        dout = v.wide[rows, :]
        for k in range(2):
            v.d_pre[k, rows, :] = (dout * v.pre[k, rows, :]).astype(BF16)

    loop(T // CHUNK, glu_back, unroll=4)

    R4 = R // 4 if R % 4 == 0 else R // 2
    sizes = {None: R4, AX_X: NG, AX_Y: 2, AX_Z: 2 if R % 4 == 0 else 1}

    def places(r, b):
        return {AX_X: b, AX_Y: lax.rem(r, 2), AX_Z: lax.rem(lax.div(r, 2), sizes[AX_Z]), None: lax.div(r, 2 * sizes[AX_Z])}

    mine = places(me_r, lax.div(me_s, 2))
    partner = {
        AX_X: {STATE: far},
        AX_Y: {ROWS: pair_r},
        AX_Z: {ROWS: me_r + 2 - 4 * mine[AX_Z]},
    }

    def slot(route, r, b):
        at, index = places(r, b), 0
        for axis in route.axes[1:] + route.others:
            index = index * sizes[axis] + at[axis]
        return at[route.axes[0]], index

    def owner(route, n):
        at = dict(mine)
        for axis in reversed(route.others):
            at[axis] = lax.rem(n, sizes[axis])
            n = lax.div(n, sizes[axis])
        return {ROWS: at[AX_Y] + 2 * (at[AX_Z] + sizes[AX_Z] * at[None]), STATE: 2 * at[AX_X] + mine_s}

    for part in parts:
        for route in part.routes:
            route.others = tuple(axis for axis in sizes if axis not in route.axes)
            route.number = 0
            for axis in route.others:
                route.number = route.number * sizes[axis] + mine[axis]

    def first_send(part):
        for b in range(NG):
            send(part.full.at[:, cols(2 * b + 1 - mine_s, LANES)], part.r1.at[b], part.step, {STATE: sib})

    def first_wait(part):
        wait_bytes(part.r1, part.step, True)

    def first_sum(route):
        part = route.part

        def one(r):
            rows = pl.ds(pl.multiple_of(r * HB + route.first, route.lines), route.lines)
            for b in range(NG):
                total = part.full[rows, cols(2 * b + mine_s, LANES)].astype(F32) + part.r1[b, rows, :].astype(F32)
                route.a[0][slot(route, r, b)] = total.astype(gdt)

        loop(R, one, unroll=4)
        pass_half(route, 0)

    def pass_half(route, i):
        axis = route.axes[i]
        send(route.a[i].at[1 - mine[axis]], route.r[i], route.step + i, partner[axis])

    def next_sum(route, i):
        wait_bytes(route.r[i], route.step + i, True)
        count, last = route.r[i].shape[0], i + 1 == len(route.axes)

        def one(n):
            total = route.a[i][mine[route.axes[i]], n].astype(F32) + route.r[i][n].astype(F32)
            to = n if last else (lax.div(n, count // 2), lax.rem(n, count // 2))
            route.a[i + 1][to] = total.astype(gdt)

        loop(count, one, unroll=4)
        if not last:
            pass_half(route, i + 1)
            return
        done = route.a[i + 1]
        route.last[route.number] = done[route.number]

        def give(d, carry):
            n = d + jnp.where(d >= route.number, 1, 0)
            send(done.at[n], route.last.at[route.number], route.step + len(route.axes), owner(route, n))
            return carry

        lax.fori_loop(0, count - 1, give, 0)

    def last_sum(route):
        count = route.last.shape[0]
        if count > 1:
            wait_bytes(route.last.at[pl.ds(0, count - 1)], route.step + len(route.axes), True)

        def one(n, total):
            return total + route.last[n].astype(F32)

        total = lax.fori_loop(0, count, one, jnp.zeros((route.lines, LANES), F32), unroll=4)
        gsum[route.first : route.first + route.lines, route.part.at : route.part.at + LANES] = total

    def all_sent(part):
        wait_bytes(part.r1, part.step, False)
        for route in part.routes:
            for i in range(len(route.axes)):
                wait_bytes(route.r[i], route.step + i, False)
            if route.last.shape[0] > 1:
                wait_bytes(route.last.at[pl.ds(0, route.last.shape[0] - 1)], route.step + len(route.axes), False)

    def glu_first():
        for part in (g_lin, g_gate):
            first_wait(part)
            first_sum(part.routes[0])

    def glu_next():
        for part in (g_lin, g_gate):
            next_sum(part.routes[0], 0)

    v.wide[...] = nt(v.d_pre[0], v.wglu[0]) + nt(v.d_pre[1], v.wglu[1])

    def gelu_back(i, total):
        rows = rows_of(i)
        d_mixed = v.wide[rows, :] * v.dgelu[rows, :]
        v.d_mixed[rows, :] = d_mixed
        v.d_rec[rows, :] = d_mixed.astype(BF16)
        return total + fold(d_mixed * (v.normed[rows, :] * gain + bias))

    d_skip = lax.fori_loop(0, T // CHUNK, gelu_back, jnp.zeros((SUB, H), F32), unroll=4)
    d_skip = jnp.sum(d_skip, axis=0, keepdims=True)
    v.source[...] = nt(v.d_rec[...], v.wout[...].reshape(CH, H))
    def retreat(k, source, carry):
        ok = seg * L + k < my_len
        adjoint, new = [], []
        for a in range(NG):
            re, im = carry[a][0] + source[a][0], carry[a][1] - source[a][1]
            adjoint.append((re, im))
            nre, nim = conj_mul(lamb[a], (re, im))
            new.append((jnp.where(ok, nre, re), jnp.where(ok, nim, im)))
        return ok, adjoint, tuple(new)

    def bwd_first(i, carry):
        k = L - 1 - i
        return retreat(k, load_c(v.source, step_of(k)), carry)[2]

    heads = lax.fori_loop(0, L, bwd_first, zeros, unroll=4)
    heads = across(heads, v.hs_b, False)
    exchange(behind, [tuple(x[0:1, :] for x in heads[a]) for a in range(NG)])
    after = [
        tuple(jnp.where(seg < SEG - 1, pltpu.roll(x, SEG - 1, 0), 0.0) for x in heads[a])
        for a in range(NG)
    ]
    for k, part in ((0, g_lin), (1, g_gate)):
        part.full[...] = nn(v.act_t[...], v.d_pre[k]).astype(gdt)
        first_send(part)
    g_out.full[...] = tn(v.d_rec[...], v.state_g[...]).astype(gdt)
    first_send(g_out)
    glu_first()
    first_wait(g_out)
    first_sum(g_out.routes[0])
    omegas = collect(behind)
    carry = []
    for a in range(NG):
        add = conj_mul((v.tail_pow[a, 0], v.tail_pow[a, 1]), omegas[a])
        carry.append((after[a][0] + add[0], after[a][1] + add[1]))

    def bwd_second(i, item):
        k = L - 1 - i
        carry, sums = item
        ok, adjoint, carry = retreat(k, load_c(v.source, step_of(k)), carry)
        previous = load_c(v.state, step_of(k))
        proj = load_c(v.proj, step_of(k))
        new_sums, low_out = [], []
        for a in range(NG):
            re, im = (jnp.where(ok, x, 0.0) for x in adjoint[a])
            dre, dim = conj_mul(previous[a], (re, im))
            dg = re * proj[a][0] + im * proj[a][1]
            new_sums.append(tuple(x + fold(y) for x, y in zip(sums[a], (dre, dim, dg))))
            low_out.append((gamb[a] * re, gamb[a] * im))
        low_out = to_g(low_out)
        for s in range(S):
            v.d_proj[step_of(k), lanes(s)] = low_out[s].astype(BF16)
        return carry, tuple(new_sums)

    zero = jnp.zeros((SUB, LANES), F32)
    _, sums = lax.fori_loop(
        0, L, bwd_second, (tuple(carry), tuple((zero, zero, zero) for _ in range(NG))), unroll=2
    )

    g_in.full[...] = nn(v.mixed_t[...], v.d_proj[...]).astype(gdt)
    first_send(g_in)
    for copy in by_shard:
        copy.wait()
    v.wide[...] = nn(v.d_proj[...], v.win_g[...].reshape(CH, H))
    glu_next()

    def norm_back(i, totals):
        rows = rows_of(i)
        d_mixed_in = v.wide[rows, :] + skip * v.d_mixed[rows, :]
        normed = v.normed[rows, :]
        inverse = jnp.concatenate([v.inverse[rows, :]] * (H // LANES), axis=1)
        g = d_mixed_in * gain
        first = jnp.mean(g, -1, keepdims=True)
        second = jnp.mean(g * normed, -1, keepdims=True)
        v.din_low[rows, :] = (inverse * (g - first - normed * second)).astype(BF16)
        return totals[0] + fold(d_mixed_in * normed), totals[1] + fold(d_mixed_in)

    zero_h = jnp.zeros((SUB, H), F32)
    d_gain, d_nbias = lax.fori_loop(0, T // CHUNK, norm_back, (zero_h, zero_h), unroll=4)
    d_gain = jnp.sum(d_gain, axis=0, keepdims=True)
    d_nbias = jnp.sum(d_nbias, axis=0, keepdims=True)
    ones = jnp.ones((2 * SUB, T), BF16)
    d_bias = [nn(ones, v.d_pre[k])[0:1, :] for k in range(2)]
    small = v.small
    small[...] = jnp.zeros((S, SUB, LANES), F32)
    for a in range(NG):
        sr, si, sg = (jnp.sum(x, axis=0, keepdims=True) for x in sums[a])
        d_nu = -rate[a] * (sr * lam[a][0] + si * lam[a][1])
        d_theta = angle[a] * (si * lam[a][0] - sr * lam[a][1])
        pair = swap_halves(d_nu, d_theta, low1)
        pair_g = swap_halves(gam[a] * sg, jnp.zeros_like(sg), low1)
        for u in range(2):
            small[2 * a + u, 0:1, :] = pair[u]
            small[2 * a + u, 1:2, :] = pair_g[u]
    for s in range(S):
        here = slice(s * W, (s + 1) * W)
        small[s, 2:3, :] = d_skip[:, here]
        small[s, 3:4, :] = d_bias[0][:, here]
        small[s, 4:5, :] = d_bias[1][:, here]
        small[s, 5:6, :] = d_gain[:, here]
        small[s, 6:7, :] = d_nbias[:, here]
    v.small_r[me_s] = small[...]
    to_state(lambda t: small, v.small_r.at[me_s], SM)
    first_wait(g_in)
    for route in g_in.routes:
        first_sum(route)
    next_sum(g_out.routes[0], 0)
    din_copy = give_back(v.din_low, v.din_nat, din_ref, OWN_DIN)
    for t in (far, sib):
        give_to(v.din_nat, din_ref, DIN, t)
    if len(g_gate.routes[0].axes) > 1:
        next_sum(g_gate.routes[0], 1)
    wait_bytes(v.small_r.at[pl.ds(0, S - 1)], SM, True)
    group = v.small_r[0]
    for s in range(1, S):
        group = group + v.small_r[s]
    small2 = v.small2
    v.group[...] = group
    small2[0:SUB, :] = v.group[me_s]
    for s in range(S):
        small2[SUB + s : SUB + s + 1, :] = group[s, 5:6, :]
        small2[SUB + S + s : SUB + S + s + 1, :] = group[s, 6:7, :]
    v.small2_r[piece] = small2[...]
    for j in range(1, Q):
        send(small2, v.small2_r.at[piece], SN, {ROWS: group_r + lax.rem(piece + j, Q)})
    for route in g_in.routes:
        next_sum(route, 0)
    wait_bytes(v.small2_r.at[pl.ds(0, Q - 1)], SN, True)
    small3 = v.small2_r[0]
    for j in range(1, Q):
        small3 = small3 + v.small2_r[j]
    block = lax.div(me_r, Q)
    v.small3_r[block] = small3

    def small_blocks(d, carry):
        send(v.small3_r.at[block], v.small3_r.at[block], SB, {ROWS: lax.rem(me_r + d * Q, R)})
        return carry

    lax.fori_loop(1, NB, small_blocks, 0)
    if len(g_out.routes[0].axes) > 1:
        next_sum(g_out.routes[0], 1)
    give_to(v.din_nat, din_ref, DIN, sib_far)
    for part in (g_lin, g_gate, g_out):
        last_sum(part.routes[0])
    if NB > 1:
        wait_bytes(v.small3_r.at[pl.ds(0, NB - 1)], SB, True)
    total = v.small3_r[0]
    for i in range(1, NB):
        total = total + v.small3_r[i]
    vec[...] = total
    for route in g_in.routes:
        last_sum(route)

    out_copy.wait()
    din_copy.wait()
    wait_bytes(out_ref.at[pl.ds(0, S - 1)], OUT, True)
    wait_bytes(din_ref.at[pl.ds(0, S - 1)], DIN, True)
    wait_bytes(out_ref.at[pl.ds(0, S - 1)], OUT, False)
    wait_bytes(din_ref.at[pl.ds(0, S - 1)], DIN, False)
    wait_bytes(v.par_s.at[pl.ds(0, S - 1)], PAR_S, False)
    wait_bytes(v.info.at[pl.ds(0, Q - 1)], INFO, False)
    if NB > 1:
        wait_bytes(v.info.at[pl.ds(0, R - Q)], INFO_ALL, False)
    wait_bytes(v.xin.at[:, pl.ds(0, (S - 1) * W)], X, False)
    for w in (wt_in, wt_out):
        w_sent(w)
    wait_bytes(glu_own, wt_glu + SIB, False)
    for i, block in enumerate(far_blocks):
        wait_bytes(block, wt_glu + GLU_FAR + i, False)
        wait_bytes(block, wt_glu + GLU_SIB + i, False)
    wait_bytes(last_block(v.wglu, far), wt_last.step + FAR_SIB, False)
    wait_bytes(last_block(v.wglu, far, piece), wt_last.step + FAR, False)
    wait_bytes(wt_last.rest, wt_last.step + PEER, False)
    wait_bytes(v.cin.at[:, pl.ds(0, (S - 1) * W)], C, False)
    carries_sent(ahead)
    carries_sent(behind)
    wait_bytes(v.small_r.at[pl.ds(0, S - 1)], SM, False)
    wait_bytes(v.small2_r.at[pl.ds(0, Q - 1)], SN, False)
    if NB > 1:
        wait_bytes(v.small3_r.at[pl.ds(0, NB - 1)], SB, False)
    for part in parts:
        all_sent(part)


def routes_of(R, H):
    HB = H // R
    if HB % (4 * SUB) == 0:
        routes = [(0, (AX_Y,), 0, HB // 2), (0, (AX_Z if R % 4 == 0 else AX_X,), HB // 2, HB // 2)]
    else:
        routes = [(0, (AX_Y,), 0, HB)]
    if R % 4 == 0:
        return routes + [(1, (AX_X, AX_Y), 0, HB), (2, (AX_Y,), 0, HB), (3, (AX_Z, AX_Y), 0, HB)]
    return routes + [(1, (AX_X,), 0, HB), (2, (AX_Y,), 0, HB), (3, (AX_X,), 0, HB)]


def run_block(dims, *args):
    R, S, T, H, W = dims.R, dims.S, dims.T, dims.H, dims.W
    NR, NG, HB = R * S, S // 2, H // R
    CH, levels = S * LANES, len(LEVELS)
    gdt = BF16 if HB % (2 * SUB) == 0 else F32
    dims.gdt = gdt
    bits = T.bit_length()
    shapes = dict(
        xin=((T, H), BF16),
        cin=((T, H), BF16),
        win=((2, S * HALF, H), BF16),
        wout=((2, S * HALF, H), BF16),
        win_g=((S, 2, HALF, H), BF16),
        by_shard=((CH, CH), BF16),
        state_g=((T, CH), BF16),
        wglu=((2, H, H), BF16),
        glu_raw=((2 * H, W), BF16),
        glu_wide=((2 * CHUNK, W), F32),
        perm=((T, T), BF16),
        back=((T, T), BF16),
        eye=((T, T), BF16),
        mixed_t=((H, T), BF16),
        act_t=((H, T), BF16),
        nu=((1, HALF), F32),
        theta=((1, HALF), F32),
        gamma=((1, HALF), F32),
        skip=((1, W), F32),
        glu_bias=((2, W), F32),
        gain=((1, H), F32),
        bias=((1, H), F32),
        par=((2 * SUB, LANES), F32),
        par_s=((S, 2 * SUB, LANES), F32),
        pows=((bits, NG, 2, SUB, LANES), F32),
        hs_f=((levels, NG, 2, SEG, LANES), F32),
        hs_b=((levels, NG, 2, SEG, LANES), F32),
        lead_pow=((NG, 2, SEG, LANES), F32),
        tail_pow=((NG, 2, SEG, LANES), F32),
        row_pow=((2 * NG, NR, LANES), F32),
        row_hit=((NR, LANES), F32),
        row_len=((4 * SUB, LANES), F32),
        info=((R, S, LANES), F32),
        msg_f=((2 * NG, LANES), F32),
        msg_b=((2 * NG, LANES), F32),
        chain_f=((NR, 2 * NG, LANES), F32),
        chain_b=((NR, 2 * NG, LANES), F32),
        weight_f=((2, NR, 2 * NG, LANES), F32),
        weight_b=((2, NR, 2 * NG, LANES), F32),
        x=((T, H), F32),
        normed=((T, H), F32),
        inverse=((T, LANES), F32),
        mixed_low=((T, H), BF16),
        wide=((T, max(H, CH)), F32),
        proj=((T, CH), F32),
        state=((T + SEG, CH), F32),
        state_low=((T, CH), BF16),
        act=((T, H), BF16),
        dgelu=((T, H), F32),
        pre=((2, T, H), F32),
        out_low=((T, H), BF16),
        out_nat=((T, H), BF16),
        d_pre=((2, T, H), BF16),
        d_mixed=((T, H), F32),
        d_rec=((T, H), BF16),
        source=((T, CH), F32),
        d_proj=((T, CH), BF16),
        din_low=((T, H), BF16),
        din_nat=((T, H), BF16),
        small=((S, SUB, LANES), F32),
        small_r=((S, S, SUB, LANES), F32),
        group=((S, SUB, LANES), F32),
        small2=((2 * SUB, LANES), F32),
        small2_r=((4, 2 * SUB, LANES), F32),
        small3_r=((R // 2, 2 * SUB, LANES), F32),
    )
    scalars = dict(bucket=(S,), lengths=(S,))
    flags = dict(block_in=1, all_in=1)
    copies = dict(here=OWN_WIN_G + S, sent=G2 + 20, received=G2 + 20, sent_f=NR, received_f=NR, sent_b=NR, received_b=NR)
    dims.names = [*shapes, *scalars, *flags, *copies]
    parts = []
    for _ in range(4):
        parts += [(H, CH), (NG, H, LANES)]
    routes = routes_of(R, H)
    for _, axes, _, lines in routes:
        left = [2 * R >> (i + 1) for i in range(len(axes))]
        parts += [(2, n, lines, LANES) for n in left] + [(left[-1], lines, LANES)]
        parts += [(n, lines, LANES) for n in left] + [(left[-1], lines, LANES)]
    scratch = [pltpu.VMEM(shape, dtype) for shape, dtype in shapes.values()]
    scratch += [pltpu.SMEM(shape, jnp.int32) for shape in scalars.values()]
    scratch += [pltpu.SemaphoreType.REGULAR for _ in flags]
    scratch += [pltpu.SemaphoreType.DMA((n,)) for n in copies.values()]
    scratch += [pltpu.VMEM(shape, gdt) for shape in parts]
    any_spec = pl.BlockSpec(memory_space=pl.ANY)
    vmem = pl.BlockSpec(memory_space=pltpu.VMEM)
    macs = T * H * (2 * CH + 2 * H) * 3 + 4 * T * T * H
    return pl.pallas_call(
        functools.partial(block_kernel, dims),
        out_shape=(
            jax.ShapeDtypeStruct((S, T, W), BF16),
            jax.ShapeDtypeStruct((S, T, W), BF16),
            jax.ShapeDtypeStruct((HB, 4 * LANES), F32),
            jax.ShapeDtypeStruct((2 * SUB, LANES), F32),
        ),
        in_specs=[any_spec] * 14,
        out_specs=(any_spec, any_spec, vmem, vmem),
        scratch_shapes=scratch,
        compiler_params=pltpu.CompilerParams(
            collective_id=0, has_side_effects=True, vmem_limit_bytes=56 * 2**20
        ),
        cost_estimate=pl.CostEstimate(flops=2 * macs, bytes_accessed=8 * 2**20, transcendentals=4 * T * H),
    )(*args)


def on_device(
    inputs,
    bucket,
    lengths,
    nu_log,
    theta_log,
    gamma_log,
    in_proj,
    out_proj,
    skip,
    norm_gain,
    norm_bias,
    glu_weight,
    glu_bias,
    output_cotangent,
):
    row_count, seq, part = inputs.shape
    width = norm_gain.shape[0]
    chans = nu_log.shape[0]
    R, S = lax.axis_size(ROWS), lax.axis_size(STATE)
    dims = SimpleNamespace(R=R, S=S, T=seq, H=width, W=part)
    assert row_count == S and 2 * chans == LANES and part == LANES and S % 2 == 0 and R % 2 == 0

    outputs, d_norm, gsum, vec = run_block(
        dims,
        inputs,
        output_cotangent,
        in_proj.transpose(1, 2, 0),
        out_proj,
        glu_weight.reshape(2 * width, part),
        bucket,
        lengths,
        nu_log[None],
        theta_log[None],
        gamma_log[None],
        skip[None],
        glu_bias,
        norm_gain[None],
        norm_bias[None],
    )
    return finish(dims, lengths, outputs, d_norm, output_cotangent, gsum, vec)


def finish_kernel(dims, *refs):
    S, T, HB = dims.S, dims.T, dims.H // dims.R
    (lengths, out_in, d_norm, cot, gsum, vec) = refs[:6]
    (out, d_inputs, d_nu, d_theta, d_gamma, d_in, d_out, d_skip, d_gain, d_bias, d_glu, d_glu_bias) = refs[6:]
    out[...] = out_in[...]
    for row in range(S):
        for first in range(0, T, CHUNK):
            lines = slice(first, first + CHUNK)
            place = lax.broadcasted_iota(jnp.int32, (CHUNK, LANES), 0) + first
            direct = jnp.where(place < lengths[row], cot[row, lines, :].astype(F32), 0.0)
            d_inputs[row, lines, :] = d_norm[row, lines, :].astype(F32) + direct
    d_nu[...] = vec[0:1, 0:HALF]
    d_theta[...] = pltpu.roll(vec[0:1, :], HALF, 1)[:, 0:HALF]
    d_gamma[...] = vec[1:2, 0:HALF]
    d_skip[...] = vec[2:3, :]
    d_glu_bias[...] = vec[3:5, :]
    for s in range(S):
        here = slice(s * LANES, (s + 1) * LANES)
        d_gain[:, here] = vec[SUB + s : SUB + s + 1, :]
        d_bias[:, here] = vec[SUB + S + s : SUB + S + s + 1, :]
    both = gsum[:, 0:LANES]
    d_in[pl.ds(0, HB, stride=2), :] = both[:, 0:HALF]
    d_in[pl.ds(1, HB, stride=2), :] = pltpu.roll(both, HALF, 1)[:, 0:HALF]
    d_out[...] = gsum[:, LANES : 2 * LANES].T
    d_glu[pl.ds(0, HB, stride=2), :] = gsum[:, 2 * LANES : 3 * LANES]
    d_glu[pl.ds(1, HB, stride=2), :] = gsum[:, 3 * LANES : 4 * LANES]


def finish(dims, lengths, outputs, d_norm, cot, gsum, vec):
    R, S, T, H, W = dims.R, dims.S, dims.T, dims.H, dims.W
    HB = H // R
    vmem = pl.BlockSpec(memory_space=pltpu.VMEM)
    small = [(1, HALF)] * 3 + [(2 * HB, HALF), (LANES, HB), (1, W), (1, H), (1, H), (2 * HB, W), (2, W)]
    got = pl.pallas_call(
        functools.partial(finish_kernel, dims),
        out_shape=(
            jax.ShapeDtypeStruct((S, T, W), BF16),
            jax.ShapeDtypeStruct((S, T, W), F32),
            *(jax.ShapeDtypeStruct(shape, F32) for shape in small),
        ),
        in_specs=[pl.BlockSpec(memory_space=pltpu.SMEM)] + [vmem] * 5,
        out_specs=(vmem,) * 12,
    )(lengths, outputs, d_norm, cot, gsum, vec)
    out, d_inputs, d_nu, d_theta, d_gamma, d_in, d_out, d_skip, d_gain, d_bias, d_glu, d_glu_bias = got
    return (
        out,
        d_inputs,
        d_nu.reshape(HALF),
        d_theta.reshape(HALF),
        d_gamma.reshape(HALF),
        d_in.reshape(HB, 2, HALF),
        d_out.reshape(2, HALF, HB),
        d_skip.reshape(W),
        d_gain.reshape(H),
        d_bias.reshape(H),
        d_glu.reshape(HB, 2, W),
        d_glu_bias,
    )


def solution(mesh):
    return jax.shard_map(
        on_device,
        mesh=mesh,
        in_specs=(
            P(ROWS, None, STATE),
            P(ROWS),
            P(ROWS),
            P(STATE),
            P(STATE),
            P(STATE),
            P(None, None, STATE),
            P(None, STATE, None),
            P(STATE),
            P(),
            P(),
            P(None, None, STATE),
            P(None, STATE),
            P(ROWS, None, STATE),
        ),
        out_specs=(
            P(ROWS, None, STATE),
            P(ROWS, None, STATE),
            P(STATE),
            P(STATE),
            P(STATE),
            P(ROWS, None, STATE),
            P(None, STATE, ROWS),
            P(STATE),
            P(),
            P(),
            P(ROWS, None, STATE),
            P(None, STATE),
        ),
        check_vma=False,
    )
```
